32 devices in a mesh: patch: 8 (over y, x, core), frame: 4 (over z).
Axes of the slice: x: 2, y: 2, z: 4, core: 2. Of those that a mesh axis runs over, the one named last changes fastest.
Arguments:
- block_input: float32 [20, 512, 1152], P('frame', 'patch'), may hold values from -6 to 6
- out_cotangent: float32 [20, 512, 1152], P('frame', 'patch'), may hold values from -6 to 6
- caption: float32 [4, 120, 1152], replicated, may hold values from -6 to 6
- cond: float32 [4, 1152], replicated, may hold values from -6 to 6
- ada_weight: float32 [1152, 6912], P('patch'), may hold values from -0.1875 to 0.1875
- ada_bias: float32 [6912], P('patch'), may hold values from -3 to 3
- qkv_weight: float32 [1152, 3456], P('patch'), may hold values from -0.1875 to 0.1875
- q_bias: float32 [1152], P('patch'), may hold values from -3 to 3
- v_bias: float32 [1152], P('patch'), may hold values from -3 to 3
- attn_out_weight: float32 [1152, 1152], P('patch'), may hold values from -0.5 to 0.5
- attn_out_bias: float32 [1152], P('patch'), may hold values from -3 to 3
- cross_q_weight: float32 [1152, 1152], P('patch'), may hold values from -0.1875 to 0.1875
- cross_q_bias: float32 [1152], P('patch'), may hold values from -3 to 3
- cross_kv_weight: float32 [1152, 2304], P('patch'), may hold values from -0.1875 to 0.1875
- cross_v_bias: float32 [1152], P('patch'), may hold values from -3 to 3
- cross_out_weight: float32 [1152, 1152], P('patch'), may hold values from -0.5 to 0.5
- cross_out_bias: float32 [1152], P('patch'), may hold values from -3 to 3
- fc1_weight: float32 [1152, 4608], P('patch'), may hold values from -0.1875 to 0.1875
- fc1_bias: float32 [4608], P('patch'), may hold values from -3 to 3
- fc2_weight: float32 [4608, 1152], P('patch'), may hold values from -0.09375 to 0.09375
- fc2_bias: float32 [1152], P('patch'), may hold values from -3 to 3
- frame_slot: int32 [20], P('frame'), may hold values from 0 to 17, as said below
- clip_id: int32 [512], P('patch'), may hold values from 0 to 3, never falling along the last dimension, each value on 1 to 256 neighbouring positions
- patch_mask: int32 [512], P('patch'), may hold values 0 or 1
- caption_mask: int32 [4, 120], replicated, may hold values from 0 to 1, as said below
Outputs:
- block_out: float32 [20, 512, 1152], P('frame', 'patch')
- input_grad: float32 [20, 512, 1152], P('frame', 'patch')
- caption_grad: float32 [4, 120, 1152], replicated
- cond_grad: float32 [4, 1152], replicated
- ada_weight_grad: float32 [1152, 6912], P('patch')
- ada_bias_grad: float32 [6912], P('patch')
- qkv_weight_grad: float32 [1152, 3456], P('patch')
- q_bias_grad: float32 [1152], P('patch')
- v_bias_grad: float32 [1152], P('patch')
- attn_out_weight_grad: float32 [1152, 1152], P('patch')
- attn_out_bias_grad: float32 [1152], P('patch')
- cross_q_weight_grad: float32 [1152, 1152], P('patch')
- cross_q_bias_grad: float32 [1152], P('patch')
- cross_kv_weight_grad: float32 [1152, 2304], P('patch')
- cross_v_bias_grad: float32 [1152], P('patch')
- cross_out_weight_grad: float32 [1152, 1152], P('patch')
- cross_out_bias_grad: float32 [1152], P('patch')
- fc1_weight_grad: float32 [1152, 4608], P('patch')
- fc1_bias_grad: float32 [4608], P('patch')
- fc2_weight_grad: float32 [4608, 1152], P('patch')
- fc2_bias_grad: float32 [1152], P('patch')
The draws below stay inside these ranges and needn't reach their ends.
Inputs may be any that keep to these rules, and one draw needn't show every extreme that they name: `frame_slot`: each of the 17 frames is named by exactly one slot, in increasing order along the slots; the other slots hold 17 and are empty; every index of frame holds at least one frame. `clip_id`: clip numbers never fall along the columns. `caption_mask`: each row is ones followed by zeros, with at least 30 ones.
All inputs are finite; a program needn't handle non-finite values. No bound on the sum of `patch_mask` on one device may be relied on, other than what follows from the above.
Results may differ from the reference program's by a relative error of at most 0.0003.
Values sent between devices are 32-bit elements; how exact they have to be, the bound alone decides.
A program may use at most 448 MiB of HBM per device.

```python
import math
from functools import partial
import jax
import jax.numpy as jnp
import numpy as np
from jax import lax

D = 1152
H = 16
FF = 4608
HD = 72
CAP = 120
FRAMES = 17
CLIPS = 4
SLOTS = 20
COLS = 512


def draw_frame_slot(key, part):
    key = jax.random.fold_in(key, 11)
    order = jax.random.permutation(key, SLOTS)
    empty = order < SLOTS - FRAMES
    filled = jnp.where(empty, 0, 1).astype(jnp.int32)
    rank = jnp.cumsum(filled) - 1
    return jnp.where(empty, FRAMES, rank).astype(jnp.int32)


def draw_caption_mask(key, part):
    key = jax.random.fold_in(key, 23)
    lengths = jax.random.randint(key, (CLIPS,), CAP // 4, CAP + 1)
    positions = jnp.arange(CAP, dtype=jnp.int32)
    return (positions[None, :] < lengths[:, None]).astype(jnp.int32)


def with_ends(drawn, rng, low, high):
    longest = drawn.shape.index(max(drawn.shape))
    spots = []
    for shift in (0, 1):
        where = [jax.random.randint(jax.random.fold_in(rng, axis), (), 0, length) for axis, length in enumerate(drawn.shape)]
        where[longest] = (where[longest] + shift) % drawn.shape[longest]
        spots.append(tuple(where))
    return drawn.at[spots[0]].set(low).at[spots[1]].set(high)


def steps_of(own_key, dims, split, smallest, high):
    gain = 1.0
    for dim, blocks in split:
        steps = jax.random.uniform(jax.random.fold_in(jax.random.fold_in(own_key, 6), dim), (blocks,), jnp.float32, smallest / len(split), high / len(split))
        gain = gain * jnp.repeat(jnp.exp(steps), dims[dim] // blocks).reshape((-1,) + (1,) * (len(dims) - 1 - dim))
    return gain


def length_profile(count, total, most, slope):
    weights = [(1 << 20) // math.isqrt(rank ** slope) + 1 for rank in range(2, count + 1)]
    rest, counts = total - most - (count - 1), [1] * (count - 1)
    while rest > 0:
        candidates = [i for i in range(count - 1) if counts[i] < most]
        pool, remaining = sum([weights[i] for i in candidates]), rest
        for i in candidates:
            addition = min(most - counts[i], max(1, remaining * weights[i] // pool), rest)
            counts[i] = counts[i] + addition
            rest = rest - addition
    return np.array([most] + counts)


def uneven(key, count, total, bound, skew):
    if count == 2:
        one = jax.random.randint(key, (), max(1, total - bound), min(bound, total - 1) + 1)
        return jnp.stack([one, total - one])
    tallies = jnp.asarray(length_profile(count, total, bound, skew), jnp.int32)
    couples = (count - 1) // 2
    giver, receiver = tallies[1:1 + 2 * couples:2], tallies[2:2 + 2 * couples:2]
    slack = jnp.minimum(giver - 1, bound - receiver)
    moved = jax.random.randint(jax.random.fold_in(key, 1), (couples,), 0, 1 << 20) % (slack + 1)
    tallies = tallies.at[1:1 + 2 * couples:2].set(giver - moved).at[2:2 + 2 * couples:2].set(receiver + moved)
    return tallies[jax.random.permutation(jax.random.fold_in(key, 2), count)]


def noise(stream_key, extent, deviation, limit, cuts=(), kind=jnp.bfloat16):
    result = jax.random.normal(stream_key, extent, jnp.float32) * deviation
    if len(cuts) > 0:
        result = steps_of(stream_key, extent, cuts, -0.22, 0.18) * result
    return jnp.clip(result, min=-limit, max=limit).astype(kind)


def setup_inputs(seed: int = 0) -> dict:
    splits = jax.random.split(jax.random.key(seed), 26)
    return {
        "block_input": noise(splits[0], (SLOTS, COLS, D), 1.0, 6.0, ((0, 4), (1, 8)), jnp.float32),
        "out_cotangent": noise(splits[1], (SLOTS, COLS, D), 1.0, 6.0, ((0, 4), (1, 8)), jnp.float32),
        "caption": noise(splits[2], (CLIPS, CAP, D), 1.0, 6.0, (), jnp.float32),
        "cond": noise(splits[3], (CLIPS, D), 1.0, 6.0, (), jnp.float32),
        "ada_weight": noise(splits[4], (D, 6 * D), D ** -0.5, 0.1875, ((0, 8),), jnp.float32),
        "ada_bias": noise(splits[5], (6 * D,), 0.5, 3.0, ((0, 8),), jnp.float32),
        "qkv_weight": noise(splits[6], (D, 3 * D), D ** -0.5, 0.1875, ((0, 8),), jnp.float32),
        "q_bias": noise(splits[7], (D,), 0.5, 3.0, ((0, 8),), jnp.float32),
        "v_bias": noise(splits[8], (D,), 0.5, 3.0, ((0, 8),), jnp.float32),
        "attn_out_weight": noise(splits[9], (D, D), (D // 8) ** -0.5, 0.5, ((0, 8),), jnp.float32),
        "attn_out_bias": noise(splits[10], (D,), 0.5, 3.0, ((0, 8),), jnp.float32),
        "cross_q_weight": noise(splits[11], (D, D), D ** -0.5, 0.1875, ((0, 8),), jnp.float32),
        "cross_q_bias": noise(splits[12], (D,), 0.5, 3.0, ((0, 8),), jnp.float32),
        "cross_kv_weight": noise(splits[13], (D, 2 * D), D ** -0.5, 0.1875, ((0, 8),), jnp.float32),
        "cross_v_bias": noise(splits[14], (D,), 0.5, 3.0, ((0, 8),), jnp.float32),
        "cross_out_weight": noise(splits[15], (D, D), (D // 8) ** -0.5, 0.5, ((0, 8),), jnp.float32),
        "cross_out_bias": noise(splits[16], (D,), 0.5, 3.0, ((0, 8),), jnp.float32),
        "fc1_weight": noise(splits[17], (D, FF), D ** -0.5, 0.1875, ((0, 8),), jnp.float32),
        "fc1_bias": noise(splits[18], (FF,), 0.5, 3.0, ((0, 8),), jnp.float32),
        "fc2_weight": noise(splits[19], (FF, D), FF ** -0.5, 0.09375, ((0, 8),), jnp.float32),
        "fc2_bias": noise(splits[20], (D,), 0.5, 3.0, ((0, 8),), jnp.float32),
        "frame_slot": draw_frame_slot(jax.random.fold_in(splits[25], 71), 0),
        "clip_id": jnp.searchsorted(jnp.cumsum(uneven(splits[22], CLIPS, COLS, COLS // 2, 0)), jnp.arange(COLS), side="right").astype(jnp.int32),
        "patch_mask": with_ends((jax.random.randint(splits[23], (COLS,), 0, 4) < 3).astype(jnp.int32), jax.random.fold_in(splits[23], 1), 0, 1),
        "caption_mask": draw_caption_mask(jax.random.fold_in(splits[25], 71), 0),
    }


@jax.custom_vjp
def low(v):
    return lax.optimization_barrier(v.astype(jnp.bfloat16)).astype(jnp.float32)

@jax.custom_vjp
def low_back(v):
    return v

def low_keep(v):
    return (low(v), None)

def low_pass(kept, grad):
    return (grad,)

def back_keep(v):
    return (v, None)

def back_low(kept, grad):
    return (low(grad),)
low.defvjp(low_keep, low_pass)
low_back.defvjp(back_keep, back_low)
EPSILON = 1e-06
BEST = lax.Precision.HIGHEST

def matmul(left, right):
    return jnp.dot(left, right, precision=BEST)

def contract(form, left, right):
    return jnp.einsum(form, left, right, precision=BEST)

def normalize(rows):
    average = lax.optimization_barrier(jnp.mean(rows, axis=-1, keepdims=True))
    centred = rows - average
    spread = lax.optimization_barrier(jnp.mean(centred * centred, axis=-1, keepdims=True))
    return centred * lax.rsqrt(spread + EPSILON)

def forward_block(frame_slot, clip_id, patch_mask, caption_mask, block_input, caption, cond, ada_weight, ada_bias, qkv_weight, q_bias, v_bias, attn_out_weight, attn_out_bias, cross_q_weight, cross_q_bias, cross_kv_weight, cross_v_bias, cross_out_weight, cross_out_bias, fc1_weight, fc1_bias, fc2_weight, fc2_bias):
    scaling = HD ** (-0.5)
    slopes = 2.0 ** (-8.0 * (jnp.arange(H).astype(jnp.float32) + 1.0) / H)
    clip_onehot = (clip_id[:, None] == jnp.arange(CLIPS, dtype=jnp.int32)[None, :]).astype(jnp.float32)
    cond_act = jax.nn.silu(cond)
    modulation = matmul(cond_act, ada_weight) + ada_bias
    per_column = matmul(clip_onehot, modulation)
    shift_one = per_column[:, 0:D]
    scale_one = per_column[:, D:2 * D]
    gate_one = per_column[:, 2 * D:3 * D]
    shift_two = per_column[:, 3 * D:4 * D]
    scale_two = per_column[:, 4 * D:5 * D]
    gate_two = per_column[:, 5 * D:6 * D]
    column_mask = patch_mask.astype(jnp.float32)[:, None]
    normed_one = normalize(block_input)
    hidden_one = normed_one * (1.0 + scale_one) + shift_one
    qkv_rows = matmul(hidden_one.reshape(SLOTS * COLS, D), qkv_weight)
    queries = (qkv_rows[:, :D] + q_bias).reshape(SLOTS, COLS, H, HD)
    key_rows = qkv_rows[:, D:2 * D].reshape(SLOTS, COLS, H, HD)
    value_rows = (qkv_rows[:, 2 * D:] + v_bias).reshape(SLOTS, COLS, H, HD)
    frame_pos = frame_slot.astype(jnp.float32)
    distance = jnp.abs(frame_pos[:, None] - frame_pos[None, :])
    scores = contract('fchd,schd->chfs', queries, key_rows) * scaling - slopes[None, :, None, None] * distance[None, None]
    key_valid = (frame_slot < FRAMES)[None, None, None, :]
    probs = jax.nn.softmax(jnp.where(key_valid, scores, -1e+30), axis=-1)
    attended = contract('chfs,schd->fchd', probs, value_rows).reshape(SLOTS * COLS, D)
    attn_branch = (matmul(attended, attn_out_weight) + attn_out_bias).reshape(SLOTS, COLS, D)
    after_attn = block_input + column_mask * gate_one * attn_branch
    cross_queries = (matmul(after_attn.reshape(SLOTS * COLS, D), cross_q_weight) + cross_q_bias).reshape(SLOTS, COLS, H, HD)
    caption_kv = matmul(caption.reshape(CLIPS * CAP, D), cross_kv_weight)
    cross_keys = caption_kv[:, :D].reshape(CLIPS * CAP, H, HD)
    cross_values = (caption_kv[:, D:] + cross_v_bias).reshape(CLIPS * CAP, H, HD)
    key_clip = jnp.arange(CLIPS * CAP, dtype=jnp.int32) // CAP
    caption_ok = ((clip_id[:, None] == key_clip[None, :]) & (caption_mask.reshape(CLIPS * CAP)[None, :] > 0))[:, None, :]

    def cross_slot(slot_queries):
        slot_scores = contract('chd,khd->chk', slot_queries, cross_keys) * scaling
        slot_probs = jax.nn.softmax(jnp.where(caption_ok, slot_scores, -1e+30), axis=-1)
        return contract('chk,khd->chd', slot_probs, cross_values).reshape(COLS, D)
    cross_att = lax.map(jax.checkpoint(cross_slot), cross_queries)
    cross_branch = (matmul(cross_att.reshape(SLOTS * COLS, D), cross_out_weight) + cross_out_bias).reshape(SLOTS, COLS, D)
    after_cross = after_attn + column_mask * cross_branch
    normed_two = normalize(after_cross)
    hidden_two = normed_two * (1.0 + scale_two) + shift_two
    pre_act = matmul(hidden_two.reshape(SLOTS * COLS, D), fc1_weight) + fc1_bias
    activated = jax.nn.gelu(pre_act, approximate=True)
    mlp_branch = (matmul(activated, fc2_weight) + fc2_bias).reshape(SLOTS, COLS, D)
    return after_cross + column_mask * gate_two * mlp_branch

def reference(block_input, out_cotangent, caption, cond, ada_weight, ada_bias, qkv_weight, q_bias, v_bias, attn_out_weight, attn_out_bias, cross_q_weight, cross_q_bias, cross_kv_weight, cross_v_bias, cross_out_weight, cross_out_bias, fc1_weight, fc1_bias, fc2_weight, fc2_bias, frame_slot, clip_id, patch_mask, caption_mask):
    floats = (block_input, caption, cond, ada_weight, ada_bias, qkv_weight, q_bias, v_bias, attn_out_weight, attn_out_bias, cross_q_weight, cross_q_bias, cross_kv_weight, cross_v_bias, cross_out_weight, cross_out_bias, fc1_weight, fc1_bias, fc2_weight, fc2_bias)
    block_out, pull = jax.vjp(partial(forward_block, frame_slot, clip_id, patch_mask, caption_mask), *floats)
    grads = pull(out_cotangent)
    return (block_out, grads[0], grads[1], grads[2], grads[3], grads[4], grads[5], grads[6], grads[7], grads[8], grads[9], grads[10], grads[11], grads[12], grads[13], grads[14], grads[15], grads[16], grads[17], grads[18], grads[19])
```

```python
from functools import partial

import jax
import jax.numpy as jnp
from jax import lax
from jax.sharding import PartitionSpec as P

H = 16
CAP = 120
FRAMES = 17
CLIPS = 4


EPSILON = 1e-06
BEST = lax.Precision.HIGH


def matmul(left, right):
    return jnp.dot(left, right, precision=BEST)


def contract(form, left, right):
    return jnp.einsum(form, left, right, precision=BEST)


def matmul_nt(left, right):
    return lax.dot_general(left, right, (((1,), (1,)), ((), ())), precision=BEST)


def matmul_tn(left, right):
    return lax.dot_general(left, right, (((0,), (0,)), ((), ())), precision=BEST)


def normalize(rows):
    average = jnp.mean(rows, axis=-1, keepdims=True)
    centred = rows - average
    spread = jnp.mean(centred * centred, axis=-1, keepdims=True)
    inverse = lax.rsqrt(spread + EPSILON)
    return (centred * inverse, inverse)


def normalize_back(grad_normed, normed, inverse):
    first_mean = jnp.mean(grad_normed, axis=-1, keepdims=True)
    second_mean = jnp.mean(grad_normed * normed, axis=-1, keepdims=True)
    return inverse * (grad_normed - first_mean - normed * second_mean)


def softmax_rows(scores, allowed):
    masked = jnp.where(allowed, scores, -1e30)
    highest = jnp.max(masked, axis=-1, keepdims=True)
    exponent = jnp.exp(masked - highest)
    return exponent / jnp.sum(exponent, axis=-1, keepdims=True)


def swap(value, axis, bit):
    size = lax.axis_size(axis)
    return lax.ppermute(value, axis, [(i, i ^ bit) for i in range(size)])


def all_sum(value, axis):
    bit = 1
    while bit < lax.axis_size(axis):
        value = value + swap(value, axis, bit)
        bit *= 2
    return value


def placed(vector, axis):
    length = vector.shape[-1]
    whole = jnp.zeros(vector.shape[:-1] + (length * lax.axis_size(axis),), vector.dtype)
    return lax.dynamic_update_slice_in_dim(
        whole, vector, lax.axis_index(axis) * length, axis=vector.ndim - 1
    )


def own_part(array, axis, dim):
    length = array.shape[dim] // lax.axis_size(axis)
    return lax.dynamic_slice_in_dim(array, lax.axis_index(axis) * length, length, axis=dim)


def gather_rows(shard):
    return lax.all_gather(shard, "patch", axis=0, tiled=True)


def scatter_rows(whole):
    return lax.psum_scatter(whole, "patch", scatter_dimension=0, tiled=True)


def on_device(
    block_input,
    out_cotangent,
    caption,
    cond,
    ada_weight,
    ada_bias,
    qkv_weight,
    q_bias,
    v_bias,
    attn_out_weight,
    attn_out_bias,
    cross_q_weight,
    cross_q_bias,
    cross_kv_weight,
    cross_v_bias,
    cross_out_weight,
    cross_out_bias,
    fc1_weight,
    fc1_bias,
    fc2_weight,
    fc2_bias,
    frame_slot,
    clip_id,
    patch_mask,
    caption_mask,
):
    width = block_input.shape[-1]
    head_dim = width // H
    scaling = head_dim ** (-0.5)
    to_columns = partial(
        lax.all_to_all, axis_name="frame", split_axis=1, concat_axis=0, tiled=True
    )
    to_slots = partial(
        lax.all_to_all, axis_name="frame", split_axis=0, concat_axis=1, tiled=True
    )
    tokens_in = to_columns(block_input)
    cotangent = to_columns(out_cotangent)
    slots, cols, _ = tokens_in.shape
    rows = slots * cols
    clip_own = own_part(clip_id, "frame", 0)
    column_mask = own_part(patch_mask, "frame", 0).astype(jnp.float32)[:, None]
    frame_pos = all_sum(placed(frame_slot.astype(jnp.float32), "frame"), "frame")

    cond_act, silu_pull = jax.vjp(jax.nn.silu, cond)
    cond_own = own_part(cond_act, "patch", 1)
    modulation_part = matmul(cond_own, ada_weight)
    biases = (ada_bias, q_bias, v_bias, attn_out_bias, cross_q_bias, cross_v_bias, cross_out_bias, fc2_bias)
    small = all_sum(
        jnp.concatenate(
            [modulation_part.reshape(-1)] + [placed(b, "patch") for b in biases]
        ),
        "patch",
    )
    place = modulation_part.size
    modulation = small[:place].reshape(modulation_part.shape)
    whole = []
    for b in biases:
        length = b.shape[0] * lax.axis_size("patch")
        whole.append(small[place : place + length])
        place += length
    b_ada, b_query, b_value, b_attn, b_cross_q, b_cross_v, b_cross_o, b_second = whole
    modulation = modulation + b_ada
    clip_onehot = (clip_own[:, None] == jnp.arange(CLIPS, dtype=jnp.int32)[None, :]).astype(
        jnp.float32
    )
    per_column = jnp.dot(clip_onehot, modulation, precision=lax.Precision.HIGHEST)
    shift_one, scale_one, gate_one, shift_two, scale_two, gate_two = jnp.split(
        per_column, 6, axis=1
    )

    caption_rows = caption.reshape(CLIPS * CAP, width)
    caption_share = own_part(own_part(caption_rows, "frame", 0), "patch", 1)
    caption_kv_share = lax.psum(matmul(caption_share, cross_kv_weight), "patch")
    caption_kv = lax.all_gather(caption_kv_share, "frame", axis=0, tiled=True)
    cross_keys = caption_kv[:, :width].reshape(CLIPS * CAP, H, head_dim)
    cross_values = (caption_kv[:, width:] + b_cross_v).reshape(CLIPS * CAP, H, head_dim)

    w_qkv = gather_rows(qkv_weight)
    w_attn = gather_rows(attn_out_weight)
    w_cross_q = gather_rows(cross_q_weight)
    w_cross_o = gather_rows(cross_out_weight)
    w_first = lax.all_to_all(fc1_weight, "patch", 1, 0, tiled=True)
    grad_mlp = (column_mask * gate_two * cotangent).reshape(rows, width)
    grad_mlp_all = gather_rows(grad_mlp)

    normed_one, inverse_one = normalize(tokens_in)
    hidden_one = (normed_one * (1.0 + scale_one) + shift_one).reshape(rows, width)
    qkv_rows = matmul(hidden_one, w_qkv)
    queries = (qkv_rows[:, :width] + b_query).reshape(slots, cols, H, head_dim)
    keys = qkv_rows[:, width : 2 * width].reshape(slots, cols, H, head_dim)
    values = (qkv_rows[:, 2 * width :] + b_value).reshape(slots, cols, H, head_dim)
    slopes = 2.0 ** (-8.0 * (jnp.arange(H).astype(jnp.float32) + 1.0) / H)
    distance = jnp.abs(frame_pos[:, None] - frame_pos[None, :])
    bias_table = -slopes[:, None, None] * distance[None]
    key_valid = (frame_pos < FRAMES - 0.5)[None, None, None, :]
    scores = contract("fchd,schd->chfs", queries, keys) * scaling + bias_table[None]
    probs = softmax_rows(scores, key_valid)
    attended = contract("chfs,schd->fchd", probs, values)
    attended_rows = attended.reshape(rows, width)
    attn_branch = (matmul(attended_rows, w_attn) + b_attn).reshape(slots, cols, width)
    after_attn = tokens_in + column_mask * gate_one * attn_branch
    after_attn_rows = after_attn.reshape(rows, width)
    cross_queries = (matmul(after_attn_rows, w_cross_q) + b_cross_q).reshape(
        slots, cols, H, head_dim
    )
    key_clip = jnp.arange(CLIPS * CAP, dtype=jnp.int32) // CAP
    caption_ok = (
        (clip_own[:, None] == key_clip[None, :]) & (caption_mask.reshape(CLIPS * CAP)[None, :] > 0)
    )[None, :, None, :]
    cross_scores = contract("fchd,khd->fchk", cross_queries, cross_keys) * scaling
    cross_probs = softmax_rows(cross_scores, caption_ok)
    cross_att = contract("fchk,khd->fchd", cross_probs, cross_values)
    cross_rows = cross_att.reshape(rows, width)
    cross_branch = (matmul(cross_rows, w_cross_o) + b_cross_o).reshape(slots, cols, width)
    after_cross = after_attn + column_mask * cross_branch
    normed_two, inverse_two = normalize(after_cross)
    hidden_two = (normed_two * (1.0 + scale_two) + shift_two).reshape(rows, width)

    hidden_all = gather_rows(hidden_two)
    pre_act = matmul(hidden_all, w_first) + fc1_bias
    activated, gelu_pull = jax.vjp(partial(jax.nn.gelu, approximate=True), pre_act)
    grad_pre = gelu_pull(matmul_nt(grad_mlp_all, fc2_weight))[0]
    grad_hidden_two = scatter_rows(matmul_nt(grad_pre, w_first)).reshape(slots, cols, width)
    mlp_sum = scatter_rows(matmul(activated, fc2_weight))
    grad_w_second = lax.psum(matmul_tn(activated, grad_mlp_all), "frame")
    grad_w_first = lax.psum(
        lax.all_to_all(matmul_tn(hidden_all, grad_pre), "patch", 0, 1, tiled=True), "frame"
    )
    grad_b_first = all_sum(jnp.sum(grad_pre, axis=0), "frame")
    mlp_branch = (mlp_sum + b_second).reshape(slots, cols, width)
    block_out = to_slots(after_cross + column_mask * gate_two * mlp_branch)
    grad_gate_two = jnp.sum(column_mask * mlp_branch * cotangent, axis=0)
    grad_b_second = jnp.sum(grad_mlp, axis=0)

    grad_shift_two = jnp.sum(grad_hidden_two, axis=0)
    grad_scale_two = jnp.sum(grad_hidden_two * normed_two, axis=0)
    grad_after_cross = cotangent + normalize_back(
        grad_hidden_two * (1.0 + scale_two), normed_two, inverse_two
    )
    grad_cross_branch = (column_mask * grad_after_cross).reshape(rows, width)
    grad_w_cross_o = matmul_tn(cross_rows, grad_cross_branch)
    grad_b_cross_o = jnp.sum(grad_cross_branch, axis=0)
    grad_cross_att = matmul_nt(grad_cross_branch, w_cross_o).reshape(slots, cols, H, head_dim)
    cross_row_terms = jnp.sum(grad_cross_att * cross_att, axis=-1)[..., None]
    grad_cross_probs = contract("fchd,khd->fchk", grad_cross_att, cross_values)
    grad_cross_scores = cross_probs * (grad_cross_probs - cross_row_terms) * scaling
    grad_cross_queries = contract("fchk,khd->fchd", grad_cross_scores, cross_keys).reshape(
        rows, width
    )
    grad_cross_keys = contract("fchk,fchd->khd", grad_cross_scores, cross_queries).reshape(
        CLIPS * CAP, width
    )
    grad_cross_values = contract("fchk,fchd->khd", cross_probs, grad_cross_att).reshape(
        CLIPS * CAP, width
    )
    grad_kv = jnp.concatenate([grad_cross_keys, grad_cross_values], axis=1)
    grad_kv_share = lax.psum(
        lax.psum_scatter(grad_kv, "frame", scatter_dimension=0, tiled=True), "patch"
    )
    grad_w_cross_kv = lax.psum(matmul_tn(caption_share, grad_kv_share), "frame")
    grad_b_cross_v = jnp.sum(grad_kv_share[:, width:], axis=0)
    grad_caption_share = lax.all_gather(
        matmul_nt(grad_kv_share, cross_kv_weight), "patch", axis=1, tiled=True
    )
    grad_caption = lax.all_gather(grad_caption_share, "frame", axis=0, tiled=True).reshape(
        caption.shape
    )
    grad_w_cross_q = matmul_tn(after_attn_rows, grad_cross_queries)
    grad_b_cross_q = jnp.sum(grad_cross_queries, axis=0)
    grad_after_attn = grad_after_cross + matmul_nt(grad_cross_queries, w_cross_q).reshape(
        slots, cols, width
    )
    grad_attn_rows = (column_mask * gate_one * grad_after_attn).reshape(rows, width)
    grad_gate_one = jnp.sum(column_mask * attn_branch * grad_after_attn, axis=0)
    grad_w_attn = matmul_tn(attended_rows, grad_attn_rows)
    grad_b_attn = jnp.sum(grad_attn_rows, axis=0)
    grad_attended = matmul_nt(grad_attn_rows, w_attn).reshape(slots, cols, H, head_dim)
    row_terms = jnp.transpose(jnp.sum(grad_attended * attended, axis=-1), (1, 2, 0))[..., None]
    grad_probs = contract("fchd,schd->chfs", grad_attended, values)
    grad_scores = probs * (grad_probs - row_terms)
    grad_queries = (contract("chfs,schd->fchd", grad_scores, keys) * scaling).reshape(rows, width)
    grad_keys = (contract("chfs,fchd->schd", grad_scores, queries) * scaling).reshape(rows, width)
    grad_values = contract("chfs,fchd->schd", probs, grad_attended).reshape(rows, width)
    grad_qkv = jnp.concatenate([grad_queries, grad_keys, grad_values], axis=1)
    grad_w_qkv = matmul_tn(hidden_one, grad_qkv)
    grad_b_query = jnp.sum(grad_queries, axis=0)
    grad_b_value = jnp.sum(grad_values, axis=0)
    grad_hidden_one = matmul_nt(grad_qkv, w_qkv).reshape(slots, cols, width)
    grad_shift_one = jnp.sum(grad_hidden_one, axis=0)
    grad_scale_one = jnp.sum(grad_hidden_one * normed_one, axis=0)
    input_grad = to_slots(
        grad_after_attn
        + normalize_back(grad_hidden_one * (1.0 + scale_one), normed_one, inverse_one)
    )
    grad_per_column = jnp.concatenate(
        [
            grad_shift_one,
            grad_scale_one,
            grad_gate_one,
            grad_shift_two,
            grad_scale_two,
            grad_gate_two,
        ],
        axis=1,
    )
    grad_modulation_part = jnp.dot(
        clip_onehot.T, grad_per_column, precision=lax.Precision.HIGHEST
    )
    first = (lax.axis_index("patch") == 0).astype(jnp.float32)
    bias_grads = (
        grad_b_query,
        grad_b_value,
        grad_b_attn,
        grad_b_cross_q,
        grad_b_cross_v * first,
        grad_b_cross_o,
        grad_b_second,
    )
    small_grads = all_sum(
        all_sum(
            jnp.concatenate([grad_modulation_part.reshape(-1)] + list(bias_grads)), "patch"
        ),
        "frame",
    )
    place = grad_modulation_part.size
    grad_modulation = small_grads[:place].reshape(grad_modulation_part.shape)
    own_biases = []
    for b in bias_grads:
        own_biases.append(own_part(small_grads[place : place + b.shape[0]], "patch", 0))
        place += b.shape[0]
    g_query, g_value, g_attn, g_cross_q, g_cross_v, g_cross_o, g_second = own_biases
    grad_w_ada = matmul_tn(cond_own, grad_modulation)
    grad_b_ada = own_part(jnp.sum(grad_modulation, axis=0), "patch", 0)
    grad_cond_act = all_sum(placed(matmul_nt(grad_modulation, ada_weight), "patch"), "patch")
    grad_cond = silu_pull(grad_cond_act)[0]

    def finish(whole_grad):
        return lax.psum(scatter_rows(whole_grad), "frame")

    return (
        block_out,
        input_grad,
        grad_caption,
        grad_cond,
        grad_w_ada,
        grad_b_ada,
        finish(grad_w_qkv),
        g_query,
        g_value,
        finish(grad_w_attn),
        g_attn,
        finish(grad_w_cross_q),
        g_cross_q,
        grad_w_cross_kv,
        g_cross_v,
        finish(grad_w_cross_o),
        g_cross_o,
        grad_w_first,
        grad_b_first,
        grad_w_second,
        g_second,
    )


def solution(mesh):
    tokens = P("frame", "patch", None)
    weight = P("patch", None)
    vector = P("patch")
    parameters = (
        weight, vector, weight, vector, vector, weight, vector, weight, vector,
        weight, vector, weight, vector, weight, vector, weight, vector,
    )
    in_specs = (tokens, tokens, P(), P()) + parameters + (P("frame"), vector, vector, P())
    out_specs = (tokens, tokens, P(), P()) + parameters
    return jax.shard_map(
        on_device, mesh=mesh, in_specs=in_specs, out_specs=out_specs, check_vma=False
    )
```

```python
from functools import partial

import jax
import jax.numpy as jnp
from jax import lax
from jax.experimental import pallas as pl
from jax.experimental.pallas import tpu as pltpu
from jax.sharding import PartitionSpec as P

H = 16
CAP = 120
FRAMES = 17
CLIPS = 4


EPSILON = 1e-06
BEST = lax.Precision.HIGH


def matmul(left, right):
    return jnp.dot(left, right, precision=BEST)


def contract(form, left, right):
    return jnp.einsum(form, left, right, precision=BEST)


def matmul_nt(left, right):
    return lax.dot_general(left, right, (((1,), (1,)), ((), ())), precision=BEST)


def matmul_tn(left, right):
    return lax.dot_general(left, right, (((0,), (0,)), ((), ())), precision=BEST)


def normalize(rows):
    average = jnp.mean(rows, axis=-1, keepdims=True)
    centred = rows - average
    spread = jnp.mean(centred * centred, axis=-1, keepdims=True)
    inverse = lax.rsqrt(spread + EPSILON)
    return (centred * inverse, inverse)


def normalize_back(grad_normed, normed, inverse):
    first_mean = jnp.mean(grad_normed, axis=-1, keepdims=True)
    second_mean = jnp.mean(grad_normed * normed, axis=-1, keepdims=True)
    return inverse * (grad_normed - first_mean - normed * second_mean)


def softmax_rows(scores, allowed):
    masked = jnp.where(allowed, scores, -1e30)
    highest = jnp.max(masked, axis=-1, keepdims=True)
    exponent = jnp.exp(masked - highest)
    return exponent / jnp.sum(exponent, axis=-1, keepdims=True)


def swap(value, axis, bit):
    size = lax.axis_size(axis)
    return lax.ppermute(value, axis, [(i, i ^ bit) for i in range(size)])


def all_sum(value, axis):
    bit = 1
    while bit < lax.axis_size(axis):
        value = value + swap(value, axis, bit)
        bit *= 2
    return value


def placed(vector, axis):
    length = vector.shape[-1]
    whole = jnp.zeros(vector.shape[:-1] + (length * lax.axis_size(axis),), vector.dtype)
    return lax.dynamic_update_slice_in_dim(
        whole, vector, lax.axis_index(axis) * length, axis=vector.ndim - 1
    )


def own_part(array, axis, dim):
    length = array.shape[dim] // lax.axis_size(axis)
    return lax.dynamic_slice_in_dim(array, lax.axis_index(axis) * length, length, axis=dim)


def after(value, done):
    return lax.optimization_barrier((value, done))[0]


def small_patch():
    return lax.axis_size("patch") == 8


def gather_blocks(shard, done):
    half = shard.shape[0] // 2
    sent = after(shard, done)
    along_x = swap(sent, "patch", 2)
    along_y = swap(sent, "patch", 4)
    x_half, y_half = lax.optimization_barrier((along_x[:half], along_y[half:]))
    across_y, across_x = swap(x_half, "patch", 4), swap(y_half, "patch", 2)
    across = jnp.concatenate([across_y, across_x], axis=0)
    blocks = []
    for block in (shard, along_x, along_y, across):
        blocks += [block, swap(block, "patch", 1)]
    return blocks, (across_y, across_x)


def assemble_kernel(*refs):
    blocks, whole, semaphores = refs[:-2], refs[-2], refs[-1]
    own = lax.axis_index("patch")
    copies = []
    for k, block in enumerate(blocks):
        length = block.shape[0]
        row = pl.multiple_of((own ^ k) * length, 8)
        copies.append(
            pltpu.make_async_copy(block, whole.at[pl.ds(row, length)], semaphores.at[k])
        )
    for copy in copies:
        copy.start()
    for copy in copies:
        copy.wait()


def assemble(blocks):
    length, width = blocks[0].shape
    return pl.pallas_call(
        assemble_kernel,
        out_shape=jax.ShapeDtypeStruct((length * len(blocks), width), jnp.float32),
        in_specs=[pl.BlockSpec(memory_space=pl.ANY)] * len(blocks),
        out_specs=pl.BlockSpec(memory_space=pl.ANY),
        scratch_shapes=[pltpu.SemaphoreType.DMA((len(blocks),))],
        cost_estimate=pl.CostEstimate(
            flops=0, bytes_accessed=8 * length * len(blocks) * width, transcendentals=0
        ),
    )(*blocks)


def gather_rows(shard, done):
    if not small_patch():
        return lax.all_gather(shard, "patch", axis=0, tiled=True), done
    blocks, done = gather_blocks(shard, done)
    return assemble(blocks), done


def scatter_chips(chips):
    half = chips[0].shape[0] // 2
    second = swap(chips[3][:half], "patch", 2)
    first = swap(chips[3][half:], "patch", 4)
    for_y = jnp.concatenate([chips[2][:half] + second, chips[2][half:]], axis=0)
    for_x = jnp.concatenate([chips[1][:half], chips[1][half:] + first], axis=0)
    return chips[0] + swap(for_x, "patch", 2) + swap(for_y, "patch", 4)


def scatter_rows(whole):
    if not small_patch():
        return lax.psum_scatter(whole, "patch", scatter_dimension=0, tiled=True)
    own = lax.axis_index("patch")
    core, chip = own % 2, own // 2
    length = whole.shape[0] // 8
    parts = whole.reshape(4, 2, length, whole.shape[1])
    sent = lax.dynamic_index_in_dim(parts, 1 - core, axis=1, keepdims=False)
    kept = lax.dynamic_index_in_dim(parts, core, axis=1, keepdims=False)
    kept = kept + swap(sent, "patch", 1)
    return scatter_chips(
        [lax.dynamic_index_in_dim(kept, chip ^ j, axis=0, keepdims=False) for j in range(4)]
    )


def gather_tokens(rows, done):
    if not small_patch():
        return [lax.all_gather(rows, "patch", axis=0, tiled=True)], done
    blocks, done = gather_blocks(rows, done)
    return [jnp.concatenate(blocks[2 * j : 2 * j + 2], axis=0) for j in range(4)], done


def scatter_tokens(groups):
    if not small_patch():
        return lax.psum_scatter(groups[0], "patch", scatter_dimension=0, tiled=True)
    half = groups[0].shape[0] // 2
    return scatter_chips([g[:half] + swap(g[half:], "patch", 1) for g in groups])


def sum_chips(value, done):
    if not small_patch():
        bit = 2
        while bit < lax.axis_size("patch"):
            value = value + swap(value, "patch", bit)
            bit *= 2
        return value, done
    half = value.shape[0] // 2
    upper, lower = after((value[:half], value[half:]), done)
    upper = upper + swap(upper, "patch", 2)
    lower = lower + swap(lower, "patch", 4)
    from_y, from_x = swap(upper, "patch", 4), swap(lower, "patch", 2)
    return jnp.concatenate([upper + from_y, lower + from_x], axis=0), (from_y, from_x)


def exchange(parts, axis):
    return [parts[0]] + [swap(parts[k], axis, k) for k in range(1, len(parts))]


def frame_sum(value):
    if lax.axis_size("frame") != 4:
        return lax.psum(value, "frame")
    place = lax.axis_index("frame")
    inner = (place == 1) | (place == 2)
    value = value + lax.ppermute(value, "frame", [(0, 1), (3, 2)])
    value = value + lax.ppermute(value, "frame", [(1, 2), (2, 1)])
    return jnp.where(inner, value, lax.ppermute(value, "frame", [(1, 0), (2, 3)]))


def half_over_cores(value, core):
    width = value.shape[1] // 2
    sent = lax.dynamic_slice_in_dim(value, (1 - core) * width, width, axis=1)
    kept = lax.dynamic_slice_in_dim(value, core * width, width, axis=1)
    return kept + swap(sent, "patch", 1)


def both_halves(half, core):
    other = swap(half, "patch", 1)
    return jnp.concatenate(
        [jnp.where(core == 0, half, other), jnp.where(core == 0, other, half)], axis=1
    )


def in_order(parts, axis):
    length = parts[0].shape[0]
    whole = jnp.zeros((length * len(parts),) + parts[0].shape[1:], parts[0].dtype)
    for k, part in enumerate(parts):
        start = (lax.axis_index(axis) ^ k) * length
        whole = lax.dynamic_update_slice_in_dim(whole, part, start, axis=0)
    return whole


def block_of(array, axis_name, k, dim):
    length = array.shape[dim] // lax.axis_size(axis_name)
    start = (lax.axis_index(axis_name) ^ k) * length
    return lax.dynamic_slice_in_dim(array, start, length, axis=dim)


def to_own_columns(weight, done):
    if not small_patch():
        return lax.all_to_all(weight, "patch", 1, 0, tiled=True), done
    blocks = [block_of(weight, "patch", k, 1) for k in range(8)]
    pairs = []
    for j in range(4):
        kept, sent = blocks[2 * j], blocks[2 * j + 1]
        pairs.append((kept, sent))
    theirs = swap(jnp.concatenate([sent for _, sent in pairs], axis=0), "patch", 1)
    length = weight.shape[0]
    both = [
        jnp.concatenate([kept, theirs[j * length : (j + 1) * length]], axis=0)
        for j, (kept, _) in enumerate(pairs)
    ]
    sent_x, sent_y, sent_xy = after(tuple(both[1:]), done)
    arrived = [
        both[0],
        swap(sent_x, "patch", 2),
        swap(sent_y, "patch", 4),
        swap(sent_xy, "patch", 6),
    ]
    halves = []
    for block in arrived:
        halves += [block[:length], block[length:]]
    return assemble(halves), tuple(arrived[1:])


def back_to_rows(grad):
    count = lax.axis_size("patch")
    if not small_patch():
        return lax.all_to_all(grad, "patch", 0, 1, tiled=True)
    parts = exchange([block_of(grad, "patch", k, 0) for k in range(count)], "patch")
    length, width = parts[0].shape
    whole = jnp.zeros((length, width * count), grad.dtype)
    for k, part in enumerate(parts):
        start = (lax.axis_index("patch") ^ k) * width
        whole = lax.dynamic_update_slice_in_dim(whole, part, start, axis=1)
    return whole


def to_columns(x):
    return lax.all_to_all(x, "frame", split_axis=1, concat_axis=0, tiled=True)


def to_slots(x):
    count = lax.axis_size("frame")
    length = x.shape[0] // count
    parts = exchange([block_of(x, "frame", k, 0) for k in range(count)], "frame")
    whole = jnp.zeros((length, x.shape[1] * count, x.shape[2]), x.dtype)
    for k, part in enumerate(parts):
        start = (lax.axis_index("frame") ^ k) * x.shape[1]
        whole = lax.dynamic_update_slice_in_dim(whole, part, start, axis=1)
    return whole


def on_device(
    block_input,
    out_cotangent,
    caption,
    cond,
    ada_weight,
    ada_bias,
    qkv_weight,
    q_bias,
    v_bias,
    attn_out_weight,
    attn_out_bias,
    cross_q_weight,
    cross_q_bias,
    cross_kv_weight,
    cross_v_bias,
    cross_out_weight,
    cross_out_bias,
    fc1_weight,
    fc1_bias,
    fc2_weight,
    fc2_bias,
    frame_slot,
    clip_id,
    patch_mask,
    caption_mask,
):
    width = block_input.shape[-1]
    head_dim = width // H
    scaling = head_dim ** (-0.5)
    tokens_in = to_columns(block_input)
    cotangent = to_columns(out_cotangent)
    slots, cols, _ = tokens_in.shape
    rows = slots * cols
    clip_own = own_part(clip_id, "frame", 0)
    column_mask = own_part(patch_mask, "frame", 0).astype(jnp.float32)[:, None]
    frame_count = lax.axis_size("frame")
    frame_pos = all_sum(placed(frame_slot.astype(jnp.float32), "frame"), "frame")
    w_qkv, done = gather_rows(qkv_weight, ())

    cond_act, silu_pull = jax.vjp(jax.nn.silu, cond)
    cond_own = own_part(cond_act, "patch", 1)
    modulation_part = matmul(cond_own, ada_weight)
    biases = (ada_bias, q_bias, v_bias, attn_out_bias, cross_q_bias, cross_v_bias, cross_out_bias, fc2_bias)
    small = all_sum(
        jnp.concatenate(
            [modulation_part.reshape(-1)] + [placed(b, "patch") for b in biases]
        ),
        "patch",
    )
    place = modulation_part.size
    modulation = small[:place].reshape(modulation_part.shape)
    whole = []
    for b in biases:
        length = b.shape[0] * lax.axis_size("patch")
        whole.append(small[place : place + length])
        place += length
    b_ada, b_query, b_value, b_attn, b_cross_q, b_cross_v, b_cross_o, b_second = whole
    modulation = modulation + b_ada
    clip_onehot = (clip_own[:, None] == jnp.arange(CLIPS, dtype=jnp.int32)[None, :]).astype(
        jnp.float32
    )
    per_column = jnp.dot(clip_onehot, modulation, precision=lax.Precision.HIGHEST)
    shift_one, scale_one, gate_one, shift_two, scale_two, gate_two = jnp.split(
        per_column, 6, axis=1
    )

    caption_rows = caption.reshape(CLIPS * CAP, width)
    caption_share = own_part(own_part(caption_rows, "frame", 0), "patch", 1)
    core = lax.axis_index("patch") % 2
    kv_part = matmul(caption_share, cross_kv_weight)
    kv_half, done = sum_chips(half_over_cores(kv_part, core), done)
    kv_halves = in_order(exchange([kv_half] * frame_count, "frame"), "frame")
    caption_kv = both_halves(kv_halves, core)
    cross_keys = caption_kv[:, :width].reshape(CLIPS * CAP, H, head_dim)
    cross_values = (caption_kv[:, width:] + b_cross_v).reshape(CLIPS * CAP, H, head_dim)

    w_three, done = gather_rows(
        jnp.concatenate([attn_out_weight, cross_q_weight, cross_out_weight], axis=1), done
    )
    w_attn, w_cross_q, w_cross_o = jnp.split(w_three, 3, axis=1)
    w_first, done = to_own_columns(fc1_weight, done)
    grad_mlp = (column_mask * gate_two * cotangent).reshape(rows, width)
    grad_mlp_groups, done = gather_tokens(grad_mlp, done)

    normed_one, inverse_one = normalize(tokens_in)
    hidden_one = (normed_one * (1.0 + scale_one) + shift_one).reshape(rows, width)
    qkv_rows = matmul(hidden_one, w_qkv)
    queries = (qkv_rows[:, :width] + b_query).reshape(slots, cols, H, head_dim)
    keys = qkv_rows[:, width : 2 * width].reshape(slots, cols, H, head_dim)
    values = (qkv_rows[:, 2 * width :] + b_value).reshape(slots, cols, H, head_dim)
    slopes = 2.0 ** (-8.0 * (jnp.arange(H).astype(jnp.float32) + 1.0) / H)
    distance = jnp.abs(frame_pos[:, None] - frame_pos[None, :])
    bias_table = -slopes[:, None, None] * distance[None]
    key_valid = (frame_pos < FRAMES - 0.5)[None, None, None, :]
    scores = contract("fchd,schd->chfs", queries, keys) * scaling + bias_table[None]
    probs = softmax_rows(scores, key_valid)
    attended = contract("chfs,schd->fchd", probs, values)
    attended_rows = attended.reshape(rows, width)
    attn_branch = (matmul(attended_rows, w_attn) + b_attn).reshape(slots, cols, width)
    after_attn = tokens_in + column_mask * gate_one * attn_branch
    after_attn_rows = after_attn.reshape(rows, width)
    cross_queries = (matmul(after_attn_rows, w_cross_q) + b_cross_q).reshape(
        slots, cols, H, head_dim
    )
    key_clip = jnp.arange(CLIPS * CAP, dtype=jnp.int32) // CAP
    caption_ok = (
        (clip_own[:, None] == key_clip[None, :]) & (caption_mask.reshape(CLIPS * CAP)[None, :] > 0)
    )[None, :, None, :]
    cross_scores = contract("fchd,khd->fchk", cross_queries, cross_keys) * scaling
    cross_probs = softmax_rows(cross_scores, caption_ok)
    cross_att = contract("fchk,khd->fchd", cross_probs, cross_values)
    cross_rows = cross_att.reshape(rows, width)
    cross_branch = (matmul(cross_rows, w_cross_o) + b_cross_o).reshape(slots, cols, width)
    after_cross = after_attn + column_mask * cross_branch
    normed_two, inverse_two = normalize(after_cross)
    hidden_two = (normed_two * (1.0 + scale_two) + shift_two).reshape(rows, width)

    hidden_groups, done = gather_tokens(hidden_two, done)
    mlp_parts, hidden_parts = [], []
    grad_w_second, grad_w_first, grad_b_first = 0.0, 0.0, 0.0
    for hidden, cotan in zip(hidden_groups, grad_mlp_groups):
        pre_act = matmul(hidden, w_first) + fc1_bias
        activated, gelu_pull = jax.vjp(partial(jax.nn.gelu, approximate=True), pre_act)
        grad_pre = gelu_pull(matmul_nt(cotan, fc2_weight))[0]
        hidden_parts.append(matmul_nt(grad_pre, w_first))
        mlp_parts.append(matmul(activated, fc2_weight))
        grad_w_second = grad_w_second + matmul_tn(activated, cotan)
        grad_w_first = grad_w_first + matmul_tn(hidden, grad_pre)
        grad_b_first = grad_b_first + jnp.sum(grad_pre, axis=0)
    grad_hidden_two = scatter_tokens(hidden_parts).reshape(slots, cols, width)
    mlp_sum = scatter_tokens(after(mlp_parts, grad_hidden_two))
    grad_w_second = frame_sum(grad_w_second)
    grad_w_first = frame_sum(back_to_rows(grad_w_first))
    grad_b_first = all_sum(grad_b_first, "frame")
    mlp_branch = (mlp_sum + b_second).reshape(slots, cols, width)
    block_out = to_slots(after_cross + column_mask * gate_two * mlp_branch)
    grad_gate_two = jnp.sum(column_mask * mlp_branch * cotangent, axis=0)
    grad_b_second = jnp.sum(grad_mlp, axis=0)

    grad_shift_two = jnp.sum(grad_hidden_two, axis=0)
    grad_scale_two = jnp.sum(grad_hidden_two * normed_two, axis=0)
    grad_after_cross = cotangent + normalize_back(
        grad_hidden_two * (1.0 + scale_two), normed_two, inverse_two
    )
    grad_cross_branch = (column_mask * grad_after_cross).reshape(rows, width)
    grad_w_cross_o = matmul_tn(cross_rows, grad_cross_branch)
    grad_b_cross_o = jnp.sum(grad_cross_branch, axis=0)
    grad_cross_att = matmul_nt(grad_cross_branch, w_cross_o).reshape(slots, cols, H, head_dim)
    cross_row_terms = jnp.sum(grad_cross_att * cross_att, axis=-1)[..., None]
    grad_cross_probs = contract("fchd,khd->fchk", grad_cross_att, cross_values)
    grad_cross_scores = cross_probs * (grad_cross_probs - cross_row_terms) * scaling
    grad_cross_queries = contract("fchk,khd->fchd", grad_cross_scores, cross_keys).reshape(
        rows, width
    )
    grad_cross_keys = contract("fchk,fchd->khd", grad_cross_scores, cross_queries).reshape(
        CLIPS * CAP, width
    )
    grad_cross_values = contract("fchk,fchd->khd", cross_probs, grad_cross_att).reshape(
        CLIPS * CAP, width
    )
    grad_kv = jnp.concatenate([grad_cross_keys, grad_cross_values], axis=1)
    half_kv = half_over_cores(grad_kv, core)
    half_share = sum(
        exchange([block_of(half_kv, "frame", k, 0) for k in range(frame_count)], "frame")
    )
    grad_kv_share = both_halves(sum_chips(half_share, ())[0], core)
    grad_w_cross_kv = frame_sum(matmul_tn(caption_share, grad_kv_share))
    grad_b_cross_v = jnp.sum(grad_kv_share[:, width:], axis=0)
    grad_caption_share = all_sum(
        placed(matmul_nt(grad_kv_share, cross_kv_weight), "patch"), "patch"
    )
    grad_caption = in_order(
        exchange([grad_caption_share] * frame_count, "frame"), "frame"
    ).reshape(caption.shape)
    grad_w_cross_q = matmul_tn(after_attn_rows, grad_cross_queries)
    grad_b_cross_q = jnp.sum(grad_cross_queries, axis=0)
    grad_after_attn = grad_after_cross + matmul_nt(grad_cross_queries, w_cross_q).reshape(
        slots, cols, width
    )
    grad_attn_rows = (column_mask * gate_one * grad_after_attn).reshape(rows, width)
    grad_gate_one = jnp.sum(column_mask * attn_branch * grad_after_attn, axis=0)
    grad_w_attn = matmul_tn(attended_rows, grad_attn_rows)
    grad_b_attn = jnp.sum(grad_attn_rows, axis=0)
    grad_attended = matmul_nt(grad_attn_rows, w_attn).reshape(slots, cols, H, head_dim)
    row_terms = jnp.transpose(jnp.sum(grad_attended * attended, axis=-1), (1, 2, 0))[..., None]
    grad_probs = contract("fchd,schd->chfs", grad_attended, values)
    grad_scores = probs * (grad_probs - row_terms)
    grad_queries = (contract("chfs,schd->fchd", grad_scores, keys) * scaling).reshape(rows, width)
    grad_keys = (contract("chfs,fchd->schd", grad_scores, queries) * scaling).reshape(rows, width)
    grad_values = contract("chfs,fchd->schd", probs, grad_attended).reshape(rows, width)
    grad_qkv = jnp.concatenate([grad_queries, grad_keys, grad_values], axis=1)
    grad_w_qkv = matmul_tn(hidden_one, grad_qkv)
    grad_b_query = jnp.sum(grad_queries, axis=0)
    grad_b_value = jnp.sum(grad_values, axis=0)
    grad_hidden_one = matmul_nt(grad_qkv, w_qkv).reshape(slots, cols, width)
    grad_shift_one = jnp.sum(grad_hidden_one, axis=0)
    grad_scale_one = jnp.sum(grad_hidden_one * normed_one, axis=0)
    input_grad = to_slots(
        grad_after_attn
        + normalize_back(grad_hidden_one * (1.0 + scale_one), normed_one, inverse_one)
    )
    grad_per_column = jnp.concatenate(
        [
            grad_shift_one,
            grad_scale_one,
            grad_gate_one,
            grad_shift_two,
            grad_scale_two,
            grad_gate_two,
        ],
        axis=1,
    )
    grad_modulation_part = jnp.dot(
        clip_onehot.T, grad_per_column, precision=lax.Precision.HIGHEST
    )
    first = (lax.axis_index("patch") == 0).astype(jnp.float32)
    bias_grads = (
        grad_b_query,
        grad_b_value,
        grad_b_attn,
        grad_b_cross_q,
        grad_b_cross_v * first,
        grad_b_cross_o,
        grad_b_second,
    )
    small_grads = all_sum(
        all_sum(
            jnp.concatenate([grad_modulation_part.reshape(-1)] + list(bias_grads)), "patch"
        ),
        "frame",
    )
    place = grad_modulation_part.size
    grad_modulation = small_grads[:place].reshape(grad_modulation_part.shape)
    own_biases = []
    for b in bias_grads:
        own_biases.append(own_part(small_grads[place : place + b.shape[0]], "patch", 0))
        place += b.shape[0]
    g_query, g_value, g_attn, g_cross_q, g_cross_v, g_cross_o, g_second = own_biases
    grad_w_ada = matmul_tn(cond_own, grad_modulation)
    grad_b_ada = own_part(jnp.sum(grad_modulation, axis=0), "patch", 0)
    grad_cond_act = all_sum(placed(matmul_nt(grad_modulation, ada_weight), "patch"), "patch")
    grad_cond = silu_pull(grad_cond_act)[0]

    def finish(whole_grad):
        return frame_sum(scatter_rows(whole_grad))

    return (
        block_out,
        input_grad,
        grad_caption,
        grad_cond,
        grad_w_ada,
        grad_b_ada,
        finish(grad_w_qkv),
        g_query,
        g_value,
        finish(grad_w_attn),
        g_attn,
        finish(grad_w_cross_q),
        g_cross_q,
        grad_w_cross_kv,
        g_cross_v,
        finish(grad_w_cross_o),
        g_cross_o,
        grad_w_first,
        grad_b_first,
        grad_w_second,
        g_second,
    )


def solution(mesh):
    tokens = P("frame", "patch", None)
    weight = P("patch", None)
    vector = P("patch")
    parameters = (
        weight, vector, weight, vector, vector, weight, vector, weight, vector,
        weight, vector, weight, vector, weight, vector, weight, vector,
    )
    in_specs = (tokens, tokens, P(), P()) + parameters + (P("frame"), vector, vector, P())
    out_specs = (tokens, tokens, P(), P()) + parameters
    return jax.shard_map(
        on_device, mesh=mesh, in_specs=in_specs, out_specs=out_specs, check_vma=False
    )
```

```python
from functools import partial

import jax
import jax.numpy as jnp
from jax import lax
from jax.experimental import pallas as pl
from jax.experimental.pallas import tpu as pltpu
from jax.sharding import PartitionSpec as P

H = 16
CAP = 120
FRAMES = 17
CLIPS = 4


EPSILON = 1e-06
BEST = lax.Precision.HIGH


def matmul(left, right):
    return jnp.dot(left, right, precision=BEST)


def contract(form, left, right):
    return jnp.einsum(form, left, right, precision=BEST)


def matmul_nt(left, right):
    return lax.dot_general(left, right, (((1,), (1,)), ((), ())), precision=BEST)


def matmul_tn(left, right):
    return lax.dot_general(left, right, (((0,), (0,)), ((), ())), precision=BEST)


def normalize(rows):
    average = jnp.mean(rows, axis=-1, keepdims=True)
    centred = rows - average
    spread = jnp.mean(centred * centred, axis=-1, keepdims=True)
    inverse = lax.rsqrt(spread + EPSILON)
    return (centred * inverse, inverse)


def normalize_back(grad_normed, normed, inverse):
    first_mean = jnp.mean(grad_normed, axis=-1, keepdims=True)
    second_mean = jnp.mean(grad_normed * normed, axis=-1, keepdims=True)
    return inverse * (grad_normed - first_mean - normed * second_mean)


def softmax_rows(scores, allowed):
    masked = jnp.where(allowed, scores, -1e30)
    highest = jnp.max(masked, axis=-1, keepdims=True)
    exponent = jnp.exp(masked - highest)
    return exponent / jnp.sum(exponent, axis=-1, keepdims=True)


def swap(value, axis, bit):
    size = lax.axis_size(axis)
    return lax.ppermute(value, axis, [(i, i ^ bit) for i in range(size)])


def all_sum(value, axis):
    bit = 1
    while bit < lax.axis_size(axis):
        value = value + swap(value, axis, bit)
        bit *= 2
    return value


def placed(vector, axis):
    length = vector.shape[-1]
    whole = jnp.zeros(vector.shape[:-1] + (length * lax.axis_size(axis),), vector.dtype)
    return lax.dynamic_update_slice_in_dim(
        whole, vector, lax.axis_index(axis) * length, axis=vector.ndim - 1
    )


def own_part(array, axis, dim):
    length = array.shape[dim] // lax.axis_size(axis)
    return lax.dynamic_slice_in_dim(array, lax.axis_index(axis) * length, length, axis=dim)


def after(value, done):
    return lax.optimization_barrier((value, done))[0]


def small_patch():
    return lax.axis_size("patch") == 8


def greet(partners):
    barrier = pltpu.get_barrier_semaphore()
    for partner in partners:
        pl.semaphore_signal(barrier, inc=1, device_id={"patch": partner}, device_id_type=pl.DeviceIdType.MESH)
    pl.semaphore_wait(barrier, len(partners))


def remote(source, target, send_sems, recv_sems, index, device):
    return pltpu.make_async_remote_copy(
        src_ref=source, dst_ref=target, send_sem=send_sems.at[index], recv_sem=recv_sems.at[index],
        device_id={"patch": device}, device_id_type=pl.DeviceIdType.MESH)


def token_gather_kernel(rows, whole, local_sem, send_sems, recv_sems):
    own = lax.axis_index("patch")
    core, along_x, along_y, across = own ^ 1, own ^ 2, own ^ 4, own ^ 6
    greet((core, along_x, along_y))
    length = rows.shape[0] // 4
    sent = []

    def piece(owner, q):
        return whole.at[owner, pl.ds(q * length, length)]

    def send(source, owner, q, index, device):
        copy = remote(source, piece(owner, q), send_sems, recv_sems, index, device)
        copy.start()
        sent.append(copy)

    def arrived(owner, q, index, device):
        remote(piece(owner, q), piece(owner, q), send_sems, recv_sems, index, device).wait_recv()

    mine = pltpu.make_async_copy(rows, whole.at[own], local_sem)
    mine.start()
    for q_x, q_y in ((0, 2), (1, 3), (2, 0), (3, 1)):
        send(rows.at[pl.ds(q_x * length, length)], own, q_x, q_x, along_x)
        send(rows.at[pl.ds(q_y * length, length)], own, q_y, 4 + q_y, along_y)
    for q in range(4):
        send(rows.at[pl.ds(q * length, length)], own, q, 12 + q, core)
    for q_x, q_y in ((0, 2), (1, 3), (2, 0), (3, 1)):
        arrived(along_x, q_x, q_x, along_x)
        if q_x < 2:
            send(piece(along_x, q_x), along_x, q_x, 8 + q_x, along_y)
        send(piece(along_x, q_x), along_x, q_x, 16 + q_x, core)
        arrived(along_y, q_y, 4 + q_y, along_y)
        if q_y >= 2:
            send(piece(along_y, q_y), along_y, q_y, 8 + q_y, along_x)
        send(piece(along_y, q_y), along_y, q_y, 20 + q_y, core)
    for q in (0, 2, 1, 3):
        arrived(across, q, 8 + q, along_y if q < 2 else along_x)
        send(piece(across, q), across, q, 24 + q, core)
    for q in range(4):
        arrived(core, q, 12 + q, core)
        arrived(core ^ 2, q, 16 + q, core)
        arrived(core ^ 4, q, 20 + q, core)
        arrived(core ^ 6, q, 24 + q, core)
    for copy in sent:
        copy.wait_send()
    mine.wait()


def token_gather(rows):
    length, width = rows.shape
    return pl.pallas_call(
        token_gather_kernel,
        out_shape=jax.ShapeDtypeStruct((8, length, width), jnp.float32),
        in_specs=[pl.BlockSpec(memory_space=pltpu.VMEM)],
        out_specs=pl.BlockSpec(memory_space=pl.ANY),
        scratch_shapes=[pltpu.SemaphoreType.DMA, pltpu.SemaphoreType.DMA((28,)), pltpu.SemaphoreType.DMA((28,))],
        compiler_params=pltpu.CompilerParams(collective_id=0, has_side_effects=True, vmem_limit_bytes=16 << 20),
        cost_estimate=pl.CostEstimate(flops=0, bytes_accessed=64 * length * width, transcendentals=0),
    )(rows).reshape(8 * length, width)


def token_scatter_kernel(parts, total, kept, theirs, by_x, by_y, from_x, from_y, local_sems, send_sems, recv_sems):
    own = lax.axis_index("patch")
    core, along_x, along_y = own ^ 1, own ^ 2, own ^ 4
    greet((core, along_x, along_y))
    half = total.shape[0] // 2
    upper, lower = pl.ds(0, half), pl.ds(half, half)
    order = (3, 2, 1, 0)
    sent, loads = [], {}

    def send(source, target, index, device):
        copy = remote(source, target, send_sems, recv_sems, index, device)
        copy.start()
        sent.append(copy)

    def arrived(target, index, device):
        remote(target, target, send_sems, recv_sems, index, device).wait_recv()

    for j in order:
        send(parts.at[core ^ (2 * j)], theirs.at[j], j, core)
        loads[j] = pltpu.make_async_copy(parts.at[own ^ (2 * j)], kept.at[j], local_sems.at[j])
        loads[j].start()

    def add_cores(j):
        loads[j].wait()
        arrived(theirs.at[j], j, core)
        kept[j] = kept[j] + theirs[j]

    add_cores(3)
    send(kept.at[3, upper], by_x, 4, along_x)
    send(kept.at[3, lower], by_y, 5, along_y)
    add_cores(2)
    send(kept.at[2, lower], from_y.at[lower], 6, along_y)
    add_cores(1)
    send(kept.at[1, upper], from_x.at[upper], 7, along_x)
    add_cores(0)
    arrived(by_x, 4, along_x)
    kept[2, upper] = kept[2, upper] + by_x[...]
    send(kept.at[2, upper], from_y.at[upper], 8, along_y)
    arrived(by_y, 5, along_y)
    kept[1, lower] = kept[1, lower] + by_y[...]
    send(kept.at[1, lower], from_x.at[lower], 9, along_x)
    arrived(from_y.at[lower], 6, along_y)
    arrived(from_x.at[upper], 7, along_x)
    arrived(from_y.at[upper], 8, along_y)
    arrived(from_x.at[lower], 9, along_x)
    total[...] = kept[0] + from_x[...] + from_y[...]
    for copy in sent:
        copy.wait_send()


def token_scatter(parts):
    length, width = parts.shape[0] // 8, parts.shape[1]
    block = (length, width)
    return pl.pallas_call(
        token_scatter_kernel,
        out_shape=jax.ShapeDtypeStruct(block, jnp.float32),
        in_specs=[pl.BlockSpec(memory_space=pl.ANY)],
        out_specs=pl.BlockSpec(memory_space=pltpu.VMEM),
        scratch_shapes=[
            pltpu.VMEM((4,) + block, jnp.float32), pltpu.VMEM((4,) + block, jnp.float32),
            pltpu.VMEM((length // 2, width), jnp.float32), pltpu.VMEM((length // 2, width), jnp.float32),
            pltpu.VMEM(block, jnp.float32), pltpu.VMEM(block, jnp.float32),
            pltpu.SemaphoreType.DMA((4,)), pltpu.SemaphoreType.DMA((10,)), pltpu.SemaphoreType.DMA((10,)),
        ],
        compiler_params=pltpu.CompilerParams(collective_id=1, has_side_effects=True, vmem_limit_bytes=32 << 20),
        cost_estimate=pl.CostEstimate(flops=0, bytes_accessed=48 * length * width, transcendentals=0),
    )(parts.reshape((8,) + block))


def assemble_kernel(axis, dim, *refs):
    blocks, whole = refs[:-1], refs[-1]
    own = lax.axis_index(axis)
    for k, block in enumerate(blocks):
        length = block.shape[dim]
        start = pl.multiple_of((own ^ k) * length, length)
        where = (slice(None),) * dim + (pl.ds(start, length),)
        whole[where] = block[...]


def assemble(blocks, axis, dim):
    shape = list(blocks[0].shape)
    shape[dim] *= len(blocks)
    size = 4 * len(blocks) * blocks[0].size
    return pl.pallas_call(
        partial(assemble_kernel, axis, dim),
        out_shape=jax.ShapeDtypeStruct(tuple(shape), jnp.float32),
        in_specs=[pl.BlockSpec(memory_space=pltpu.VMEM)] * len(blocks),
        out_specs=pl.BlockSpec(memory_space=pltpu.VMEM),
        compiler_params=pltpu.CompilerParams(vmem_limit_bytes=24 << 20),
        cost_estimate=pl.CostEstimate(flops=0, bytes_accessed=2 * size, transcendentals=0),
    )(*blocks)


def gather_rows(shard):
    return lax.all_gather(shard, "patch", axis=0, tiled=True)


def scatter_rows(whole):
    return lax.psum_scatter(whole, "patch", scatter_dimension=0, tiled=True)


def gather_tokens(rows):
    return token_gather(rows) if small_patch() else gather_rows(rows)


def scatter_tokens(parts):
    return token_scatter(parts) if small_patch() else scatter_rows(parts)


def sum_chips(value):
    if not small_patch():
        bit = 2
        while bit < lax.axis_size("patch"):
            value = value + swap(value, "patch", bit)
            bit *= 2
        return value
    half = value.shape[0] // 2
    upper, lower = value[:half], value[half:]
    upper = upper + swap(upper, "patch", 2)
    lower = lower + swap(lower, "patch", 4)
    from_y, from_x = swap(upper, "patch", 4), swap(lower, "patch", 2)
    return jnp.concatenate([upper + from_y, lower + from_x], axis=0)


def exchange(parts, axis):
    return [parts[0]] + [swap(parts[k], axis, k) for k in range(1, len(parts))]


def frame_sum(value):
    if lax.axis_size("frame") != 4:
        return lax.psum(value, "frame")
    place = lax.axis_index("frame")
    inner = (place == 1) | (place == 2)
    value = value + lax.ppermute(value, "frame", [(0, 1), (3, 2)])
    value = value + lax.ppermute(value, "frame", [(1, 2), (2, 1)])
    return jnp.where(inner, value, lax.ppermute(value, "frame", [(1, 0), (2, 3)]))


def half_over_cores(value, core):
    width = value.shape[1] // 2
    sent = lax.dynamic_slice_in_dim(value, (1 - core) * width, width, axis=1)
    kept = lax.dynamic_slice_in_dim(value, core * width, width, axis=1)
    return kept + swap(sent, "patch", 1)


def both_halves(half, core):
    other = swap(half, "patch", 1)
    return jnp.concatenate(
        [jnp.where(core == 0, half, other), jnp.where(core == 0, other, half)], axis=1
    )


def block_of(array, axis_name, k, dim):
    length = array.shape[dim] // lax.axis_size(axis_name)
    start = (lax.axis_index(axis_name) ^ k) * length
    return lax.dynamic_slice_in_dim(array, start, length, axis=dim)


def pair_up(kept, theirs, core):
    return jnp.where(
        core == 0,
        jnp.concatenate([kept, theirs], axis=-1),
        jnp.concatenate([theirs, kept], axis=-1),
    )


def over_chips(blocks):
    return [
        blocks[0],
        swap(blocks[1], "patch", 2),
        swap(blocks[2], "patch", 4),
        swap(blocks[3], "patch", 6),
    ]


def to_own_columns(weight):
    if not small_patch():
        return lax.all_to_all(weight, "patch", 1, 0, tiled=True)
    length = weight.shape[0]
    blocks = [block_of(weight, "patch", k, 1) for k in range(8)]
    theirs = swap(jnp.concatenate(blocks[1::2], axis=0), "patch", 1)
    both = [
        jnp.concatenate([kept, theirs[j * length : (j + 1) * length]], axis=0)
        for j, kept in enumerate(blocks[::2])
    ]
    halves = []
    for block in over_chips(both):
        halves += [block[:length], block[length:]]
    return assemble(halves, "patch", 0)


def back_to_rows(grad):
    core = lax.axis_index("patch") % 2
    blocks = [block_of(grad, "patch", k, 0) for k in range(8)]
    length = blocks[0].shape[0]
    theirs = swap(jnp.concatenate(blocks[1::2], axis=0), "patch", 1)
    both = [
        pair_up(kept, theirs[j * length : (j + 1) * length], core)
        for j, kept in enumerate(blocks[::2])
    ]
    return jnp.concatenate(over_chips(both), axis=0)


def side_by_side_kernel(stack, whole):
    own = lax.axis_index("patch") // 2
    length, width = whole.shape[0], stack.shape[1]
    for j in range(4):
        start = pl.multiple_of((own ^ j) * width, width)
        whole[:, pl.ds(start, width)] = stack[j * length : (j + 1) * length, :]


def side_by_side(stack):
    length, width = stack.shape[0] // 4, stack.shape[1]
    return pl.pallas_call(
        side_by_side_kernel,
        out_shape=jax.ShapeDtypeStruct((length, 4 * width), jnp.float32),
        in_specs=[pl.BlockSpec(memory_space=pltpu.VMEM)],
        out_specs=pl.BlockSpec(memory_space=pltpu.VMEM),
        compiler_params=pltpu.CompilerParams(vmem_limit_bytes=24 << 20),
        cost_estimate=pl.CostEstimate(flops=0, bytes_accessed=8 * stack.size, transcendentals=0),
    )(stack)


def to_columns(x):
    return lax.all_to_all(x, "frame", split_axis=1, concat_axis=0, tiled=True)


def to_slots(x):
    count = lax.axis_size("frame")
    parts = exchange([block_of(x, "frame", k, 0) for k in range(count)], "frame")
    return assemble(parts, "frame", 1)


def on_device(
    block_input,
    out_cotangent,
    caption,
    cond,
    ada_weight,
    ada_bias,
    qkv_weight,
    q_bias,
    v_bias,
    attn_out_weight,
    attn_out_bias,
    cross_q_weight,
    cross_q_bias,
    cross_kv_weight,
    cross_v_bias,
    cross_out_weight,
    cross_out_bias,
    fc1_weight,
    fc1_bias,
    fc2_weight,
    fc2_bias,
    frame_slot,
    clip_id,
    patch_mask,
    caption_mask,
):
    width = block_input.shape[-1]
    head_dim = width // H
    scaling = head_dim ** (-0.5)
    tokens_in = to_columns(block_input)
    cotangent = to_columns(out_cotangent)
    slots, cols, _ = tokens_in.shape
    rows = slots * cols
    clip_own = own_part(clip_id, "frame", 0)
    column_mask = own_part(patch_mask, "frame", 0).astype(jnp.float32)[:, None]
    frame_count = lax.axis_size("frame")
    frame_pos = all_sum(placed(frame_slot.astype(jnp.float32), "frame"), "frame")
    w_qkv = gather_rows(qkv_weight)

    cond_act, silu_pull = jax.vjp(jax.nn.silu, cond)
    cond_own = own_part(cond_act, "patch", 1)
    modulation_part = matmul(cond_own, ada_weight)
    biases = (ada_bias, q_bias, v_bias, attn_out_bias, cross_q_bias, cross_v_bias, cross_out_bias, fc2_bias)
    small = all_sum(
        jnp.concatenate(
            [modulation_part.reshape(-1)] + [placed(b, "patch") for b in biases]
        ),
        "patch",
    )
    place = modulation_part.size
    modulation = small[:place].reshape(modulation_part.shape)
    whole = []
    for b in biases:
        length = b.shape[0] * lax.axis_size("patch")
        whole.append(small[place : place + length])
        place += length
    b_ada, b_query, b_value, b_attn, b_cross_q, b_cross_v, b_cross_o, b_second = whole
    modulation = modulation + b_ada
    clip_onehot = (clip_own[:, None] == jnp.arange(CLIPS, dtype=jnp.int32)[None, :]).astype(
        jnp.float32
    )
    per_column = jnp.dot(clip_onehot, modulation, precision=lax.Precision.HIGHEST)
    shift_one, scale_one, gate_one, shift_two, scale_two, gate_two = jnp.split(
        per_column, 6, axis=1
    )

    caption_rows = caption.reshape(CLIPS * CAP, width)
    caption_share = own_part(own_part(caption_rows, "frame", 0), "patch", 1)
    core = lax.axis_index("patch") % 2
    kv_part = matmul(caption_share, cross_kv_weight)
    kv_half = sum_chips(half_over_cores(kv_part, core))
    kv_halves = assemble(exchange([kv_half] * frame_count, "frame"), "frame", 0)
    caption_kv = both_halves(kv_halves, core)
    cross_keys = caption_kv[:, :width].reshape(CLIPS * CAP, H, head_dim)
    cross_values = (caption_kv[:, width:] + b_cross_v).reshape(CLIPS * CAP, H, head_dim)

    w_three = gather_rows(
        jnp.concatenate([attn_out_weight, cross_q_weight, cross_out_weight], axis=1)
    )
    w_attn, w_cross_q, w_cross_o = jnp.split(w_three, 3, axis=1)
    w_first = to_own_columns(after(fc1_weight, w_qkv))
    grad_mlp = (column_mask * gate_two * cotangent).reshape(rows, width)
    grad_mlp_all = gather_rows(after(grad_mlp, w_three))

    normed_one, inverse_one = normalize(tokens_in)
    hidden_one = (normed_one * (1.0 + scale_one) + shift_one).reshape(rows, width)
    qkv_rows = matmul(hidden_one, w_qkv)
    queries = (qkv_rows[:, :width] + b_query).reshape(slots, cols, H, head_dim)
    keys = qkv_rows[:, width : 2 * width].reshape(slots, cols, H, head_dim)
    values = (qkv_rows[:, 2 * width :] + b_value).reshape(slots, cols, H, head_dim)
    slopes = 2.0 ** (-8.0 * (jnp.arange(H).astype(jnp.float32) + 1.0) / H)
    distance = jnp.abs(frame_pos[:, None] - frame_pos[None, :])
    bias_table = -slopes[:, None, None] * distance[None]
    key_valid = (frame_pos < FRAMES - 0.5)[None, None, None, :]
    scores = contract("fchd,schd->chfs", queries, keys) * scaling + bias_table[None]
    probs = softmax_rows(scores, key_valid)
    attended = contract("chfs,schd->fchd", probs, values)
    attended_rows = attended.reshape(rows, width)
    attn_branch = (matmul(attended_rows, w_attn) + b_attn).reshape(slots, cols, width)
    after_attn = tokens_in + column_mask * gate_one * attn_branch
    after_attn_rows = after_attn.reshape(rows, width)
    cross_queries = (matmul(after_attn_rows, w_cross_q) + b_cross_q).reshape(
        slots, cols, H, head_dim
    )
    key_clip = jnp.arange(CLIPS * CAP, dtype=jnp.int32) // CAP
    caption_ok = (
        (clip_own[:, None] == key_clip[None, :]) & (caption_mask.reshape(CLIPS * CAP)[None, :] > 0)
    )[None, :, None, :]
    cross_scores = contract("fchd,khd->fchk", cross_queries, cross_keys) * scaling
    cross_probs = softmax_rows(cross_scores, caption_ok)
    cross_att = contract("fchk,khd->fchd", cross_probs, cross_values)
    cross_rows = cross_att.reshape(rows, width)
    cross_branch = (matmul(cross_rows, w_cross_o) + b_cross_o).reshape(slots, cols, width)
    after_cross = after_attn + column_mask * cross_branch
    normed_two, inverse_two = normalize(after_cross)
    hidden_two = (normed_two * (1.0 + scale_two) + shift_two).reshape(rows, width)

    hidden_all = gather_tokens(hidden_two)
    pre_act = matmul(hidden_all, w_first) + fc1_bias
    activated, gelu_pull = jax.vjp(partial(jax.nn.gelu, approximate=True), pre_act)
    grad_pre = gelu_pull(matmul_nt(grad_mlp_all, fc2_weight))[0]
    grad_hidden_two = scatter_tokens(matmul_nt(grad_pre, w_first))
    grad_hidden_two = grad_hidden_two.reshape(slots, cols, width)
    grad_b_second = jnp.sum(grad_mlp, axis=0)

    grad_shift_two = jnp.sum(grad_hidden_two, axis=0)
    grad_scale_two = jnp.sum(grad_hidden_two * normed_two, axis=0)
    grad_after_cross = cotangent + normalize_back(
        grad_hidden_two * (1.0 + scale_two), normed_two, inverse_two
    )
    grad_cross_branch = (column_mask * grad_after_cross).reshape(rows, width)
    grad_w_cross_o = matmul_tn(cross_rows, grad_cross_branch)
    grad_b_cross_o = jnp.sum(grad_cross_branch, axis=0)
    activated, grad_pre = after((activated, grad_pre), grad_w_cross_o)
    grad_w_first = matmul_tn(hidden_all, grad_pre)
    grad_w_second = matmul_tn(activated, grad_mlp_all)
    grad_cross_branch = after(grad_cross_branch, (grad_w_first, grad_w_second))
    grad_w_second = frame_sum(grad_w_second)
    if small_patch():
        grad_w_first = side_by_side(frame_sum(back_to_rows(grad_w_first)))
    else:
        grad_w_first = frame_sum(lax.all_to_all(grad_w_first, "patch", 0, 1, tiled=True))
    grad_b_first = all_sum(jnp.sum(grad_pre, axis=0), "frame")
    mlp_parts = matmul(activated, fc2_weight)
    grad_cross_att = matmul_nt(grad_cross_branch, w_cross_o).reshape(slots, cols, H, head_dim)
    cross_row_terms = jnp.sum(grad_cross_att * cross_att, axis=-1)[..., None]
    grad_cross_probs = contract("fchd,khd->fchk", grad_cross_att, cross_values)
    grad_cross_scores = cross_probs * (grad_cross_probs - cross_row_terms) * scaling
    grad_cross_queries = contract("fchk,khd->fchd", grad_cross_scores, cross_keys).reshape(
        rows, width
    )
    grad_cross_keys = contract("fchk,fchd->khd", grad_cross_scores, cross_queries).reshape(
        CLIPS * CAP, width
    )
    grad_cross_values = contract("fchk,fchd->khd", cross_probs, grad_cross_att).reshape(
        CLIPS * CAP, width
    )
    grad_kv = jnp.concatenate([grad_cross_keys, grad_cross_values], axis=1)
    half_kv = half_over_cores(grad_kv, core)
    half_share = sum(
        exchange([block_of(half_kv, "frame", k, 0) for k in range(frame_count)], "frame")
    )
    grad_kv_share = both_halves(sum_chips(half_share), core)
    grad_w_cross_kv = frame_sum(matmul_tn(caption_share, grad_kv_share))
    grad_b_cross_v = jnp.sum(grad_kv_share[:, width:], axis=0)
    grad_caption_share = all_sum(
        placed(matmul_nt(grad_kv_share, cross_kv_weight), "patch"), "patch"
    )
    grad_caption = assemble(
        exchange([grad_caption_share] * frame_count, "frame"), "frame", 0
    ).reshape(caption.shape)
    grad_w_cross_q = matmul_tn(after_attn_rows, grad_cross_queries)
    grad_b_cross_q = jnp.sum(grad_cross_queries, axis=0)
    grad_cross_queries = after(grad_cross_queries, grad_w_cross_q)
    grad_after_attn = grad_after_cross + matmul_nt(grad_cross_queries, w_cross_q).reshape(
        slots, cols, width
    )
    grad_attn_rows = (column_mask * gate_one * grad_after_attn).reshape(rows, width)
    grad_gate_one = jnp.sum(column_mask * attn_branch * grad_after_attn, axis=0)
    grad_w_attn = matmul_tn(attended_rows, grad_attn_rows)
    grad_b_attn = jnp.sum(grad_attn_rows, axis=0)
    grad_attn_rows = after(grad_attn_rows, grad_w_attn)
    mlp_sum = scatter_tokens(after(mlp_parts, grad_w_attn))
    mlp_branch = (mlp_sum + b_second).reshape(slots, cols, width)
    block_out = to_slots(after_cross + column_mask * gate_two * mlp_branch)
    grad_gate_two = jnp.sum(column_mask * mlp_branch * cotangent, axis=0)
    grad_attended = matmul_nt(grad_attn_rows, w_attn).reshape(slots, cols, H, head_dim)
    row_terms = jnp.transpose(jnp.sum(grad_attended * attended, axis=-1), (1, 2, 0))[..., None]
    grad_probs = contract("fchd,schd->chfs", grad_attended, values)
    grad_scores = probs * (grad_probs - row_terms)
    grad_queries = (contract("chfs,schd->fchd", grad_scores, keys) * scaling).reshape(rows, width)
    grad_keys = (contract("chfs,fchd->schd", grad_scores, queries) * scaling).reshape(rows, width)
    grad_values = contract("chfs,fchd->schd", probs, grad_attended).reshape(rows, width)
    grad_qkv = jnp.concatenate([grad_queries, grad_keys, grad_values], axis=1)
    grad_w_qkv = matmul_tn(hidden_one, grad_qkv)
    grad_b_query = jnp.sum(grad_queries, axis=0)
    grad_b_value = jnp.sum(grad_values, axis=0)
    grad_hidden_one = matmul_nt(grad_qkv, w_qkv).reshape(slots, cols, width)
    grad_shift_one = jnp.sum(grad_hidden_one, axis=0)
    grad_scale_one = jnp.sum(grad_hidden_one * normed_one, axis=0)
    input_grad = to_slots(
        grad_after_attn
        + normalize_back(grad_hidden_one * (1.0 + scale_one), normed_one, inverse_one)
    )
    grad_per_column = jnp.concatenate(
        [
            grad_shift_one,
            grad_scale_one,
            grad_gate_one,
            grad_shift_two,
            grad_scale_two,
            grad_gate_two,
        ],
        axis=1,
    )
    grad_modulation_part = jnp.dot(
        clip_onehot.T, grad_per_column, precision=lax.Precision.HIGHEST
    )
    first = (lax.axis_index("patch") == 0).astype(jnp.float32)
    bias_grads = (
        grad_b_query,
        grad_b_value,
        grad_b_attn,
        grad_b_cross_q,
        grad_b_cross_v * first,
        grad_b_cross_o,
        grad_b_second,
    )
    small_grads = all_sum(
        all_sum(
            jnp.concatenate([grad_modulation_part.reshape(-1)] + list(bias_grads)), "patch"
        ),
        "frame",
    )
    place = grad_modulation_part.size
    grad_modulation = small_grads[:place].reshape(grad_modulation_part.shape)
    own_biases = []
    for b in bias_grads:
        own_biases.append(own_part(small_grads[place : place + b.shape[0]], "patch", 0))
        place += b.shape[0]
    g_query, g_value, g_attn, g_cross_q, g_cross_v, g_cross_o, g_second = own_biases
    grad_w_ada = matmul_tn(cond_own, grad_modulation)
    grad_b_ada = own_part(jnp.sum(grad_modulation, axis=0), "patch", 0)
    grad_cond_act = all_sum(placed(matmul_nt(grad_modulation, ada_weight), "patch"), "patch")
    grad_cond = silu_pull(grad_cond_act)[0]

    def finish(whole_grad):
        return frame_sum(scatter_rows(whole_grad))

    return (
        block_out,
        input_grad,
        grad_caption,
        grad_cond,
        grad_w_ada,
        grad_b_ada,
        finish(grad_w_qkv),
        g_query,
        g_value,
        finish(grad_w_attn),
        g_attn,
        finish(grad_w_cross_q),
        g_cross_q,
        grad_w_cross_kv,
        g_cross_v,
        finish(grad_w_cross_o),
        g_cross_o,
        grad_w_first,
        grad_b_first,
        grad_w_second,
        g_second,
    )


def solution(mesh):
    tokens = P("frame", "patch", None)
    weight = P("patch", None)
    vector = P("patch")
    parameters = (
        weight, vector, weight, vector, vector, weight, vector, weight, vector,
        weight, vector, weight, vector, weight, vector, weight, vector,
    )
    in_specs = (tokens, tokens, P(), P()) + parameters + (P("frame"), vector, vector, P())
    out_specs = (tokens, tokens, P(), P()) + parameters
    return jax.shard_map(
        on_device, mesh=mesh, in_specs=in_specs, out_specs=out_specs, check_vma=False
    )
```

```python
from functools import partial

import jax
import jax.numpy as jnp
from jax import lax
from jax.experimental import pallas as pl
from jax.experimental.pallas import tpu as pltpu
from jax.sharding import PartitionSpec as P

H = 16
CAP = 120
FRAMES = 17
CLIPS = 4


EPSILON = 1e-06
BEST = lax.Precision.HIGH


def matmul(left, right):
    return jnp.dot(left, right, precision=BEST)


def contract(form, left, right):
    return jnp.einsum(form, left, right, precision=BEST)


def matmul_nt(left, right):
    return lax.dot_general(left, right, (((1,), (1,)), ((), ())), precision=BEST)


def matmul_tn(left, right):
    return lax.dot_general(left, right, (((0,), (0,)), ((), ())), precision=BEST)


def normalize(rows):
    average = jnp.mean(rows, axis=-1, keepdims=True)
    centred = rows - average
    spread = jnp.mean(centred * centred, axis=-1, keepdims=True)
    inverse = lax.rsqrt(spread + EPSILON)
    return (centred * inverse, inverse)


def normalize_back(grad_normed, normed, inverse):
    first_mean = jnp.mean(grad_normed, axis=-1, keepdims=True)
    second_mean = jnp.mean(grad_normed * normed, axis=-1, keepdims=True)
    return inverse * (grad_normed - first_mean - normed * second_mean)


def softmax_rows(scores, allowed):
    masked = jnp.where(allowed, scores, -1e30)
    highest = jnp.max(masked, axis=-1, keepdims=True)
    exponent = jnp.exp(masked - highest)
    return exponent / jnp.sum(exponent, axis=-1, keepdims=True)


def swap(value, axis, bit):
    size = lax.axis_size(axis)
    return lax.ppermute(value, axis, [(i, i ^ bit) for i in range(size)])


def all_sum(value, axis):
    bit = 1
    while bit < lax.axis_size(axis):
        value = value + swap(value, axis, bit)
        bit *= 2
    return value


def placed(vector, axis):
    length = vector.shape[-1]
    whole = jnp.zeros(vector.shape[:-1] + (length * lax.axis_size(axis),), vector.dtype)
    return lax.dynamic_update_slice_in_dim(
        whole, vector, lax.axis_index(axis) * length, axis=vector.ndim - 1
    )


def own_part(array, axis, dim):
    length = array.shape[dim] // lax.axis_size(axis)
    return lax.dynamic_slice_in_dim(array, lax.axis_index(axis) * length, length, axis=dim)


def after(value, done):
    return lax.optimization_barrier((value, done))[0]


def small_patch():
    return lax.axis_size("patch") == 8 and lax.axis_size("frame") == 4


def padded(vector, rows):
    return jnp.pad(vector, (0, rows * 128 - vector.shape[0])).reshape(rows, 128)


def greet(partners):
    barrier = pltpu.get_barrier_semaphore()
    for partner in partners:
        pl.semaphore_signal(barrier, inc=1, device_id={"patch": partner}, device_id_type=pl.DeviceIdType.MESH)
    pl.semaphore_wait(barrier, len(partners))


def remote(source, target, send_sems, recv_sems, index, device):
    return pltpu.make_async_remote_copy(
        src_ref=source, dst_ref=target, send_sem=send_sems.at[index], recv_sem=recv_sems.at[index],
        device_id={"patch": device}, device_id_type=pl.DeviceIdType.MESH)


def token_gather_kernel(rows, whole, local_sem, send_sems, recv_sems):
    own = lax.axis_index("patch")
    core, along_x, along_y, across = own ^ 1, own ^ 2, own ^ 4, own ^ 6
    greet((core, along_x, along_y))
    length = rows.shape[0] // 4
    sent = []

    def piece(owner, q):
        return whole.at[owner, pl.ds(q * length, length)]

    def send(source, owner, q, index, device):
        copy = remote(source, piece(owner, q), send_sems, recv_sems, index, device)
        copy.start()
        sent.append(copy)

    def arrived(owner, q, index, device):
        remote(piece(owner, q), piece(owner, q), send_sems, recv_sems, index, device).wait_recv()

    mine = pltpu.make_async_copy(rows, whole.at[own], local_sem)
    mine.start()
    for q_x, q_y in ((0, 2), (1, 3), (2, 0), (3, 1)):
        send(rows.at[pl.ds(q_x * length, length)], own, q_x, q_x, along_x)
        send(rows.at[pl.ds(q_y * length, length)], own, q_y, 4 + q_y, along_y)
    for q in range(4):
        send(rows.at[pl.ds(q * length, length)], own, q, 12 + q, core)
    for q_x, q_y in ((0, 2), (1, 3), (2, 0), (3, 1)):
        arrived(along_x, q_x, q_x, along_x)
        if q_x < 2:
            send(piece(along_x, q_x), along_x, q_x, 8 + q_x, along_y)
        send(piece(along_x, q_x), along_x, q_x, 16 + q_x, core)
        arrived(along_y, q_y, 4 + q_y, along_y)
        if q_y >= 2:
            send(piece(along_y, q_y), along_y, q_y, 8 + q_y, along_x)
        send(piece(along_y, q_y), along_y, q_y, 20 + q_y, core)
    for q in (0, 2, 1, 3):
        arrived(across, q, 8 + q, along_y if q < 2 else along_x)
        send(piece(across, q), across, q, 24 + q, core)
    for q in range(4):
        arrived(core, q, 12 + q, core)
        arrived(core ^ 2, q, 16 + q, core)
        arrived(core ^ 4, q, 20 + q, core)
        arrived(core ^ 6, q, 24 + q, core)
    for copy in sent:
        copy.wait_send()
    mine.wait()


def token_gather(rows):
    length, width = rows.shape
    return pl.pallas_call(
        token_gather_kernel,
        out_shape=jax.ShapeDtypeStruct((8, length, width), jnp.float32),
        in_specs=[pl.BlockSpec(memory_space=pltpu.VMEM)],
        out_specs=pl.BlockSpec(memory_space=pl.ANY),
        scratch_shapes=[pltpu.SemaphoreType.DMA, pltpu.SemaphoreType.DMA((28,)), pltpu.SemaphoreType.DMA((28,))],
        compiler_params=pltpu.CompilerParams(collective_id=0, has_side_effects=True, vmem_limit_bytes=16 << 20),
        cost_estimate=pl.CostEstimate(flops=0, bytes_accessed=64 * length * width, transcendentals=0),
    )(rows).reshape(8 * length, width)


def token_scatter_kernel(parts, total, kept, theirs, by_x, by_y, from_x, from_y, local_sems, send_sems, recv_sems):
    own = lax.axis_index("patch")
    core, along_x, along_y = own ^ 1, own ^ 2, own ^ 4
    greet((core, along_x, along_y))
    half = total.shape[0] // 2
    upper, lower = pl.ds(0, half), pl.ds(half, half)
    order = (3, 2, 1, 0)
    sent, loads = [], {}

    def send(source, target, index, device):
        copy = remote(source, target, send_sems, recv_sems, index, device)
        copy.start()
        sent.append(copy)

    def arrived(target, index, device):
        remote(target, target, send_sems, recv_sems, index, device).wait_recv()

    for j in order:
        send(parts.at[core ^ (2 * j)], theirs.at[j], j, core)
        loads[j] = pltpu.make_async_copy(parts.at[own ^ (2 * j)], kept.at[j], local_sems.at[j])
        loads[j].start()

    def add_cores(j):
        loads[j].wait()
        arrived(theirs.at[j], j, core)
        kept[j] = kept[j] + theirs[j]

    add_cores(3)
    send(kept.at[3, upper], by_x, 4, along_x)
    send(kept.at[3, lower], by_y, 5, along_y)
    add_cores(2)
    send(kept.at[2, lower], from_y.at[lower], 6, along_y)
    add_cores(1)
    send(kept.at[1, upper], from_x.at[upper], 7, along_x)
    add_cores(0)
    arrived(by_x, 4, along_x)
    kept[2, upper] = kept[2, upper] + by_x[...]
    send(kept.at[2, upper], from_y.at[upper], 8, along_y)
    arrived(by_y, 5, along_y)
    kept[1, lower] = kept[1, lower] + by_y[...]
    send(kept.at[1, lower], from_x.at[lower], 9, along_x)
    arrived(from_y.at[lower], 6, along_y)
    arrived(from_x.at[upper], 7, along_x)
    arrived(from_y.at[upper], 8, along_y)
    arrived(from_x.at[lower], 9, along_x)
    total[...] = kept[0] + from_x[...] + from_y[...]
    for copy in sent:
        copy.wait_send()


def token_scatter(parts):
    length, width = parts.shape[0] // 8, parts.shape[1]
    block = (length, width)
    return pl.pallas_call(
        token_scatter_kernel,
        out_shape=jax.ShapeDtypeStruct(block, jnp.float32),
        in_specs=[pl.BlockSpec(memory_space=pl.ANY)],
        out_specs=pl.BlockSpec(memory_space=pltpu.VMEM),
        scratch_shapes=[
            pltpu.VMEM((4,) + block, jnp.float32), pltpu.VMEM((4,) + block, jnp.float32),
            pltpu.VMEM((length // 2, width), jnp.float32), pltpu.VMEM((length // 2, width), jnp.float32),
            pltpu.VMEM(block, jnp.float32), pltpu.VMEM(block, jnp.float32),
            pltpu.SemaphoreType.DMA((4,)), pltpu.SemaphoreType.DMA((10,)), pltpu.SemaphoreType.DMA((10,)),
        ],
        compiler_params=pltpu.CompilerParams(collective_id=1, has_side_effects=True, vmem_limit_bytes=32 << 20),
        cost_estimate=pl.CostEstimate(flops=0, bytes_accessed=48 * length * width, transcendentals=0),
    )(parts.reshape((8,) + block))


class Links:
    def __init__(self, send_sems, recv_sems):
        self.send_sems, self.recv_sems = send_sems, recv_sems
        self.count = 0
        self.sent = []

    def plan(self):
        self.count += 1
        return self.count - 1

    def copy(self, source, target, index, device):
        return pltpu.make_async_remote_copy(
            src_ref=source, dst_ref=target, send_sem=self.send_sems.at[index],
            recv_sem=self.recv_sems.at[index], device_id=device,
            device_id_type=pl.DeviceIdType.MESH,
        )

    def send(self, source, target, index, device):
        self.copy(source, target, index, device).start()
        self.sent.append((source, index, device))

    def wait(self, target, index, device):
        self.copy(target, target, index, device).wait_recv()

    def drain(self):
        for source, index, device in self.sent:
            self.copy(source, source, index, device).wait_send()


def greet_all(devices):
    barrier = pltpu.get_barrier_semaphore()
    for device in devices:
        pl.semaphore_signal(barrier, inc=1, device_id=device, device_id_type=pl.DeviceIdType.MESH)
    pl.semaphore_wait(barrier, len(devices))


def begin_kernel(
    tokens, slots, small, kv,
    tokens_out, slots_out, small_out, kv_out,
    small_1, small_2, small_got, kv_1, kv_2, kv_got_core, kv_got_1, kv_got_2,
    send_sems, recv_sems,
):
    me, z = lax.axis_index("patch"), lax.axis_index("frame")
    core, x, y = ({"patch": me ^ k} for k in (1, 2, 4))
    frames = [None] + [{"frame": z ^ k} for k in (1, 2, 3)]
    greet_all([core, x, y] + frames[1:])
    links = Links(send_sems, recv_sems)
    count, part = tokens.shape[0], tokens.shape[1] // 4
    rows, width = kv_1.shape

    def columns(k):
        return pl.ds(pl.multiple_of((z ^ k) * part, part), part)

    def of_slots(k):
        return pl.ds((z ^ k) * count, count)

    half = pl.multiple_of((me % 2) * width, 128)
    other = pl.multiple_of((1 - me % 2) * width, 128)
    mine, theirs = pl.ds(half, width), pl.ds(other, width)

    at = links.plan()
    links.send(small, small_got.at[0], at, core)
    at_kv = links.plan()
    links.send(kv.at[:, theirs], kv_got_core, at_kv, core)
    token_at = [None] + [links.plan() for _ in range(3)]
    slot_at = [None] + [links.plan() for _ in range(3)]
    for k in (1, 2, 3):
        links.send(slots, slots_out.at[z], slot_at[k], frames[k])
        links.send(tokens.at[:, columns(k)], tokens_out.at[of_slots(0)], token_at[k], frames[k])
    slots_out[z] = slots[...]
    tokens_out[of_slots(0)] = tokens[:, columns(0)]

    links.wait(small_got.at[0], at, core)
    small_1[...] = small[...] + small_got[0]
    at = links.plan()
    links.send(small_1, small_got.at[1], at, x)
    links.wait(kv_got_core, at_kv, core)
    kv_1[...] = kv[:, mine] + kv_got_core[...]
    upper, lower = pl.ds(0, 64), pl.ds(64, rows - 64)
    at_u, at_l = links.plan(), links.plan()
    links.send(kv_1.at[upper], kv_got_1.at[upper], at_u, x)
    links.send(kv_1.at[lower], kv_got_1.at[lower], at_l, y)
    links.wait(small_got.at[1], at, x)
    small_2[...] = small_1[...] + small_got[1]
    at = links.plan()
    links.send(small_2, small_got.at[2], at, y)
    links.wait(kv_got_1.at[upper], at_u, x)
    links.wait(kv_got_1.at[lower], at_l, y)
    kv_2[...] = kv_1[...] + kv_got_1[...]
    at_u, at_l = links.plan(), links.plan()
    links.send(kv_2.at[upper], kv_got_2.at[upper], at_u, y)
    links.send(kv_2.at[lower], kv_got_2.at[lower], at_l, x)
    links.wait(small_got.at[2], at, y)
    small_out[...] = small_2[...] + small_got[2]
    links.wait(kv_got_2.at[upper], at_u, y)
    links.wait(kv_got_2.at[lower], at_l, x)

    def share(k, columns):
        return kv_out.at[pl.ds(pl.multiple_of((z ^ k) * rows, rows), rows), columns]

    kv_out[pl.ds(pl.multiple_of(z * rows, rows), rows), mine] = kv_2[...] + kv_got_2[...]
    kv_at = [None] + [links.plan() for _ in range(3)]
    core_at = [links.plan() for _ in range(4)]
    for k in (1, 2, 3):
        links.send(share(0, mine), share(0, mine), kv_at[k], frames[k])
    links.send(share(0, mine), share(0, mine), core_at[0], core)
    for k in (1, 2, 3):
        links.wait(share(k, mine), kv_at[k], frames[k])
        links.send(share(k, mine), share(k, mine), core_at[k], core)
    for k in (1, 2, 3):
        links.wait(slots_out.at[z ^ k], slot_at[k], frames[k])
        links.wait(tokens_out.at[of_slots(k)], token_at[k], frames[k])
    for k in range(4):
        links.wait(share(k, theirs), core_at[k], core)
    links.drain()


def begin(tokens, slots, small, kv):
    count, cols, width = tokens.shape
    rows = kv.shape[0]
    f32, vmem = jnp.float32, pl.BlockSpec(memory_space=pltpu.VMEM)
    half = pltpu.VMEM((rows, width), f32)
    return pl.pallas_call(
        begin_kernel,
        out_shape=(
            jax.ShapeDtypeStruct((4 * count, cols // 4, width), f32),
            jax.ShapeDtypeStruct((4,) + slots.shape, f32),
            jax.ShapeDtypeStruct(small.shape, f32),
            jax.ShapeDtypeStruct((4 * rows, 2 * width), f32),
        ),
        in_specs=[vmem] * 4,
        out_specs=[vmem] * 4,
        scratch_shapes=[
            pltpu.VMEM(small.shape, f32), pltpu.VMEM(small.shape, f32),
            pltpu.VMEM((3,) + small.shape, f32), half, half, half, half, half,
            pltpu.SemaphoreType.DMA((24,)), pltpu.SemaphoreType.DMA((24,)),
        ],
        compiler_params=pltpu.CompilerParams(
            collective_id=2, has_side_effects=True, vmem_limit_bytes=32 << 20
        ),
        cost_estimate=pl.CostEstimate(flops=0, bytes_accessed=32 << 20, transcendentals=0),
    )(tokens, slots, small, kv)


UNITS = 6


def finish_kernel(
    first, attn, cross_q, cross_o, kv, tokens, small, caption,
    first_out, attn_out, cross_q_out, cross_o_out, kv_out, tokens_out, small_out, caption_out,
    kept, theirs, by_x, by_y, from_x, from_y, along_z, across_z,
    small_sums, small_got, small_z, load_sems, credit, send_sems, recv_sems,
):
    me, z = lax.axis_index("patch"), lax.axis_index("frame")
    outer = (z == 0) | (z == 3)
    inner = (z == 1) | (z == 2)
    core, x, y = ({"patch": me ^ k} for k in (1, 2, 4))
    frames = [None] + [{"frame": z ^ k} for k in (1, 2, 3)]
    near, facing = frames[1], frames[3]
    greet_all([core, x, y] + frames[1:])
    links = Links(send_sems, recv_sems)
    rows, width = by_x.shape[1] * 2, by_x.shape[2]
    upper, lower = pl.ds(0, rows // 2), pl.ds(rows // 2, rows // 2)
    count, part = tokens_out.shape[0], tokens_out.shape[1] // 4

    token_at = [None] + [links.plan() for _ in range(3)]

    def send_tokens():
        for k in (1, 2, 3):
            links.send(
                tokens.at[pl.ds((z ^ k) * count, count)],
                tokens_out.at[:, pl.ds(pl.multiple_of(z * part, part), part)],
                token_at[k], frames[k],
            )
        tokens_out[:, pl.ds(pl.multiple_of(z * part, part), part)] = tokens[pl.ds(z * count, count)]

    def frame_steps(value, result, near_got, facing_got):
        up, over, down = links.plan(), links.plan(), links.plan()

        def one():
            @pl.when(outer)
            def _():
                links.copy(value, near_got, up, near).start()

        def two():
            @pl.when(inner)
            def _():
                links.wait(near_got, up, near)
                near_got[...] = near_got[...] + value[...]
                links.copy(near_got, facing_got, over, facing).start()

        def three():
            @pl.when(inner)
            def _():
                links.wait(facing_got, over, facing)
                result[...] = near_got[...] + facing_got[...]
                links.copy(result, near_got, down, near).start()

        def four():
            @pl.when(outer)
            def _():
                links.wait(near_got, down, near)
                result[...] = near_got[...]
                links.copy(value, value, up, near).wait_send()

            @pl.when(inner)
            def _():
                links.copy(near_got, near_got, over, facing).wait_send()
                links.copy(result, result, down, near).wait_send()

        return one, two, three, four

    def piece(ref, u):
        return ref.at[:, pl.ds(u * width, width)]

    outs = [piece(first_out, u) for u in range(3)] + [attn_out, cross_q_out, cross_o_out]
    steps = [
        frame_steps(kept.at[u, 0], outs[u], along_z.at[u], across_z.at[u]) for u in range(UNITS)
    ] + [
        frame_steps(piece(kv, u), piece(kv_out, u), along_z.at[UNITS + u], across_z.at[UNITS + u])
        for u in range(2)
    ]
    small_steps = frame_steps(small_sums.at[2], small_out, small_z.at[0], small_z.at[1])

    core_at = [[links.plan() for _ in range(4)] for _ in range(UNITS)]
    link_at = [[links.plan() for _ in range(6)] for _ in range(UNITS)]

    def source(u, device, j):
        start = pl.multiple_of((device ^ (2 * j)) * rows, rows)
        ref = first if u < 3 else (attn, cross_q, cross_o)[u - 3]
        return ref.at[pl.ds(start, rows), pl.ds((u % 3) * width if u < 3 else 0, width)]

    def load(u, j):
        return pltpu.make_async_copy(source(u, me, j), kept.at[u, j], load_sems.at[u, j])

    def to_core(u):
        if u >= 3:
            pl.semaphore_wait(credit.at[u - 3], 1)
        for j in (3, 2, 1, 0):
            links.send(source(u, me ^ 1, j), theirs.at[u % 3, j], core_at[u][j], core)

    def add_cores(u, j):
        load(u, j).wait()
        links.wait(theirs.at[u % 3, j], core_at[u][j], core)
        kept[u, j] = kept[u, j] + theirs[u % 3, j]

    def stage_one(u):
        at = link_at[u]
        add_cores(u, 3)
        links.send(kept.at[u, 3, upper], by_x.at[u], at[0], x)
        links.send(kept.at[u, 3, lower], by_y.at[u], at[1], y)
        add_cores(u, 2)
        links.send(kept.at[u, 2, lower], from_y.at[u, lower], at[2], y)
        add_cores(u, 1)
        links.send(kept.at[u, 1, upper], from_x.at[u, upper], at[3], x)
        add_cores(u, 0)
        if u + 3 < UNITS:
            pl.semaphore_signal(
                credit.at[u], inc=1, device_id=core, device_id_type=pl.DeviceIdType.MESH
            )
            to_core(u + 3)

    def stage_two(u):
        at = link_at[u]
        links.wait(by_x.at[u], at[0], x)
        kept[u, 2, upper] = kept[u, 2, upper] + by_x[u]
        links.send(kept.at[u, 2, upper], from_y.at[u, upper], at[4], y)
        links.wait(by_y.at[u], at[1], y)
        kept[u, 1, lower] = kept[u, 1, lower] + by_y[u]
        links.send(kept.at[u, 1, lower], from_x.at[u, lower], at[5], x)

    def stage_three(u):
        at = link_at[u]
        links.wait(from_y.at[u, lower], at[2], y)
        links.wait(from_x.at[u, upper], at[3], x)
        links.wait(from_y.at[u, upper], at[4], y)
        links.wait(from_x.at[u, lower], at[5], x)
        kept[u, 0] = kept[u, 0] + from_x[u] + from_y[u]
        steps[u][0]()

    caption_at = [links.plan() for _ in range(10)]

    def caption_frames():
        caption_out[me, z] = caption[...]
        for k in (1, 2, 3):
            links.send(caption, caption_out.at[me, z], caption_at[k - 1], frames[k])

    def caption_x():
        for k in (1, 2, 3):
            links.wait(caption_out.at[me, z ^ k], caption_at[k - 1], frames[k])
        links.send(caption_out.at[me], caption_out.at[me], caption_at[3], x)

    def caption_y():
        links.wait(caption_out.at[me ^ 2], caption_at[3], x)
        for i, k in enumerate((0, 2)):
            links.send(caption_out.at[me ^ k], caption_out.at[me ^ k], caption_at[4 + i], y)

    def caption_core():
        for i, k in enumerate((0, 2)):
            links.wait(caption_out.at[me ^ 4 ^ k], caption_at[4 + i], y)
        for i, k in enumerate((0, 2, 4, 6)):
            links.send(caption_out.at[me ^ k], caption_out.at[me ^ k], caption_at[6 + i], core)

    def caption_end():
        for i, k in enumerate((0, 2, 4, 6)):
            links.wait(caption_out.at[me ^ 1 ^ k], caption_at[6 + i], core)

    small_at = [links.plan() for _ in range(3)]
    links.send(small, small_got.at[0], small_at[0], core)
    caption_frames()
    for u in range(UNITS):
        for j in (3, 2, 1, 0):
            load(u, j).start()
    steps[6][0]()
    steps[7][0]()
    for u in range(3):
        to_core(u)
    links.wait(small_got.at[0], small_at[0], core)
    small_sums[0] = small[...] + small_got[0]
    links.send(small_sums.at[0], small_got.at[1], small_at[1], x)
    stage_one(0)
    links.wait(small_got.at[1], small_at[1], x)
    small_sums[1] = small_sums[0] + small_got[1]
    links.send(small_sums.at[1], small_got.at[2], small_at[2], y)
    stage_one(1)
    steps[6][1]()
    steps[7][1]()
    links.wait(small_got.at[2], small_at[2], y)
    small_sums[2] = small_sums[1] + small_got[2]
    small_steps[0]()
    stage_two(0)
    caption_x()
    stage_one(2)
    send_tokens()
    small_steps[1]()
    steps[6][2]()
    steps[7][2]()
    small_steps[2]()
    for u in range(1, UNITS):
        stage_two(u)
        if u + 2 < UNITS:
            stage_one(u + 2)
        stage_three(u - 1)
        if u >= 2:
            steps[u - 2][1]()
        if u >= 3:
            steps[u - 3][2]()
        if u == 2:
            caption_y()
        if u == 4:
            caption_core()
    stage_three(UNITS - 1)
    steps[UNITS - 2][1]()
    steps[UNITS - 3][2]()
    steps[UNITS - 1][1]()
    steps[UNITS - 2][2]()
    steps[UNITS - 1][2]()
    for step in steps + [small_steps]:
        step[3]()
    caption_end()
    for k in (1, 2, 3):
        where = pl.ds(pl.multiple_of((z ^ k) * part, part), part)
        links.wait(tokens_out.at[:, where], token_at[k], frames[k])
    links.drain()


def finish(first, attn, cross_q, cross_o, kv, tokens, small, caption):
    rows, width = first.shape[0] // 8, first.shape[1] // 3
    count, part = tokens.shape[0] // 4, tokens.shape[1]
    f32, vmem = jnp.float32, pl.BlockSpec(memory_space=pltpu.VMEM)
    hbm = pl.BlockSpec(memory_space=pl.ANY)

    def shape(*sizes):
        return jax.ShapeDtypeStruct(sizes, f32)

    return pl.pallas_call(
        finish_kernel,
        out_shape=(
            shape(rows, 3 * width), shape(rows, width), shape(rows, width), shape(rows, width),
            shape(rows, 2 * width), shape(count, 4 * part, tokens.shape[2]), shape(*small.shape),
            shape(8, 4, *caption.shape),
        ),
        in_specs=[hbm] * 4 + [vmem] * 4,
        out_specs=[vmem] * 8,
        scratch_shapes=[
            pltpu.VMEM((UNITS, 4, rows, width), f32), pltpu.VMEM((3, 4, rows, width), f32),
            pltpu.VMEM((UNITS, rows // 2, width), f32), pltpu.VMEM((UNITS, rows // 2, width), f32),
            pltpu.VMEM((UNITS, rows, width), f32), pltpu.VMEM((UNITS, rows, width), f32),
            pltpu.VMEM((UNITS + 2, rows, width), f32), pltpu.VMEM((UNITS + 2, rows, width), f32),
            pltpu.VMEM((3,) + small.shape, f32), pltpu.VMEM((3,) + small.shape, f32),
            pltpu.VMEM((2,) + small.shape, f32),
            pltpu.SemaphoreType.DMA((UNITS, 4)), pltpu.SemaphoreType.REGULAR((3,)),
            pltpu.SemaphoreType.DMA((112,)), pltpu.SemaphoreType.DMA((112,)),
        ],
        compiler_params=pltpu.CompilerParams(
            collective_id=3, has_side_effects=True, vmem_limit_bytes=60 << 20
        ),
        cost_estimate=pl.CostEstimate(flops=0, bytes_accessed=256 << 20, transcendentals=0),
    )(first, attn, cross_q, cross_o, kv, tokens, small, caption)


def middle_kernel(
    parts, kv,
    total, kv_out,
    kept, theirs, by_x, by_y, from_x, from_y,
    kv_half, kv_core, kv_got, kv_1, kv_2, kv_got_1, kv_got_2,
    load_sems, send_sems, recv_sems,
):
    me, z = lax.axis_index("patch"), lax.axis_index("frame")
    core, x, y = ({"patch": me ^ k} for k in (1, 2, 4))
    frames = [None] + [{"frame": z ^ k} for k in (1, 2, 3)]
    greet_all([core, x, y] + frames[1:])
    links = Links(send_sems, recv_sems)
    rows, width = kv_1.shape
    half = pl.multiple_of((me % 2) * width, 128)
    other = pl.multiple_of((1 - me % 2) * width, 128)
    mine, others = pl.ds(half, width), pl.ds(other, width)

    def share(ref, k):
        return ref.at[pl.ds(pl.multiple_of((z ^ k) * rows, rows), rows)]

    at_kv = links.plan()
    links.send(kv.at[:, others], kv_core, at_kv, core)
    core_at = [links.plan() for _ in range(4)]
    loads = [
        pltpu.make_async_copy(parts.at[me ^ (2 * j)], kept.at[j], load_sems.at[j])
        for j in range(4)
    ]
    for j in (3, 2, 1, 0):
        links.send(parts.at[me ^ 1 ^ (2 * j)], theirs.at[j], core_at[j], core)
        loads[j].start()
    links.wait(kv_core, at_kv, core)
    kv_half[...] = kv[:, mine] + kv_core[...]
    kv_at = [None] + [links.plan() for _ in range(3)]
    for k in (1, 2, 3):
        links.send(share(kv_half, k), kv_got.at[k - 1], kv_at[k], frames[k])

    count = total.shape[0] // 2
    upper, lower = pl.ds(0, count), pl.ds(count, count)
    at = [links.plan() for _ in range(6)]

    def add_cores(j):
        loads[j].wait()
        links.wait(theirs.at[j], core_at[j], core)
        kept[j] = kept[j] + theirs[j]

    add_cores(3)
    links.send(kept.at[3, upper], by_x, at[0], x)
    links.send(kept.at[3, lower], by_y, at[1], y)
    add_cores(2)
    links.send(kept.at[2, lower], from_y.at[lower], at[2], y)
    add_cores(1)
    links.send(kept.at[1, upper], from_x.at[upper], at[3], x)
    add_cores(0)
    links.wait(by_x, at[0], x)
    kept[2, upper] = kept[2, upper] + by_x[...]
    links.send(kept.at[2, upper], from_y.at[upper], at[4], y)
    links.wait(by_y, at[1], y)
    kept[1, lower] = kept[1, lower] + by_y[...]
    links.send(kept.at[1, lower], from_x.at[lower], at[5], x)

    for k in (1, 2, 3):
        links.wait(kv_got.at[k - 1], kv_at[k], frames[k])
    kv_1[...] = share(kv_half, 0)[...] + kv_got[0] + (kv_got[1] + kv_got[2])
    top, bottom = pl.ds(0, 64), pl.ds(64, rows - 64)
    at_u, at_l = links.plan(), links.plan()
    links.send(kv_1.at[top], kv_got_1.at[top], at_u, x)
    links.send(kv_1.at[bottom], kv_got_1.at[bottom], at_l, y)
    links.wait(from_y.at[lower], at[2], y)
    links.wait(from_x.at[upper], at[3], x)
    links.wait(from_y.at[upper], at[4], y)
    links.wait(from_x.at[lower], at[5], x)
    total[...] = kept[0] + from_x[...] + from_y[...]
    links.wait(kv_got_1.at[top], at_u, x)
    links.wait(kv_got_1.at[bottom], at_l, y)
    kv_2[...] = kv_1[...] + kv_got_1[...]
    at_u, at_l = links.plan(), links.plan()
    links.send(kv_2.at[top], kv_got_2.at[top], at_u, y)
    links.send(kv_2.at[bottom], kv_got_2.at[bottom], at_l, x)
    links.wait(kv_got_2.at[top], at_u, y)
    links.wait(kv_got_2.at[bottom], at_l, x)
    kv_out[:, mine] = kv_2[...] + kv_got_2[...]
    at_core = links.plan()
    links.send(kv_out.at[:, mine], kv_out.at[:, mine], at_core, core)
    links.wait(kv_out.at[:, others], at_core, core)
    links.drain()


def middle(parts, kv):
    length, width = parts.shape[0] // 8, parts.shape[1]
    rows = kv.shape[0] // 4
    f32, vmem = jnp.float32, pl.BlockSpec(memory_space=pltpu.VMEM)
    block, half = (length, width), pltpu.VMEM((rows, width), f32)
    return pl.pallas_call(
        middle_kernel,
        out_shape=(
            jax.ShapeDtypeStruct(block, f32), jax.ShapeDtypeStruct((rows, 2 * width), f32),
        ),
        in_specs=[pl.BlockSpec(memory_space=pl.ANY), vmem],
        out_specs=[vmem] * 2,
        scratch_shapes=[
            pltpu.VMEM((4,) + block, f32), pltpu.VMEM((4,) + block, f32),
            pltpu.VMEM((length // 2, width), f32), pltpu.VMEM((length // 2, width), f32),
            pltpu.VMEM(block, f32), pltpu.VMEM(block, f32),
            pltpu.VMEM((4 * rows, width), f32), pltpu.VMEM((4 * rows, width), f32),
            pltpu.VMEM((3, rows, width), f32), half, half, half, half,
            pltpu.SemaphoreType.DMA((4,)), pltpu.SemaphoreType.DMA((24,)),
            pltpu.SemaphoreType.DMA((24,)),
        ],
        compiler_params=pltpu.CompilerParams(
            collective_id=4, has_side_effects=True, vmem_limit_bytes=48 << 20
        ),
        cost_estimate=pl.CostEstimate(flops=0, bytes_accessed=64 << 20, transcendentals=0),
    )(parts.reshape((8,) + block), kv)


def spread_kernel(block, whole, send_sems, recv_sems):
    me = lax.axis_index("patch")
    peers = [None] + [{"patch": me ^ k} for k in range(1, 8)]
    greet_all(peers[1:])
    links = Links(send_sems, recv_sems)
    at = [links.plan() for _ in range(8)]
    for k in range(1, 8):
        links.send(block, whole.at[me], at[k], peers[k])
    whole[me] = block[...]
    for k in range(1, 8):
        links.wait(whole.at[me ^ k], at[k], peers[k])
    links.drain()


def spread(block):
    vmem = pl.BlockSpec(memory_space=pltpu.VMEM)
    return pl.pallas_call(
        spread_kernel,
        out_shape=jax.ShapeDtypeStruct((8,) + block.shape, jnp.float32),
        in_specs=[vmem],
        out_specs=vmem,
        scratch_shapes=[pltpu.SemaphoreType.DMA((8,)), pltpu.SemaphoreType.DMA((8,))],
        compiler_params=pltpu.CompilerParams(collective_id=5, has_side_effects=True),
    )(block)


def assemble_kernel(axis, dim, *refs):
    blocks, whole = refs[:-1], refs[-1]
    own = lax.axis_index(axis)
    for k, block in enumerate(blocks):
        length = block.shape[dim]
        start = pl.multiple_of((own ^ k) * length, length)
        where = (slice(None),) * dim + (pl.ds(start, length),)
        whole[where] = block[...]


def assemble(blocks, axis, dim):
    shape = list(blocks[0].shape)
    shape[dim] *= len(blocks)
    size = 4 * len(blocks) * blocks[0].size
    return pl.pallas_call(
        partial(assemble_kernel, axis, dim),
        out_shape=jax.ShapeDtypeStruct(tuple(shape), jnp.float32),
        in_specs=[pl.BlockSpec(memory_space=pltpu.VMEM)] * len(blocks),
        out_specs=pl.BlockSpec(memory_space=pltpu.VMEM),
        compiler_params=pltpu.CompilerParams(vmem_limit_bytes=24 << 20),
        cost_estimate=pl.CostEstimate(flops=0, bytes_accessed=2 * size, transcendentals=0),
    )(*blocks)


def gather_rows(shard):
    return lax.all_gather(shard, "patch", axis=0, tiled=True)


def scatter_rows(whole):
    return lax.psum_scatter(whole, "patch", scatter_dimension=0, tiled=True)


def gather_tokens(rows):
    return token_gather(rows) if small_patch() else gather_rows(rows)


def block_of(array, axis_name, k, dim):
    length = array.shape[dim] // lax.axis_size(axis_name)
    start = (lax.axis_index(axis_name) ^ k) * length
    return lax.dynamic_slice_in_dim(array, start, length, axis=dim)


def pair_up(kept, theirs, core):
    return jnp.where(
        core == 0,
        jnp.concatenate([kept, theirs], axis=-1),
        jnp.concatenate([theirs, kept], axis=-1),
    )


def over_chips(blocks):
    return [
        blocks[0],
        swap(blocks[1], "patch", 2),
        swap(blocks[2], "patch", 4),
        swap(blocks[3], "patch", 6),
    ]


def to_own_columns(weight):
    if not small_patch():
        return lax.all_to_all(weight, "patch", 1, 0, tiled=True)
    length = weight.shape[0]
    blocks = [block_of(weight, "patch", k, 1) for k in range(8)]
    theirs = swap(jnp.concatenate(blocks[1::2], axis=0), "patch", 1)
    both = [
        jnp.concatenate([kept, theirs[j * length : (j + 1) * length]], axis=0)
        for j, kept in enumerate(blocks[::2])
    ]
    halves = []
    for block in over_chips(both):
        halves += [block[:length], block[length:]]
    return assemble(halves, "patch", 0)


def back_to_rows(grad):
    core = lax.axis_index("patch") % 2
    blocks = [block_of(grad, "patch", k, 0) for k in range(8)]
    length = blocks[0].shape[0]
    theirs = swap(jnp.concatenate(blocks[1::2], axis=0), "patch", 1)
    both = [
        pair_up(kept, theirs[j * length : (j + 1) * length], core)
        for j, kept in enumerate(blocks[::2])
    ]
    return jnp.concatenate(over_chips(both), axis=0)


def side_by_side_kernel(stack, whole):
    own = lax.axis_index("patch") // 2
    length, width = whole.shape[0], stack.shape[1]
    for j in range(4):
        start = pl.multiple_of((own ^ j) * width, width)
        whole[:, pl.ds(start, width)] = stack[j * length : (j + 1) * length, :]


def side_by_side(stack):
    length, width = stack.shape[0] // 4, stack.shape[1]
    return pl.pallas_call(
        side_by_side_kernel,
        out_shape=jax.ShapeDtypeStruct((length, 4 * width), jnp.float32),
        in_specs=[pl.BlockSpec(memory_space=pltpu.VMEM)],
        out_specs=pl.BlockSpec(memory_space=pltpu.VMEM),
        compiler_params=pltpu.CompilerParams(vmem_limit_bytes=24 << 20),
        cost_estimate=pl.CostEstimate(flops=0, bytes_accessed=8 * stack.size, transcendentals=0),
    )(stack)


def to_columns(x):
    return lax.all_to_all(x, "frame", split_axis=1, concat_axis=0, tiled=True)


def to_slots(x):
    return lax.all_to_all(x, "frame", split_axis=0, concat_axis=1, tiled=True)


def scatter_tokens(parts):
    return token_scatter(parts) if small_patch() else scatter_rows(parts)


def open_up(block_input, frame_slot, small, kv_part):
    frame_number = frame_slot.astype(jnp.float32)
    if not small_patch():
        kv = all_sum(kv_part, "patch")
        return (
            to_columns(block_input),
            all_sum(placed(frame_number, "frame"), "frame"),
            all_sum(small, "patch"),
            lax.all_gather(kv, "frame", axis=0, tiled=True),
        )
    count = frame_slot.shape[0]
    rows = -(-small.shape[0] // 1024) * 8
    tokens, slots, summed, kv = begin(
        block_input, padded(frame_number, 8), padded(small, rows), kv_part
    )
    return tokens, slots[:, 0, :count].reshape(-1), summed.reshape(-1)[: small.shape[0]], kv


def mid_way(parts, kv):
    if not small_patch():
        kv = lax.psum_scatter(all_sum(kv, "patch"), "frame", scatter_dimension=0, tiled=True)
        return scatter_rows(parts), kv
    return middle(parts, kv)


def close_up(weights, kv, tokens, small, caption):
    clips, length = lax.axis_size("frame"), caption.shape[1]
    if not small_patch():
        weights = [lax.psum(scatter_rows(w), "frame") for w in weights]
        whole = lax.all_gather(caption, "patch", axis=0, tiled=True)
        whole = lax.all_gather(whole, "frame", axis=0)
        whole = jnp.transpose(whole, (0, 2, 1))
        small = all_sum(all_sum(small, "patch"), "frame")
        return weights, lax.psum(kv, "frame"), to_slots(tokens), small, whole
    rows = -(-small.shape[0] // 1024) * 8
    *weights, kv, tokens, summed, whole = finish(
        *weights, kv, tokens, padded(small, rows), caption
    )
    whole = jnp.transpose(whole, (1, 3, 0, 2)).reshape(clips, length, -1)
    return weights, kv, tokens, summed.reshape(-1)[: small.shape[0]], whole


def on_device(
    block_input,
    out_cotangent,
    caption,
    cond,
    ada_weight,
    ada_bias,
    qkv_weight,
    q_bias,
    v_bias,
    attn_out_weight,
    attn_out_bias,
    cross_q_weight,
    cross_q_bias,
    cross_kv_weight,
    cross_v_bias,
    cross_out_weight,
    cross_out_bias,
    fc1_weight,
    fc1_bias,
    fc2_weight,
    fc2_bias,
    frame_slot,
    clip_id,
    patch_mask,
    caption_mask,
):
    width = block_input.shape[-1]
    head_dim = width // H
    scaling = head_dim ** (-0.5)
    cond_act, silu_pull = jax.vjp(jax.nn.silu, cond)
    cond_own = own_part(cond_act, "patch", 1)
    modulation_part = matmul(cond_own, ada_weight)
    biases = (
        ada_bias, q_bias, v_bias, attn_out_bias, cross_q_bias, cross_v_bias, cross_out_bias,
        fc2_bias,
    )
    small = jnp.concatenate(
        [modulation_part.reshape(-1)] + [placed(b, "patch") for b in biases]
    )
    caption_rows = caption.reshape(CLIPS * CAP, width)
    caption_share = own_part(own_part(caption_rows, "frame", 0), "patch", 1)
    tokens_in, frame_pos, small, caption_kv = open_up(
        block_input, frame_slot, small, matmul(caption_share, cross_kv_weight)
    )
    cotangent = to_columns(after(out_cotangent, tokens_in))
    w_qkv = gather_rows(qkv_weight)
    three = jnp.concatenate([attn_out_weight, cross_q_weight, cross_out_weight], axis=1)
    w_three = gather_rows(after(three, tokens_in))
    w_attn, w_cross_q, w_cross_o = jnp.split(w_three, 3, axis=1)
    slots, cols, _ = tokens_in.shape
    rows = slots * cols
    clip_own = own_part(clip_id, "frame", 0)
    column_mask = own_part(patch_mask, "frame", 0).astype(jnp.float32)[:, None]
    place = modulation_part.size
    modulation = small[:place].reshape(modulation_part.shape)
    whole = []
    for b in biases:
        length = b.shape[0] * lax.axis_size("patch")
        whole.append(small[place : place + length])
        place += length
    b_ada, b_query, b_value, b_attn, b_cross_q, b_cross_v, b_cross_o, b_second = whole
    modulation = modulation + b_ada
    clip_onehot = (clip_own[:, None] == jnp.arange(CLIPS, dtype=jnp.int32)[None, :]).astype(
        jnp.float32
    )
    per_column = jnp.dot(clip_onehot, modulation, precision=lax.Precision.HIGHEST)
    shift_one, scale_one, gate_one, shift_two, scale_two, gate_two = jnp.split(
        per_column, 6, axis=1
    )

    cross_keys = caption_kv[:, :width].reshape(CLIPS * CAP, H, head_dim)
    cross_values = (caption_kv[:, width:] + b_cross_v).reshape(CLIPS * CAP, H, head_dim)

    grad_mlp = (column_mask * gate_two * cotangent).reshape(rows, width)
    normed_one, inverse_one = normalize(tokens_in)
    hidden_one = (normed_one * (1.0 + scale_one) + shift_one).reshape(rows, width)
    qkv_rows = matmul(hidden_one, w_qkv)
    w_first = to_own_columns(after(fc1_weight, qkv_rows))
    grad_mlp_all = gather_rows(after(grad_mlp, qkv_rows))
    queries = (qkv_rows[:, :width] + b_query).reshape(slots, cols, H, head_dim)
    keys = qkv_rows[:, width : 2 * width].reshape(slots, cols, H, head_dim)
    values = (qkv_rows[:, 2 * width :] + b_value).reshape(slots, cols, H, head_dim)
    slopes = 2.0 ** (-8.0 * (jnp.arange(H).astype(jnp.float32) + 1.0) / H)
    distance = jnp.abs(frame_pos[:, None] - frame_pos[None, :])
    bias_table = -slopes[:, None, None] * distance[None]
    key_valid = (frame_pos < FRAMES - 0.5)[None, None, None, :]
    scores = contract("fchd,schd->chfs", queries, keys) * scaling + bias_table[None]
    probs = softmax_rows(scores, key_valid)
    attended = contract("chfs,schd->fchd", probs, values)
    attended_rows = attended.reshape(rows, width)
    attn_branch = (matmul(attended_rows, w_attn) + b_attn).reshape(slots, cols, width)
    after_attn = tokens_in + column_mask * gate_one * attn_branch
    after_attn_rows = after_attn.reshape(rows, width)
    cross_queries = (matmul(after_attn_rows, w_cross_q) + b_cross_q).reshape(
        slots, cols, H, head_dim
    )
    key_clip = jnp.arange(CLIPS * CAP, dtype=jnp.int32) // CAP
    caption_ok = (
        (clip_own[:, None] == key_clip[None, :]) & (caption_mask.reshape(CLIPS * CAP)[None, :] > 0)
    )[None, :, None, :]
    cross_scores = contract("fchd,khd->fchk", cross_queries, cross_keys) * scaling
    cross_probs = softmax_rows(cross_scores, caption_ok)
    cross_att = contract("fchk,khd->fchd", cross_probs, cross_values)
    cross_rows = cross_att.reshape(rows, width)
    cross_branch = (matmul(cross_rows, w_cross_o) + b_cross_o).reshape(slots, cols, width)
    after_cross = after_attn + column_mask * cross_branch
    normed_two, inverse_two = normalize(after_cross)
    hidden_two = (normed_two * (1.0 + scale_two) + shift_two).reshape(rows, width)

    hidden_all = gather_tokens(hidden_two)
    pre_act = matmul(hidden_all, w_first) + fc1_bias
    activated, gelu_pull = jax.vjp(partial(jax.nn.gelu, approximate=True), pre_act)
    grad_pre = gelu_pull(matmul_nt(grad_mlp_all, fc2_weight))[0]
    grad_hidden_two = scatter_tokens(matmul_nt(grad_pre, w_first))
    grad_hidden_two = grad_hidden_two.reshape(slots, cols, width)
    grad_b_second = jnp.sum(grad_mlp, axis=0)

    grad_shift_two = jnp.sum(grad_hidden_two, axis=0)
    grad_scale_two = jnp.sum(grad_hidden_two * normed_two, axis=0)
    grad_after_cross = cotangent + normalize_back(
        grad_hidden_two * (1.0 + scale_two), normed_two, inverse_two
    )
    grad_cross_branch = (column_mask * grad_after_cross).reshape(rows, width)
    grad_w_cross_o = matmul_tn(cross_rows, grad_cross_branch)
    grad_b_cross_o = jnp.sum(grad_cross_branch, axis=0)
    activated, grad_pre = after((activated, grad_pre), grad_w_cross_o)
    grad_w_first = matmul_tn(hidden_all, grad_pre)
    grad_w_second = matmul_tn(activated, grad_mlp_all)
    if small_patch():
        grad_w_first = back_to_rows(grad_w_first)
    else:
        grad_w_first = lax.all_to_all(grad_w_first, "patch", 0, 1, tiled=True)
    grad_cross_branch = after(grad_cross_branch, (grad_w_first, grad_w_second))
    grad_w_first, grad_w_second = lax.psum((grad_w_first, grad_w_second), "frame")
    if small_patch():
        grad_w_first = side_by_side(grad_w_first)
    grad_b_first = jnp.sum(grad_pre, axis=0)
    mlp_parts = matmul(activated, fc2_weight)
    grad_cross_att = matmul_nt(grad_cross_branch, w_cross_o).reshape(slots, cols, H, head_dim)
    cross_row_terms = jnp.sum(grad_cross_att * cross_att, axis=-1)[..., None]
    grad_cross_probs = contract("fchd,khd->fchk", grad_cross_att, cross_values)
    grad_cross_scores = cross_probs * (grad_cross_probs - cross_row_terms) * scaling
    grad_cross_queries = contract("fchk,khd->fchd", grad_cross_scores, cross_keys).reshape(
        rows, width
    )
    grad_cross_keys = contract("fchk,fchd->khd", grad_cross_scores, cross_queries).reshape(
        CLIPS * CAP, width
    )
    grad_cross_values = contract("fchk,fchd->khd", cross_probs, grad_cross_att).reshape(
        CLIPS * CAP, width
    )
    grad_kv = jnp.concatenate([grad_cross_keys, grad_cross_values], axis=1)
    grad_w_cross_q = matmul_tn(after_attn_rows, grad_cross_queries)
    grad_b_cross_q = jnp.sum(grad_cross_queries, axis=0)
    grad_cross_queries = after(grad_cross_queries, grad_w_cross_q)
    grad_after_attn = grad_after_cross + matmul_nt(grad_cross_queries, w_cross_q).reshape(
        slots, cols, width
    )
    grad_attn_rows = (column_mask * gate_one * grad_after_attn).reshape(rows, width)
    grad_gate_one = jnp.sum(column_mask * attn_branch * grad_after_attn, axis=0)
    grad_w_attn = matmul_tn(attended_rows, grad_attn_rows)
    grad_b_attn = jnp.sum(grad_attn_rows, axis=0)
    grad_attn_rows = after(grad_attn_rows, grad_w_attn)
    mlp_sum, grad_kv_share = mid_way(after(mlp_parts, grad_w_attn), grad_kv)
    grad_attn_rows = after(grad_attn_rows, mlp_sum)
    grad_w_cross_kv = matmul_tn(caption_share, grad_kv_share)
    grad_b_cross_v = jnp.sum(grad_kv_share[:, width:], axis=0)
    grad_caption_share = matmul_nt(cross_kv_weight, grad_kv_share)
    mlp_branch = (mlp_sum + b_second).reshape(slots, cols, width)
    block_out = to_slots(after_cross + column_mask * gate_two * mlp_branch)
    grad_gate_two = jnp.sum(column_mask * mlp_branch * cotangent, axis=0)
    grad_attended = matmul_nt(grad_attn_rows, w_attn).reshape(slots, cols, H, head_dim)
    row_terms = jnp.transpose(jnp.sum(grad_attended * attended, axis=-1), (1, 2, 0))[..., None]
    grad_probs = contract("fchd,schd->chfs", grad_attended, values)
    grad_scores = probs * (grad_probs - row_terms)
    grad_queries = (contract("chfs,schd->fchd", grad_scores, keys) * scaling).reshape(rows, width)
    grad_keys = (contract("chfs,fchd->schd", grad_scores, queries) * scaling).reshape(rows, width)
    grad_values = contract("chfs,fchd->schd", probs, grad_attended).reshape(rows, width)
    grad_qkv = jnp.concatenate([grad_queries, grad_keys, grad_values], axis=1)
    grad_w_qkv = matmul_tn(hidden_one, grad_qkv)
    grad_b_query = jnp.sum(grad_queries, axis=0)
    grad_b_value = jnp.sum(grad_values, axis=0)
    grad_hidden_one = matmul_nt(grad_qkv, w_qkv).reshape(slots, cols, width)
    grad_shift_one = jnp.sum(grad_hidden_one, axis=0)
    grad_scale_one = jnp.sum(grad_hidden_one * normed_one, axis=0)
    input_grad = grad_after_attn + normalize_back(
        grad_hidden_one * (1.0 + scale_one), normed_one, inverse_one
    )
    grad_per_column = jnp.concatenate(
        [
            grad_shift_one,
            grad_scale_one,
            grad_gate_one,
            grad_shift_two,
            grad_scale_two,
            grad_gate_two,
        ],
        axis=1,
    )
    grad_modulation_part = jnp.dot(
        clip_onehot.T, grad_per_column, precision=lax.Precision.HIGHEST
    )
    first = (lax.axis_index("patch") == 0).astype(jnp.float32)
    bias_grads = (
        grad_b_query,
        grad_b_value,
        grad_b_attn,
        grad_b_cross_q,
        grad_b_cross_v * first,
        grad_b_cross_o,
        grad_b_second,
    )
    small_grads = jnp.concatenate(
        [grad_modulation_part.reshape(-1)] + list(bias_grads) + [placed(grad_b_first, "patch")]
    )
    weights, grad_w_cross_kv, input_grad, small_grads, grad_caption = close_up(
        (grad_w_qkv, grad_w_attn, grad_w_cross_q, grad_w_cross_o),
        grad_w_cross_kv, input_grad, small_grads, grad_caption_share,
    )
    place = grad_modulation_part.size
    grad_modulation = small_grads[:place].reshape(grad_modulation_part.shape)
    own_biases = []
    for b in bias_grads:
        own_biases.append(own_part(small_grads[place : place + b.shape[0]], "patch", 0))
        place += b.shape[0]
    g_query, g_value, g_attn, g_cross_q, g_cross_v, g_cross_o, g_second = own_biases
    grad_b_first = own_part(small_grads[place:], "patch", 0)
    grad_w_ada = matmul_tn(cond_own, grad_modulation)
    grad_b_ada = own_part(jnp.sum(grad_modulation, axis=0), "patch", 0)
    grad_cond_own = matmul_nt(grad_modulation, ada_weight)
    if small_patch():
        grad_cond_act = jnp.transpose(spread(grad_cond_own), (1, 0, 2)).reshape(cond.shape)
    else:
        grad_cond_act = all_sum(placed(grad_cond_own, "patch"), "patch")
    grad_cond = silu_pull(grad_cond_act)[0]

    grad_w_qkv, grad_w_attn, grad_w_cross_q, grad_w_cross_o = weights
    return (
        block_out,
        input_grad,
        grad_caption,
        grad_cond,
        grad_w_ada,
        grad_b_ada,
        grad_w_qkv,
        g_query,
        g_value,
        grad_w_attn,
        g_attn,
        grad_w_cross_q,
        g_cross_q,
        grad_w_cross_kv,
        g_cross_v,
        grad_w_cross_o,
        g_cross_o,
        grad_w_first,
        grad_b_first,
        grad_w_second,
        g_second,
    )


def solution(mesh):
    tokens = P("frame", "patch", None)
    weight = P("patch", None)
    vector = P("patch")
    parameters = (
        weight, vector, weight, vector, vector, weight, vector, weight, vector,
        weight, vector, weight, vector, weight, vector, weight, vector,
    )
    in_specs = (tokens, tokens, P(), P()) + parameters + (P("frame"), vector, vector, P())
    out_specs = (tokens, tokens, P(), P()) + parameters
    return jax.shard_map(
        on_device, mesh=mesh, in_specs=in_specs, out_specs=out_specs, check_vma=False
    )
```

```python
from functools import partial

import jax
import jax.numpy as jnp
from jax import lax
from jax.experimental import pallas as pl
from jax.experimental.pallas import tpu as pltpu
from jax.sharding import PartitionSpec as P

H = 16
CAP = 120
FRAMES = 17
CLIPS = 4


EPSILON = 1e-06
BEST = lax.Precision.HIGH
LIGHT = pl.CostEstimate(flops=0, bytes_accessed=1 << 16, transcendentals=0)


def matmul(left, right):
    return jnp.dot(left, right, precision=BEST)


def matmul_nt(left, right):
    return lax.dot_general(left, right, (((1,), (1,)), ((), ())), precision=BEST)


def matmul_tn(left, right):
    return lax.dot_general(left, right, (((0,), (0,)), ((), ())), precision=BEST)


def normalize(rows):
    average = jnp.mean(rows, axis=-1, keepdims=True)
    centred = rows - average
    spread = jnp.mean(centred * centred, axis=-1, keepdims=True)
    inverse = lax.rsqrt(spread + EPSILON)
    return (centred * inverse, inverse)


def normalize_back(grad_normed, normed, inverse):
    first_mean = jnp.mean(grad_normed, axis=-1, keepdims=True)
    second_mean = jnp.mean(grad_normed * normed, axis=-1, keepdims=True)
    return inverse * (grad_normed - first_mean - normed * second_mean)


def swap(value, axis, bit):
    size = lax.axis_size(axis)
    return lax.ppermute(value, axis, [(i, i ^ bit) for i in range(size)])


def all_sum(value, axis):
    bit = 1
    while bit < lax.axis_size(axis):
        value = value + swap(value, axis, bit)
        bit *= 2
    return value


def placed(vector, axis):
    length = vector.shape[-1]
    whole = jnp.zeros(vector.shape[:-1] + (length * lax.axis_size(axis),), vector.dtype)
    return lax.dynamic_update_slice_in_dim(
        whole, vector, lax.axis_index(axis) * length, axis=vector.ndim - 1
    )


def own_part(array, axis, dim):
    length = array.shape[dim] // lax.axis_size(axis)
    return lax.dynamic_slice_in_dim(array, lax.axis_index(axis) * length, length, axis=dim)


def after(value, done):
    return lax.optimization_barrier((value, done))[0]


def small_patch():
    return lax.axis_size("patch") == 8 and lax.axis_size("frame") == 4


def padded(vector, rows):
    return jnp.pad(vector, (0, rows * 128 - vector.shape[0])).reshape(rows, 128)


def greet(partners):
    barrier = pltpu.get_barrier_semaphore()
    for partner in partners:
        pl.semaphore_signal(barrier, inc=1, device_id={"patch": partner}, device_id_type=pl.DeviceIdType.MESH)
    pl.semaphore_wait(barrier, len(partners))


def remote(source, target, send_sems, recv_sems, index, device):
    return pltpu.make_async_remote_copy(
        src_ref=source, dst_ref=target, send_sem=send_sems.at[index], recv_sem=recv_sems.at[index],
        device_id={"patch": device}, device_id_type=pl.DeviceIdType.MESH)


def token_gather_kernel(rows, whole, local_sem, send_sems, recv_sems):
    own = lax.axis_index("patch")
    core, along_x, along_y, across = own ^ 1, own ^ 2, own ^ 4, own ^ 6
    greet((core, along_x, along_y))
    length = rows.shape[0] // 4
    sent = []

    def piece(owner, q):
        return whole.at[owner, pl.ds(q * length, length)]

    def send(source, owner, q, index, device):
        copy = remote(source, piece(owner, q), send_sems, recv_sems, index, device)
        copy.start()
        sent.append(copy)

    def arrived(owner, q, index, device):
        remote(piece(owner, q), piece(owner, q), send_sems, recv_sems, index, device).wait_recv()

    mine = pltpu.make_async_copy(rows, whole.at[own], local_sem)
    mine.start()
    for q_x, q_y in ((0, 2), (1, 3), (2, 0), (3, 1)):
        send(rows.at[pl.ds(q_x * length, length)], own, q_x, q_x, along_x)
        send(rows.at[pl.ds(q_y * length, length)], own, q_y, 4 + q_y, along_y)
    for q in range(4):
        send(rows.at[pl.ds(q * length, length)], own, q, 12 + q, core)
    for q_x, q_y in ((0, 2), (1, 3), (2, 0), (3, 1)):
        arrived(along_x, q_x, q_x, along_x)
        if q_x < 2:
            send(piece(along_x, q_x), along_x, q_x, 8 + q_x, along_y)
        send(piece(along_x, q_x), along_x, q_x, 16 + q_x, core)
        arrived(along_y, q_y, 4 + q_y, along_y)
        if q_y >= 2:
            send(piece(along_y, q_y), along_y, q_y, 8 + q_y, along_x)
        send(piece(along_y, q_y), along_y, q_y, 20 + q_y, core)
    for q in (0, 2, 1, 3):
        arrived(across, q, 8 + q, along_y if q < 2 else along_x)
        send(piece(across, q), across, q, 24 + q, core)
    for q in range(4):
        arrived(core, q, 12 + q, core)
        arrived(core ^ 2, q, 16 + q, core)
        arrived(core ^ 4, q, 20 + q, core)
        arrived(core ^ 6, q, 24 + q, core)
    for copy in sent:
        copy.wait_send()
    mine.wait()


def token_gather(rows):
    length, width = rows.shape
    return pl.pallas_call(
        token_gather_kernel,
        out_shape=jax.ShapeDtypeStruct((8, length, width), jnp.float32),
        in_specs=[pl.BlockSpec(memory_space=pltpu.VMEM)],
        out_specs=pl.BlockSpec(memory_space=pl.ANY),
        scratch_shapes=[pltpu.SemaphoreType.DMA, pltpu.SemaphoreType.DMA((28,)), pltpu.SemaphoreType.DMA((28,))],
        compiler_params=pltpu.CompilerParams(collective_id=0, has_side_effects=True, vmem_limit_bytes=16 << 20),
        cost_estimate=LIGHT,
    )(rows).reshape(8 * length, width)


def token_scatter_kernel(parts, total, kept, theirs, by_x, by_y, from_x, from_y, local_sems, send_sems, recv_sems):
    own = lax.axis_index("patch")
    core, along_x, along_y = own ^ 1, own ^ 2, own ^ 4
    greet((core, along_x, along_y))
    half = total.shape[0] // 2
    upper, lower = pl.ds(0, half), pl.ds(half, half)
    order = (3, 2, 1, 0)
    sent, loads = [], {}

    def send(source, target, index, device):
        copy = remote(source, target, send_sems, recv_sems, index, device)
        copy.start()
        sent.append(copy)

    def arrived(target, index, device):
        remote(target, target, send_sems, recv_sems, index, device).wait_recv()

    for j in order:
        send(parts.at[core ^ (2 * j)], theirs.at[j], j, core)
        loads[j] = pltpu.make_async_copy(parts.at[own ^ (2 * j)], kept.at[j], local_sems.at[j])
        loads[j].start()

    def add_cores(j):
        loads[j].wait()
        arrived(theirs.at[j], j, core)
        kept[j] = kept[j] + theirs[j]

    add_cores(3)
    send(kept.at[3, upper], by_x, 4, along_x)
    send(kept.at[3, lower], by_y, 5, along_y)
    add_cores(2)
    send(kept.at[2, lower], from_y.at[lower], 6, along_y)
    add_cores(1)
    send(kept.at[1, upper], from_x.at[upper], 7, along_x)
    add_cores(0)
    arrived(by_x, 4, along_x)
    kept[2, upper] = kept[2, upper] + by_x[...]
    send(kept.at[2, upper], from_y.at[upper], 8, along_y)
    arrived(by_y, 5, along_y)
    kept[1, lower] = kept[1, lower] + by_y[...]
    send(kept.at[1, lower], from_x.at[lower], 9, along_x)
    arrived(from_y.at[lower], 6, along_y)
    arrived(from_x.at[upper], 7, along_x)
    arrived(from_y.at[upper], 8, along_y)
    arrived(from_x.at[lower], 9, along_x)
    total[...] = kept[0] + from_x[...] + from_y[...]
    for copy in sent:
        copy.wait_send()


def token_scatter(parts):
    length, width = parts.shape[0] // 8, parts.shape[1]
    block = (length, width)
    return pl.pallas_call(
        token_scatter_kernel,
        out_shape=jax.ShapeDtypeStruct(block, jnp.float32),
        in_specs=[pl.BlockSpec(memory_space=pl.ANY)],
        out_specs=pl.BlockSpec(memory_space=pltpu.VMEM),
        scratch_shapes=[
            pltpu.VMEM((4,) + block, jnp.float32), pltpu.VMEM((4,) + block, jnp.float32),
            pltpu.VMEM((length // 2, width), jnp.float32), pltpu.VMEM((length // 2, width), jnp.float32),
            pltpu.VMEM(block, jnp.float32), pltpu.VMEM(block, jnp.float32),
            pltpu.SemaphoreType.DMA((4,)), pltpu.SemaphoreType.DMA((10,)), pltpu.SemaphoreType.DMA((10,)),
        ],
        compiler_params=pltpu.CompilerParams(collective_id=1, has_side_effects=True, vmem_limit_bytes=32 << 20),
        cost_estimate=LIGHT,
    )(parts.reshape((8,) + block))


class Links:
    def __init__(self, send_sems, recv_sems):
        self.send_sems, self.recv_sems = send_sems, recv_sems
        self.count = 0
        self.sent = []

    def plan(self):
        self.count += 1
        return self.count - 1

    def copy(self, source, target, index, device):
        return pltpu.make_async_remote_copy(
            src_ref=source, dst_ref=target, send_sem=self.send_sems.at[index],
            recv_sem=self.recv_sems.at[index], device_id=device,
            device_id_type=pl.DeviceIdType.MESH,
        )

    def send(self, source, target, index, device):
        self.copy(source, target, index, device).start()
        self.sent.append((source, index, device))

    def wait(self, target, index, device):
        self.copy(target, target, index, device).wait_recv()

    def drain(self):
        for source, index, device in self.sent:
            self.copy(source, source, index, device).wait_send()


def greet_all(devices):
    barrier = pltpu.get_barrier_semaphore()
    for device in devices:
        pl.semaphore_signal(barrier, inc=1, device_id=device, device_id_type=pl.DeviceIdType.MESH)
    pl.semaphore_wait(barrier, len(devices))


def begin_kernel(
    tokens, later, slots, small, kv, weight,
    tokens_out, later_out, slots_out, small_out, kv_out, weight_out,
    weight_sem, small_1, small_2, small_got, kv_1, kv_2, kv_got_core, kv_got_1, kv_got_2,
    send_sems, recv_sems,
):
    me, z = lax.axis_index("patch"), lax.axis_index("frame")
    core, x, y = ({"patch": me ^ k} for k in (1, 2, 4))
    frames = [None] + [{"frame": z ^ k} for k in (1, 2, 3)]
    chips = {2: x, 4: y, 6: {"patch": me ^ 6}}
    greet_all([core, x, y, chips[6]] + frames[1:])
    links = Links(send_sems, recv_sems)
    count, part = tokens.shape[0], tokens.shape[1] // 4
    rows, width = kv_1.shape

    def columns(k):
        return pl.ds(pl.multiple_of((z ^ k) * part, part), part)

    def of_slots(k):
        return pl.ds((z ^ k) * count, count)

    half = pl.multiple_of((me % 2) * width, 128)
    other = pl.multiple_of((1 - me % 2) * width, 128)
    mine, theirs = pl.ds(half, width), pl.ds(other, width)

    at = links.plan()
    links.send(small, small_got.at[0], at, core)
    at_kv = links.plan()
    links.send(kv.at[:, theirs], kv_got_core, at_kv, core)
    token_at = [None] + [links.plan() for _ in range(3)]
    slot_at = [None] + [links.plan() for _ in range(3)]
    chip_width = weight.shape[1] // 4
    own_chip = weight_out.at[me]
    own_copy = pltpu.make_async_copy(
        weight.at[:, pl.ds(pl.multiple_of(me // 2 * chip_width, 128), chip_width)],
        own_chip, weight_sem,
    )
    own_copy.start()
    weight_at = {k: links.plan() for k in (2, 4, 6)}
    pair_at = {k: links.plan() for k in (0, 2, 4, 6)}
    for k, device in chips.items():
        start = pl.multiple_of((me ^ k) // 2 * chip_width, 128)
        links.send(weight.at[:, pl.ds(start, chip_width)], own_chip, weight_at[k], device)
    for k in (1, 2, 3):
        links.send(slots, slots_out.at[z], slot_at[k], frames[k])
        links.send(tokens.at[:, columns(k)], tokens_out.at[of_slots(0)], token_at[k], frames[k])
    slots_out[z] = slots[...]
    tokens_out[of_slots(0)] = tokens[:, columns(0)]

    links.wait(small_got.at[0], at, core)
    small_1[...] = small[...] + small_got[0]
    at = links.plan()
    links.send(small_1, small_got.at[1], at, x)
    links.wait(kv_got_core, at_kv, core)
    kv_1[...] = kv[:, mine] + kv_got_core[...]
    upper, lower = pl.ds(0, 64), pl.ds(64, rows - 64)
    at_u, at_l = links.plan(), links.plan()
    links.send(kv_1.at[upper], kv_got_1.at[upper], at_u, x)
    links.send(kv_1.at[lower], kv_got_1.at[lower], at_l, y)
    links.wait(small_got.at[1], at, x)
    small_2[...] = small_1[...] + small_got[1]
    at = links.plan()
    links.send(small_2, small_got.at[2], at, y)
    links.wait(kv_got_1.at[upper], at_u, x)
    links.wait(kv_got_1.at[lower], at_l, y)
    kv_2[...] = kv_1[...] + kv_got_1[...]
    at_u, at_l = links.plan(), links.plan()
    links.send(kv_2.at[upper], kv_got_2.at[upper], at_u, y)
    links.send(kv_2.at[lower], kv_got_2.at[lower], at_l, x)
    links.wait(small_got.at[2], at, y)
    small_out[...] = small_2[...] + small_got[2]
    links.wait(kv_got_2.at[upper], at_u, y)
    links.wait(kv_got_2.at[lower], at_l, x)

    def share(k, columns):
        return kv_out.at[pl.ds(pl.multiple_of((z ^ k) * rows, rows), rows), columns]

    kv_out[pl.ds(pl.multiple_of(z * rows, rows), rows), mine] = kv_2[...] + kv_got_2[...]
    kv_at = [None] + [links.plan() for _ in range(3)]
    core_at = [links.plan() for _ in range(4)]
    for k in (1, 2, 3):
        links.send(share(0, mine), share(0, mine), kv_at[k], frames[k])
    links.send(share(0, mine), share(0, mine), core_at[0], core)
    later_at = [None] + [links.plan() for _ in range(3)]
    for k in (1, 2, 3):
        links.send(later.at[:, columns(k)], later_out.at[of_slots(0)], later_at[k], frames[k])
    later_out[of_slots(0)] = later[:, columns(0)]
    for k in (1, 2, 3):
        links.wait(share(k, mine), kv_at[k], frames[k])
        links.send(share(k, mine), share(k, mine), core_at[k], core)
    for k in (1, 2, 3):
        links.wait(slots_out.at[z ^ k], slot_at[k], frames[k])
        links.wait(tokens_out.at[of_slots(k)], token_at[k], frames[k])
    for k in range(4):
        links.wait(share(k, theirs), core_at[k], core)
    own_copy.wait()
    for k in (0, 2, 4, 6):
        if k:
            links.wait(weight_out.at[me ^ k], weight_at[k], chips[k])
        links.send(weight_out.at[me ^ k], weight_out.at[me ^ k], pair_at[k], core)
    for k in (0, 2, 4, 6):
        links.wait(weight_out.at[me ^ 1 ^ k], pair_at[k], core)
    for k in (1, 2, 3):
        links.wait(later_out.at[of_slots(k)], later_at[k], frames[k])
    links.drain()


def begin(tokens, later, slots, small, kv, weight):
    count, cols, width = tokens.shape
    rows = kv.shape[0]
    f32, vmem = jnp.float32, pl.BlockSpec(memory_space=pltpu.VMEM)
    half = pltpu.VMEM((rows, width), f32)
    return pl.pallas_call(
        begin_kernel,
        out_shape=(
            jax.ShapeDtypeStruct((4 * count, cols // 4, width), f32),
            jax.ShapeDtypeStruct((4 * count, cols // 4, width), f32),
            jax.ShapeDtypeStruct((4,) + slots.shape, f32),
            jax.ShapeDtypeStruct(small.shape, f32),
            jax.ShapeDtypeStruct((4 * rows, 2 * width), f32),
            jax.ShapeDtypeStruct((8, weight.shape[0], weight.shape[1] // 4), f32),
        ),
        in_specs=[vmem] * 5 + [pl.BlockSpec(memory_space=pl.ANY)],
        out_specs=[vmem] * 6,
        scratch_shapes=[
            pltpu.SemaphoreType.DMA,
            pltpu.VMEM(small.shape, f32), pltpu.VMEM(small.shape, f32),
            pltpu.VMEM((3,) + small.shape, f32), half, half, half, half, half,
            pltpu.SemaphoreType.DMA((32,)), pltpu.SemaphoreType.DMA((32,)),
        ],
        compiler_params=pltpu.CompilerParams(
            collective_id=2, has_side_effects=True, vmem_limit_bytes=40 << 20
        ),
        cost_estimate=LIGHT,
    )(tokens, later, slots, small, kv, weight)


UNITS = 6


def finish_kernel(
    first, attn, cross_q, cross_o, kv, tokens, small, caption,
    first_out, attn_out, cross_q_out, cross_o_out, kv_out, tokens_out, small_out, caption_out,
    kept, theirs, by_x, by_y, from_x, from_y, along_z, across_z,
    small_sums, small_got, small_z, load_sems, credit, send_sems, recv_sems,
):
    me, z = lax.axis_index("patch"), lax.axis_index("frame")
    outer = (z == 0) | (z == 3)
    inner = (z == 1) | (z == 2)
    core, x, y = ({"patch": me ^ k} for k in (1, 2, 4))
    frames = [None] + [{"frame": z ^ k} for k in (1, 2, 3)]
    near, facing = frames[1], frames[3]
    greet_all([core, x, y] + frames[1:])
    links = Links(send_sems, recv_sems)
    rows, width = by_x.shape[1] * 2, by_x.shape[2]
    upper, lower = pl.ds(0, rows // 2), pl.ds(rows // 2, rows // 2)
    count, part = tokens_out.shape[0], tokens_out.shape[1] // 4

    token_at = [None] + [links.plan() for _ in range(3)]

    def send_tokens(k):
        where = pl.ds(pl.multiple_of(z * part, part), part)
        if k == 0:
            tokens_out[:, where] = tokens[pl.ds(z * count, count)]
        else:
            source = tokens.at[pl.ds((z ^ k) * count, count)]
            links.send(source, tokens_out.at[:, where], token_at[k], frames[k])

    def frame_steps(value, result, near_got, facing_got):
        up, over, down = links.plan(), links.plan(), links.plan()

        def one():
            @pl.when(outer)
            def _():
                links.copy(value, near_got, up, near).start()

        def two():
            @pl.when(inner)
            def _():
                links.wait(near_got, up, near)
                near_got[...] = near_got[...] + value[...]
                links.copy(near_got, facing_got, over, facing).start()

        def three():
            @pl.when(inner)
            def _():
                links.wait(facing_got, over, facing)
                result[...] = near_got[...] + facing_got[...]
                links.copy(result, near_got, down, near).start()

        def four():
            @pl.when(outer)
            def _():
                links.wait(near_got, down, near)
                result[...] = near_got[...]
                links.copy(value, value, up, near).wait_send()

            @pl.when(inner)
            def _():
                links.copy(near_got, near_got, over, facing).wait_send()
                links.copy(result, result, down, near).wait_send()

        return one, two, three, four

    def piece(ref, u):
        return ref.at[:, pl.ds(u * width, width)]

    outs = [piece(first_out, u) for u in range(3)] + [attn_out, cross_q_out, cross_o_out]
    steps = [
        frame_steps(kept.at[u, 0], outs[u], along_z.at[u], across_z.at[u]) for u in range(UNITS)
    ] + [
        frame_steps(piece(kv, u), piece(kv_out, u), along_z.at[UNITS + u], across_z.at[UNITS + u])
        for u in range(2)
    ]
    small_steps = frame_steps(small_sums.at[2], small_out, small_z.at[0], small_z.at[1])

    core_at = [[links.plan() for _ in range(4)] for _ in range(UNITS)]
    link_at = [[links.plan() for _ in range(6)] for _ in range(UNITS)]

    def source(u, device, j):
        start = pl.multiple_of((device ^ (2 * j)) * rows, rows)
        ref = first if u < 3 else (attn, cross_q, cross_o)[u - 3]
        return ref.at[pl.ds(start, rows), pl.ds((u % 3) * width if u < 3 else 0, width)]

    def load(u, j):
        return pltpu.make_async_copy(source(u, me, j), kept.at[u, j], load_sems.at[u, j])

    def to_core(u):
        if u >= 3:
            pl.semaphore_wait(credit.at[u - 3], 1)
        for j in (3, 2, 1, 0):
            links.send(source(u, me ^ 1, j), theirs.at[u % 3, j], core_at[u][j], core)

    def add_cores(u, j):
        load(u, j).wait()
        links.wait(theirs.at[u % 3, j], core_at[u][j], core)
        kept[u, j] = kept[u, j] + theirs[u % 3, j]

    def stage_one(u):
        at = link_at[u]
        add_cores(u, 3)
        links.send(kept.at[u, 3, upper], by_x.at[u], at[0], x)
        links.send(kept.at[u, 3, lower], by_y.at[u], at[1], y)
        add_cores(u, 2)
        links.send(kept.at[u, 2, lower], from_y.at[u, lower], at[2], y)
        add_cores(u, 1)
        links.send(kept.at[u, 1, upper], from_x.at[u, upper], at[3], x)
        add_cores(u, 0)
        if u + 3 < UNITS:
            pl.semaphore_signal(
                credit.at[u], inc=1, device_id=core, device_id_type=pl.DeviceIdType.MESH
            )
            to_core(u + 3)

    def stage_two(u):
        at = link_at[u]
        links.wait(by_x.at[u], at[0], x)
        kept[u, 2, upper] = kept[u, 2, upper] + by_x[u]
        links.send(kept.at[u, 2, upper], from_y.at[u, upper], at[4], y)
        links.wait(by_y.at[u], at[1], y)
        kept[u, 1, lower] = kept[u, 1, lower] + by_y[u]
        links.send(kept.at[u, 1, lower], from_x.at[u, lower], at[5], x)

    def stage_three(u):
        at = link_at[u]
        links.wait(from_y.at[u, lower], at[2], y)
        links.wait(from_x.at[u, upper], at[3], x)
        links.wait(from_y.at[u, upper], at[4], y)
        links.wait(from_x.at[u, lower], at[5], x)
        kept[u, 0] = kept[u, 0] + from_x[u] + from_y[u]
        steps[u][0]()

    caption_at = [links.plan() for _ in range(10)]

    def caption_frames():
        caption_out[me, z] = caption[...]
        for k in (1, 2, 3):
            links.send(caption, caption_out.at[me, z], caption_at[k - 1], frames[k])

    def caption_x():
        for k in (1, 2, 3):
            links.wait(caption_out.at[me, z ^ k], caption_at[k - 1], frames[k])
        links.send(caption_out.at[me], caption_out.at[me], caption_at[3], x)

    def caption_y():
        links.wait(caption_out.at[me ^ 2], caption_at[3], x)
        for i, k in enumerate((0, 2)):
            links.send(caption_out.at[me ^ k], caption_out.at[me ^ k], caption_at[4 + i], y)

    def caption_core():
        for i, k in enumerate((0, 2)):
            links.wait(caption_out.at[me ^ 4 ^ k], caption_at[4 + i], y)
        for i, k in enumerate((0, 2, 4, 6)):
            links.send(caption_out.at[me ^ k], caption_out.at[me ^ k], caption_at[6 + i], core)

    def caption_end():
        for i, k in enumerate((0, 2, 4, 6)):
            links.wait(caption_out.at[me ^ 1 ^ k], caption_at[6 + i], core)

    small_at = [links.plan() for _ in range(3)]
    links.send(small, small_got.at[0], small_at[0], core)
    caption_frames()
    for u in range(UNITS):
        for j in (3, 2, 1, 0):
            load(u, j).start()
    steps[6][0]()
    steps[7][0]()
    for u in range(3):
        to_core(u)
    links.wait(small_got.at[0], small_at[0], core)
    small_sums[0] = small[...] + small_got[0]
    links.send(small_sums.at[0], small_got.at[1], small_at[1], x)
    stage_one(0)
    links.wait(small_got.at[1], small_at[1], x)
    small_sums[1] = small_sums[0] + small_got[1]
    links.send(small_sums.at[1], small_got.at[2], small_at[2], y)
    stage_one(1)
    stage_two(0)
    links.wait(small_got.at[2], small_at[2], y)
    small_sums[2] = small_sums[1] + small_got[2]
    small_steps[0]()
    caption_x()
    stage_one(2)
    steps[6][1]()
    steps[7][1]()
    send_tokens(0)
    send_tokens(1)
    stage_two(1)
    stage_three(0)
    stage_one(3)
    steps[6][2]()
    steps[7][2]()
    small_steps[1]()
    send_tokens(2)
    stage_two(2)
    stage_three(1)
    stage_one(4)
    steps[0][1]()
    small_steps[2]()
    caption_y()
    send_tokens(3)
    stage_two(3)
    stage_three(2)
    stage_one(5)
    steps[1][1]()
    steps[0][2]()
    stage_two(4)
    stage_three(3)
    stage_two(5)
    steps[2][1]()
    steps[1][2]()
    caption_core()
    stage_three(4)
    steps[3][1]()
    steps[2][2]()
    stage_three(5)
    steps[4][1]()
    steps[3][2]()
    steps[5][1]()
    steps[4][2]()
    steps[5][2]()
    for step in steps + [small_steps]:
        step[3]()
    caption_end()
    for k in (1, 2, 3):
        where = pl.ds(pl.multiple_of((z ^ k) * part, part), part)
        links.wait(tokens_out.at[:, where], token_at[k], frames[k])
    links.drain()


def finish(first, attn, cross_q, cross_o, kv, tokens, small, caption):
    rows, width = first.shape[0] // 8, first.shape[1] // 3
    count, part = tokens.shape[0] // 4, tokens.shape[1]
    f32, vmem = jnp.float32, pl.BlockSpec(memory_space=pltpu.VMEM)
    hbm = pl.BlockSpec(memory_space=pl.ANY)

    def shape(*sizes):
        return jax.ShapeDtypeStruct(sizes, f32)

    return pl.pallas_call(
        finish_kernel,
        out_shape=(
            shape(rows, 3 * width), shape(rows, width), shape(rows, width), shape(rows, width),
            shape(rows, 2 * width), shape(count, 4 * part, tokens.shape[2]), shape(*small.shape),
            shape(8, 4, *caption.shape),
        ),
        in_specs=[hbm] * 4 + [vmem] * 4,
        out_specs=[vmem] * 8,
        scratch_shapes=[
            pltpu.VMEM((UNITS, 4, rows, width), f32), pltpu.VMEM((3, 4, rows, width), f32),
            pltpu.VMEM((UNITS, rows // 2, width), f32), pltpu.VMEM((UNITS, rows // 2, width), f32),
            pltpu.VMEM((UNITS, rows, width), f32), pltpu.VMEM((UNITS, rows, width), f32),
            pltpu.VMEM((UNITS + 2, rows, width), f32), pltpu.VMEM((UNITS + 2, rows, width), f32),
            pltpu.VMEM((3,) + small.shape, f32), pltpu.VMEM((3,) + small.shape, f32),
            pltpu.VMEM((2,) + small.shape, f32),
            pltpu.SemaphoreType.DMA((UNITS, 4)), pltpu.SemaphoreType.REGULAR((3,)),
            pltpu.SemaphoreType.DMA((112,)), pltpu.SemaphoreType.DMA((112,)),
        ],
        compiler_params=pltpu.CompilerParams(
            collective_id=3, has_side_effects=True, vmem_limit_bytes=60 << 20
        ),
        cost_estimate=LIGHT,
    )(first, attn, cross_q, cross_o, kv, tokens, small, caption)


def middle_kernel(
    parts, kv,
    total, kv_out,
    kept, theirs, by_x, by_y, from_x, from_y,
    kv_half, kv_core, kv_got, kv_1, kv_2, kv_got_1, kv_got_2,
    load_sems, send_sems, recv_sems,
):
    me, z = lax.axis_index("patch"), lax.axis_index("frame")
    core, x, y = ({"patch": me ^ k} for k in (1, 2, 4))
    frames = [None] + [{"frame": z ^ k} for k in (1, 2, 3)]
    greet_all([core, x, y] + frames[1:])
    links = Links(send_sems, recv_sems)
    rows, width = kv_1.shape
    half = pl.multiple_of((me % 2) * width, 128)
    other = pl.multiple_of((1 - me % 2) * width, 128)
    mine, others = pl.ds(half, width), pl.ds(other, width)

    def share(ref, k):
        return ref.at[pl.ds(pl.multiple_of((z ^ k) * rows, rows), rows)]

    at_kv = links.plan()
    links.send(kv.at[:, others], kv_core, at_kv, core)
    core_at = [links.plan() for _ in range(4)]
    loads = [
        pltpu.make_async_copy(parts.at[me ^ (2 * j)], kept.at[j], load_sems.at[j])
        for j in range(4)
    ]
    for j in (3, 2, 1, 0):
        links.send(parts.at[me ^ 1 ^ (2 * j)], theirs.at[j], core_at[j], core)
        loads[j].start()
    links.wait(kv_core, at_kv, core)
    kv_half[...] = kv[:, mine] + kv_core[...]
    kv_at = [None] + [links.plan() for _ in range(3)]
    for k in (1, 2, 3):
        links.send(share(kv_half, k), kv_got.at[k - 1], kv_at[k], frames[k])

    count = total.shape[0] // 2
    upper, lower = pl.ds(0, count), pl.ds(count, count)
    at = [links.plan() for _ in range(6)]

    def add_cores(j):
        loads[j].wait()
        links.wait(theirs.at[j], core_at[j], core)
        kept[j] = kept[j] + theirs[j]

    add_cores(3)
    links.send(kept.at[3, upper], by_x, at[0], x)
    links.send(kept.at[3, lower], by_y, at[1], y)
    add_cores(2)
    links.send(kept.at[2, lower], from_y.at[lower], at[2], y)
    add_cores(1)
    links.send(kept.at[1, upper], from_x.at[upper], at[3], x)
    add_cores(0)
    links.wait(by_x, at[0], x)
    kept[2, upper] = kept[2, upper] + by_x[...]
    links.send(kept.at[2, upper], from_y.at[upper], at[4], y)
    links.wait(by_y, at[1], y)
    kept[1, lower] = kept[1, lower] + by_y[...]
    links.send(kept.at[1, lower], from_x.at[lower], at[5], x)

    for k in (1, 2, 3):
        links.wait(kv_got.at[k - 1], kv_at[k], frames[k])
    kv_1[...] = share(kv_half, 0)[...] + kv_got[0] + (kv_got[1] + kv_got[2])
    top, bottom = pl.ds(0, 64), pl.ds(64, rows - 64)
    at_u, at_l = links.plan(), links.plan()
    links.send(kv_1.at[top], kv_got_1.at[top], at_u, x)
    links.send(kv_1.at[bottom], kv_got_1.at[bottom], at_l, y)
    links.wait(from_y.at[lower], at[2], y)
    links.wait(from_x.at[upper], at[3], x)
    links.wait(from_y.at[upper], at[4], y)
    links.wait(from_x.at[lower], at[5], x)
    total[...] = kept[0] + from_x[...] + from_y[...]
    links.wait(kv_got_1.at[top], at_u, x)
    links.wait(kv_got_1.at[bottom], at_l, y)
    kv_2[...] = kv_1[...] + kv_got_1[...]
    at_u, at_l = links.plan(), links.plan()
    links.send(kv_2.at[top], kv_got_2.at[top], at_u, y)
    links.send(kv_2.at[bottom], kv_got_2.at[bottom], at_l, x)
    links.wait(kv_got_2.at[top], at_u, y)
    links.wait(kv_got_2.at[bottom], at_l, x)
    kv_out[:, mine] = kv_2[...] + kv_got_2[...]
    at_core = links.plan()
    links.send(kv_out.at[:, mine], kv_out.at[:, mine], at_core, core)
    links.wait(kv_out.at[:, others], at_core, core)
    links.drain()


def middle(parts, kv):
    length, width = parts.shape[0] // 8, parts.shape[1]
    rows = kv.shape[0] // 4
    f32, vmem = jnp.float32, pl.BlockSpec(memory_space=pltpu.VMEM)
    block, half = (length, width), pltpu.VMEM((rows, width), f32)
    return pl.pallas_call(
        middle_kernel,
        out_shape=(
            jax.ShapeDtypeStruct(block, f32), jax.ShapeDtypeStruct((rows, 2 * width), f32),
        ),
        in_specs=[pl.BlockSpec(memory_space=pl.ANY), vmem],
        out_specs=[vmem] * 2,
        scratch_shapes=[
            pltpu.VMEM((4,) + block, f32), pltpu.VMEM((4,) + block, f32),
            pltpu.VMEM((length // 2, width), f32), pltpu.VMEM((length // 2, width), f32),
            pltpu.VMEM(block, f32), pltpu.VMEM(block, f32),
            pltpu.VMEM((4 * rows, width), f32), pltpu.VMEM((4 * rows, width), f32),
            pltpu.VMEM((3, rows, width), f32), half, half, half, half,
            pltpu.SemaphoreType.DMA((4,)), pltpu.SemaphoreType.DMA((24,)),
            pltpu.SemaphoreType.DMA((24,)),
        ],
        compiler_params=pltpu.CompilerParams(
            collective_id=4, has_side_effects=True, vmem_limit_bytes=48 << 20
        ),
        cost_estimate=LIGHT,
    )(parts.reshape((8,) + block), kv)


def spread_kernel(block, whole, send_sems, recv_sems):
    me = lax.axis_index("patch")
    peers = [None] + [{"patch": me ^ k} for k in range(1, 8)]
    greet_all(peers[1:])
    links = Links(send_sems, recv_sems)
    at = [links.plan() for _ in range(8)]
    for k in range(1, 8):
        links.send(block, whole.at[me], at[k], peers[k])
    whole[me] = block[...]
    for k in range(1, 8):
        links.wait(whole.at[me ^ k], at[k], peers[k])
    links.drain()


def spread(block):
    vmem = pl.BlockSpec(memory_space=pltpu.VMEM)
    return pl.pallas_call(
        spread_kernel,
        out_shape=jax.ShapeDtypeStruct((8,) + block.shape, jnp.float32),
        in_specs=[vmem],
        out_specs=vmem,
        scratch_shapes=[pltpu.SemaphoreType.DMA((8,)), pltpu.SemaphoreType.DMA((8,))],
        compiler_params=pltpu.CompilerParams(collective_id=5, has_side_effects=True),
    )(block)


def halves(x):
    high = x.astype(jnp.bfloat16)
    return high, (x - high.astype(jnp.float32)).astype(jnp.bfloat16)


NN, NT, TN = (((1,), (0,)), ((), ())), (((1,), (1,)), ((), ())), (((0,), (0,)), ((), ()))


def three(left, right, dims):
    def dot(a, b):
        return lax.dot_general(a, b, dims, preferred_element_type=jnp.float32)

    return dot(left[0], right[0]) + (dot(left[0], right[1]) + dot(left[1], right[0]))


WINDOW = 256


def head_window(head, head_dim, width):
    start = jnp.minimum(head * head_dim // 128 * 128, width - WINDOW)
    lane = lax.broadcasted_iota(jnp.int32, (1, WINDOW), 1) - (head * head_dim - start)
    mask = ((lane >= 0) & (lane < head_dim)).astype(jnp.float32)
    return pl.ds(pl.multiple_of(start, 128), WINDOW), mask


def softmax_last(scores):
    exponent = jnp.exp(scores - jnp.max(scores, axis=-1, keepdims=True))
    return exponent / jnp.sum(exponent, axis=-1, keepdims=True)


GROUP = 8


def grouped(ref, group, lanes):
    slots = ref.shape[0]
    value = ref[:, group * GROUP : (group + 1) * GROUP, lanes]
    return value.reshape(slots * GROUP, value.shape[-1])


def store_halves(high, low, index, value):
    high[index], low[index] = halves(value)


def frame_attention_kernel(qkv, b_query, b_value, distance, allowed, probs, out, *split):
    (q_high, q_low, k_high, k_low, v_high, v_low), total = split[:6], split[6]
    slots, width = qkv.shape[0], out.shape[-1]
    head_dim = width // H
    scaling = head_dim**-0.5
    for g in range(2):
        store_halves(q_high, q_low, g, grouped(qkv, g, slice(0, width)) + b_query[...])
        store_halves(k_high, k_low, g, grouped(qkv, g, slice(width, 2 * width)))
        store_halves(
            v_high, v_low, g, grouped(qkv, g, slice(2 * width, 3 * width)) + b_value[...]
        )
    total[...] = jnp.zeros(total.shape, jnp.float32)

    def step(head, _):
        at, mask = head_window(head, head_dim, width)
        mask = mask.astype(jnp.bfloat16)
        slope = jnp.exp2(-8.0 / H * (jnp.full((1, 1), head, jnp.int32).astype(jnp.float32) + 1.0))
        for g in range(2):
            query = (q_high[g, :, at] * mask, q_low[g, :, at] * mask)
            scores = three(query, (k_high[g, :, at], k_low[g, :, at]), NT)
            scores = jnp.where(allowed[...] > 0, scores * scaling - slope * distance[...], -1e30)
            prob = softmax_last(scores)
            probs[head, g] = prob
            value = (v_high[g, :, at] * mask, v_low[g, :, at] * mask)
            total[g, :, at] = total[g, :, at] + three(halves(prob), value, NN)
        return 0

    lax.fori_loop(0, H, step, 0, unroll=4)
    for g in range(2):
        out[:, g * GROUP : (g + 1) * GROUP, :] = total[g].reshape(slots, GROUP, width)


def frame_tables(frame_pos):
    slots = frame_pos.shape[0]
    position = jnp.repeat(frame_pos, GROUP)
    column = jnp.tile(jnp.arange(GROUP), slots)
    distance = jnp.abs(position[:, None] - position[None, :])
    same = column[:, None] == column[None, :]
    return distance, (same & (position[None, :] < FRAMES - 0.5)).astype(jnp.float32)


VMEM_SPEC = pl.BlockSpec(memory_space=pltpu.VMEM)


def frame_attention(qkv, b_query, b_value, distance, allowed):
    slots, cols, width = qkv.shape[0], qkv.shape[1], qkv.shape[2] // 3
    rows = slots * GROUP
    part = pltpu.VMEM((2, rows, width), jnp.bfloat16)
    return pl.pallas_call(
        frame_attention_kernel,
        out_shape=(
            jax.ShapeDtypeStruct((H, 2, rows, rows), jnp.float32),
            jax.ShapeDtypeStruct((slots, cols, width), jnp.float32),
        ),
        in_specs=[VMEM_SPEC] * 5,
        out_specs=[VMEM_SPEC] * 2,
        scratch_shapes=[part] * 6 + [pltpu.VMEM((2, rows, width), jnp.float32)],
        compiler_params=pltpu.CompilerParams(vmem_limit_bytes=40 << 20),
        cost_estimate=LIGHT,
    )(qkv, b_query.reshape(1, width), b_value.reshape(1, width), distance, allowed)


def frame_attention_back_kernel(qkv, b_query, b_value, probs, attended, grad, out, *split):
    width = attended.shape[-1]
    slots, head_dim = qkv.shape[0], width // H
    scaling = head_dim**-0.5
    names = [(split[2 * i], split[2 * i + 1]) for i in range(4)]
    (q_high, q_low), (k_high, k_low), (v_high, v_low), (g_high, g_low) = names
    total, product = split[8], split[9]
    for g in range(2):
        store_halves(q_high, q_low, g, grouped(qkv, g, slice(0, width)) + b_query[...])
        store_halves(k_high, k_low, g, grouped(qkv, g, slice(width, 2 * width)))
        store_halves(
            v_high, v_low, g, grouped(qkv, g, slice(2 * width, 3 * width)) + b_value[...]
        )
        upstream = grouped(grad, g, slice(0, width))
        store_halves(g_high, g_low, g, upstream)
        product[g] = upstream * grouped(attended, g, slice(0, width))
    total[...] = jnp.zeros(total.shape, jnp.float32)

    def step(head, _):
        at, mask = head_window(head, head_dim, width)
        small = mask.astype(jnp.bfloat16)

        def masked(high, low, g):
            return high[g, :, at] * small, low[g, :, at] * small

        for g in range(2):
            upstream = masked(g_high, g_low, g)
            prob = probs[head, g]
            grad_prob = three(upstream, (v_high[g, :, at], v_low[g, :, at]), NT)
            term = jnp.sum(product[g, :, at] * mask, axis=-1, keepdims=True)
            score = halves(prob * (grad_prob - term) * scaling)
            total[0, g, :, at] = total[0, g, :, at] + three(score, masked(k_high, k_low, g), NN)
            total[1, g, :, at] = total[1, g, :, at] + three(score, masked(q_high, q_low, g), TN)
            total[2, g, :, at] = total[2, g, :, at] + three(halves(prob), upstream, TN)
        return 0

    lax.fori_loop(0, H, step, 0, unroll=4)
    for g in range(2):
        for i in range(3):
            out[:, g * GROUP : (g + 1) * GROUP, i * width : (i + 1) * width] = total[
                i, g
            ].reshape(slots, GROUP, width)


def frame_attention_back(qkv, b_query, b_value, probs, attended, grad):
    slots, cols, width = attended.shape
    rows = slots * GROUP
    part = pltpu.VMEM((2, rows, width), jnp.bfloat16)
    return pl.pallas_call(
        frame_attention_back_kernel,
        out_shape=jax.ShapeDtypeStruct((slots, cols, 3 * width), jnp.float32),
        in_specs=[VMEM_SPEC] * 6,
        out_specs=VMEM_SPEC,
        scratch_shapes=[part] * 8
        + [pltpu.VMEM((3, 2, rows, width), jnp.float32), pltpu.VMEM((2, rows, width), jnp.float32)],
        compiler_params=pltpu.CompilerParams(vmem_limit_bytes=48 << 20),
        cost_estimate=LIGHT,
    )(qkv, b_query.reshape(1, width), b_value.reshape(1, width), probs, attended, grad)


def cross_attention_kernel(queries, b_query, kv, b_value, allowed, probs, out, *split):
    q_high, q_low, k_high, k_low, v_high, v_low = split
    width = out.shape[-1]
    head_dim = width // H
    scaling = head_dim**-0.5
    store_halves(q_high, q_low, Ellipsis, queries[...] + b_query[...])
    store_halves(k_high, k_low, Ellipsis, kv[:, 0:width])
    store_halves(v_high, v_low, Ellipsis, kv[:, width : 2 * width] + b_value[...])
    out[...] = jnp.zeros(out.shape, jnp.float32)

    def step(head, _):
        at, mask = head_window(head, head_dim, width)
        mask = mask.astype(jnp.bfloat16)
        query = (q_high[:, at] * mask, q_low[:, at] * mask)
        scores = three(query, (k_high[:, at], k_low[:, at]), NT)
        prob = softmax_last(jnp.where(allowed[...] > 0, scores * scaling, -1e30))
        probs[head] = prob
        value = (v_high[:, at] * mask, v_low[:, at] * mask)
        out[:, at] = out[:, at] + three(halves(prob), value, NN)
        return 0

    lax.fori_loop(0, H, step, 0, unroll=4)


def cross_attention(queries, b_query, kv, b_value, allowed):
    rows, width = queries.shape
    keys = kv.shape[0]
    q_part = pltpu.VMEM((rows, width), jnp.bfloat16)
    k_part = pltpu.VMEM((keys, width), jnp.bfloat16)
    return pl.pallas_call(
        cross_attention_kernel,
        out_shape=(
            jax.ShapeDtypeStruct((H, rows, keys), jnp.float32),
            jax.ShapeDtypeStruct((rows, width), jnp.float32),
        ),
        in_specs=[VMEM_SPEC] * 5,
        out_specs=[VMEM_SPEC] * 2,
        scratch_shapes=[q_part] * 2 + [k_part] * 4,
        compiler_params=pltpu.CompilerParams(vmem_limit_bytes=48 << 20),
        cost_estimate=LIGHT,
    )(queries, b_query.reshape(1, width), kv, b_value.reshape(1, width), allowed)


def cross_attention_back_kernel(
    queries, b_query, kv, b_value, probs, attended, grad, grad_q, grad_kv, *split
):
    names = [(split[2 * i], split[2 * i + 1]) for i in range(4)]
    (q_high, q_low), (g_high, g_low), (k_high, k_low), (v_high, v_low) = names
    product = split[8]
    width = grad_q.shape[-1]
    head_dim = width // H
    scaling = head_dim**-0.5
    store_halves(q_high, q_low, Ellipsis, queries[...] + b_query[...])
    store_halves(k_high, k_low, Ellipsis, kv[:, 0:width])
    store_halves(v_high, v_low, Ellipsis, kv[:, width : 2 * width] + b_value[...])
    store_halves(g_high, g_low, Ellipsis, grad[...])
    product[...] = grad[...] * attended[...]
    grad_q[...] = jnp.zeros(grad_q.shape, jnp.float32)
    grad_kv[...] = jnp.zeros(grad_kv.shape, jnp.float32)

    def step(head, _):
        at, mask = head_window(head, head_dim, width)
        start = jnp.minimum(head * head_dim // 128 * 128, width - WINDOW)
        at_value = pl.ds(pl.multiple_of(start + width, 128), WINDOW)
        small = mask.astype(jnp.bfloat16)

        def masked(high, low):
            return high[:, at] * small, low[:, at] * small

        upstream = masked(g_high, g_low)
        prob = probs[head]
        grad_prob = three(upstream, (v_high[:, at], v_low[:, at]), NT)
        term = jnp.sum(product[:, at] * mask, axis=-1, keepdims=True)
        score = halves(prob * (grad_prob - term) * scaling)
        grad_q[:, at] = grad_q[:, at] + three(score, masked(k_high, k_low), NN)
        grad_kv[:, at] = grad_kv[:, at] + three(score, masked(q_high, q_low), TN)
        grad_kv[:, at_value] = grad_kv[:, at_value] + three(halves(prob), upstream, TN)
        return 0

    lax.fori_loop(0, H, step, 0, unroll=4)


def cross_attention_back(queries, b_query, kv, b_value, probs, attended, grad):
    rows, width = queries.shape
    keys = kv.shape[0]
    q_part = pltpu.VMEM((rows, width), jnp.bfloat16)
    k_part = pltpu.VMEM((keys, width), jnp.bfloat16)
    return pl.pallas_call(
        cross_attention_back_kernel,
        out_shape=(
            jax.ShapeDtypeStruct((rows, width), jnp.float32),
            jax.ShapeDtypeStruct(kv.shape, jnp.float32),
        ),
        in_specs=[VMEM_SPEC] * 7,
        out_specs=[VMEM_SPEC] * 2,
        scratch_shapes=[q_part] * 4 + [k_part] * 4 + [pltpu.VMEM((rows, width), jnp.float32)],
        compiler_params=pltpu.CompilerParams(vmem_limit_bytes=52 << 20),
        cost_estimate=LIGHT,
    )(queries, b_query.reshape(1, width), kv, b_value.reshape(1, width), probs, attended, grad)


def assemble_kernel(axis, dim, *refs):
    blocks, whole = refs[:-1], refs[-1]
    own = lax.axis_index(axis)
    for k, block in enumerate(blocks):
        length = block.shape[dim]
        start = pl.multiple_of((own ^ k) * length, length)
        where = (slice(None),) * dim + (pl.ds(start, length),)
        whole[where] = block[...]


def assemble(blocks, axis, dim):
    shape = list(blocks[0].shape)
    shape[dim] *= len(blocks)
    size = 4 * len(blocks) * blocks[0].size
    return pl.pallas_call(
        partial(assemble_kernel, axis, dim),
        out_shape=jax.ShapeDtypeStruct(tuple(shape), jnp.float32),
        in_specs=[pl.BlockSpec(memory_space=pltpu.VMEM)] * len(blocks),
        out_specs=pl.BlockSpec(memory_space=pltpu.VMEM),
        compiler_params=pltpu.CompilerParams(vmem_limit_bytes=24 << 20),
        cost_estimate=LIGHT,
    )(*blocks)


def gather_rows(shard):
    return lax.all_gather(shard, "patch", axis=0, tiled=True)


def scatter_rows(whole):
    return lax.psum_scatter(whole, "patch", scatter_dimension=0, tiled=True)


def gather_tokens(rows):
    return token_gather(rows) if small_patch() else gather_rows(rows)


def block_of(array, axis_name, k, dim):
    length = array.shape[dim] // lax.axis_size(axis_name)
    start = (lax.axis_index(axis_name) ^ k) * length
    return lax.dynamic_slice_in_dim(array, start, length, axis=dim)


def pair_up(kept, theirs, core):
    return jnp.where(
        core == 0,
        jnp.concatenate([kept, theirs], axis=-1),
        jnp.concatenate([theirs, kept], axis=-1),
    )


def over_chips(blocks):
    return [
        blocks[0],
        swap(blocks[1], "patch", 2),
        swap(blocks[2], "patch", 4),
        swap(blocks[3], "patch", 6),
    ]


def back_to_rows(grad):
    core = lax.axis_index("patch") % 2
    blocks = [block_of(grad, "patch", k, 0) for k in range(8)]
    length = blocks[0].shape[0]
    theirs = swap(jnp.concatenate(blocks[1::2], axis=0), "patch", 1)
    both = [
        pair_up(kept, theirs[j * length : (j + 1) * length], core)
        for j, kept in enumerate(blocks[::2])
    ]
    return jnp.concatenate(over_chips(both), axis=0)


def side_by_side_kernel(stack, whole):
    own = lax.axis_index("patch") // 2
    length, width = whole.shape[0], stack.shape[1]
    for j in range(4):
        start = pl.multiple_of((own ^ j) * width, width)
        whole[:, pl.ds(start, width)] = stack[j * length : (j + 1) * length, :]


def side_by_side(stack):
    length, width = stack.shape[0] // 4, stack.shape[1]
    return pl.pallas_call(
        side_by_side_kernel,
        out_shape=jax.ShapeDtypeStruct((length, 4 * width), jnp.float32),
        in_specs=[pl.BlockSpec(memory_space=pltpu.VMEM)],
        out_specs=pl.BlockSpec(memory_space=pltpu.VMEM),
        compiler_params=pltpu.CompilerParams(vmem_limit_bytes=24 << 20),
        cost_estimate=LIGHT,
    )(stack)


def to_columns(x):
    return lax.all_to_all(x, "frame", split_axis=1, concat_axis=0, tiled=True)


def to_slots(x):
    return lax.all_to_all(x, "frame", split_axis=0, concat_axis=1, tiled=True)


def scatter_tokens(parts):
    return token_scatter(parts) if small_patch() else scatter_rows(parts)


def open_up(block_input, cotangent, frame_slot, small, kv_part, fc1_weight):
    frame_number = frame_slot.astype(jnp.float32)
    if not small_patch():
        kv = all_sum(kv_part, "patch")
        return (
            to_columns(block_input),
            to_columns(cotangent),
            all_sum(placed(frame_number, "frame"), "frame"),
            all_sum(small, "patch"),
            lax.all_gather(kv, "frame", axis=0, tiled=True),
            lax.all_to_all(fc1_weight, "patch", 1, 0, tiled=True),
        )
    count = frame_slot.shape[0]
    rows = -(-small.shape[0] // 1024) * 8
    tokens, later, slots, summed, kv, pairs = begin(
        block_input, cotangent, padded(frame_number, 8), padded(small, rows), kv_part, fc1_weight
    )
    half = pairs.shape[2] // 2
    weight = jnp.where(lax.axis_index("patch") % 2 == 0, pairs[..., :half], pairs[..., half:])
    summed = summed.reshape(-1)[: small.shape[0]]
    slots = slots[:, 0, :count].reshape(-1)
    return tokens, later, slots, summed, kv, weight.reshape(-1, half)


def mid_way(parts, kv):
    if not small_patch():
        kv = lax.psum_scatter(all_sum(kv, "patch"), "frame", scatter_dimension=0, tiled=True)
        return scatter_rows(parts), kv
    return middle(parts, kv)


def close_up(weights, kv, tokens, small, caption):
    clips, length = lax.axis_size("frame"), caption.shape[1]
    if not small_patch():
        weights = [lax.psum(scatter_rows(w), "frame") for w in weights]
        whole = lax.all_gather(caption, "patch", axis=0, tiled=True)
        whole = lax.all_gather(whole, "frame", axis=0)
        whole = jnp.transpose(whole, (0, 2, 1))
        small = all_sum(all_sum(small, "patch"), "frame")
        return weights, lax.psum(kv, "frame"), to_slots(tokens), small, whole
    rows = -(-small.shape[0] // 1024) * 8
    *weights, kv, tokens, summed, whole = finish(
        *weights, kv, tokens, padded(small, rows), caption
    )
    whole = jnp.transpose(whole, (1, 3, 0, 2)).reshape(clips, length, -1)
    return weights, kv, tokens, summed.reshape(-1)[: small.shape[0]], whole


def on_device(
    block_input,
    out_cotangent,
    caption,
    cond,
    ada_weight,
    ada_bias,
    qkv_weight,
    q_bias,
    v_bias,
    attn_out_weight,
    attn_out_bias,
    cross_q_weight,
    cross_q_bias,
    cross_kv_weight,
    cross_v_bias,
    cross_out_weight,
    cross_out_bias,
    fc1_weight,
    fc1_bias,
    fc2_weight,
    fc2_bias,
    frame_slot,
    clip_id,
    patch_mask,
    caption_mask,
):
    width = block_input.shape[-1]
    cond_act, silu_pull = jax.vjp(jax.nn.silu, cond)
    cond_own = own_part(cond_act, "patch", 1)
    modulation_part = matmul(cond_own, ada_weight)
    biases = (
        ada_bias, q_bias, v_bias, attn_out_bias, cross_q_bias, cross_v_bias, cross_out_bias,
        fc2_bias,
    )
    small = jnp.concatenate(
        [modulation_part.reshape(-1)] + [placed(b, "patch") for b in biases]
    )
    caption_rows = caption.reshape(CLIPS * CAP, width)
    caption_share = own_part(own_part(caption_rows, "frame", 0), "patch", 1)
    tokens_in, cotangent, frame_pos, small, caption_kv, w_first = open_up(
        block_input,
        out_cotangent,
        frame_slot,
        small,
        matmul(caption_share, cross_kv_weight),
        fc1_weight,
    )
    w_qkv = gather_rows(qkv_weight)
    three = jnp.concatenate([attn_out_weight, cross_q_weight, cross_out_weight], axis=1)
    w_three = gather_rows(after(three, tokens_in))
    w_attn, w_cross_q, w_cross_o = jnp.split(w_three, 3, axis=1)
    slots, cols, _ = tokens_in.shape
    rows = slots * cols
    clip_own = own_part(clip_id, "frame", 0)
    column_mask = own_part(patch_mask, "frame", 0).astype(jnp.float32)[:, None]
    place = modulation_part.size
    modulation = small[:place].reshape(modulation_part.shape)
    whole = []
    for b in biases:
        length = b.shape[0] * lax.axis_size("patch")
        whole.append(small[place : place + length])
        place += length
    b_ada, b_query, b_value, b_attn, b_cross_q, b_cross_v, b_cross_o, b_second = whole
    modulation = modulation + b_ada
    clip_onehot = (clip_own[:, None] == jnp.arange(CLIPS, dtype=jnp.int32)[None, :]).astype(
        jnp.float32
    )
    per_column = jnp.dot(clip_onehot, modulation, precision=lax.Precision.HIGHEST)
    shift_one, scale_one, gate_one, shift_two, scale_two, gate_two = jnp.split(
        per_column, 6, axis=1
    )

    grad_mlp = (column_mask * gate_two * cotangent).reshape(rows, width)
    normed_one, inverse_one = normalize(tokens_in)
    hidden_one = (normed_one * (1.0 + scale_one) + shift_one).reshape(rows, width)
    qkv_rows = matmul(hidden_one, w_qkv)
    grad_mlp_all = gather_rows(after(grad_mlp, qkv_rows))
    qkv = qkv_rows.reshape(slots, cols, 3 * width)
    probs, attended = frame_attention(qkv, b_query, b_value, *frame_tables(frame_pos))
    attended_rows = attended.reshape(rows, width)
    attn_branch = (matmul(attended_rows, w_attn) + b_attn).reshape(slots, cols, width)
    after_attn = tokens_in + column_mask * gate_one * attn_branch
    after_attn_rows = after_attn.reshape(rows, width)
    cross_queries = matmul(after_attn_rows, w_cross_q)
    key_clip = jnp.arange(CLIPS * CAP, dtype=jnp.int32) // CAP
    caption_ok = (clip_own[:, None] == key_clip[None, :]) & (
        caption_mask.reshape(CLIPS * CAP)[None, :] > 0
    )
    caption_ok = jnp.tile(caption_ok.astype(jnp.float32), (slots, 1))
    cross_probs, cross_rows = cross_attention(
        cross_queries, b_cross_q, caption_kv, b_cross_v, caption_ok
    )
    cross_branch = (matmul(cross_rows, w_cross_o) + b_cross_o).reshape(slots, cols, width)
    after_cross = after_attn + column_mask * cross_branch
    normed_two, inverse_two = normalize(after_cross)
    hidden_two = (normed_two * (1.0 + scale_two) + shift_two).reshape(rows, width)

    hidden_all = gather_tokens(hidden_two)
    pre_act = matmul(hidden_all, w_first) + fc1_bias
    activated, gelu_pull = jax.vjp(partial(jax.nn.gelu, approximate=True), pre_act)
    grad_pre = gelu_pull(matmul_nt(grad_mlp_all, fc2_weight))[0]
    grad_hidden_two = scatter_tokens(matmul_nt(grad_pre, w_first))
    grad_hidden_two = grad_hidden_two.reshape(slots, cols, width)
    grad_b_second = jnp.sum(grad_mlp, axis=0)

    grad_shift_two = jnp.sum(grad_hidden_two, axis=0)
    grad_scale_two = jnp.sum(grad_hidden_two * normed_two, axis=0)
    grad_after_cross = cotangent + normalize_back(
        grad_hidden_two * (1.0 + scale_two), normed_two, inverse_two
    )
    grad_cross_branch = (column_mask * grad_after_cross).reshape(rows, width)
    grad_w_cross_o = matmul_tn(cross_rows, grad_cross_branch)
    grad_b_cross_o = jnp.sum(grad_cross_branch, axis=0)
    activated, grad_pre = after((activated, grad_pre), grad_w_cross_o)
    grad_w_first = matmul_tn(hidden_all, grad_pre)
    grad_w_second = matmul_tn(activated, grad_mlp_all)
    grad_cross_branch = after(grad_cross_branch, (grad_w_first, grad_w_second))
    if small_patch():
        grad_w_first = back_to_rows(grad_w_first)
    else:
        grad_w_first = lax.all_to_all(grad_w_first, "patch", 0, 1, tiled=True)
    first_sent = grad_w_first
    grad_w_first, grad_w_second = lax.psum((grad_w_first, grad_w_second), "frame")
    if small_patch():
        grad_w_first = side_by_side(grad_w_first)
    grad_b_first = jnp.sum(grad_pre, axis=0)
    mlp_parts = matmul(activated, fc2_weight)
    grad_cross_rows = matmul_nt(grad_cross_branch, w_cross_o)
    grad_cross_queries, grad_kv = cross_attention_back(
        cross_queries, b_cross_q, caption_kv, b_cross_v, cross_probs, cross_rows, grad_cross_rows
    )
    grad_w_cross_q = matmul_tn(after_attn_rows, grad_cross_queries)
    grad_b_cross_q = jnp.sum(grad_cross_queries, axis=0)
    grad_cross_queries = after(grad_cross_queries, grad_w_cross_q)
    grad_after_attn = grad_after_cross + matmul_nt(grad_cross_queries, w_cross_q).reshape(
        slots, cols, width
    )
    grad_attn_rows = (column_mask * gate_one * grad_after_attn).reshape(rows, width)
    grad_gate_one = jnp.sum(column_mask * attn_branch * grad_after_attn, axis=0)
    grad_w_attn = matmul_tn(attended_rows, grad_attn_rows)
    grad_b_attn = jnp.sum(grad_attn_rows, axis=0)
    grad_attn_rows = after(grad_attn_rows, grad_w_attn)
    mlp_sum, grad_kv_share = mid_way(after(mlp_parts, (grad_w_attn, first_sent)), grad_kv)
    grad_attn_rows = after(grad_attn_rows, mlp_sum)
    grad_w_cross_kv = matmul_tn(caption_share, grad_kv_share)
    grad_b_cross_v = jnp.sum(grad_kv_share[:, width:], axis=0)
    grad_caption_share = matmul_nt(cross_kv_weight, grad_kv_share)
    mlp_branch = (mlp_sum + b_second).reshape(slots, cols, width)
    block_out = to_slots(after_cross + column_mask * gate_two * mlp_branch)
    grad_gate_two = jnp.sum(column_mask * mlp_branch * cotangent, axis=0)
    grad_attended = matmul_nt(grad_attn_rows, w_attn).reshape(slots, cols, width)
    grad_qkv = frame_attention_back(
        qkv, b_query, b_value, probs, attended, grad_attended
    ).reshape(rows, 3 * width)
    grad_w_qkv = matmul_tn(hidden_one, grad_qkv)
    grad_b_query = jnp.sum(grad_qkv[:, :width], axis=0)
    grad_b_value = jnp.sum(grad_qkv[:, 2 * width :], axis=0)
    grad_hidden_one = matmul_nt(grad_qkv, w_qkv).reshape(slots, cols, width)
    grad_shift_one = jnp.sum(grad_hidden_one, axis=0)
    grad_scale_one = jnp.sum(grad_hidden_one * normed_one, axis=0)
    input_grad = grad_after_attn + normalize_back(
        grad_hidden_one * (1.0 + scale_one), normed_one, inverse_one
    )
    grad_per_column = jnp.concatenate(
        [
            grad_shift_one,
            grad_scale_one,
            grad_gate_one,
            grad_shift_two,
            grad_scale_two,
            grad_gate_two,
        ],
        axis=1,
    )
    grad_modulation_part = jnp.dot(
        clip_onehot.T, grad_per_column, precision=lax.Precision.HIGHEST
    )
    first = (lax.axis_index("patch") == 0).astype(jnp.float32)
    bias_grads = (
        grad_b_query,
        grad_b_value,
        grad_b_attn,
        grad_b_cross_q,
        grad_b_cross_v * first,
        grad_b_cross_o,
        grad_b_second,
    )
    small_grads = jnp.concatenate(
        [grad_modulation_part.reshape(-1)] + list(bias_grads) + [placed(grad_b_first, "patch")]
    )
    weights, grad_w_cross_kv, input_grad, small_grads, grad_caption = close_up(
        (grad_w_qkv, grad_w_attn, grad_w_cross_q, grad_w_cross_o),
        grad_w_cross_kv, input_grad, small_grads, grad_caption_share,
    )
    place = grad_modulation_part.size
    grad_modulation = small_grads[:place].reshape(grad_modulation_part.shape)
    own_biases = []
    for b in bias_grads:
        own_biases.append(own_part(small_grads[place : place + b.shape[0]], "patch", 0))
        place += b.shape[0]
    g_query, g_value, g_attn, g_cross_q, g_cross_v, g_cross_o, g_second = own_biases
    grad_b_first = own_part(small_grads[place:], "patch", 0)
    grad_w_ada = matmul_tn(cond_own, grad_modulation)
    grad_b_ada = own_part(jnp.sum(grad_modulation, axis=0), "patch", 0)
    grad_cond_own = matmul_nt(grad_modulation, ada_weight)
    if small_patch():
        grad_cond_act = jnp.transpose(spread(grad_cond_own), (1, 0, 2)).reshape(cond.shape)
    else:
        grad_cond_act = all_sum(placed(grad_cond_own, "patch"), "patch")
    grad_cond = silu_pull(grad_cond_act)[0]

    grad_w_qkv, grad_w_attn, grad_w_cross_q, grad_w_cross_o = weights
    return (
        block_out,
        input_grad,
        grad_caption,
        grad_cond,
        grad_w_ada,
        grad_b_ada,
        grad_w_qkv,
        g_query,
        g_value,
        grad_w_attn,
        g_attn,
        grad_w_cross_q,
        g_cross_q,
        grad_w_cross_kv,
        g_cross_v,
        grad_w_cross_o,
        g_cross_o,
        grad_w_first,
        grad_b_first,
        grad_w_second,
        g_second,
    )


def solution(mesh):
    tokens = P("frame", "patch", None)
    weight = P("patch", None)
    vector = P("patch")
    parameters = (
        weight, vector, weight, vector, vector, weight, vector, weight, vector,
        weight, vector, weight, vector, weight, vector, weight, vector,
    )
    in_specs = (tokens, tokens, P(), P()) + parameters + (P("frame"), vector, vector, P())
    out_specs = (tokens, tokens, P(), P()) + parameters
    return jax.shard_map(
        on_device, mesh=mesh, in_specs=in_specs, out_specs=out_specs, check_vma=False
    )
```

```python
from functools import partial

import jax
import jax.numpy as jnp
from jax import lax
from jax.experimental import pallas as pl
from jax.experimental.pallas import tpu as pltpu
from jax.sharding import PartitionSpec as P

H = 16
CAP = 120
FRAMES = 17
CLIPS = 4


EPSILON = 1e-06
BEST = lax.Precision.HIGH
LIGHT = pl.CostEstimate(flops=0, bytes_accessed=1 << 16, transcendentals=0)


def matmul(left, right):
    return jnp.dot(left, right, precision=BEST)


def matmul_nt(left, right):
    return lax.dot_general(left, right, (((1,), (1,)), ((), ())), precision=BEST)


def matmul_tn(left, right):
    return lax.dot_general(left, right, (((0,), (0,)), ((), ())), precision=BEST)


def normalize(rows):
    average = jnp.mean(rows, axis=-1, keepdims=True)
    centred = rows - average
    spread = jnp.mean(centred * centred, axis=-1, keepdims=True)
    inverse = lax.rsqrt(spread + EPSILON)
    return (centred * inverse, inverse)


def normalize_back(grad_normed, normed, inverse):
    first_mean = jnp.mean(grad_normed, axis=-1, keepdims=True)
    second_mean = jnp.mean(grad_normed * normed, axis=-1, keepdims=True)
    return inverse * (grad_normed - first_mean - normed * second_mean)


def swap(value, axis, bit):
    size = lax.axis_size(axis)
    return lax.ppermute(value, axis, [(i, i ^ bit) for i in range(size)])


def all_sum(value, axis):
    bit = 1
    while bit < lax.axis_size(axis):
        value = value + swap(value, axis, bit)
        bit *= 2
    return value


def placed(vector, axis):
    length = vector.shape[-1]
    whole = jnp.zeros(vector.shape[:-1] + (length * lax.axis_size(axis),), vector.dtype)
    return lax.dynamic_update_slice_in_dim(
        whole, vector, lax.axis_index(axis) * length, axis=vector.ndim - 1
    )


def own_part(array, axis, dim):
    length = array.shape[dim] // lax.axis_size(axis)
    return lax.dynamic_slice_in_dim(array, lax.axis_index(axis) * length, length, axis=dim)


def after(value, done):
    return lax.optimization_barrier((value, done))[0]


def small_patch():
    return lax.axis_size("patch") == 8 and lax.axis_size("frame") == 4


def padded(vector, rows):
    return jnp.pad(vector, (0, rows * 128 - vector.shape[0])).reshape(rows, 128)


def greet(partners):
    barrier = pltpu.get_barrier_semaphore()
    for partner in partners:
        pl.semaphore_signal(barrier, inc=1, device_id={"patch": partner}, device_id_type=pl.DeviceIdType.MESH)
    pl.semaphore_wait(barrier, len(partners))


def remote(source, target, send_sems, recv_sems, index, device):
    return pltpu.make_async_remote_copy(
        src_ref=source, dst_ref=target, send_sem=send_sems.at[index], recv_sem=recv_sems.at[index],
        device_id={"patch": device}, device_id_type=pl.DeviceIdType.MESH)


def token_gather_kernel(rows, whole, local_sem, send_sems, recv_sems):
    own = lax.axis_index("patch")
    core, along_x, along_y, across = own ^ 1, own ^ 2, own ^ 4, own ^ 6
    greet((core, along_x, along_y))
    length = rows.shape[0] // 4
    sent = []

    def piece(owner, q):
        return whole.at[owner, pl.ds(q * length, length)]

    def send(source, owner, q, index, device):
        copy = remote(source, piece(owner, q), send_sems, recv_sems, index, device)
        copy.start()
        sent.append(copy)

    def arrived(owner, q, index, device):
        remote(piece(owner, q), piece(owner, q), send_sems, recv_sems, index, device).wait_recv()

    mine = pltpu.make_async_copy(rows, whole.at[own], local_sem)
    mine.start()
    for q_x, q_y in ((0, 2), (1, 3), (2, 0), (3, 1)):
        send(rows.at[pl.ds(q_x * length, length)], own, q_x, q_x, along_x)
        send(rows.at[pl.ds(q_y * length, length)], own, q_y, 4 + q_y, along_y)
    for q in range(4):
        send(rows.at[pl.ds(q * length, length)], own, q, 12 + q, core)
    for q_x, q_y in ((0, 2), (1, 3), (2, 0), (3, 1)):
        arrived(along_x, q_x, q_x, along_x)
        if q_x < 2:
            send(piece(along_x, q_x), along_x, q_x, 8 + q_x, along_y)
        send(piece(along_x, q_x), along_x, q_x, 16 + q_x, core)
        arrived(along_y, q_y, 4 + q_y, along_y)
        if q_y >= 2:
            send(piece(along_y, q_y), along_y, q_y, 8 + q_y, along_x)
        send(piece(along_y, q_y), along_y, q_y, 20 + q_y, core)
    for q in (0, 2, 1, 3):
        arrived(across, q, 8 + q, along_y if q < 2 else along_x)
        send(piece(across, q), across, q, 24 + q, core)
    for q in range(4):
        arrived(core, q, 12 + q, core)
        arrived(core ^ 2, q, 16 + q, core)
        arrived(core ^ 4, q, 20 + q, core)
        arrived(core ^ 6, q, 24 + q, core)
    for copy in sent:
        copy.wait_send()
    mine.wait()


def token_gather(rows):
    length, width = rows.shape
    return pl.pallas_call(
        token_gather_kernel,
        out_shape=jax.ShapeDtypeStruct((8, length, width), jnp.float32),
        in_specs=[pl.BlockSpec(memory_space=pltpu.VMEM)],
        out_specs=pl.BlockSpec(memory_space=pl.ANY),
        scratch_shapes=[pltpu.SemaphoreType.DMA, pltpu.SemaphoreType.DMA((28,)), pltpu.SemaphoreType.DMA((28,))],
        compiler_params=pltpu.CompilerParams(collective_id=0, has_side_effects=True, vmem_limit_bytes=16 << 20),
        cost_estimate=LIGHT,
    )(rows).reshape(8 * length, width)


def token_scatter_kernel(parts, total, kept, theirs, by_x, by_y, from_x, from_y, local_sems, send_sems, recv_sems):
    own = lax.axis_index("patch")
    core, along_x, along_y = own ^ 1, own ^ 2, own ^ 4
    greet((core, along_x, along_y))
    half = total.shape[0] // 2
    upper, lower = pl.ds(0, half), pl.ds(half, half)
    order = (3, 2, 1, 0)
    sent, loads = [], {}

    def send(source, target, index, device):
        copy = remote(source, target, send_sems, recv_sems, index, device)
        copy.start()
        sent.append(copy)

    def arrived(target, index, device):
        remote(target, target, send_sems, recv_sems, index, device).wait_recv()

    for j in order:
        send(parts.at[core ^ (2 * j)], theirs.at[j], j, core)
        loads[j] = pltpu.make_async_copy(parts.at[own ^ (2 * j)], kept.at[j], local_sems.at[j])
        loads[j].start()

    def add_cores(j):
        loads[j].wait()
        arrived(theirs.at[j], j, core)
        kept[j] = kept[j] + theirs[j]

    add_cores(3)
    send(kept.at[3, upper], by_x, 4, along_x)
    send(kept.at[3, lower], by_y, 5, along_y)
    add_cores(2)
    send(kept.at[2, lower], from_y.at[lower], 6, along_y)
    add_cores(1)
    send(kept.at[1, upper], from_x.at[upper], 7, along_x)
    add_cores(0)
    arrived(by_x, 4, along_x)
    kept[2, upper] = kept[2, upper] + by_x[...]
    send(kept.at[2, upper], from_y.at[upper], 8, along_y)
    arrived(by_y, 5, along_y)
    kept[1, lower] = kept[1, lower] + by_y[...]
    send(kept.at[1, lower], from_x.at[lower], 9, along_x)
    arrived(from_y.at[lower], 6, along_y)
    arrived(from_x.at[upper], 7, along_x)
    arrived(from_y.at[upper], 8, along_y)
    arrived(from_x.at[lower], 9, along_x)
    total[...] = kept[0] + from_x[...] + from_y[...]
    for copy in sent:
        copy.wait_send()


def token_scatter(parts):
    length, width = parts.shape[0] // 8, parts.shape[1]
    block = (length, width)
    return pl.pallas_call(
        token_scatter_kernel,
        out_shape=jax.ShapeDtypeStruct(block, jnp.float32),
        in_specs=[pl.BlockSpec(memory_space=pl.ANY)],
        out_specs=pl.BlockSpec(memory_space=pltpu.VMEM),
        scratch_shapes=[
            pltpu.VMEM((4,) + block, jnp.float32), pltpu.VMEM((4,) + block, jnp.float32),
            pltpu.VMEM((length // 2, width), jnp.float32), pltpu.VMEM((length // 2, width), jnp.float32),
            pltpu.VMEM(block, jnp.float32), pltpu.VMEM(block, jnp.float32),
            pltpu.SemaphoreType.DMA((4,)), pltpu.SemaphoreType.DMA((10,)), pltpu.SemaphoreType.DMA((10,)),
        ],
        compiler_params=pltpu.CompilerParams(collective_id=1, has_side_effects=True, vmem_limit_bytes=32 << 20),
        cost_estimate=LIGHT,
    )(parts.reshape((8,) + block))


class Links:
    def __init__(self, send_sems, recv_sems):
        self.send_sems, self.recv_sems = send_sems, recv_sems
        self.count = 0
        self.sent = []

    def plan(self):
        self.count += 1
        return self.count - 1

    def copy(self, source, target, index, device):
        return pltpu.make_async_remote_copy(
            src_ref=source, dst_ref=target, send_sem=self.send_sems.at[index],
            recv_sem=self.recv_sems.at[index], device_id=device,
            device_id_type=pl.DeviceIdType.MESH,
        )

    def send(self, source, target, index, device):
        self.copy(source, target, index, device).start()
        self.sent.append((source, index, device))

    def wait(self, target, index, device):
        self.copy(target, target, index, device).wait_recv()

    def drain(self):
        for source, index, device in self.sent:
            self.copy(source, source, index, device).wait_send()


def greet_all(devices):
    barrier = pltpu.get_barrier_semaphore()
    for device in devices:
        pl.semaphore_signal(barrier, inc=1, device_id=device, device_id_type=pl.DeviceIdType.MESH)
    pl.semaphore_wait(barrier, len(devices))


def begin_kernel(
    tokens, later, slots, small, kv, weight,
    tokens_out, later_out, slots_out, small_out, kv_out, weight_out,
    weight_sem, small_1, small_2, small_got, kv_1, kv_2, kv_got_core, kv_got_1, kv_got_2,
    send_sems, recv_sems,
):
    me, z = lax.axis_index("patch"), lax.axis_index("frame")
    core, x, y = ({"patch": me ^ k} for k in (1, 2, 4))
    frames = [None] + [{"frame": z ^ k} for k in (1, 2, 3)]
    greet_all([core, x, y] + frames[1:])
    links = Links(send_sems, recv_sems)
    count, part = tokens.shape[0], tokens.shape[1] // 4
    rows, width = kv_1.shape

    def columns(k):
        return pl.ds(pl.multiple_of((z ^ k) * part, part), part)

    def of_slots(k):
        return pl.ds((z ^ k) * count, count)

    half = pl.multiple_of((me % 2) * width, 128)
    other = pl.multiple_of((1 - me % 2) * width, 128)
    mine, theirs = pl.ds(half, width), pl.ds(other, width)

    length = weight.shape[0]
    weight_at = [[links.plan() for _ in range(7)] for _ in range(3)]
    weight_core = links.plan()

    def piece(k, u, first=0, size=length):
        start = pl.multiple_of((me ^ k) * length + first, 8)
        return weight_out.at[pl.ds(start, size), pl.ds(u * width, width)]

    whole = weight_out.at[pl.ds(pl.multiple_of(me * length, 8), length)]
    sibling = weight_out.at[pl.ds(pl.multiple_of((me ^ 1) * length, 8), length)]
    own_copy = pltpu.make_async_copy(weight, whole, weight_sem)

    def weight_links(u):
        source = weight.at[:, pl.ds(u * width, width)]
        links.send(source, piece(0, u), weight_at[u][0], x)
        links.send(source, piece(0, u), weight_at[u][1], y)

    def weight_across(u):
        middle_row = length // 2
        links.wait(piece(2, u), weight_at[u][0], x)
        upper = piece(2, u, 0, middle_row)
        links.send(upper, upper, weight_at[u][2], y)
        links.send(piece(2, u), piece(2, u), weight_at[u][4], core)
        links.wait(piece(4, u), weight_at[u][1], y)
        lower = piece(4, u, middle_row, middle_row)
        links.send(lower, lower, weight_at[u][3], x)
        links.send(piece(4, u), piece(4, u), weight_at[u][5], core)

    def weight_last(u):
        middle_row = length // 2
        links.wait(piece(6, u, 0, middle_row), weight_at[u][2], y)
        links.wait(piece(6, u, middle_row, middle_row), weight_at[u][3], x)
        links.send(piece(6, u), piece(6, u), weight_at[u][6], core)

    at = links.plan()
    links.send(small, small_got.at[0], at, core)
    at_kv = links.plan()
    links.send(kv.at[:, theirs], kv_got_core, at_kv, core)
    own_copy.start()
    token_at = [None] + [links.plan() for _ in range(3)]
    slot_at = [None] + [links.plan() for _ in range(3)]
    later_at = [None] + [links.plan() for _ in range(3)]
    for k in (1, 2, 3):
        links.send(slots, slots_out.at[z], slot_at[k], frames[k])
        links.send(tokens.at[:, columns(k)], tokens_out.at[of_slots(0)], token_at[k], frames[k])
    for k in (1, 2, 3):
        links.send(later.at[:, columns(k)], later_out.at[of_slots(0)], later_at[k], frames[k])

    links.wait(small_got.at[0], at, core)
    small_1[...] = small[...] + small_got[0]
    at = links.plan()
    links.send(small_1, small_got.at[1], at, x)
    links.wait(kv_got_core, at_kv, core)
    kv_1[...] = kv[:, mine] + kv_got_core[...]
    upper, lower = pl.ds(0, 64), pl.ds(64, rows - 64)
    at_u, at_l = links.plan(), links.plan()
    links.send(kv_1.at[upper], kv_got_1.at[upper], at_u, x)
    links.send(kv_1.at[lower], kv_got_1.at[lower], at_l, y)
    weight_links(0)
    links.send(weight, whole, weight_core, core)
    slots_out[z] = slots[...]
    tokens_out[of_slots(0)] = tokens[:, columns(0)]
    later_out[of_slots(0)] = later[:, columns(0)]
    links.wait(small_got.at[1], at, x)
    small_2[...] = small_1[...] + small_got[1]
    at = links.plan()
    links.send(small_2, small_got.at[2], at, y)
    links.wait(kv_got_1.at[upper], at_u, x)
    links.wait(kv_got_1.at[lower], at_l, y)
    kv_2[...] = kv_1[...] + kv_got_1[...]
    at_u, at_l = links.plan(), links.plan()
    links.send(kv_2.at[upper], kv_got_2.at[upper], at_u, y)
    links.send(kv_2.at[lower], kv_got_2.at[lower], at_l, x)
    weight_links(1)
    links.wait(small_got.at[2], at, y)
    small_out[...] = small_2[...] + small_got[2]
    weight_across(0)
    weight_links(2)
    links.wait(kv_got_2.at[upper], at_u, y)
    links.wait(kv_got_2.at[lower], at_l, x)

    def share(k, columns):
        return kv_out.at[pl.ds(pl.multiple_of((z ^ k) * rows, rows), rows), columns]

    kv_out[pl.ds(pl.multiple_of(z * rows, rows), rows), mine] = kv_2[...] + kv_got_2[...]
    kv_at = [None] + [links.plan() for _ in range(3)]
    core_at = [links.plan() for _ in range(4)]
    for k in (1, 2, 3):
        links.send(share(0, mine), share(0, mine), kv_at[k], frames[k])
    links.send(share(0, mine), share(0, mine), core_at[0], core)
    weight_across(1)
    weight_last(0)
    weight_across(2)
    weight_last(1)
    for k in (1, 2, 3):
        links.wait(slots_out.at[z ^ k], slot_at[k], frames[k])
        links.wait(tokens_out.at[of_slots(k)], token_at[k], frames[k])
        links.wait(later_out.at[of_slots(k)], later_at[k], frames[k])
    for k in (1, 2, 3):
        links.wait(share(k, mine), kv_at[k], frames[k])
        links.send(share(k, mine), share(k, mine), core_at[k], core)
    weight_last(2)
    for k in range(4):
        links.wait(share(k, theirs), core_at[k], core)
    links.wait(sibling, weight_core, core)
    for u in range(3):
        for i, k in enumerate((2, 4, 6)):
            links.wait(piece(k ^ 1, u), weight_at[u][4 + i], core)
    own_copy.wait()
    links.drain()


def begin(tokens, later, slots, small, kv, weight):
    count, cols, width = tokens.shape
    rows = kv.shape[0]
    f32, vmem = jnp.float32, pl.BlockSpec(memory_space=pltpu.VMEM)
    hbm = pl.BlockSpec(memory_space=pl.ANY)
    half = pltpu.VMEM((rows, width), f32)
    return pl.pallas_call(
        begin_kernel,
        out_shape=(
            jax.ShapeDtypeStruct((4 * count, cols // 4, width), f32),
            jax.ShapeDtypeStruct((4 * count, cols // 4, width), f32),
            jax.ShapeDtypeStruct((4,) + slots.shape, f32),
            jax.ShapeDtypeStruct(small.shape, f32),
            jax.ShapeDtypeStruct((4 * rows, 2 * width), f32),
            jax.ShapeDtypeStruct((8 * weight.shape[0], weight.shape[1]), f32),
        ),
        in_specs=[vmem] * 5 + [hbm],
        out_specs=[vmem] * 5 + [hbm],
        scratch_shapes=[
            pltpu.SemaphoreType.DMA,
            pltpu.VMEM(small.shape, f32), pltpu.VMEM(small.shape, f32),
            pltpu.VMEM((3,) + small.shape, f32), half, half, half, half, half,
            pltpu.SemaphoreType.DMA((48,)), pltpu.SemaphoreType.DMA((48,)),
        ],
        compiler_params=pltpu.CompilerParams(
            collective_id=2, has_side_effects=True, vmem_limit_bytes=36 << 20
        ),
        cost_estimate=LIGHT,
    )(tokens, later, slots, small, kv, weight)


UNITS = 6


def finish_kernel(
    first, attn, cross_q, cross_o, kv, tokens, small, caption, columns,
    first_out, attn_out, cross_q_out, cross_o_out, kv_out, tokens_out, small_out, caption_out,
    columns_out, columns_got, columns_sem,
    kept, theirs, by_x, by_y, from_x, from_y, along_z, across_z,
    small_sums, small_got, small_z, load_sems, credit, send_sems, recv_sems,
):
    me, z = lax.axis_index("patch"), lax.axis_index("frame")
    outer = (z == 0) | (z == 3)
    inner = (z == 1) | (z == 2)
    core, x, y = ({"patch": me ^ k} for k in (1, 2, 4))
    frames = [None] + [{"frame": z ^ k} for k in (1, 2, 3)]
    near, facing = frames[1], frames[3]
    chips = {2: x, 4: y, 6: {"patch": me ^ 6}}
    greet_all([core, x, y, chips[6]] + frames[1:])
    links = Links(send_sems, recv_sems)
    rows, width = by_x.shape[1] * 2, by_x.shape[2]
    upper, lower = pl.ds(0, rows // 2), pl.ds(rows // 2, rows // 2)
    count, part = tokens_out.shape[0], tokens_out.shape[1] // 4

    token_at = [None] + [links.plan() for _ in range(3)]

    def send_tokens(k):
        where = pl.ds(pl.multiple_of(z * part, part), part)
        if k == 0:
            tokens_out[:, where] = tokens[pl.ds(z * count, count)]
        else:
            source = tokens.at[pl.ds((z ^ k) * count, count)]
            links.send(source, tokens_out.at[:, where], token_at[k], frames[k])

    def frame_steps(value, result, near_got, facing_got):
        up, over, down = links.plan(), links.plan(), links.plan()

        def one():
            @pl.when(outer)
            def _():
                links.copy(value, near_got, up, near).start()

        def two():
            @pl.when(inner)
            def _():
                links.wait(near_got, up, near)
                near_got[...] = near_got[...] + value[...]
                links.copy(near_got, facing_got, over, facing).start()

        def three():
            @pl.when(inner)
            def _():
                links.wait(facing_got, over, facing)
                result[...] = near_got[...] + facing_got[...]
                links.copy(result, near_got, down, near).start()

        def four():
            @pl.when(outer)
            def _():
                links.wait(near_got, down, near)
                result[...] = near_got[...]
                links.copy(value, value, up, near).wait_send()

            @pl.when(inner)
            def _():
                links.copy(near_got, near_got, over, facing).wait_send()
                links.copy(result, result, down, near).wait_send()

        return one, two, three, four

    def piece(ref, u):
        return ref.at[:, pl.ds(u * width, width)]

    outs = [piece(first_out, u) for u in range(3)] + [attn_out, cross_q_out, cross_o_out]
    steps = [
        frame_steps(kept.at[u, 0], outs[u], along_z.at[u], across_z.at[u]) for u in range(UNITS)
    ] + [
        frame_steps(piece(kv, u), piece(kv_out, u), along_z.at[UNITS + u], across_z.at[UNITS + u])
        for u in range(2)
    ]
    small_steps = frame_steps(small_sums.at[2], small_out, small_z.at[0], small_z.at[1])

    core_at = [[links.plan() for _ in range(4)] for _ in range(UNITS)]
    link_at = [[links.plan() for _ in range(6)] for _ in range(UNITS)]

    def source(u, device, j):
        start = pl.multiple_of((device ^ (2 * j)) * rows, rows)
        ref = first if u < 3 else (attn, cross_q, cross_o)[u - 3]
        return ref.at[pl.ds(start, rows), pl.ds((u % 3) * width if u < 3 else 0, width)]

    def load(u, j):
        return pltpu.make_async_copy(source(u, me, j), kept.at[u, j], load_sems.at[u, j])

    def to_core(u):
        if u >= 2:
            pl.semaphore_wait(credit.at[u - 2], 1)
        for j in (3, 2, 1, 0):
            links.send(source(u, me ^ 1, j), theirs.at[u % 2, j], core_at[u][j], core)

    def add_cores(u, j):
        load(u, j).wait()
        links.wait(theirs.at[u % 2, j], core_at[u][j], core)
        kept[u, j] = kept[u, j] + theirs[u % 2, j]

    def stage_one(u):
        at = link_at[u]
        add_cores(u, 3)
        links.send(kept.at[u, 3, upper], by_x.at[u], at[0], x)
        links.send(kept.at[u, 3, lower], by_y.at[u], at[1], y)
        add_cores(u, 2)
        links.send(kept.at[u, 2, lower], from_y.at[u, lower], at[2], y)
        add_cores(u, 1)
        links.send(kept.at[u, 1, upper], from_x.at[u, upper], at[3], x)
        add_cores(u, 0)
        if u + 2 < UNITS:
            pl.semaphore_signal(
                credit.at[u], inc=1, device_id=core, device_id_type=pl.DeviceIdType.MESH
            )
            to_core(u + 2)

    def stage_two(u):
        at = link_at[u]
        links.wait(by_x.at[u], at[0], x)
        kept[u, 2, upper] = kept[u, 2, upper] + by_x[u]
        links.send(kept.at[u, 2, upper], from_y.at[u, upper], at[4], y)
        links.wait(by_y.at[u], at[1], y)
        kept[u, 1, lower] = kept[u, 1, lower] + by_y[u]
        links.send(kept.at[u, 1, lower], from_x.at[u, lower], at[5], x)

    def stage_three(u):
        at = link_at[u]
        links.wait(from_y.at[u, lower], at[2], y)
        links.wait(from_x.at[u, upper], at[3], x)
        links.wait(from_y.at[u, upper], at[4], y)
        links.wait(from_x.at[u, lower], at[5], x)
        kept[u, 0] = kept[u, 0] + from_x[u] + from_y[u]
        steps[u][0]()

    block = columns_got.shape[1] // 2
    columns_at = {k: links.plan() for k in (2, 4, 6)}
    columns_core = {k: links.plan() for k in (0, 2, 4, 6)}

    def chip_rows(k):
        return columns.at[pl.ds(pl.multiple_of((me ^ k) // 2 * (2 * block), 8), 2 * block)]

    own_rows = pltpu.make_async_copy(chip_rows(0), columns_got.at[0], columns_sem.at[0])

    def own_block(k):
        core_rows = pl.ds(pl.multiple_of(me % 2 * block, 8), block)
        return pltpu.make_async_copy(
            columns_got.at[k // 2, core_rows], columns_out.at[me ^ k], columns_sem.at[1 + k // 2]
        )

    def send_columns(k):
        links.send(chip_rows(k), columns_got.at[k // 2], columns_at[k], chips[k])

    def columns_over():
        other_rows = pl.ds(pl.multiple_of((1 - me % 2) * block, 8), block)
        own_rows.wait()
        for k in (0, 2, 4, 6):
            if k:
                links.wait(columns_got.at[k // 2], columns_at[k], chips[k])
            links.send(
                columns_got.at[k // 2, other_rows], columns_out.at[me ^ k], columns_core[k], core
            )
            own_block(k).start()

    def columns_end():
        for k in (0, 2, 4, 6):
            links.wait(columns_out.at[me ^ 1 ^ k], columns_core[k], core)
            own_block(k).wait()

    caption_at = [links.plan() for _ in range(10)]

    def caption_frames():
        caption_out[me, z] = caption[...]
        for k in (1, 2, 3):
            links.send(caption, caption_out.at[me, z], caption_at[k - 1], frames[k])

    def caption_x():
        for k in (1, 2, 3):
            links.wait(caption_out.at[me, z ^ k], caption_at[k - 1], frames[k])
        links.send(caption_out.at[me], caption_out.at[me], caption_at[3], x)

    def caption_y():
        links.wait(caption_out.at[me ^ 2], caption_at[3], x)
        for i, k in enumerate((0, 2)):
            links.send(caption_out.at[me ^ k], caption_out.at[me ^ k], caption_at[4 + i], y)

    def caption_core():
        for i, k in enumerate((0, 2)):
            links.wait(caption_out.at[me ^ 4 ^ k], caption_at[4 + i], y)
        for i, k in enumerate((0, 2, 4, 6)):
            links.send(caption_out.at[me ^ k], caption_out.at[me ^ k], caption_at[6 + i], core)

    def caption_end():
        for i, k in enumerate((0, 2, 4, 6)):
            links.wait(caption_out.at[me ^ 1 ^ k], caption_at[6 + i], core)

    small_at = [links.plan() for _ in range(3)]
    links.send(small, small_got.at[0], small_at[0], core)
    caption_frames()
    own_rows.start()
    for u in range(UNITS):
        for j in (3, 2, 1, 0):
            load(u, j).start()
    steps[6][0]()
    steps[7][0]()
    for u in range(2):
        to_core(u)
    links.wait(small_got.at[0], small_at[0], core)
    small_sums[0] = small[...] + small_got[0]
    links.send(small_sums.at[0], small_got.at[1], small_at[1], x)
    stage_one(0)
    links.wait(small_got.at[1], small_at[1], x)
    small_sums[1] = small_sums[0] + small_got[1]
    links.send(small_sums.at[1], small_got.at[2], small_at[2], y)
    stage_one(1)
    stage_two(0)
    links.wait(small_got.at[2], small_at[2], y)
    small_sums[2] = small_sums[1] + small_got[2]
    small_steps[0]()
    caption_x()
    stage_one(2)
    steps[6][1]()
    steps[7][1]()
    send_tokens(0)
    send_tokens(1)
    stage_two(1)
    stage_three(0)
    stage_one(3)
    steps[6][2]()
    steps[7][2]()
    small_steps[1]()
    send_tokens(2)
    stage_two(2)
    stage_three(1)
    stage_one(4)
    steps[0][1]()
    small_steps[2]()
    caption_y()
    send_tokens(3)
    stage_two(3)
    stage_three(2)
    stage_one(5)
    steps[1][1]()
    steps[0][2]()
    for k in (2, 4, 6):
        send_columns(k)
    stage_two(4)
    stage_three(3)
    stage_two(5)
    steps[2][1]()
    steps[1][2]()
    caption_core()
    stage_three(4)
    steps[3][1]()
    steps[2][2]()
    stage_three(5)
    steps[4][1]()
    steps[3][2]()
    steps[5][1]()
    steps[4][2]()
    steps[5][2]()
    for step in steps + [small_steps]:
        step[3]()
    columns_over()
    caption_end()
    columns_end()
    for k in (1, 2, 3):
        where = pl.ds(pl.multiple_of((z ^ k) * part, part), part)
        links.wait(tokens_out.at[:, where], token_at[k], frames[k])
    links.drain()


def finish(first, attn, cross_q, cross_o, kv, tokens, small, caption, columns):
    rows, width = first.shape[0] // 8, first.shape[1] // 3
    count, part = tokens.shape[0] // 4, tokens.shape[1]
    f32, vmem = jnp.float32, pl.BlockSpec(memory_space=pltpu.VMEM)
    hbm = pl.BlockSpec(memory_space=pl.ANY)

    def shape(*sizes):
        return jax.ShapeDtypeStruct(sizes, f32)

    return pl.pallas_call(
        finish_kernel,
        out_shape=(
            shape(rows, 3 * width), shape(rows, width), shape(rows, width), shape(rows, width),
            shape(rows, 2 * width), shape(count, 4 * part, tokens.shape[2]), shape(*small.shape),
            shape(8, 4, *caption.shape), shape(8, columns.shape[0] // 8, columns.shape[1]),
        ),
        in_specs=[hbm] * 4 + [vmem] * 4 + [hbm],
        out_specs=[vmem] * 8 + [hbm],
        scratch_shapes=[
            pltpu.VMEM((4, columns.shape[0] // 4, columns.shape[1]), f32),
            pltpu.SemaphoreType.DMA((5,)),
            pltpu.VMEM((UNITS, 4, rows, width), f32), pltpu.VMEM((2, 4, rows, width), f32),
            pltpu.VMEM((UNITS, rows // 2, width), f32), pltpu.VMEM((UNITS, rows // 2, width), f32),
            pltpu.VMEM((UNITS, rows, width), f32), pltpu.VMEM((UNITS, rows, width), f32),
            pltpu.VMEM((UNITS + 2, rows, width), f32), pltpu.VMEM((UNITS + 2, rows, width), f32),
            pltpu.VMEM((3,) + small.shape, f32), pltpu.VMEM((3,) + small.shape, f32),
            pltpu.VMEM((2,) + small.shape, f32),
            pltpu.SemaphoreType.DMA((UNITS, 4)), pltpu.SemaphoreType.REGULAR((4,)),
            pltpu.SemaphoreType.DMA((112,)), pltpu.SemaphoreType.DMA((112,)),
        ],
        compiler_params=pltpu.CompilerParams(
            collective_id=3, has_side_effects=True, vmem_limit_bytes=58 << 20
        ),
        cost_estimate=LIGHT,
    )(first, attn, cross_q, cross_o, kv, tokens, small, caption, columns)


def middle_kernel(
    parts, kv,
    total, kv_out,
    kept, theirs, by_x, by_y, from_x, from_y,
    kv_half, kv_core, kv_got, kv_1, kv_2, kv_got_1, kv_got_2,
    load_sems, send_sems, recv_sems,
):
    me, z = lax.axis_index("patch"), lax.axis_index("frame")
    core, x, y = ({"patch": me ^ k} for k in (1, 2, 4))
    frames = [None] + [{"frame": z ^ k} for k in (1, 2, 3)]
    greet_all([core, x, y] + frames[1:])
    links = Links(send_sems, recv_sems)
    rows, width = kv_1.shape
    half = pl.multiple_of((me % 2) * width, 128)
    other = pl.multiple_of((1 - me % 2) * width, 128)
    mine, others = pl.ds(half, width), pl.ds(other, width)

    def share(ref, k):
        return ref.at[pl.ds(pl.multiple_of((z ^ k) * rows, rows), rows)]

    at_kv = links.plan()
    links.send(kv.at[:, others], kv_core, at_kv, core)
    core_at = [links.plan() for _ in range(4)]
    loads = [
        pltpu.make_async_copy(parts.at[me ^ (2 * j)], kept.at[j], load_sems.at[j])
        for j in range(4)
    ]
    for j in (3, 2, 1, 0):
        links.send(parts.at[me ^ 1 ^ (2 * j)], theirs.at[j], core_at[j], core)
        loads[j].start()
    links.wait(kv_core, at_kv, core)
    kv_half[...] = kv[:, mine] + kv_core[...]
    kv_at = [None] + [links.plan() for _ in range(3)]
    for k in (1, 2, 3):
        links.send(share(kv_half, k), kv_got.at[k - 1], kv_at[k], frames[k])

    count = total.shape[0] // 2
    upper, lower = pl.ds(0, count), pl.ds(count, count)
    at = [links.plan() for _ in range(6)]

    def add_cores(j):
        loads[j].wait()
        links.wait(theirs.at[j], core_at[j], core)
        kept[j] = kept[j] + theirs[j]

    add_cores(3)
    links.send(kept.at[3, upper], by_x, at[0], x)
    links.send(kept.at[3, lower], by_y, at[1], y)
    add_cores(2)
    links.send(kept.at[2, lower], from_y.at[lower], at[2], y)
    add_cores(1)
    links.send(kept.at[1, upper], from_x.at[upper], at[3], x)
    add_cores(0)
    links.wait(by_x, at[0], x)
    kept[2, upper] = kept[2, upper] + by_x[...]
    links.send(kept.at[2, upper], from_y.at[upper], at[4], y)
    links.wait(by_y, at[1], y)
    kept[1, lower] = kept[1, lower] + by_y[...]
    links.send(kept.at[1, lower], from_x.at[lower], at[5], x)

    for k in (1, 2, 3):
        links.wait(kv_got.at[k - 1], kv_at[k], frames[k])
    kv_1[...] = share(kv_half, 0)[...] + kv_got[0] + (kv_got[1] + kv_got[2])
    top, bottom = pl.ds(0, 64), pl.ds(64, rows - 64)
    at_u, at_l = links.plan(), links.plan()
    links.send(kv_1.at[top], kv_got_1.at[top], at_u, x)
    links.send(kv_1.at[bottom], kv_got_1.at[bottom], at_l, y)
    links.wait(from_y.at[lower], at[2], y)
    links.wait(from_x.at[upper], at[3], x)
    links.wait(from_y.at[upper], at[4], y)
    links.wait(from_x.at[lower], at[5], x)
    total[...] = kept[0] + from_x[...] + from_y[...]
    links.wait(kv_got_1.at[top], at_u, x)
    links.wait(kv_got_1.at[bottom], at_l, y)
    kv_2[...] = kv_1[...] + kv_got_1[...]
    at_u, at_l = links.plan(), links.plan()
    links.send(kv_2.at[top], kv_got_2.at[top], at_u, y)
    links.send(kv_2.at[bottom], kv_got_2.at[bottom], at_l, x)
    links.wait(kv_got_2.at[top], at_u, y)
    links.wait(kv_got_2.at[bottom], at_l, x)
    kv_out[:, mine] = kv_2[...] + kv_got_2[...]
    at_core = links.plan()
    links.send(kv_out.at[:, mine], kv_out.at[:, mine], at_core, core)
    links.wait(kv_out.at[:, others], at_core, core)
    links.drain()


def middle(parts, kv):
    length, width = parts.shape[0] // 8, parts.shape[1]
    rows = kv.shape[0] // 4
    f32, vmem = jnp.float32, pl.BlockSpec(memory_space=pltpu.VMEM)
    block, half = (length, width), pltpu.VMEM((rows, width), f32)
    return pl.pallas_call(
        middle_kernel,
        out_shape=(
            jax.ShapeDtypeStruct(block, f32), jax.ShapeDtypeStruct((rows, 2 * width), f32),
        ),
        in_specs=[pl.BlockSpec(memory_space=pl.ANY), vmem],
        out_specs=[vmem] * 2,
        scratch_shapes=[
            pltpu.VMEM((4,) + block, f32), pltpu.VMEM((4,) + block, f32),
            pltpu.VMEM((length // 2, width), f32), pltpu.VMEM((length // 2, width), f32),
            pltpu.VMEM(block, f32), pltpu.VMEM(block, f32),
            pltpu.VMEM((4 * rows, width), f32), pltpu.VMEM((4 * rows, width), f32),
            pltpu.VMEM((3, rows, width), f32), half, half, half, half,
            pltpu.SemaphoreType.DMA((4,)), pltpu.SemaphoreType.DMA((24,)),
            pltpu.SemaphoreType.DMA((24,)),
        ],
        compiler_params=pltpu.CompilerParams(
            collective_id=4, has_side_effects=True, vmem_limit_bytes=48 << 20
        ),
        cost_estimate=LIGHT,
    )(parts.reshape((8,) + block), kv)


def spread_kernel(block, whole, send_sems, recv_sems):
    me = lax.axis_index("patch")
    peers = [None] + [{"patch": me ^ k} for k in range(1, 8)]
    greet_all(peers[1:])
    links = Links(send_sems, recv_sems)
    at = [links.plan() for _ in range(8)]
    for k in range(1, 8):
        links.send(block, whole.at[me], at[k], peers[k])
    whole[me] = block[...]
    for k in range(1, 8):
        links.wait(whole.at[me ^ k], at[k], peers[k])
    links.drain()


def spread(block):
    vmem = pl.BlockSpec(memory_space=pltpu.VMEM)
    return pl.pallas_call(
        spread_kernel,
        out_shape=jax.ShapeDtypeStruct((8,) + block.shape, jnp.float32),
        in_specs=[vmem],
        out_specs=vmem,
        scratch_shapes=[pltpu.SemaphoreType.DMA((8,)), pltpu.SemaphoreType.DMA((8,))],
        compiler_params=pltpu.CompilerParams(collective_id=5, has_side_effects=True),
    )(block)


def halves(x):
    high = x.astype(jnp.bfloat16)
    return high, (x - high.astype(jnp.float32)).astype(jnp.bfloat16)


NN, NT, TN = (((1,), (0,)), ((), ())), (((1,), (1,)), ((), ())), (((0,), (0,)), ((), ()))


def three(left, right, dims):
    def dot(a, b):
        return lax.dot_general(a, b, dims, preferred_element_type=jnp.float32)

    return dot(left[0], right[0]) + (dot(left[0], right[1]) + dot(left[1], right[0]))


WINDOW = 256


def head_window(head, head_dim, width):
    start = jnp.minimum(head * head_dim // 128 * 128, width - WINDOW)
    lane = lax.broadcasted_iota(jnp.int32, (1, WINDOW), 1) - (head * head_dim - start)
    mask = ((lane >= 0) & (lane < head_dim)).astype(jnp.float32)
    return pl.ds(pl.multiple_of(start, 128), WINDOW), mask


def softmax_last(scores):
    exponent = jnp.exp(scores - jnp.max(scores, axis=-1, keepdims=True))
    return exponent / jnp.sum(exponent, axis=-1, keepdims=True)


GROUP = 8


def grouped(ref, group, lanes):
    slots = ref.shape[0]
    value = ref[:, group * GROUP : (group + 1) * GROUP, lanes]
    return value.reshape(slots * GROUP, value.shape[-1])


def store_halves(high, low, index, value):
    high[index], low[index] = halves(value)


def frame_attention_kernel(qkv, b_query, b_value, distance, allowed, probs, out, *split):
    (q_high, q_low, k_high, k_low, v_high, v_low), total = split[:6], split[6]
    slots, width = qkv.shape[0], out.shape[-1]
    head_dim = width // H
    scaling = head_dim**-0.5
    for g in range(2):
        store_halves(q_high, q_low, g, grouped(qkv, g, slice(0, width)) + b_query[...])
        store_halves(k_high, k_low, g, grouped(qkv, g, slice(width, 2 * width)))
        store_halves(
            v_high, v_low, g, grouped(qkv, g, slice(2 * width, 3 * width)) + b_value[...]
        )
    total[...] = jnp.zeros(total.shape, jnp.float32)

    def step(head, _):
        at, mask = head_window(head, head_dim, width)
        mask = mask.astype(jnp.bfloat16)
        slope = jnp.exp2(-8.0 / H * (jnp.full((1, 1), head, jnp.int32).astype(jnp.float32) + 1.0))
        for g in range(2):
            query = (q_high[g, :, at] * mask, q_low[g, :, at] * mask)
            scores = three(query, (k_high[g, :, at], k_low[g, :, at]), NT)
            scores = jnp.where(allowed[...] > 0, scores * scaling - slope * distance[...], -1e30)
            prob = softmax_last(scores)
            probs[head, g] = prob
            value = (v_high[g, :, at] * mask, v_low[g, :, at] * mask)
            total[g, :, at] = total[g, :, at] + three(halves(prob), value, NN)
        return 0

    lax.fori_loop(0, H, step, 0, unroll=4)
    for g in range(2):
        out[:, g * GROUP : (g + 1) * GROUP, :] = total[g].reshape(slots, GROUP, width)


def frame_tables(frame_pos):
    slots = frame_pos.shape[0]
    position = jnp.repeat(frame_pos, GROUP)
    column = jnp.tile(jnp.arange(GROUP), slots)
    distance = jnp.abs(position[:, None] - position[None, :])
    same = column[:, None] == column[None, :]
    return distance, (same & (position[None, :] < FRAMES - 0.5)).astype(jnp.float32)


VMEM_SPEC = pl.BlockSpec(memory_space=pltpu.VMEM)


def frame_attention(qkv, b_query, b_value, distance, allowed):
    slots, cols, width = qkv.shape[0], qkv.shape[1], qkv.shape[2] // 3
    rows = slots * GROUP
    part = pltpu.VMEM((2, rows, width), jnp.bfloat16)
    return pl.pallas_call(
        frame_attention_kernel,
        out_shape=(
            jax.ShapeDtypeStruct((H, 2, rows, rows), jnp.float32),
            jax.ShapeDtypeStruct((slots, cols, width), jnp.float32),
        ),
        in_specs=[VMEM_SPEC] * 5,
        out_specs=[VMEM_SPEC] * 2,
        scratch_shapes=[part] * 6 + [pltpu.VMEM((2, rows, width), jnp.float32)],
        compiler_params=pltpu.CompilerParams(vmem_limit_bytes=40 << 20),
        cost_estimate=LIGHT,
    )(qkv, b_query.reshape(1, width), b_value.reshape(1, width), distance, allowed)


def frame_attention_back_kernel(qkv, b_query, b_value, probs, attended, grad, out, *split):
    width = attended.shape[-1]
    slots, head_dim = qkv.shape[0], width // H
    scaling = head_dim**-0.5
    names = [(split[2 * i], split[2 * i + 1]) for i in range(4)]
    (q_high, q_low), (k_high, k_low), (v_high, v_low), (g_high, g_low) = names
    total, product = split[8], split[9]
    for g in range(2):
        store_halves(q_high, q_low, g, grouped(qkv, g, slice(0, width)) + b_query[...])
        store_halves(k_high, k_low, g, grouped(qkv, g, slice(width, 2 * width)))
        store_halves(
            v_high, v_low, g, grouped(qkv, g, slice(2 * width, 3 * width)) + b_value[...]
        )
        upstream = grouped(grad, g, slice(0, width))
        store_halves(g_high, g_low, g, upstream)
        product[g] = upstream * grouped(attended, g, slice(0, width))
    total[...] = jnp.zeros(total.shape, jnp.float32)

    def step(head, _):
        at, mask = head_window(head, head_dim, width)
        small = mask.astype(jnp.bfloat16)

        def masked(high, low, g):
            return high[g, :, at] * small, low[g, :, at] * small

        for g in range(2):
            upstream = masked(g_high, g_low, g)
            prob = probs[head, g]
            grad_prob = three(upstream, (v_high[g, :, at], v_low[g, :, at]), NT)
            term = jnp.sum(product[g, :, at] * mask, axis=-1, keepdims=True)
            score = halves(prob * (grad_prob - term) * scaling)
            total[0, g, :, at] = total[0, g, :, at] + three(score, masked(k_high, k_low, g), NN)
            total[1, g, :, at] = total[1, g, :, at] + three(score, masked(q_high, q_low, g), TN)
            total[2, g, :, at] = total[2, g, :, at] + three(halves(prob), upstream, TN)
        return 0

    lax.fori_loop(0, H, step, 0, unroll=4)
    for g in range(2):
        for i in range(3):
            out[:, g * GROUP : (g + 1) * GROUP, i * width : (i + 1) * width] = total[
                i, g
            ].reshape(slots, GROUP, width)


def frame_attention_back(qkv, b_query, b_value, probs, attended, grad):
    slots, cols, width = attended.shape
    rows = slots * GROUP
    part = pltpu.VMEM((2, rows, width), jnp.bfloat16)
    return pl.pallas_call(
        frame_attention_back_kernel,
        out_shape=jax.ShapeDtypeStruct((slots, cols, 3 * width), jnp.float32),
        in_specs=[VMEM_SPEC] * 6,
        out_specs=VMEM_SPEC,
        scratch_shapes=[part] * 8
        + [pltpu.VMEM((3, 2, rows, width), jnp.float32), pltpu.VMEM((2, rows, width), jnp.float32)],
        compiler_params=pltpu.CompilerParams(vmem_limit_bytes=48 << 20),
        cost_estimate=LIGHT,
    )(qkv, b_query.reshape(1, width), b_value.reshape(1, width), probs, attended, grad)


def cross_attention_kernel(queries, b_query, kv, b_value, allowed, probs, out, *split):
    q_high, q_low, k_high, k_low, v_high, v_low = split
    width = out.shape[-1]
    head_dim = width // H
    scaling = head_dim**-0.5
    store_halves(q_high, q_low, Ellipsis, queries[...] + b_query[...])
    store_halves(k_high, k_low, Ellipsis, kv[:, 0:width])
    store_halves(v_high, v_low, Ellipsis, kv[:, width : 2 * width] + b_value[...])
    out[...] = jnp.zeros(out.shape, jnp.float32)

    def step(head, _):
        at, mask = head_window(head, head_dim, width)
        mask = mask.astype(jnp.bfloat16)
        query = (q_high[:, at] * mask, q_low[:, at] * mask)
        scores = three(query, (k_high[:, at], k_low[:, at]), NT)
        prob = softmax_last(jnp.where(allowed[...] > 0, scores * scaling, -1e30))
        probs[head] = prob
        value = (v_high[:, at] * mask, v_low[:, at] * mask)
        out[:, at] = out[:, at] + three(halves(prob), value, NN)
        return 0

    lax.fori_loop(0, H, step, 0, unroll=4)


def cross_attention(queries, b_query, kv, b_value, allowed):
    rows, width = queries.shape
    keys = kv.shape[0]
    q_part = pltpu.VMEM((rows, width), jnp.bfloat16)
    k_part = pltpu.VMEM((keys, width), jnp.bfloat16)
    return pl.pallas_call(
        cross_attention_kernel,
        out_shape=(
            jax.ShapeDtypeStruct((H, rows, keys), jnp.float32),
            jax.ShapeDtypeStruct((rows, width), jnp.float32),
        ),
        in_specs=[VMEM_SPEC] * 5,
        out_specs=[VMEM_SPEC] * 2,
        scratch_shapes=[q_part] * 2 + [k_part] * 4,
        compiler_params=pltpu.CompilerParams(vmem_limit_bytes=48 << 20),
        cost_estimate=LIGHT,
    )(queries, b_query.reshape(1, width), kv, b_value.reshape(1, width), allowed)


def cross_attention_back_kernel(
    queries, b_query, kv, b_value, probs, attended, grad, grad_q, grad_kv, *split
):
    names = [(split[2 * i], split[2 * i + 1]) for i in range(4)]
    (q_high, q_low), (g_high, g_low), (k_high, k_low), (v_high, v_low) = names
    product = split[8]
    width = grad_q.shape[-1]
    head_dim = width // H
    scaling = head_dim**-0.5
    store_halves(q_high, q_low, Ellipsis, queries[...] + b_query[...])
    store_halves(k_high, k_low, Ellipsis, kv[:, 0:width])
    store_halves(v_high, v_low, Ellipsis, kv[:, width : 2 * width] + b_value[...])
    store_halves(g_high, g_low, Ellipsis, grad[...])
    product[...] = grad[...] * attended[...]
    grad_q[...] = jnp.zeros(grad_q.shape, jnp.float32)
    grad_kv[...] = jnp.zeros(grad_kv.shape, jnp.float32)

    def step(head, _):
        at, mask = head_window(head, head_dim, width)
        start = jnp.minimum(head * head_dim // 128 * 128, width - WINDOW)
        at_value = pl.ds(pl.multiple_of(start + width, 128), WINDOW)
        small = mask.astype(jnp.bfloat16)

        def masked(high, low):
            return high[:, at] * small, low[:, at] * small

        upstream = masked(g_high, g_low)
        prob = probs[head]
        grad_prob = three(upstream, (v_high[:, at], v_low[:, at]), NT)
        term = jnp.sum(product[:, at] * mask, axis=-1, keepdims=True)
        score = halves(prob * (grad_prob - term) * scaling)
        grad_q[:, at] = grad_q[:, at] + three(score, masked(k_high, k_low), NN)
        grad_kv[:, at] = grad_kv[:, at] + three(score, masked(q_high, q_low), TN)
        grad_kv[:, at_value] = grad_kv[:, at_value] + three(halves(prob), upstream, TN)
        return 0

    lax.fori_loop(0, H, step, 0, unroll=4)


def cross_attention_back(queries, b_query, kv, b_value, probs, attended, grad):
    rows, width = queries.shape
    keys = kv.shape[0]
    q_part = pltpu.VMEM((rows, width), jnp.bfloat16)
    k_part = pltpu.VMEM((keys, width), jnp.bfloat16)
    return pl.pallas_call(
        cross_attention_back_kernel,
        out_shape=(
            jax.ShapeDtypeStruct((rows, width), jnp.float32),
            jax.ShapeDtypeStruct(kv.shape, jnp.float32),
        ),
        in_specs=[VMEM_SPEC] * 7,
        out_specs=[VMEM_SPEC] * 2,
        scratch_shapes=[q_part] * 4 + [k_part] * 4 + [pltpu.VMEM((rows, width), jnp.float32)],
        compiler_params=pltpu.CompilerParams(vmem_limit_bytes=52 << 20),
        cost_estimate=LIGHT,
    )(queries, b_query.reshape(1, width), kv, b_value.reshape(1, width), probs, attended, grad)


def assemble_kernel(axis, dim, *refs):
    blocks, whole = refs[:-1], refs[-1]
    own = lax.axis_index(axis)
    for k, block in enumerate(blocks):
        length = block.shape[dim]
        start = pl.multiple_of((own ^ k) * length, length)
        where = (slice(None),) * dim + (pl.ds(start, length),)
        whole[where] = block[...]


def assemble(blocks, axis, dim):
    shape = list(blocks[0].shape)
    shape[dim] *= len(blocks)
    size = 4 * len(blocks) * blocks[0].size
    return pl.pallas_call(
        partial(assemble_kernel, axis, dim),
        out_shape=jax.ShapeDtypeStruct(tuple(shape), jnp.float32),
        in_specs=[pl.BlockSpec(memory_space=pltpu.VMEM)] * len(blocks),
        out_specs=pl.BlockSpec(memory_space=pltpu.VMEM),
        compiler_params=pltpu.CompilerParams(vmem_limit_bytes=24 << 20),
        cost_estimate=LIGHT,
    )(*blocks)


def gather_rows(shard):
    return lax.all_gather(shard, "patch", axis=0, tiled=True)


def scatter_rows(whole):
    return lax.psum_scatter(whole, "patch", scatter_dimension=0, tiled=True)


def gather_tokens(rows):
    return token_gather(rows) if small_patch() else gather_rows(rows)


def block_of(array, axis_name, k, dim):
    length = array.shape[dim] // lax.axis_size(axis_name)
    start = (lax.axis_index(axis_name) ^ k) * length
    return lax.dynamic_slice_in_dim(array, start, length, axis=dim)


def over_chips(blocks):
    return [
        blocks[0],
        swap(blocks[1], "patch", 2),
        swap(blocks[2], "patch", 4),
        swap(blocks[3], "patch", 6),
    ]


def to_own_columns(weight):
    if not small_patch():
        return lax.all_to_all(weight, "patch", 1, 0, tiled=True)
    length = weight.shape[0]
    blocks = [block_of(weight, "patch", k, 1) for k in range(8)]
    theirs = swap(jnp.concatenate(blocks[1::2], axis=0), "patch", 1)
    both = [
        jnp.concatenate([kept, theirs[j * length : (j + 1) * length]], axis=0)
        for j, kept in enumerate(blocks[::2])
    ]
    halves = []
    for block in over_chips(both):
        halves += [block[:length], block[length:]]
    return assemble(halves, "patch", 0)


def to_columns(x):
    return lax.all_to_all(x, "frame", split_axis=1, concat_axis=0, tiled=True)


def to_slots(x):
    return lax.all_to_all(x, "frame", split_axis=0, concat_axis=1, tiled=True)


def scatter_tokens(parts):
    return token_scatter(parts) if small_patch() else scatter_rows(parts)


def open_up(block_input, cotangent, frame_slot, small, kv_part, weight):
    frame_number = frame_slot.astype(jnp.float32)
    if not small_patch():
        kv = all_sum(kv_part, "patch")
        return (
            to_columns(block_input),
            to_columns(cotangent),
            all_sum(placed(frame_number, "frame"), "frame"),
            all_sum(small, "patch"),
            lax.all_gather(kv, "frame", axis=0, tiled=True),
            gather_rows(weight),
        )
    count = frame_slot.shape[0]
    rows = -(-small.shape[0] // 1024) * 8
    tokens, later, slots, summed, kv, whole = begin(
        block_input, cotangent, padded(frame_number, 8), padded(small, rows), kv_part, weight
    )
    summed = summed.reshape(-1)[: small.shape[0]]
    slots = slots[:, 0, :count].reshape(-1)
    return tokens, later, slots, summed, kv, whole


def mid_way(parts, kv):
    if not small_patch():
        kv = lax.psum_scatter(all_sum(kv, "patch"), "frame", scatter_dimension=0, tiled=True)
        return scatter_rows(parts), kv
    return middle(parts, kv)


def close_up(weights, kv, tokens, small, caption, columns):
    clips, length = lax.axis_size("frame"), caption.shape[1]
    if not small_patch():
        weights = [lax.psum(scatter_rows(w), "frame") for w in weights]
        whole = lax.all_gather(caption, "patch", axis=0, tiled=True)
        whole = lax.all_gather(whole, "frame", axis=0)
        whole = jnp.transpose(whole, (0, 2, 1))
        small = all_sum(all_sum(small, "patch"), "frame")
        columns = lax.all_to_all(columns, "patch", 0, 1, tiled=True)
        return weights, lax.psum(kv, "frame"), to_slots(tokens), small, whole, columns
    rows = -(-small.shape[0] // 1024) * 8
    *weights, kv, tokens, summed, whole, blocks = finish(
        *weights, kv, tokens, padded(small, rows), caption, columns
    )
    columns = jnp.transpose(blocks, (1, 0, 2)).reshape(blocks.shape[1], -1)
    whole = jnp.transpose(whole, (1, 3, 0, 2)).reshape(clips, length, -1)
    return weights, kv, tokens, summed.reshape(-1)[: small.shape[0]], whole, columns


def on_device(
    block_input,
    out_cotangent,
    caption,
    cond,
    ada_weight,
    ada_bias,
    qkv_weight,
    q_bias,
    v_bias,
    attn_out_weight,
    attn_out_bias,
    cross_q_weight,
    cross_q_bias,
    cross_kv_weight,
    cross_v_bias,
    cross_out_weight,
    cross_out_bias,
    fc1_weight,
    fc1_bias,
    fc2_weight,
    fc2_bias,
    frame_slot,
    clip_id,
    patch_mask,
    caption_mask,
):
    width = block_input.shape[-1]
    cond_act, silu_pull = jax.vjp(jax.nn.silu, cond)
    cond_own = own_part(cond_act, "patch", 1)
    modulation_part = matmul(cond_own, ada_weight)
    biases = (
        ada_bias, q_bias, v_bias, attn_out_bias, cross_q_bias, cross_v_bias, cross_out_bias,
        fc2_bias,
    )
    small = jnp.concatenate(
        [modulation_part.reshape(-1)] + [placed(b, "patch") for b in biases]
    )
    caption_rows = caption.reshape(CLIPS * CAP, width)
    caption_share = own_part(own_part(caption_rows, "frame", 0), "patch", 1)
    tokens_in, cotangent, frame_pos, small, caption_kv, w_qkv = open_up(
        block_input,
        out_cotangent,
        frame_slot,
        small,
        matmul(caption_share, cross_kv_weight),
        qkv_weight,
    )
    w_two = gather_rows(jnp.concatenate([attn_out_weight, cross_q_weight], axis=1))
    w_attn, w_cross_q = jnp.split(w_two, 2, axis=1)
    w_cross_o = gather_rows(cross_out_weight)
    slots, cols, _ = tokens_in.shape
    rows = slots * cols
    clip_own = own_part(clip_id, "frame", 0)
    column_mask = own_part(patch_mask, "frame", 0).astype(jnp.float32)[:, None]
    place = modulation_part.size
    modulation = small[:place].reshape(modulation_part.shape)
    whole = []
    for b in biases:
        length = b.shape[0] * lax.axis_size("patch")
        whole.append(small[place : place + length])
        place += length
    b_ada, b_query, b_value, b_attn, b_cross_q, b_cross_v, b_cross_o, b_second = whole
    modulation = modulation + b_ada
    clip_onehot = (clip_own[:, None] == jnp.arange(CLIPS, dtype=jnp.int32)[None, :]).astype(
        jnp.float32
    )
    per_column = jnp.dot(clip_onehot, modulation, precision=lax.Precision.HIGHEST)
    shift_one, scale_one, gate_one, shift_two, scale_two, gate_two = jnp.split(
        per_column, 6, axis=1
    )

    grad_mlp = (column_mask * gate_two * cotangent).reshape(rows, width)
    normed_one, inverse_one = normalize(tokens_in)
    hidden_one = (normed_one * (1.0 + scale_one) + shift_one).reshape(rows, width)
    qkv_rows = matmul(hidden_one, w_qkv)
    w_first = to_own_columns(after(fc1_weight, qkv_rows))
    grad_mlp_all = gather_rows(after(grad_mlp, qkv_rows))
    qkv = qkv_rows.reshape(slots, cols, 3 * width)
    probs, attended = frame_attention(qkv, b_query, b_value, *frame_tables(frame_pos))
    attended_rows = attended.reshape(rows, width)
    attn_branch = (matmul(attended_rows, w_attn) + b_attn).reshape(slots, cols, width)
    after_attn = tokens_in + column_mask * gate_one * attn_branch
    after_attn_rows = after_attn.reshape(rows, width)
    after_attn_rows = after(after_attn_rows, w_first)
    cross_queries = matmul(after_attn_rows, w_cross_q)
    key_clip = jnp.arange(CLIPS * CAP, dtype=jnp.int32) // CAP
    caption_ok = (clip_own[:, None] == key_clip[None, :]) & (
        caption_mask.reshape(CLIPS * CAP)[None, :] > 0
    )
    caption_ok = jnp.tile(caption_ok.astype(jnp.float32), (slots, 1))
    cross_probs, cross_rows = cross_attention(
        cross_queries, b_cross_q, caption_kv, b_cross_v, caption_ok
    )
    cross_branch = (matmul(cross_rows, w_cross_o) + b_cross_o).reshape(slots, cols, width)
    after_cross = after_attn + column_mask * cross_branch
    normed_two, inverse_two = normalize(after_cross)
    hidden_two = (normed_two * (1.0 + scale_two) + shift_two).reshape(rows, width)

    hidden_all = gather_tokens(hidden_two)
    pre_act = matmul(hidden_all, w_first) + fc1_bias
    activated, gelu_pull = jax.vjp(partial(jax.nn.gelu, approximate=True), pre_act)
    grad_pre = gelu_pull(matmul_nt(grad_mlp_all, fc2_weight))[0]
    grad_hidden_two = scatter_tokens(matmul_nt(grad_pre, w_first))
    grad_hidden_two = grad_hidden_two.reshape(slots, cols, width)
    grad_b_second = jnp.sum(grad_mlp, axis=0)

    grad_shift_two = jnp.sum(grad_hidden_two, axis=0)
    grad_scale_two = jnp.sum(grad_hidden_two * normed_two, axis=0)
    grad_after_cross = cotangent + normalize_back(
        grad_hidden_two * (1.0 + scale_two), normed_two, inverse_two
    )
    grad_cross_branch = (column_mask * grad_after_cross).reshape(rows, width)
    grad_w_cross_o = matmul_tn(cross_rows, grad_cross_branch)
    grad_b_cross_o = jnp.sum(grad_cross_branch, axis=0)
    activated, grad_pre = after((activated, grad_pre), grad_w_cross_o)
    grad_w_first = matmul_tn(hidden_all, grad_pre)
    grad_w_second = matmul_tn(activated, grad_mlp_all)
    grad_cross_branch = after(grad_cross_branch, (grad_w_first, grad_w_second))
    grad_w_first, grad_w_second = lax.psum((grad_w_first, grad_w_second), "frame")
    grad_b_first = jnp.sum(grad_pre, axis=0)
    mlp_parts = matmul(activated, fc2_weight)
    grad_cross_rows = matmul_nt(grad_cross_branch, w_cross_o)
    grad_cross_queries, grad_kv = cross_attention_back(
        cross_queries, b_cross_q, caption_kv, b_cross_v, cross_probs, cross_rows, grad_cross_rows
    )
    grad_w_cross_q = matmul_tn(after_attn_rows, grad_cross_queries)
    grad_b_cross_q = jnp.sum(grad_cross_queries, axis=0)
    grad_cross_queries = after(grad_cross_queries, grad_w_cross_q)
    grad_after_attn = grad_after_cross + matmul_nt(grad_cross_queries, w_cross_q).reshape(
        slots, cols, width
    )
    grad_attn_rows = (column_mask * gate_one * grad_after_attn).reshape(rows, width)
    grad_gate_one = jnp.sum(column_mask * attn_branch * grad_after_attn, axis=0)
    grad_w_attn = matmul_tn(attended_rows, grad_attn_rows)
    grad_b_attn = jnp.sum(grad_attn_rows, axis=0)
    grad_attn_rows = after(grad_attn_rows, grad_w_attn)
    mlp_sum, grad_kv_share = mid_way(after(mlp_parts, grad_w_attn), grad_kv)
    grad_attn_rows = after(grad_attn_rows, mlp_sum)
    grad_w_cross_kv = matmul_tn(caption_share, grad_kv_share)
    grad_b_cross_v = jnp.sum(grad_kv_share[:, width:], axis=0)
    grad_caption_share = matmul_nt(cross_kv_weight, grad_kv_share)
    mlp_branch = (mlp_sum + b_second).reshape(slots, cols, width)
    block_out = to_slots(after_cross + column_mask * gate_two * mlp_branch)
    grad_gate_two = jnp.sum(column_mask * mlp_branch * cotangent, axis=0)
    grad_attended = matmul_nt(grad_attn_rows, w_attn).reshape(slots, cols, width)
    grad_qkv = frame_attention_back(
        qkv, b_query, b_value, probs, attended, grad_attended
    ).reshape(rows, 3 * width)
    grad_w_qkv = matmul_tn(hidden_one, grad_qkv)
    grad_b_query = jnp.sum(grad_qkv[:, :width], axis=0)
    grad_b_value = jnp.sum(grad_qkv[:, 2 * width :], axis=0)
    grad_hidden_one = matmul_nt(grad_qkv, w_qkv).reshape(slots, cols, width)
    grad_shift_one = jnp.sum(grad_hidden_one, axis=0)
    grad_scale_one = jnp.sum(grad_hidden_one * normed_one, axis=0)
    input_grad = grad_after_attn + normalize_back(
        grad_hidden_one * (1.0 + scale_one), normed_one, inverse_one
    )
    grad_per_column = jnp.concatenate(
        [
            grad_shift_one,
            grad_scale_one,
            grad_gate_one,
            grad_shift_two,
            grad_scale_two,
            grad_gate_two,
        ],
        axis=1,
    )
    grad_modulation_part = jnp.dot(
        clip_onehot.T, grad_per_column, precision=lax.Precision.HIGHEST
    )
    first = (lax.axis_index("patch") == 0).astype(jnp.float32)
    bias_grads = (
        grad_b_query,
        grad_b_value,
        grad_b_attn,
        grad_b_cross_q,
        grad_b_cross_v * first,
        grad_b_cross_o,
        grad_b_second,
    )
    small_grads = jnp.concatenate(
        [grad_modulation_part.reshape(-1)] + list(bias_grads) + [placed(grad_b_first, "patch")]
    )
    weights, grad_w_cross_kv, input_grad, small_grads, grad_caption, grad_w_first = close_up(
        (grad_w_qkv, grad_w_attn, grad_w_cross_q, grad_w_cross_o),
        grad_w_cross_kv, input_grad, small_grads, grad_caption_share, grad_w_first,
    )
    place = grad_modulation_part.size
    grad_modulation = small_grads[:place].reshape(grad_modulation_part.shape)
    own_biases = []
    for b in bias_grads:
        own_biases.append(own_part(small_grads[place : place + b.shape[0]], "patch", 0))
        place += b.shape[0]
    g_query, g_value, g_attn, g_cross_q, g_cross_v, g_cross_o, g_second = own_biases
    grad_b_first = own_part(small_grads[place:], "patch", 0)
    grad_w_ada = matmul_tn(cond_own, grad_modulation)
    grad_b_ada = own_part(jnp.sum(grad_modulation, axis=0), "patch", 0)
    grad_cond_own = matmul_nt(grad_modulation, ada_weight)
    if small_patch():
        grad_cond_act = jnp.transpose(spread(grad_cond_own), (1, 0, 2)).reshape(cond.shape)
    else:
        grad_cond_act = all_sum(placed(grad_cond_own, "patch"), "patch")
    grad_cond = silu_pull(grad_cond_act)[0]

    grad_w_qkv, grad_w_attn, grad_w_cross_q, grad_w_cross_o = weights
    return (
        block_out,
        input_grad,
        grad_caption,
        grad_cond,
        grad_w_ada,
        grad_b_ada,
        grad_w_qkv,
        g_query,
        g_value,
        grad_w_attn,
        g_attn,
        grad_w_cross_q,
        g_cross_q,
        grad_w_cross_kv,
        g_cross_v,
        grad_w_cross_o,
        g_cross_o,
        grad_w_first,
        grad_b_first,
        grad_w_second,
        g_second,
    )


def solution(mesh):
    tokens = P("frame", "patch", None)
    weight = P("patch", None)
    vector = P("patch")
    parameters = (
        weight, vector, weight, vector, vector, weight, vector, weight, vector,
        weight, vector, weight, vector, weight, vector, weight, vector,
    )
    in_specs = (tokens, tokens, P(), P()) + parameters + (P("frame"), vector, vector, P())
    out_specs = (tokens, tokens, P(), P()) + parameters
    return jax.shard_map(
        on_device, mesh=mesh, in_specs=in_specs, out_specs=out_specs, check_vma=False
    )
```

```python
from functools import partial

import jax
import jax.numpy as jnp
from jax import lax
from jax.experimental import pallas as pl
from jax.experimental.pallas import tpu as pltpu
from jax.sharding import PartitionSpec as P

H = 16
CAP = 120
FRAMES = 17
CLIPS = 4


EPSILON = 1e-06
BEST = lax.Precision.HIGH
LIGHT = pl.CostEstimate(flops=0, bytes_accessed=1 << 16, transcendentals=0)


def matmul(left, right):
    return jnp.dot(left, right, precision=BEST)


def matmul_nt(left, right):
    return lax.dot_general(left, right, (((1,), (1,)), ((), ())), precision=BEST)


def matmul_tn(left, right):
    return lax.dot_general(left, right, (((0,), (0,)), ((), ())), precision=BEST)


def normalize(rows):
    average = jnp.mean(rows, axis=-1, keepdims=True)
    centred = rows - average
    spread = jnp.mean(centred * centred, axis=-1, keepdims=True)
    inverse = lax.rsqrt(spread + EPSILON)
    return (centred * inverse, inverse)


def normalize_back(grad_normed, normed, inverse):
    first_mean = jnp.mean(grad_normed, axis=-1, keepdims=True)
    second_mean = jnp.mean(grad_normed * normed, axis=-1, keepdims=True)
    return inverse * (grad_normed - first_mean - normed * second_mean)


def swap(value, axis, bit):
    size = lax.axis_size(axis)
    return lax.ppermute(value, axis, [(i, i ^ bit) for i in range(size)])


def all_sum(value, axis):
    bit = 1
    while bit < lax.axis_size(axis):
        value = value + swap(value, axis, bit)
        bit *= 2
    return value


def placed(vector, axis):
    length = vector.shape[-1]
    whole = jnp.zeros(vector.shape[:-1] + (length * lax.axis_size(axis),), vector.dtype)
    return lax.dynamic_update_slice_in_dim(
        whole, vector, lax.axis_index(axis) * length, axis=vector.ndim - 1
    )


def own_part(array, axis, dim):
    length = array.shape[dim] // lax.axis_size(axis)
    return lax.dynamic_slice_in_dim(array, lax.axis_index(axis) * length, length, axis=dim)


def after(value, done):
    return lax.optimization_barrier((value, done))[0]


def small_patch():
    return lax.axis_size("patch") == 8 and lax.axis_size("frame") == 4


def padded(vector, rows):
    return jnp.pad(vector, (0, rows * 128 - vector.shape[0])).reshape(rows, 128)


def greet(partners):
    barrier = pltpu.get_barrier_semaphore()
    for partner in partners:
        pl.semaphore_signal(barrier, inc=1, device_id={"patch": partner}, device_id_type=pl.DeviceIdType.MESH)
    pl.semaphore_wait(barrier, len(partners))


def remote(source, target, send_sems, recv_sems, index, device):
    return pltpu.make_async_remote_copy(
        src_ref=source, dst_ref=target, send_sem=send_sems.at[index], recv_sem=recv_sems.at[index],
        device_id={"patch": device}, device_id_type=pl.DeviceIdType.MESH)


def token_gather_kernel(rows, whole, local_sem, send_sems, recv_sems):
    own = lax.axis_index("patch")
    core, along_x, along_y, across = own ^ 1, own ^ 2, own ^ 4, own ^ 6
    greet((core, along_x, along_y))
    length = rows.shape[0] // 4
    sent = []

    def piece(owner, q):
        return whole.at[owner, pl.ds(q * length, length)]

    def send(source, owner, q, index, device):
        copy = remote(source, piece(owner, q), send_sems, recv_sems, index, device)
        copy.start()
        sent.append(copy)

    def arrived(owner, q, index, device):
        remote(piece(owner, q), piece(owner, q), send_sems, recv_sems, index, device).wait_recv()

    mine = pltpu.make_async_copy(rows, whole.at[own], local_sem)
    mine.start()
    for q_x, q_y in ((0, 2), (1, 3), (2, 0), (3, 1)):
        send(rows.at[pl.ds(q_x * length, length)], own, q_x, q_x, along_x)
        send(rows.at[pl.ds(q_y * length, length)], own, q_y, 4 + q_y, along_y)
    for q in range(4):
        send(rows.at[pl.ds(q * length, length)], own, q, 12 + q, core)
    for q_x, q_y in ((0, 2), (1, 3), (2, 0), (3, 1)):
        arrived(along_x, q_x, q_x, along_x)
        if q_x < 2:
            send(piece(along_x, q_x), along_x, q_x, 8 + q_x, along_y)
        send(piece(along_x, q_x), along_x, q_x, 16 + q_x, core)
        arrived(along_y, q_y, 4 + q_y, along_y)
        if q_y >= 2:
            send(piece(along_y, q_y), along_y, q_y, 8 + q_y, along_x)
        send(piece(along_y, q_y), along_y, q_y, 20 + q_y, core)
    for q in (0, 2, 1, 3):
        arrived(across, q, 8 + q, along_y if q < 2 else along_x)
        send(piece(across, q), across, q, 24 + q, core)
    for q in range(4):
        arrived(core, q, 12 + q, core)
        arrived(core ^ 2, q, 16 + q, core)
        arrived(core ^ 4, q, 20 + q, core)
        arrived(core ^ 6, q, 24 + q, core)
    for copy in sent:
        copy.wait_send()
    mine.wait()


def token_gather(rows):
    length, width = rows.shape
    return pl.pallas_call(
        token_gather_kernel,
        out_shape=jax.ShapeDtypeStruct((8, length, width), jnp.float32),
        in_specs=[pl.BlockSpec(memory_space=pltpu.VMEM)],
        out_specs=pl.BlockSpec(memory_space=pl.ANY),
        scratch_shapes=[pltpu.SemaphoreType.DMA, pltpu.SemaphoreType.DMA((28,)), pltpu.SemaphoreType.DMA((28,))],
        compiler_params=pltpu.CompilerParams(collective_id=0, has_side_effects=True, vmem_limit_bytes=16 << 20),
        cost_estimate=LIGHT,
    )(rows).reshape(8 * length, width)


def token_scatter_kernel(parts, total, kept, theirs, by_x, by_y, from_x, from_y, local_sems, send_sems, recv_sems):
    own = lax.axis_index("patch")
    core, along_x, along_y = own ^ 1, own ^ 2, own ^ 4
    greet((core, along_x, along_y))
    half = total.shape[0] // 2
    upper, lower = pl.ds(0, half), pl.ds(half, half)
    order = (3, 2, 1, 0)
    sent, loads = [], {}

    def send(source, target, index, device):
        copy = remote(source, target, send_sems, recv_sems, index, device)
        copy.start()
        sent.append(copy)

    def arrived(target, index, device):
        remote(target, target, send_sems, recv_sems, index, device).wait_recv()

    for j in order:
        send(parts.at[core ^ (2 * j)], theirs.at[j], j, core)
        loads[j] = pltpu.make_async_copy(parts.at[own ^ (2 * j)], kept.at[j], local_sems.at[j])
        loads[j].start()

    def add_cores(j):
        loads[j].wait()
        arrived(theirs.at[j], j, core)
        kept[j] = kept[j] + theirs[j]

    add_cores(3)
    send(kept.at[3, upper], by_x, 4, along_x)
    send(kept.at[3, lower], by_y, 5, along_y)
    add_cores(2)
    send(kept.at[2, lower], from_y.at[lower], 6, along_y)
    add_cores(1)
    send(kept.at[1, upper], from_x.at[upper], 7, along_x)
    add_cores(0)
    arrived(by_x, 4, along_x)
    kept[2, upper] = kept[2, upper] + by_x[...]
    send(kept.at[2, upper], from_y.at[upper], 8, along_y)
    arrived(by_y, 5, along_y)
    kept[1, lower] = kept[1, lower] + by_y[...]
    send(kept.at[1, lower], from_x.at[lower], 9, along_x)
    arrived(from_y.at[lower], 6, along_y)
    arrived(from_x.at[upper], 7, along_x)
    arrived(from_y.at[upper], 8, along_y)
    arrived(from_x.at[lower], 9, along_x)
    total[...] = kept[0] + from_x[...] + from_y[...]
    for copy in sent:
        copy.wait_send()


def token_scatter(parts):
    length, width = parts.shape[0] // 8, parts.shape[1]
    block = (length, width)
    return pl.pallas_call(
        token_scatter_kernel,
        out_shape=jax.ShapeDtypeStruct(block, jnp.float32),
        in_specs=[pl.BlockSpec(memory_space=pl.ANY)],
        out_specs=pl.BlockSpec(memory_space=pltpu.VMEM),
        scratch_shapes=[
            pltpu.VMEM((4,) + block, jnp.float32), pltpu.VMEM((4,) + block, jnp.float32),
            pltpu.VMEM((length // 2, width), jnp.float32), pltpu.VMEM((length // 2, width), jnp.float32),
            pltpu.VMEM(block, jnp.float32), pltpu.VMEM(block, jnp.float32),
            pltpu.SemaphoreType.DMA((4,)), pltpu.SemaphoreType.DMA((10,)), pltpu.SemaphoreType.DMA((10,)),
        ],
        compiler_params=pltpu.CompilerParams(collective_id=1, has_side_effects=True, vmem_limit_bytes=32 << 20),
        cost_estimate=LIGHT,
    )(parts.reshape((8,) + block))


class Links:
    def __init__(self, send_sems, recv_sems):
        self.send_sems, self.recv_sems = send_sems, recv_sems
        self.count = 0
        self.sent = []

    def plan(self):
        self.count += 1
        return self.count - 1

    def copy(self, source, target, index, device):
        return pltpu.make_async_remote_copy(
            src_ref=source, dst_ref=target, send_sem=self.send_sems.at[index],
            recv_sem=self.recv_sems.at[index], device_id=device,
            device_id_type=pl.DeviceIdType.MESH,
        )

    def send(self, source, target, index, device):
        self.copy(source, target, index, device).start()
        self.sent.append((source, index, device))

    def wait(self, target, index, device):
        self.copy(target, target, index, device).wait_recv()

    def drain(self):
        for source, index, device in self.sent:
            self.copy(source, source, index, device).wait_send()


def greet_all(devices):
    barrier = pltpu.get_barrier_semaphore()
    for device in devices:
        pl.semaphore_signal(barrier, inc=1, device_id=device, device_id_type=pl.DeviceIdType.MESH)
    pl.semaphore_wait(barrier, len(devices))


def begin_kernel(
    tokens, later, slots, small, kv, weight,
    tokens_out, later_out, slots_out, small_out, kv_out, weight_out,
    weight_sem, small_1, small_2, small_got, kv_1, kv_2, kv_got_core, kv_got_1, kv_got_2,
    send_sems, recv_sems,
):
    me, z = lax.axis_index("patch"), lax.axis_index("frame")
    core, x, y = ({"patch": me ^ k} for k in (1, 2, 4))
    frames = [None] + [{"frame": z ^ k} for k in (1, 2, 3)]
    greet_all([core, x, y] + frames[1:])
    links = Links(send_sems, recv_sems)
    count, part = tokens.shape[0], tokens.shape[1] // 4
    rows, width = kv_1.shape

    def columns(k):
        return pl.ds(pl.multiple_of((z ^ k) * part, part), part)

    def of_slots(k):
        return pl.ds((z ^ k) * count, count)

    half = pl.multiple_of((me % 2) * width, 128)
    other = pl.multiple_of((1 - me % 2) * width, 128)
    mine, theirs = pl.ds(half, width), pl.ds(other, width)

    length = weight.shape[0]
    weight_at = [[links.plan() for _ in range(7)] for _ in range(3)]
    weight_core = links.plan()

    def piece(k, u, first=0, size=length):
        start = pl.multiple_of((me ^ k) * length + first, 8)
        return weight_out.at[pl.ds(start, size), pl.ds(u * width, width)]

    whole = weight_out.at[pl.ds(pl.multiple_of(me * length, 8), length)]
    sibling = weight_out.at[pl.ds(pl.multiple_of((me ^ 1) * length, 8), length)]
    own_copy = pltpu.make_async_copy(weight, whole, weight_sem)

    def weight_links(u):
        source = weight.at[:, pl.ds(u * width, width)]
        links.send(source, piece(0, u), weight_at[u][0], x)
        links.send(source, piece(0, u), weight_at[u][1], y)

    def weight_across(u):
        middle_row = length // 2
        links.wait(piece(2, u), weight_at[u][0], x)
        upper = piece(2, u, 0, middle_row)
        links.send(upper, upper, weight_at[u][2], y)
        links.send(piece(2, u), piece(2, u), weight_at[u][4], core)
        links.wait(piece(4, u), weight_at[u][1], y)
        lower = piece(4, u, middle_row, middle_row)
        links.send(lower, lower, weight_at[u][3], x)
        links.send(piece(4, u), piece(4, u), weight_at[u][5], core)

    def weight_last(u):
        middle_row = length // 2
        links.wait(piece(6, u, 0, middle_row), weight_at[u][2], y)
        links.wait(piece(6, u, middle_row, middle_row), weight_at[u][3], x)
        links.send(piece(6, u), piece(6, u), weight_at[u][6], core)

    at = links.plan()
    links.send(small, small_got.at[0], at, core)
    at_kv = links.plan()
    links.send(kv.at[:, theirs], kv_got_core, at_kv, core)
    own_copy.start()
    token_at = [None] + [links.plan() for _ in range(3)]
    slot_at = [None] + [links.plan() for _ in range(3)]
    later_at = [None] + [links.plan() for _ in range(3)]
    for k in (1, 2, 3):
        links.send(slots, slots_out.at[z], slot_at[k], frames[k])
        links.send(tokens.at[:, columns(k)], tokens_out.at[of_slots(0)], token_at[k], frames[k])
    for k in (1, 2, 3):
        links.send(later.at[:, columns(k)], later_out.at[of_slots(0)], later_at[k], frames[k])

    links.wait(small_got.at[0], at, core)
    small_1[...] = small[...] + small_got[0]
    at = links.plan()
    links.send(small_1, small_got.at[1], at, x)
    links.wait(kv_got_core, at_kv, core)
    kv_1[...] = kv[:, mine] + kv_got_core[...]
    upper, lower = pl.ds(0, 64), pl.ds(64, rows - 64)
    at_u, at_l = links.plan(), links.plan()
    links.send(kv_1.at[upper], kv_got_1.at[upper], at_u, x)
    links.send(kv_1.at[lower], kv_got_1.at[lower], at_l, y)
    weight_links(0)
    links.send(weight, whole, weight_core, core)
    slots_out[z] = slots[...]
    tokens_out[of_slots(0)] = tokens[:, columns(0)]
    later_out[of_slots(0)] = later[:, columns(0)]
    links.wait(small_got.at[1], at, x)
    small_2[...] = small_1[...] + small_got[1]
    at = links.plan()
    links.send(small_2, small_got.at[2], at, y)
    links.wait(kv_got_1.at[upper], at_u, x)
    links.wait(kv_got_1.at[lower], at_l, y)
    kv_2[...] = kv_1[...] + kv_got_1[...]
    at_u, at_l = links.plan(), links.plan()
    links.send(kv_2.at[upper], kv_got_2.at[upper], at_u, y)
    links.send(kv_2.at[lower], kv_got_2.at[lower], at_l, x)
    weight_links(1)
    links.wait(small_got.at[2], at, y)
    small_out[...] = small_2[...] + small_got[2]
    weight_across(0)
    weight_links(2)
    links.wait(kv_got_2.at[upper], at_u, y)
    links.wait(kv_got_2.at[lower], at_l, x)

    def share(k, columns):
        return kv_out.at[pl.ds(pl.multiple_of((z ^ k) * rows, rows), rows), columns]

    kv_out[pl.ds(pl.multiple_of(z * rows, rows), rows), mine] = kv_2[...] + kv_got_2[...]
    kv_at = [None] + [links.plan() for _ in range(3)]
    core_at = [links.plan() for _ in range(4)]
    for k in (1, 2, 3):
        links.send(share(0, mine), share(0, mine), kv_at[k], frames[k])
    links.send(share(0, mine), share(0, mine), core_at[0], core)
    weight_across(1)
    weight_last(0)
    weight_across(2)
    weight_last(1)
    for k in (1, 2, 3):
        links.wait(slots_out.at[z ^ k], slot_at[k], frames[k])
        links.wait(tokens_out.at[of_slots(k)], token_at[k], frames[k])
        links.wait(later_out.at[of_slots(k)], later_at[k], frames[k])
    for k in (1, 2, 3):
        links.wait(share(k, mine), kv_at[k], frames[k])
        links.send(share(k, mine), share(k, mine), core_at[k], core)
    weight_last(2)
    for k in range(4):
        links.wait(share(k, theirs), core_at[k], core)
    links.wait(sibling, weight_core, core)
    for u in range(3):
        for i, k in enumerate((2, 4, 6)):
            links.wait(piece(k ^ 1, u), weight_at[u][4 + i], core)
    own_copy.wait()
    links.drain()


def begin(tokens, later, slots, small, kv, weight):
    count, cols, width = tokens.shape
    rows = kv.shape[0]
    f32, vmem = jnp.float32, pl.BlockSpec(memory_space=pltpu.VMEM)
    hbm = pl.BlockSpec(memory_space=pl.ANY)
    half = pltpu.VMEM((rows, width), f32)
    return pl.pallas_call(
        begin_kernel,
        out_shape=(
            jax.ShapeDtypeStruct((4 * count, cols // 4, width), f32),
            jax.ShapeDtypeStruct((4 * count, cols // 4, width), f32),
            jax.ShapeDtypeStruct((4,) + slots.shape, f32),
            jax.ShapeDtypeStruct(small.shape, f32),
            jax.ShapeDtypeStruct((4 * rows, 2 * width), f32),
            jax.ShapeDtypeStruct((8 * weight.shape[0], weight.shape[1]), f32),
        ),
        in_specs=[vmem] * 5 + [hbm],
        out_specs=[vmem] * 5 + [hbm],
        scratch_shapes=[
            pltpu.SemaphoreType.DMA,
            pltpu.VMEM(small.shape, f32), pltpu.VMEM(small.shape, f32),
            pltpu.VMEM((3,) + small.shape, f32), half, half, half, half, half,
            pltpu.SemaphoreType.DMA((48,)), pltpu.SemaphoreType.DMA((48,)),
        ],
        compiler_params=pltpu.CompilerParams(
            collective_id=2, has_side_effects=True, vmem_limit_bytes=36 << 20
        ),
        cost_estimate=LIGHT,
    )(tokens, later, slots, small, kv, weight)


UNITS = 6


def finish_kernel(
    first, attn, cross_q, cross_o, kv, tokens, small, caption, columns,
    first_out, attn_out, cross_q_out, cross_o_out, kv_out, tokens_out, small_out, caption_out,
    columns_out, columns_got, columns_sem,
    kept, theirs, by_x, by_y, from_x, from_y, along_z, across_z,
    small_sums, small_got, small_z, load_sems, credit, send_sems, recv_sems,
):
    me, z = lax.axis_index("patch"), lax.axis_index("frame")
    outer = (z == 0) | (z == 3)
    inner = (z == 1) | (z == 2)
    core, x, y = ({"patch": me ^ k} for k in (1, 2, 4))
    frames = [None] + [{"frame": z ^ k} for k in (1, 2, 3)]
    near, facing = frames[1], frames[3]
    chips = {2: x, 4: y, 6: {"patch": me ^ 6}}
    greet_all([core, x, y, chips[6]] + frames[1:])
    links = Links(send_sems, recv_sems)
    rows, width = by_x.shape[1] * 2, by_x.shape[2]
    upper, lower = pl.ds(0, rows // 2), pl.ds(rows // 2, rows // 2)
    count, part = tokens_out.shape[0], tokens_out.shape[1] // 4

    token_at = [None] + [links.plan() for _ in range(3)]

    def send_tokens(k):
        where = pl.ds(pl.multiple_of(z * part, part), part)
        if k == 0:
            tokens_out[:, where] = tokens[pl.ds(z * count, count)]
        else:
            source = tokens.at[pl.ds((z ^ k) * count, count)]
            links.send(source, tokens_out.at[:, where], token_at[k], frames[k])

    def frame_steps(value, result, near_got, facing_got):
        up, over, down = links.plan(), links.plan(), links.plan()

        def one():
            @pl.when(outer)
            def _():
                links.copy(value, near_got, up, near).start()

        def two():
            @pl.when(inner)
            def _():
                links.wait(near_got, up, near)
                near_got[...] = near_got[...] + value[...]
                links.copy(near_got, facing_got, over, facing).start()

        def three():
            @pl.when(inner)
            def _():
                links.wait(facing_got, over, facing)
                result[...] = near_got[...] + facing_got[...]
                links.copy(result, near_got, down, near).start()

        def four():
            @pl.when(outer)
            def _():
                links.wait(near_got, down, near)
                result[...] = near_got[...]
                links.copy(value, value, up, near).wait_send()

            @pl.when(inner)
            def _():
                links.copy(near_got, near_got, over, facing).wait_send()
                links.copy(result, result, down, near).wait_send()

        return one, two, three, four

    def piece(ref, u):
        return ref.at[:, pl.ds(u * width, width)]

    outs = [piece(first_out, u) for u in range(3)] + [attn_out, cross_q_out, cross_o_out]
    steps = [
        frame_steps(kept.at[u, 0], outs[u], along_z.at[u], across_z.at[u]) for u in range(UNITS)
    ] + [
        frame_steps(piece(kv, u), piece(kv_out, u), along_z.at[UNITS + u], across_z.at[UNITS + u])
        for u in range(2)
    ]
    small_steps = frame_steps(small_sums.at[2], small_out, small_z.at[0], small_z.at[1])

    core_at = [[links.plan() for _ in range(4)] for _ in range(UNITS)]
    link_at = [[links.plan() for _ in range(6)] for _ in range(UNITS)]

    def source(u, device, j):
        start = pl.multiple_of((device ^ (2 * j)) * rows, rows)
        ref = first if u < 3 else (attn, cross_q, cross_o)[u - 3]
        return ref.at[pl.ds(start, rows), pl.ds((u % 3) * width if u < 3 else 0, width)]

    def load(u, j):
        return pltpu.make_async_copy(source(u, me, j), kept.at[u, j], load_sems.at[u, j])

    def to_core(u):
        if u >= 2:
            pl.semaphore_wait(credit.at[u - 2], 1)
        for j in (3, 2, 1, 0):
            links.send(source(u, me ^ 1, j), theirs.at[u % 2, j], core_at[u][j], core)

    def add_cores(u, j):
        load(u, j).wait()
        links.wait(theirs.at[u % 2, j], core_at[u][j], core)
        kept[u, j] = kept[u, j] + theirs[u % 2, j]

    def stage_one(u):
        at = link_at[u]
        add_cores(u, 3)
        links.send(kept.at[u, 3, upper], by_x.at[u], at[0], x)
        links.send(kept.at[u, 3, lower], by_y.at[u], at[1], y)
        add_cores(u, 2)
        links.send(kept.at[u, 2, lower], from_y.at[u, lower], at[2], y)
        add_cores(u, 1)
        links.send(kept.at[u, 1, upper], from_x.at[u, upper], at[3], x)
        add_cores(u, 0)
        if u + 2 < UNITS:
            pl.semaphore_signal(
                credit.at[u], inc=1, device_id=core, device_id_type=pl.DeviceIdType.MESH
            )
            to_core(u + 2)

    def stage_two(u):
        at = link_at[u]
        links.wait(by_x.at[u], at[0], x)
        kept[u, 2, upper] = kept[u, 2, upper] + by_x[u]
        links.send(kept.at[u, 2, upper], from_y.at[u, upper], at[4], y)
        links.wait(by_y.at[u], at[1], y)
        kept[u, 1, lower] = kept[u, 1, lower] + by_y[u]
        links.send(kept.at[u, 1, lower], from_x.at[u, lower], at[5], x)

    def stage_three(u):
        at = link_at[u]
        links.wait(from_y.at[u, lower], at[2], y)
        links.wait(from_x.at[u, upper], at[3], x)
        links.wait(from_y.at[u, upper], at[4], y)
        links.wait(from_x.at[u, lower], at[5], x)
        kept[u, 0] = kept[u, 0] + from_x[u] + from_y[u]
        steps[u][0]()

    block = columns_got.shape[1] // 2
    columns_at = {k: links.plan() for k in (2, 4, 6)}
    columns_core = {k: links.plan() for k in (0, 2, 4, 6)}

    def chip_rows(k):
        return columns.at[pl.ds(pl.multiple_of((me ^ k) // 2 * (2 * block), 8), 2 * block)]

    own_rows = pltpu.make_async_copy(chip_rows(0), columns_got.at[0], columns_sem.at[0])

    def own_block(k):
        core_rows = pl.ds(pl.multiple_of(me % 2 * block, 8), block)
        return pltpu.make_async_copy(
            columns_got.at[k // 2, core_rows], columns_out.at[me ^ k], columns_sem.at[1 + k // 2]
        )

    def send_columns(k):
        links.send(chip_rows(k), columns_got.at[k // 2], columns_at[k], chips[k])

    def columns_over():
        other_rows = pl.ds(pl.multiple_of((1 - me % 2) * block, 8), block)
        own_rows.wait()
        for k in (0, 2, 4, 6):
            if k:
                links.wait(columns_got.at[k // 2], columns_at[k], chips[k])
            links.send(
                columns_got.at[k // 2, other_rows], columns_out.at[me ^ k], columns_core[k], core
            )
            own_block(k).start()

    def columns_end():
        for k in (0, 2, 4, 6):
            links.wait(columns_out.at[me ^ 1 ^ k], columns_core[k], core)
            own_block(k).wait()

    caption_at = [links.plan() for _ in range(10)]

    def caption_frames():
        caption_out[me, z] = caption[...]
        for k in (1, 2, 3):
            links.send(caption, caption_out.at[me, z], caption_at[k - 1], frames[k])

    def caption_x():
        for k in (1, 2, 3):
            links.wait(caption_out.at[me, z ^ k], caption_at[k - 1], frames[k])
        links.send(caption_out.at[me], caption_out.at[me], caption_at[3], x)

    def caption_y():
        links.wait(caption_out.at[me ^ 2], caption_at[3], x)
        for i, k in enumerate((0, 2)):
            links.send(caption_out.at[me ^ k], caption_out.at[me ^ k], caption_at[4 + i], y)

    def caption_core():
        for i, k in enumerate((0, 2)):
            links.wait(caption_out.at[me ^ 4 ^ k], caption_at[4 + i], y)
        for i, k in enumerate((0, 2, 4, 6)):
            links.send(caption_out.at[me ^ k], caption_out.at[me ^ k], caption_at[6 + i], core)

    def caption_end():
        for i, k in enumerate((0, 2, 4, 6)):
            links.wait(caption_out.at[me ^ 1 ^ k], caption_at[6 + i], core)

    small_at = [links.plan() for _ in range(3)]
    links.send(small, small_got.at[0], small_at[0], core)
    caption_frames()
    own_rows.start()
    for u in range(UNITS):
        for j in (3, 2, 1, 0):
            load(u, j).start()
    steps[6][0]()
    steps[7][0]()
    for u in range(2):
        to_core(u)
    links.wait(small_got.at[0], small_at[0], core)
    small_sums[0] = small[...] + small_got[0]
    links.send(small_sums.at[0], small_got.at[1], small_at[1], x)
    stage_one(0)
    links.wait(small_got.at[1], small_at[1], x)
    small_sums[1] = small_sums[0] + small_got[1]
    links.send(small_sums.at[1], small_got.at[2], small_at[2], y)
    stage_one(1)
    stage_two(0)
    links.wait(small_got.at[2], small_at[2], y)
    small_sums[2] = small_sums[1] + small_got[2]
    small_steps[0]()
    stage_one(2)
    steps[6][1]()
    steps[7][1]()
    send_tokens(0)
    send_tokens(1)
    stage_two(1)
    stage_three(0)
    stage_one(3)
    steps[6][2]()
    steps[7][2]()
    small_steps[1]()
    send_tokens(2)
    stage_two(2)
    stage_three(1)
    stage_one(4)
    steps[0][1]()
    small_steps[2]()
    send_tokens(3)
    stage_two(3)
    stage_three(2)
    stage_one(5)
    steps[1][1]()
    steps[0][2]()
    stage_two(4)
    stage_three(3)
    stage_two(5)
    caption_x()
    for k in (2, 4, 6):
        send_columns(k)
    steps[2][1]()
    steps[1][2]()
    stage_three(4)
    caption_y()
    steps[3][1]()
    steps[2][2]()
    stage_three(5)
    caption_core()
    steps[4][1]()
    steps[3][2]()
    steps[5][1]()
    steps[4][2]()
    steps[5][2]()
    for step in steps + [small_steps]:
        step[3]()
    columns_over()
    caption_end()
    columns_end()
    for k in (1, 2, 3):
        where = pl.ds(pl.multiple_of((z ^ k) * part, part), part)
        links.wait(tokens_out.at[:, where], token_at[k], frames[k])
    links.drain()


def finish(first, attn, cross_q, cross_o, kv, tokens, small, caption, columns):
    rows, width = first.shape[0] // 8, first.shape[1] // 3
    count, part = tokens.shape[0] // 4, tokens.shape[1]
    f32, vmem = jnp.float32, pl.BlockSpec(memory_space=pltpu.VMEM)
    hbm = pl.BlockSpec(memory_space=pl.ANY)

    def shape(*sizes):
        return jax.ShapeDtypeStruct(sizes, f32)

    return pl.pallas_call(
        finish_kernel,
        out_shape=(
            shape(rows, 3 * width), shape(rows, width), shape(rows, width), shape(rows, width),
            shape(rows, 2 * width), shape(count, 4 * part, tokens.shape[2]), shape(*small.shape),
            shape(8, 4, *caption.shape), shape(8, columns.shape[0] // 8, columns.shape[1]),
        ),
        in_specs=[hbm] * 4 + [vmem] * 4 + [hbm],
        out_specs=[vmem] * 8 + [hbm],
        scratch_shapes=[
            pltpu.VMEM((4, columns.shape[0] // 4, columns.shape[1]), f32),
            pltpu.SemaphoreType.DMA((5,)),
            pltpu.VMEM((UNITS, 4, rows, width), f32), pltpu.VMEM((2, 4, rows, width), f32),
            pltpu.VMEM((UNITS, rows // 2, width), f32), pltpu.VMEM((UNITS, rows // 2, width), f32),
            pltpu.VMEM((UNITS, rows, width), f32), pltpu.VMEM((UNITS, rows, width), f32),
            pltpu.VMEM((UNITS + 2, rows, width), f32), pltpu.VMEM((UNITS + 2, rows, width), f32),
            pltpu.VMEM((3,) + small.shape, f32), pltpu.VMEM((3,) + small.shape, f32),
            pltpu.VMEM((2,) + small.shape, f32),
            pltpu.SemaphoreType.DMA((UNITS, 4)), pltpu.SemaphoreType.REGULAR((4,)),
            pltpu.SemaphoreType.DMA((112,)), pltpu.SemaphoreType.DMA((112,)),
        ],
        compiler_params=pltpu.CompilerParams(
            collective_id=3, has_side_effects=True, vmem_limit_bytes=58 << 20
        ),
        cost_estimate=LIGHT,
    )(first, attn, cross_q, cross_o, kv, tokens, small, caption, columns)


def middle_kernel(
    parts, kv, residual, gate, bias,
    total, kv_out, block_out,
    block, kept, theirs, by_x, by_y, from_x, from_y,
    kv_half, kv_core, kv_got, kv_1, kv_2, kv_got_1, kv_got_2,
    load_sems, send_sems, recv_sems,
):
    me, z = lax.axis_index("patch"), lax.axis_index("frame")
    core, x, y = ({"patch": me ^ k} for k in (1, 2, 4))
    frames = [None] + [{"frame": z ^ k} for k in (1, 2, 3)]
    greet_all([core, x, y] + frames[1:])
    links = Links(send_sems, recv_sems)
    rows, width = kv_1.shape
    half = pl.multiple_of((me % 2) * width, 128)
    other = pl.multiple_of((1 - me % 2) * width, 128)
    mine, others = pl.ds(half, width), pl.ds(other, width)

    def share(ref, k):
        return ref.at[pl.ds(pl.multiple_of((z ^ k) * rows, rows), rows)]

    at_kv = links.plan()
    links.send(kv.at[:, others], kv_core, at_kv, core)
    core_at = [links.plan() for _ in range(4)]
    loads = [
        pltpu.make_async_copy(parts.at[me ^ (2 * j)], kept.at[j], load_sems.at[j])
        for j in range(4)
    ]
    for j in (3, 2, 1, 0):
        links.send(parts.at[me ^ 1 ^ (2 * j)], theirs.at[j], core_at[j], core)
        loads[j].start()
    links.wait(kv_core, at_kv, core)
    kv_half[...] = kv[:, mine] + kv_core[...]
    kv_at = [None] + [links.plan() for _ in range(3)]
    for k in (1, 2, 3):
        links.send(share(kv_half, k), kv_got.at[k - 1], kv_at[k], frames[k])

    count = total.shape[0] // 2
    upper, lower = pl.ds(0, count), pl.ds(count, count)
    at = [links.plan() for _ in range(6)]

    def add_cores(j):
        loads[j].wait()
        links.wait(theirs.at[j], core_at[j], core)
        kept[j] = kept[j] + theirs[j]

    add_cores(3)
    links.send(kept.at[3, upper], by_x, at[0], x)
    links.send(kept.at[3, lower], by_y, at[1], y)
    add_cores(2)
    links.send(kept.at[2, lower], from_y.at[lower], at[2], y)
    add_cores(1)
    links.send(kept.at[1, upper], from_x.at[upper], at[3], x)
    add_cores(0)
    links.wait(by_x, at[0], x)
    kept[2, upper] = kept[2, upper] + by_x[...]
    links.send(kept.at[2, upper], from_y.at[upper], at[4], y)
    links.wait(by_y, at[1], y)
    kept[1, lower] = kept[1, lower] + by_y[...]
    links.send(kept.at[1, lower], from_x.at[lower], at[5], x)

    for k in (1, 2, 3):
        links.wait(kv_got.at[k - 1], kv_at[k], frames[k])
    kv_1[...] = share(kv_half, 0)[...] + kv_got[0] + (kv_got[1] + kv_got[2])
    top, bottom = pl.ds(0, 64), pl.ds(64, rows - 64)
    at_u, at_l = links.plan(), links.plan()
    links.send(kv_1.at[top], kv_got_1.at[top], at_u, x)
    links.send(kv_1.at[bottom], kv_got_1.at[bottom], at_l, y)
    links.wait(from_y.at[lower], at[2], y)
    links.wait(from_x.at[upper], at[3], x)
    links.wait(from_y.at[upper], at[4], y)
    links.wait(from_x.at[lower], at[5], x)
    total[...] = kept[0] + from_x[...] + from_y[...]
    slots, part = residual.shape[0] // 4, residual.shape[1]
    block[...] = residual[...] + gate[...] * (total[...] + bias[...]).reshape(residual.shape)
    block_at = [None] + [links.plan() for _ in range(3)]
    place = pl.ds(pl.multiple_of(z * part, part), part)
    for k in (1, 2, 3):
        source = block.at[pl.ds((z ^ k) * slots, slots)]
        links.send(source, block_out.at[:, place], block_at[k], frames[k])
    block_out[:, place] = block[pl.ds(z * slots, slots)]
    links.wait(kv_got_1.at[top], at_u, x)
    links.wait(kv_got_1.at[bottom], at_l, y)
    kv_2[...] = kv_1[...] + kv_got_1[...]
    at_u, at_l = links.plan(), links.plan()
    links.send(kv_2.at[top], kv_got_2.at[top], at_u, y)
    links.send(kv_2.at[bottom], kv_got_2.at[bottom], at_l, x)
    links.wait(kv_got_2.at[top], at_u, y)
    links.wait(kv_got_2.at[bottom], at_l, x)
    kv_out[:, mine] = kv_2[...] + kv_got_2[...]
    at_core = links.plan()
    links.send(kv_out.at[:, mine], kv_out.at[:, mine], at_core, core)
    links.wait(kv_out.at[:, others], at_core, core)
    for k in (1, 2, 3):
        there = pl.ds(pl.multiple_of((z ^ k) * part, part), part)
        links.wait(block_out.at[:, there], block_at[k], frames[k])
    links.drain()


def middle(parts, kv, residual, gate, bias):
    slots, cols, _ = residual.shape
    length, width = parts.shape[0] // 8, parts.shape[1]
    rows = kv.shape[0] // 4
    f32, vmem = jnp.float32, pl.BlockSpec(memory_space=pltpu.VMEM)
    block, half = (length, width), pltpu.VMEM((rows, width), f32)
    return pl.pallas_call(
        middle_kernel,
        out_shape=(
            jax.ShapeDtypeStruct(block, f32), jax.ShapeDtypeStruct((rows, 2 * width), f32),
            jax.ShapeDtypeStruct((slots // 4, 4 * cols, width), f32),
        ),
        in_specs=[pl.BlockSpec(memory_space=pl.ANY)] + [vmem] * 4,
        out_specs=[vmem] * 3,
        scratch_shapes=[
            pltpu.VMEM((slots, cols, width), f32),
            pltpu.VMEM((4,) + block, f32), pltpu.VMEM((4,) + block, f32),
            pltpu.VMEM((length // 2, width), f32), pltpu.VMEM((length // 2, width), f32),
            pltpu.VMEM(block, f32), pltpu.VMEM(block, f32),
            pltpu.VMEM((4 * rows, width), f32), pltpu.VMEM((4 * rows, width), f32),
            pltpu.VMEM((3, rows, width), f32), half, half, half, half,
            pltpu.SemaphoreType.DMA((4,)), pltpu.SemaphoreType.DMA((24,)),
            pltpu.SemaphoreType.DMA((24,)),
        ],
        compiler_params=pltpu.CompilerParams(
            collective_id=4, has_side_effects=True, vmem_limit_bytes=48 << 20
        ),
        cost_estimate=LIGHT,
    )(parts.reshape((8,) + block), kv, residual, gate[None], bias[None])


def spread_kernel(block, whole, send_sems, recv_sems):
    me = lax.axis_index("patch")
    peers = [None] + [{"patch": me ^ k} for k in range(1, 8)]
    greet_all(peers[1:])
    links = Links(send_sems, recv_sems)
    at = [links.plan() for _ in range(8)]
    for k in range(1, 8):
        links.send(block, whole.at[me], at[k], peers[k])
    whole[me] = block[...]
    for k in range(1, 8):
        links.wait(whole.at[me ^ k], at[k], peers[k])
    links.drain()


def spread(block):
    vmem = pl.BlockSpec(memory_space=pltpu.VMEM)
    return pl.pallas_call(
        spread_kernel,
        out_shape=jax.ShapeDtypeStruct((8,) + block.shape, jnp.float32),
        in_specs=[vmem],
        out_specs=vmem,
        scratch_shapes=[pltpu.SemaphoreType.DMA((8,)), pltpu.SemaphoreType.DMA((8,))],
        compiler_params=pltpu.CompilerParams(collective_id=5, has_side_effects=True),
    )(block)


def halves(x):
    high = x.astype(jnp.bfloat16)
    return high, (x - high.astype(jnp.float32)).astype(jnp.bfloat16)


NN, NT, TN = (((1,), (0,)), ((), ())), (((1,), (1,)), ((), ())), (((0,), (0,)), ((), ()))


def three(left, right, dims):
    def dot(a, b):
        return lax.dot_general(a, b, dims, preferred_element_type=jnp.float32)

    return dot(left[0], right[0]) + (dot(left[0], right[1]) + dot(left[1], right[0]))


WINDOW = 256


def head_window(head, head_dim, width):
    start = jnp.minimum(head * head_dim // 128 * 128, width - WINDOW)
    lane = lax.broadcasted_iota(jnp.int32, (1, WINDOW), 1) - (head * head_dim - start)
    mask = ((lane >= 0) & (lane < head_dim)).astype(jnp.float32)
    return pl.ds(pl.multiple_of(start, 128), WINDOW), mask


def softmax_last(scores):
    exponent = jnp.exp(scores - jnp.max(scores, axis=-1, keepdims=True))
    return exponent / jnp.sum(exponent, axis=-1, keepdims=True)


GROUP = 8


def grouped(ref, group, lanes):
    slots = ref.shape[0]
    value = ref[:, group * GROUP : (group + 1) * GROUP, lanes]
    return value.reshape(slots * GROUP, value.shape[-1])


def store_halves(high, low, index, value):
    high[index], low[index] = halves(value)


def frame_attention_kernel(qkv, b_query, b_value, distance, allowed, probs, out, *split):
    (q_high, q_low, k_high, k_low, v_high, v_low), total = split[:6], split[6]
    slots, width = qkv.shape[0], out.shape[-1]
    head_dim = width // H
    scaling = head_dim**-0.5
    for g in range(2):
        store_halves(q_high, q_low, g, grouped(qkv, g, slice(0, width)) + b_query[...])
        store_halves(k_high, k_low, g, grouped(qkv, g, slice(width, 2 * width)))
        store_halves(
            v_high, v_low, g, grouped(qkv, g, slice(2 * width, 3 * width)) + b_value[...]
        )
    total[...] = jnp.zeros(total.shape, jnp.float32)

    def step(head, _):
        at, mask = head_window(head, head_dim, width)
        mask = mask.astype(jnp.bfloat16)
        slope = jnp.exp2(-8.0 / H * (jnp.full((1, 1), head, jnp.int32).astype(jnp.float32) + 1.0))
        for g in range(2):
            query = (q_high[g, :, at] * mask, q_low[g, :, at] * mask)
            scores = three(query, (k_high[g, :, at], k_low[g, :, at]), NT)
            scores = jnp.where(allowed[...] > 0, scores * scaling - slope * distance[...], -1e30)
            prob = softmax_last(scores)
            probs[head, g] = prob
            value = (v_high[g, :, at] * mask, v_low[g, :, at] * mask)
            total[g, :, at] = total[g, :, at] + three(halves(prob), value, NN)
        return 0

    lax.fori_loop(0, H, step, 0, unroll=4)
    for g in range(2):
        out[:, g * GROUP : (g + 1) * GROUP, :] = total[g].reshape(slots, GROUP, width)


def frame_tables(frame_pos):
    slots = frame_pos.shape[0]
    position = jnp.repeat(frame_pos, GROUP)
    column = jnp.tile(jnp.arange(GROUP), slots)
    distance = jnp.abs(position[:, None] - position[None, :])
    same = column[:, None] == column[None, :]
    return distance, (same & (position[None, :] < FRAMES - 0.5)).astype(jnp.float32)


VMEM_SPEC = pl.BlockSpec(memory_space=pltpu.VMEM)


def frame_attention(qkv, b_query, b_value, distance, allowed):
    slots, cols, width = qkv.shape[0], qkv.shape[1], qkv.shape[2] // 3
    rows = slots * GROUP
    part = pltpu.VMEM((2, rows, width), jnp.bfloat16)
    return pl.pallas_call(
        frame_attention_kernel,
        out_shape=(
            jax.ShapeDtypeStruct((H, 2, rows, rows), jnp.float32),
            jax.ShapeDtypeStruct((slots, cols, width), jnp.float32),
        ),
        in_specs=[VMEM_SPEC] * 5,
        out_specs=[VMEM_SPEC] * 2,
        scratch_shapes=[part] * 6 + [pltpu.VMEM((2, rows, width), jnp.float32)],
        compiler_params=pltpu.CompilerParams(vmem_limit_bytes=40 << 20),
        cost_estimate=LIGHT,
    )(qkv, b_query.reshape(1, width), b_value.reshape(1, width), distance, allowed)


def frame_attention_back_kernel(qkv, b_query, b_value, probs, attended, grad, out, *split):
    width = attended.shape[-1]
    slots, head_dim = qkv.shape[0], width // H
    scaling = head_dim**-0.5
    names = [(split[2 * i], split[2 * i + 1]) for i in range(4)]
    (q_high, q_low), (k_high, k_low), (v_high, v_low), (g_high, g_low) = names
    total, product = split[8], split[9]
    for g in range(2):
        store_halves(q_high, q_low, g, grouped(qkv, g, slice(0, width)) + b_query[...])
        store_halves(k_high, k_low, g, grouped(qkv, g, slice(width, 2 * width)))
        store_halves(
            v_high, v_low, g, grouped(qkv, g, slice(2 * width, 3 * width)) + b_value[...]
        )
        upstream = grouped(grad, g, slice(0, width))
        store_halves(g_high, g_low, g, upstream)
        product[g] = upstream * grouped(attended, g, slice(0, width))
    total[...] = jnp.zeros(total.shape, jnp.float32)

    def step(head, _):
        at, mask = head_window(head, head_dim, width)
        small = mask.astype(jnp.bfloat16)

        def masked(high, low, g):
            return high[g, :, at] * small, low[g, :, at] * small

        for g in range(2):
            upstream = masked(g_high, g_low, g)
            prob = probs[head, g]
            grad_prob = three(upstream, (v_high[g, :, at], v_low[g, :, at]), NT)
            term = jnp.sum(product[g, :, at] * mask, axis=-1, keepdims=True)
            score = halves(prob * (grad_prob - term) * scaling)
            total[0, g, :, at] = total[0, g, :, at] + three(score, masked(k_high, k_low, g), NN)
            total[1, g, :, at] = total[1, g, :, at] + three(score, masked(q_high, q_low, g), TN)
            total[2, g, :, at] = total[2, g, :, at] + three(halves(prob), upstream, TN)
        return 0

    lax.fori_loop(0, H, step, 0, unroll=4)
    for g in range(2):
        for i in range(3):
            out[:, g * GROUP : (g + 1) * GROUP, i * width : (i + 1) * width] = total[
                i, g
            ].reshape(slots, GROUP, width)


def frame_attention_back(qkv, b_query, b_value, probs, attended, grad):
    slots, cols, width = attended.shape
    rows = slots * GROUP
    part = pltpu.VMEM((2, rows, width), jnp.bfloat16)
    return pl.pallas_call(
        frame_attention_back_kernel,
        out_shape=jax.ShapeDtypeStruct((slots, cols, 3 * width), jnp.float32),
        in_specs=[VMEM_SPEC] * 6,
        out_specs=VMEM_SPEC,
        scratch_shapes=[part] * 8
        + [pltpu.VMEM((3, 2, rows, width), jnp.float32), pltpu.VMEM((2, rows, width), jnp.float32)],
        compiler_params=pltpu.CompilerParams(vmem_limit_bytes=48 << 20),
        cost_estimate=LIGHT,
    )(qkv, b_query.reshape(1, width), b_value.reshape(1, width), probs, attended, grad)


def cross_attention_kernel(queries, b_query, kv, b_value, allowed, probs, out, *split):
    q_high, q_low, k_high, k_low, v_high, v_low = split
    width = out.shape[-1]
    head_dim = width // H
    scaling = head_dim**-0.5
    store_halves(q_high, q_low, Ellipsis, queries[...] + b_query[...])
    store_halves(k_high, k_low, Ellipsis, kv[:, 0:width])
    store_halves(v_high, v_low, Ellipsis, kv[:, width : 2 * width] + b_value[...])
    out[...] = jnp.zeros(out.shape, jnp.float32)

    def step(head, _):
        at, mask = head_window(head, head_dim, width)
        mask = mask.astype(jnp.bfloat16)
        query = (q_high[:, at] * mask, q_low[:, at] * mask)
        scores = three(query, (k_high[:, at], k_low[:, at]), NT)
        prob = softmax_last(jnp.where(allowed[...] > 0, scores * scaling, -1e30))
        probs[head] = prob
        value = (v_high[:, at] * mask, v_low[:, at] * mask)
        out[:, at] = out[:, at] + three(halves(prob), value, NN)
        return 0

    lax.fori_loop(0, H, step, 0, unroll=4)


def cross_attention(queries, b_query, kv, b_value, allowed):
    rows, width = queries.shape
    keys = kv.shape[0]
    q_part = pltpu.VMEM((rows, width), jnp.bfloat16)
    k_part = pltpu.VMEM((keys, width), jnp.bfloat16)
    return pl.pallas_call(
        cross_attention_kernel,
        out_shape=(
            jax.ShapeDtypeStruct((H, rows, keys), jnp.float32),
            jax.ShapeDtypeStruct((rows, width), jnp.float32),
        ),
        in_specs=[VMEM_SPEC] * 5,
        out_specs=[VMEM_SPEC] * 2,
        scratch_shapes=[q_part] * 2 + [k_part] * 4,
        compiler_params=pltpu.CompilerParams(vmem_limit_bytes=48 << 20),
        cost_estimate=LIGHT,
    )(queries, b_query.reshape(1, width), kv, b_value.reshape(1, width), allowed)


def cross_attention_back_kernel(
    queries, b_query, kv, b_value, probs, attended, grad, grad_q, grad_kv, *split
):
    names = [(split[2 * i], split[2 * i + 1]) for i in range(4)]
    (q_high, q_low), (g_high, g_low), (k_high, k_low), (v_high, v_low) = names
    product = split[8]
    width = grad_q.shape[-1]
    head_dim = width // H
    scaling = head_dim**-0.5
    store_halves(q_high, q_low, Ellipsis, queries[...] + b_query[...])
    store_halves(k_high, k_low, Ellipsis, kv[:, 0:width])
    store_halves(v_high, v_low, Ellipsis, kv[:, width : 2 * width] + b_value[...])
    store_halves(g_high, g_low, Ellipsis, grad[...])
    product[...] = grad[...] * attended[...]
    grad_q[...] = jnp.zeros(grad_q.shape, jnp.float32)
    grad_kv[...] = jnp.zeros(grad_kv.shape, jnp.float32)

    def step(head, _):
        at, mask = head_window(head, head_dim, width)
        start = jnp.minimum(head * head_dim // 128 * 128, width - WINDOW)
        at_value = pl.ds(pl.multiple_of(start + width, 128), WINDOW)
        small = mask.astype(jnp.bfloat16)

        def masked(high, low):
            return high[:, at] * small, low[:, at] * small

        upstream = masked(g_high, g_low)
        prob = probs[head]
        grad_prob = three(upstream, (v_high[:, at], v_low[:, at]), NT)
        term = jnp.sum(product[:, at] * mask, axis=-1, keepdims=True)
        score = halves(prob * (grad_prob - term) * scaling)
        grad_q[:, at] = grad_q[:, at] + three(score, masked(k_high, k_low), NN)
        grad_kv[:, at] = grad_kv[:, at] + three(score, masked(q_high, q_low), TN)
        grad_kv[:, at_value] = grad_kv[:, at_value] + three(halves(prob), upstream, TN)
        return 0

    lax.fori_loop(0, H, step, 0, unroll=4)


def cross_attention_back(queries, b_query, kv, b_value, probs, attended, grad):
    rows, width = queries.shape
    keys = kv.shape[0]
    q_part = pltpu.VMEM((rows, width), jnp.bfloat16)
    k_part = pltpu.VMEM((keys, width), jnp.bfloat16)
    return pl.pallas_call(
        cross_attention_back_kernel,
        out_shape=(
            jax.ShapeDtypeStruct((rows, width), jnp.float32),
            jax.ShapeDtypeStruct(kv.shape, jnp.float32),
        ),
        in_specs=[VMEM_SPEC] * 7,
        out_specs=[VMEM_SPEC] * 2,
        scratch_shapes=[q_part] * 4 + [k_part] * 4 + [pltpu.VMEM((rows, width), jnp.float32)],
        compiler_params=pltpu.CompilerParams(vmem_limit_bytes=52 << 20),
        cost_estimate=LIGHT,
    )(queries, b_query.reshape(1, width), kv, b_value.reshape(1, width), probs, attended, grad)


def assemble_kernel(axis, dim, *refs):
    blocks, whole = refs[:-1], refs[-1]
    own = lax.axis_index(axis)
    for k, block in enumerate(blocks):
        length = block.shape[dim]
        start = pl.multiple_of((own ^ k) * length, length)
        where = (slice(None),) * dim + (pl.ds(start, length),)
        whole[where] = block[...]


def assemble(blocks, axis, dim):
    shape = list(blocks[0].shape)
    shape[dim] *= len(blocks)
    size = 4 * len(blocks) * blocks[0].size
    return pl.pallas_call(
        partial(assemble_kernel, axis, dim),
        out_shape=jax.ShapeDtypeStruct(tuple(shape), jnp.float32),
        in_specs=[pl.BlockSpec(memory_space=pltpu.VMEM)] * len(blocks),
        out_specs=pl.BlockSpec(memory_space=pltpu.VMEM),
        compiler_params=pltpu.CompilerParams(vmem_limit_bytes=24 << 20),
        cost_estimate=LIGHT,
    )(*blocks)


def gather_rows(shard):
    return lax.all_gather(shard, "patch", axis=0, tiled=True)


def scatter_rows(whole):
    return lax.psum_scatter(whole, "patch", scatter_dimension=0, tiled=True)


def gather_tokens(rows):
    return token_gather(rows) if small_patch() else gather_rows(rows)


def block_of(array, axis_name, k, dim):
    length = array.shape[dim] // lax.axis_size(axis_name)
    start = (lax.axis_index(axis_name) ^ k) * length
    return lax.dynamic_slice_in_dim(array, start, length, axis=dim)


def over_chips(blocks):
    return [
        blocks[0],
        swap(blocks[1], "patch", 2),
        swap(blocks[2], "patch", 4),
        swap(blocks[3], "patch", 6),
    ]


def to_own_columns(weight):
    if not small_patch():
        return lax.all_to_all(weight, "patch", 1, 0, tiled=True)
    length = weight.shape[0]
    blocks = [block_of(weight, "patch", k, 1) for k in range(8)]
    theirs = swap(jnp.concatenate(blocks[1::2], axis=0), "patch", 1)
    both = [
        jnp.concatenate([kept, theirs[j * length : (j + 1) * length]], axis=0)
        for j, kept in enumerate(blocks[::2])
    ]
    halves = []
    for block in over_chips(both):
        halves += [block[:length], block[length:]]
    return assemble(halves, "patch", 0)


def to_columns(x):
    return lax.all_to_all(x, "frame", split_axis=1, concat_axis=0, tiled=True)


def to_slots(x):
    return lax.all_to_all(x, "frame", split_axis=0, concat_axis=1, tiled=True)


def scatter_tokens(parts):
    return token_scatter(parts) if small_patch() else scatter_rows(parts)


def open_up(block_input, cotangent, frame_slot, small, kv_part, weight):
    frame_number = frame_slot.astype(jnp.float32)
    if not small_patch():
        kv = all_sum(kv_part, "patch")
        return (
            to_columns(block_input),
            to_columns(cotangent),
            all_sum(placed(frame_number, "frame"), "frame"),
            all_sum(small, "patch"),
            lax.all_gather(kv, "frame", axis=0, tiled=True),
            gather_rows(weight),
        )
    count = frame_slot.shape[0]
    rows = -(-small.shape[0] // 1024) * 8
    tokens, later, slots, summed, kv, whole = begin(
        block_input, cotangent, padded(frame_number, 8), padded(small, rows), kv_part, weight
    )
    summed = summed.reshape(-1)[: small.shape[0]]
    slots = slots[:, 0, :count].reshape(-1)
    return tokens, later, slots, summed, kv, whole


def mid_way(parts, kv, residual, gate, bias):
    if not small_patch():
        kv = lax.psum_scatter(all_sum(kv, "patch"), "frame", scatter_dimension=0, tiled=True)
        total = scatter_rows(parts)
        block = residual + gate * (total + bias).reshape(residual.shape)
        return total, kv, to_slots(block)
    return middle(parts, kv, residual, gate, bias)


def close_up(weights, kv, tokens, small, caption, columns):
    clips, length = lax.axis_size("frame"), caption.shape[1]
    if not small_patch():
        weights = [lax.psum(scatter_rows(w), "frame") for w in weights]
        whole = lax.all_gather(caption, "patch", axis=0, tiled=True)
        whole = lax.all_gather(whole, "frame", axis=0)
        whole = jnp.transpose(whole, (0, 2, 1))
        small = all_sum(all_sum(small, "patch"), "frame")
        columns = lax.all_to_all(columns, "patch", 0, 1, tiled=True)
        return weights, lax.psum(kv, "frame"), to_slots(tokens), small, whole, columns
    rows = -(-small.shape[0] // 1024) * 8
    *weights, kv, tokens, summed, whole, blocks = finish(
        *weights, kv, tokens, padded(small, rows), caption, columns
    )
    columns = jnp.transpose(blocks, (1, 0, 2)).reshape(blocks.shape[1], -1)
    whole = jnp.transpose(whole, (1, 3, 0, 2)).reshape(clips, length, -1)
    return weights, kv, tokens, summed.reshape(-1)[: small.shape[0]], whole, columns


def on_device(
    block_input,
    out_cotangent,
    caption,
    cond,
    ada_weight,
    ada_bias,
    qkv_weight,
    q_bias,
    v_bias,
    attn_out_weight,
    attn_out_bias,
    cross_q_weight,
    cross_q_bias,
    cross_kv_weight,
    cross_v_bias,
    cross_out_weight,
    cross_out_bias,
    fc1_weight,
    fc1_bias,
    fc2_weight,
    fc2_bias,
    frame_slot,
    clip_id,
    patch_mask,
    caption_mask,
):
    width = block_input.shape[-1]
    cond_act, silu_pull = jax.vjp(jax.nn.silu, cond)
    cond_own = own_part(cond_act, "patch", 1)
    modulation_part = matmul(cond_own, ada_weight)
    biases = (
        ada_bias, q_bias, v_bias, attn_out_bias, cross_q_bias, cross_v_bias, cross_out_bias,
        fc2_bias,
    )
    small = jnp.concatenate(
        [modulation_part.reshape(-1)] + [placed(b, "patch") for b in biases]
    )
    caption_rows = caption.reshape(CLIPS * CAP, width)
    caption_share = own_part(own_part(caption_rows, "frame", 0), "patch", 1)
    tokens_in, cotangent, frame_pos, small, caption_kv, w_qkv = open_up(
        block_input,
        out_cotangent,
        frame_slot,
        small,
        matmul(caption_share, cross_kv_weight),
        qkv_weight,
    )
    w_two = gather_rows(jnp.concatenate([attn_out_weight, cross_q_weight], axis=1))
    w_attn, w_cross_q = jnp.split(w_two, 2, axis=1)
    w_cross_o = gather_rows(cross_out_weight)
    slots, cols, _ = tokens_in.shape
    rows = slots * cols
    clip_own = own_part(clip_id, "frame", 0)
    column_mask = own_part(patch_mask, "frame", 0).astype(jnp.float32)[:, None]
    place = modulation_part.size
    modulation = small[:place].reshape(modulation_part.shape)
    whole = []
    for b in biases:
        length = b.shape[0] * lax.axis_size("patch")
        whole.append(small[place : place + length])
        place += length
    b_ada, b_query, b_value, b_attn, b_cross_q, b_cross_v, b_cross_o, b_second = whole
    modulation = modulation + b_ada
    clip_onehot = (clip_own[:, None] == jnp.arange(CLIPS, dtype=jnp.int32)[None, :]).astype(
        jnp.float32
    )
    per_column = jnp.dot(clip_onehot, modulation, precision=lax.Precision.HIGHEST)
    shift_one, scale_one, gate_one, shift_two, scale_two, gate_two = jnp.split(
        per_column, 6, axis=1
    )

    grad_mlp = (column_mask * gate_two * cotangent).reshape(rows, width)
    normed_one, inverse_one = normalize(tokens_in)
    hidden_one = (normed_one * (1.0 + scale_one) + shift_one).reshape(rows, width)
    qkv_rows = matmul(hidden_one, w_qkv)
    grad_mlp_all = gather_rows(after(grad_mlp, qkv_rows))
    qkv = qkv_rows.reshape(slots, cols, 3 * width)
    probs, attended = frame_attention(qkv, b_query, b_value, *frame_tables(frame_pos))
    attended_rows = attended.reshape(rows, width)
    attn_branch = (matmul(attended_rows, w_attn) + b_attn).reshape(slots, cols, width)
    after_attn = tokens_in + column_mask * gate_one * attn_branch
    after_attn_rows = after_attn.reshape(rows, width)
    cross_queries = matmul(after_attn_rows, w_cross_q)
    w_first = to_own_columns(after(fc1_weight, cross_queries))
    cross_queries = after(cross_queries, grad_mlp_all)
    key_clip = jnp.arange(CLIPS * CAP, dtype=jnp.int32) // CAP
    caption_ok = (clip_own[:, None] == key_clip[None, :]) & (
        caption_mask.reshape(CLIPS * CAP)[None, :] > 0
    )
    caption_ok = jnp.tile(caption_ok.astype(jnp.float32), (slots, 1))
    cross_probs, cross_rows = cross_attention(
        cross_queries, b_cross_q, caption_kv, b_cross_v, caption_ok
    )
    cross_branch = (matmul(cross_rows, w_cross_o) + b_cross_o).reshape(slots, cols, width)
    after_cross = after_attn + column_mask * cross_branch
    normed_two, inverse_two = normalize(after_cross)
    hidden_two = (normed_two * (1.0 + scale_two) + shift_two).reshape(rows, width)

    hidden_all = gather_tokens(after(hidden_two, w_first))
    pre_act = matmul(hidden_all, w_first) + fc1_bias
    activated, gelu_pull = jax.vjp(partial(jax.nn.gelu, approximate=True), pre_act)
    grad_pre = gelu_pull(matmul_nt(grad_mlp_all, fc2_weight))[0]
    grad_hidden_two = scatter_tokens(matmul_nt(grad_pre, w_first))
    grad_hidden_two = grad_hidden_two.reshape(slots, cols, width)
    grad_b_second = jnp.sum(grad_mlp, axis=0)

    grad_shift_two = jnp.sum(grad_hidden_two, axis=0)
    grad_scale_two = jnp.sum(grad_hidden_two * normed_two, axis=0)
    grad_after_cross = cotangent + normalize_back(
        grad_hidden_two * (1.0 + scale_two), normed_two, inverse_two
    )
    grad_cross_branch = (column_mask * grad_after_cross).reshape(rows, width)
    grad_w_cross_o = matmul_tn(cross_rows, grad_cross_branch)
    grad_b_cross_o = jnp.sum(grad_cross_branch, axis=0)
    activated, grad_pre = after((activated, grad_pre), grad_w_cross_o)
    grad_w_first = matmul_tn(hidden_all, grad_pre)
    grad_w_second = matmul_tn(activated, grad_mlp_all)
    grad_cross_branch = after(grad_cross_branch, (grad_w_first, grad_w_second))
    grad_w_first, grad_w_second = lax.psum((grad_w_first, grad_w_second), "frame")
    grad_b_first = jnp.sum(grad_pre, axis=0)
    mlp_parts = matmul(activated, fc2_weight)
    grad_cross_rows = matmul_nt(grad_cross_branch, w_cross_o)
    grad_cross_queries, grad_kv = cross_attention_back(
        cross_queries, b_cross_q, caption_kv, b_cross_v, cross_probs, cross_rows, grad_cross_rows
    )
    grad_w_cross_q = matmul_tn(after_attn_rows, grad_cross_queries)
    grad_b_cross_q = jnp.sum(grad_cross_queries, axis=0)
    grad_cross_queries = after(grad_cross_queries, grad_w_cross_q)
    grad_after_attn = grad_after_cross + matmul_nt(grad_cross_queries, w_cross_q).reshape(
        slots, cols, width
    )
    grad_attn_rows = (column_mask * gate_one * grad_after_attn).reshape(rows, width)
    grad_gate_one = jnp.sum(column_mask * attn_branch * grad_after_attn, axis=0)
    grad_w_attn = matmul_tn(attended_rows, grad_attn_rows)
    grad_b_attn = jnp.sum(grad_attn_rows, axis=0)
    grad_attn_rows = after(grad_attn_rows, grad_w_attn)
    mlp_sum, grad_kv_share, block_out = mid_way(
        after(mlp_parts, grad_w_attn), grad_kv, after_cross, column_mask * gate_two, b_second
    )
    grad_attn_rows = after(grad_attn_rows, mlp_sum)
    grad_w_cross_kv = matmul_tn(caption_share, grad_kv_share)
    grad_b_cross_v = jnp.sum(grad_kv_share[:, width:], axis=0)
    grad_caption_share = matmul_nt(cross_kv_weight, grad_kv_share)
    mlp_branch = (mlp_sum + b_second).reshape(slots, cols, width)
    grad_gate_two = jnp.sum(column_mask * mlp_branch * cotangent, axis=0)
    grad_attended = matmul_nt(grad_attn_rows, w_attn).reshape(slots, cols, width)
    grad_qkv = frame_attention_back(
        qkv, b_query, b_value, probs, attended, grad_attended
    ).reshape(rows, 3 * width)
    grad_w_qkv = matmul_tn(hidden_one, grad_qkv)
    grad_b_query = jnp.sum(grad_qkv[:, :width], axis=0)
    grad_b_value = jnp.sum(grad_qkv[:, 2 * width :], axis=0)
    grad_hidden_one = matmul_nt(grad_qkv, w_qkv).reshape(slots, cols, width)
    grad_shift_one = jnp.sum(grad_hidden_one, axis=0)
    grad_scale_one = jnp.sum(grad_hidden_one * normed_one, axis=0)
    input_grad = grad_after_attn + normalize_back(
        grad_hidden_one * (1.0 + scale_one), normed_one, inverse_one
    )
    grad_per_column = jnp.concatenate(
        [
            grad_shift_one,
            grad_scale_one,
            grad_gate_one,
            grad_shift_two,
            grad_scale_two,
            grad_gate_two,
        ],
        axis=1,
    )
    grad_modulation_part = jnp.dot(
        clip_onehot.T, grad_per_column, precision=lax.Precision.HIGHEST
    )
    first = (lax.axis_index("patch") == 0).astype(jnp.float32)
    bias_grads = (
        grad_b_query,
        grad_b_value,
        grad_b_attn,
        grad_b_cross_q,
        grad_b_cross_v * first,
        grad_b_cross_o,
        grad_b_second,
    )
    small_grads = jnp.concatenate(
        [grad_modulation_part.reshape(-1)] + list(bias_grads) + [placed(grad_b_first, "patch")]
    )
    weights, grad_w_cross_kv, input_grad, small_grads, grad_caption, grad_w_first = close_up(
        (grad_w_qkv, grad_w_attn, grad_w_cross_q, grad_w_cross_o),
        grad_w_cross_kv, input_grad, small_grads, grad_caption_share, grad_w_first,
    )
    place = grad_modulation_part.size
    grad_modulation = small_grads[:place].reshape(grad_modulation_part.shape)
    own_biases = []
    for b in bias_grads:
        own_biases.append(own_part(small_grads[place : place + b.shape[0]], "patch", 0))
        place += b.shape[0]
    g_query, g_value, g_attn, g_cross_q, g_cross_v, g_cross_o, g_second = own_biases
    grad_b_first = own_part(small_grads[place:], "patch", 0)
    grad_w_ada = matmul_tn(cond_own, grad_modulation)
    grad_b_ada = own_part(jnp.sum(grad_modulation, axis=0), "patch", 0)
    grad_cond_own = matmul_nt(grad_modulation, ada_weight)
    if small_patch():
        grad_cond_act = jnp.transpose(spread(grad_cond_own), (1, 0, 2)).reshape(cond.shape)
    else:
        grad_cond_act = all_sum(placed(grad_cond_own, "patch"), "patch")
    grad_cond = silu_pull(grad_cond_act)[0]

    grad_w_qkv, grad_w_attn, grad_w_cross_q, grad_w_cross_o = weights
    return (
        block_out,
        input_grad,
        grad_caption,
        grad_cond,
        grad_w_ada,
        grad_b_ada,
        grad_w_qkv,
        g_query,
        g_value,
        grad_w_attn,
        g_attn,
        grad_w_cross_q,
        g_cross_q,
        grad_w_cross_kv,
        g_cross_v,
        grad_w_cross_o,
        g_cross_o,
        grad_w_first,
        grad_b_first,
        grad_w_second,
        g_second,
    )


def solution(mesh):
    tokens = P("frame", "patch", None)
    weight = P("patch", None)
    vector = P("patch")
    parameters = (
        weight, vector, weight, vector, vector, weight, vector, weight, vector,
        weight, vector, weight, vector, weight, vector, weight, vector,
    )
    in_specs = (tokens, tokens, P(), P()) + parameters + (P("frame"), vector, vector, P())
    out_specs = (tokens, tokens, P(), P()) + parameters
    return jax.shard_map(
        on_device, mesh=mesh, in_specs=in_specs, out_specs=out_specs, check_vma=False
    )
```

```python
import math
from functools import partial

import jax
import jax.numpy as jnp
from jax import lax
from jax.experimental import pallas as pl
from jax.experimental.pallas import tpu as pltpu
from jax.sharding import PartitionSpec as P

H = 16
CAP = 120
FRAMES = 17
CLIPS = 4


EPSILON = 1e-06
BEST = lax.Precision.HIGH
LIGHT = pl.CostEstimate(flops=0, bytes_accessed=1 << 16, transcendentals=0)


def matmul(left, right):
    return jnp.dot(left, right, precision=BEST)


def matmul_nt(left, right):
    return lax.dot_general(left, right, (((1,), (1,)), ((), ())), precision=BEST)


def matmul_tn(left, right):
    return lax.dot_general(left, right, (((0,), (0,)), ((), ())), precision=BEST)


def normalize(rows):
    average = jnp.mean(rows, axis=-1, keepdims=True)
    centred = rows - average
    spread = jnp.mean(centred * centred, axis=-1, keepdims=True)
    inverse = lax.rsqrt(spread + EPSILON)
    return (centred * inverse, inverse)


def normalize_back(grad_normed, normed, inverse):
    first_mean = jnp.mean(grad_normed, axis=-1, keepdims=True)
    second_mean = jnp.mean(grad_normed * normed, axis=-1, keepdims=True)
    return inverse * (grad_normed - first_mean - normed * second_mean)


def swap(value, axis, bit):
    size = lax.axis_size(axis)
    return lax.ppermute(value, axis, [(i, i ^ bit) for i in range(size)])


def all_sum(value, axis):
    bit = 1
    while bit < lax.axis_size(axis):
        value = value + swap(value, axis, bit)
        bit *= 2
    return value


def placed(vector, axis):
    length = vector.shape[-1]
    whole = jnp.zeros(vector.shape[:-1] + (length * lax.axis_size(axis),), vector.dtype)
    return lax.dynamic_update_slice_in_dim(
        whole, vector, lax.axis_index(axis) * length, axis=vector.ndim - 1
    )


def own_part(array, axis, dim):
    length = array.shape[dim] // lax.axis_size(axis)
    return lax.dynamic_slice_in_dim(array, lax.axis_index(axis) * length, length, axis=dim)


def after(value, done):
    return lax.optimization_barrier((value, done))[0]


def small_patch():
    return lax.axis_size("patch") == 8 and lax.axis_size("frame") == 4


def padded(vector, rows):
    return jnp.pad(vector, (0, rows * 128 - vector.shape[0])).reshape(rows, 128)


def greet(partners):
    barrier = pltpu.get_barrier_semaphore()
    for partner in partners:
        pl.semaphore_signal(barrier, inc=1, device_id={"patch": partner}, device_id_type=pl.DeviceIdType.MESH)
    pl.semaphore_wait(barrier, len(partners))


def remote(source, target, send_sems, recv_sems, index, device):
    return pltpu.make_async_remote_copy(
        src_ref=source, dst_ref=target, send_sem=send_sems.at[index], recv_sem=recv_sems.at[index],
        device_id={"patch": device}, device_id_type=pl.DeviceIdType.MESH)


def token_gather_kernel(rows, whole, local_sem, send_sems, recv_sems):
    own = lax.axis_index("patch")
    core, along_x, along_y, across = own ^ 1, own ^ 2, own ^ 4, own ^ 6
    greet((core, along_x, along_y))
    length = rows.shape[0] // 4
    sent = []

    def piece(owner, q):
        return whole.at[owner, pl.ds(q * length, length)]

    def send(source, owner, q, index, device):
        copy = remote(source, piece(owner, q), send_sems, recv_sems, index, device)
        copy.start()
        sent.append(copy)

    def arrived(owner, q, index, device):
        remote(piece(owner, q), piece(owner, q), send_sems, recv_sems, index, device).wait_recv()

    mine = pltpu.make_async_copy(rows, whole.at[own], local_sem)
    mine.start()
    for q_x, q_y in ((0, 2), (1, 3), (2, 0), (3, 1)):
        send(rows.at[pl.ds(q_x * length, length)], own, q_x, q_x, along_x)
        send(rows.at[pl.ds(q_y * length, length)], own, q_y, 4 + q_y, along_y)
    for q in range(4):
        send(rows.at[pl.ds(q * length, length)], own, q, 12 + q, core)
    for q_x, q_y in ((0, 2), (1, 3), (2, 0), (3, 1)):
        arrived(along_x, q_x, q_x, along_x)
        if q_x < 2:
            send(piece(along_x, q_x), along_x, q_x, 8 + q_x, along_y)
        send(piece(along_x, q_x), along_x, q_x, 16 + q_x, core)
        arrived(along_y, q_y, 4 + q_y, along_y)
        if q_y >= 2:
            send(piece(along_y, q_y), along_y, q_y, 8 + q_y, along_x)
        send(piece(along_y, q_y), along_y, q_y, 20 + q_y, core)
    for q in (0, 2, 1, 3):
        arrived(across, q, 8 + q, along_y if q < 2 else along_x)
        send(piece(across, q), across, q, 24 + q, core)
    for q in range(4):
        arrived(core, q, 12 + q, core)
        arrived(core ^ 2, q, 16 + q, core)
        arrived(core ^ 4, q, 20 + q, core)
        arrived(core ^ 6, q, 24 + q, core)
    for copy in sent:
        copy.wait_send()
    mine.wait()


def token_gather(rows):
    length, width = rows.shape
    return pl.pallas_call(
        token_gather_kernel,
        out_shape=jax.ShapeDtypeStruct((8, length, width), jnp.float32),
        in_specs=[pl.BlockSpec(memory_space=pltpu.VMEM)],
        out_specs=pl.BlockSpec(memory_space=pl.ANY),
        scratch_shapes=[pltpu.SemaphoreType.DMA, pltpu.SemaphoreType.DMA((28,)), pltpu.SemaphoreType.DMA((28,))],
        compiler_params=pltpu.CompilerParams(collective_id=0, has_side_effects=True, vmem_limit_bytes=16 << 20),
        cost_estimate=LIGHT,
    )(rows).reshape(8 * length, width)


def token_scatter_kernel(parts, total, kept, theirs, by_x, by_y, from_x, from_y, local_sems, send_sems, recv_sems):
    own = lax.axis_index("patch")
    core, along_x, along_y = own ^ 1, own ^ 2, own ^ 4
    greet((core, along_x, along_y))
    half = total.shape[0] // 2
    upper, lower = pl.ds(0, half), pl.ds(half, half)
    order = (3, 2, 1, 0)
    sent, loads = [], {}

    def send(source, target, index, device):
        copy = remote(source, target, send_sems, recv_sems, index, device)
        copy.start()
        sent.append(copy)

    def arrived(target, index, device):
        remote(target, target, send_sems, recv_sems, index, device).wait_recv()

    for j in order:
        send(parts.at[core ^ (2 * j)], theirs.at[j], j, core)
        loads[j] = pltpu.make_async_copy(parts.at[own ^ (2 * j)], kept.at[j], local_sems.at[j])
        loads[j].start()

    def add_cores(j):
        loads[j].wait()
        arrived(theirs.at[j], j, core)
        kept[j] = kept[j] + theirs[j]

    add_cores(3)
    send(kept.at[3, upper], by_x, 4, along_x)
    send(kept.at[3, lower], by_y, 5, along_y)
    add_cores(2)
    send(kept.at[2, lower], from_y.at[lower], 6, along_y)
    add_cores(1)
    send(kept.at[1, upper], from_x.at[upper], 7, along_x)
    add_cores(0)
    arrived(by_x, 4, along_x)
    kept[2, upper] = kept[2, upper] + by_x[...]
    send(kept.at[2, upper], from_y.at[upper], 8, along_y)
    arrived(by_y, 5, along_y)
    kept[1, lower] = kept[1, lower] + by_y[...]
    send(kept.at[1, lower], from_x.at[lower], 9, along_x)
    arrived(from_y.at[lower], 6, along_y)
    arrived(from_x.at[upper], 7, along_x)
    arrived(from_y.at[upper], 8, along_y)
    arrived(from_x.at[lower], 9, along_x)
    total[...] = kept[0] + from_x[...] + from_y[...]
    for copy in sent:
        copy.wait_send()


def token_scatter(parts):
    length, width = parts.shape[0] // 8, parts.shape[1]
    block = (length, width)
    return pl.pallas_call(
        token_scatter_kernel,
        out_shape=jax.ShapeDtypeStruct(block, jnp.float32),
        in_specs=[pl.BlockSpec(memory_space=pl.ANY)],
        out_specs=pl.BlockSpec(memory_space=pltpu.VMEM),
        scratch_shapes=[
            pltpu.VMEM((4,) + block, jnp.float32), pltpu.VMEM((4,) + block, jnp.float32),
            pltpu.VMEM((length // 2, width), jnp.float32), pltpu.VMEM((length // 2, width), jnp.float32),
            pltpu.VMEM(block, jnp.float32), pltpu.VMEM(block, jnp.float32),
            pltpu.SemaphoreType.DMA((4,)), pltpu.SemaphoreType.DMA((10,)), pltpu.SemaphoreType.DMA((10,)),
        ],
        compiler_params=pltpu.CompilerParams(collective_id=1, has_side_effects=True, vmem_limit_bytes=32 << 20),
        cost_estimate=LIGHT,
    )(parts.reshape((8,) + block))


class Links:
    def __init__(self, send_sems, recv_sems):
        self.send_sems, self.recv_sems = send_sems, recv_sems
        self.count = 0
        self.sent = []

    def plan(self):
        self.count += 1
        return self.count - 1

    def copy(self, source, target, index, device):
        return pltpu.make_async_remote_copy(
            src_ref=source, dst_ref=target, send_sem=self.send_sems.at[index],
            recv_sem=self.recv_sems.at[index], device_id=device,
            device_id_type=pl.DeviceIdType.MESH,
        )

    def send(self, source, target, index, device):
        self.copy(source, target, index, device).start()
        self.sent.append((source, index, device))

    def wait(self, target, index, device):
        self.copy(target, target, index, device).wait_recv()

    def drain(self):
        for source, index, device in self.sent:
            self.copy(source, source, index, device).wait_send()


def greet_all(devices):
    barrier = pltpu.get_barrier_semaphore()
    for device in devices:
        pl.semaphore_signal(barrier, inc=1, device_id=device, device_id_type=pl.DeviceIdType.MESH)
    pl.semaphore_wait(barrier, len(devices))


def begin_kernel(
    tokens, later, slots, small, kv, weight,
    tokens_out, later_out, slots_out, small_out, kv_out, weight_out,
    weight_sem, small_1, small_2, small_got, kv_1, kv_2, kv_got_core, kv_got_1, kv_got_2,
    send_sems, recv_sems,
):
    me, z = lax.axis_index("patch"), lax.axis_index("frame")
    core, x, y = ({"patch": me ^ k} for k in (1, 2, 4))
    frames = [None] + [{"frame": z ^ k} for k in (1, 2, 3)]
    greet_all([core, x, y] + frames[1:])
    links = Links(send_sems, recv_sems)
    count, part = tokens.shape[0], tokens.shape[1] // 4
    rows, width = kv_1.shape

    def columns(k):
        return pl.ds(pl.multiple_of((z ^ k) * part, part), part)

    def of_slots(k):
        return pl.ds((z ^ k) * count, count)

    half = pl.multiple_of((me % 2) * width, 128)
    other = pl.multiple_of((1 - me % 2) * width, 128)
    mine, theirs = pl.ds(half, width), pl.ds(other, width)

    length = weight.shape[0]
    weight_at = [[links.plan() for _ in range(7)] for _ in range(3)]
    weight_core = links.plan()

    def piece(k, u, first=0, size=length):
        start = pl.multiple_of((me ^ k) * length + first, 8)
        return weight_out.at[pl.ds(start, size), pl.ds(u * width, width)]

    whole = weight_out.at[pl.ds(pl.multiple_of(me * length, 8), length)]
    sibling = weight_out.at[pl.ds(pl.multiple_of((me ^ 1) * length, 8), length)]
    own_copy = pltpu.make_async_copy(weight, whole, weight_sem)

    def weight_links(u):
        source = weight.at[:, pl.ds(u * width, width)]
        links.send(source, piece(0, u), weight_at[u][0], x)
        links.send(source, piece(0, u), weight_at[u][1], y)

    def weight_across(u):
        middle_row = length // 2
        links.wait(piece(2, u), weight_at[u][0], x)
        upper = piece(2, u, 0, middle_row)
        links.send(upper, upper, weight_at[u][2], y)
        links.send(piece(2, u), piece(2, u), weight_at[u][4], core)
        links.wait(piece(4, u), weight_at[u][1], y)
        lower = piece(4, u, middle_row, middle_row)
        links.send(lower, lower, weight_at[u][3], x)
        links.send(piece(4, u), piece(4, u), weight_at[u][5], core)

    def weight_last(u):
        middle_row = length // 2
        links.wait(piece(6, u, 0, middle_row), weight_at[u][2], y)
        links.wait(piece(6, u, middle_row, middle_row), weight_at[u][3], x)
        links.send(piece(6, u), piece(6, u), weight_at[u][6], core)

    at = links.plan()
    links.send(small, small_got.at[0], at, core)
    at_kv = links.plan()
    links.send(kv.at[:, theirs], kv_got_core, at_kv, core)
    own_copy.start()
    token_at = [None] + [links.plan() for _ in range(3)]
    slot_at = [None] + [links.plan() for _ in range(3)]
    later_at = [None] + [links.plan() for _ in range(3)]
    for k in (1, 2, 3):
        links.send(slots, slots_out.at[z], slot_at[k], frames[k])
        links.send(tokens.at[:, columns(k)], tokens_out.at[of_slots(0)], token_at[k], frames[k])
    for k in (1, 2, 3):
        links.send(later.at[:, columns(k)], later_out.at[of_slots(0)], later_at[k], frames[k])

    links.wait(small_got.at[0], at, core)
    small_1[...] = small[...] + small_got[0]
    at = links.plan()
    links.send(small_1, small_got.at[1], at, x)
    links.wait(kv_got_core, at_kv, core)
    kv_1[...] = kv[:, mine] + kv_got_core[...]
    upper, lower = pl.ds(0, 64), pl.ds(64, rows - 64)
    at_u, at_l = links.plan(), links.plan()
    links.send(kv_1.at[upper], kv_got_1.at[upper], at_u, x)
    links.send(kv_1.at[lower], kv_got_1.at[lower], at_l, y)
    weight_links(0)
    links.send(weight, whole, weight_core, core)
    slots_out[z] = slots[...]
    tokens_out[of_slots(0)] = tokens[:, columns(0)]
    later_out[of_slots(0)] = later[:, columns(0)]
    links.wait(small_got.at[1], at, x)
    small_2[...] = small_1[...] + small_got[1]
    at = links.plan()
    links.send(small_2, small_got.at[2], at, y)
    links.wait(kv_got_1.at[upper], at_u, x)
    links.wait(kv_got_1.at[lower], at_l, y)
    kv_2[...] = kv_1[...] + kv_got_1[...]
    at_u, at_l = links.plan(), links.plan()
    links.send(kv_2.at[upper], kv_got_2.at[upper], at_u, y)
    links.send(kv_2.at[lower], kv_got_2.at[lower], at_l, x)
    weight_links(1)
    links.wait(small_got.at[2], at, y)
    small_out[...] = small_2[...] + small_got[2]
    weight_across(0)
    weight_links(2)
    links.wait(kv_got_2.at[upper], at_u, y)
    links.wait(kv_got_2.at[lower], at_l, x)

    def share(k, columns):
        return kv_out.at[pl.ds(pl.multiple_of((z ^ k) * rows, rows), rows), columns]

    kv_out[pl.ds(pl.multiple_of(z * rows, rows), rows), mine] = kv_2[...] + kv_got_2[...]
    kv_at = [None] + [links.plan() for _ in range(3)]
    core_at = [links.plan() for _ in range(4)]
    for k in (1, 2, 3):
        links.send(share(0, mine), share(0, mine), kv_at[k], frames[k])
    links.send(share(0, mine), share(0, mine), core_at[0], core)
    weight_across(1)
    weight_last(0)
    weight_across(2)
    weight_last(1)
    for k in (1, 2, 3):
        links.wait(slots_out.at[z ^ k], slot_at[k], frames[k])
        links.wait(tokens_out.at[of_slots(k)], token_at[k], frames[k])
        links.wait(later_out.at[of_slots(k)], later_at[k], frames[k])
    for k in (1, 2, 3):
        links.wait(share(k, mine), kv_at[k], frames[k])
        links.send(share(k, mine), share(k, mine), core_at[k], core)
    weight_last(2)
    for k in range(4):
        links.wait(share(k, theirs), core_at[k], core)
    links.wait(sibling, weight_core, core)
    for u in range(3):
        for i, k in enumerate((2, 4, 6)):
            links.wait(piece(k ^ 1, u), weight_at[u][4 + i], core)
    own_copy.wait()
    links.drain()


def begin(tokens, later, slots, small, kv, weight):
    count, cols, width = tokens.shape
    rows = kv.shape[0]
    f32, vmem = jnp.float32, pl.BlockSpec(memory_space=pltpu.VMEM)
    hbm = pl.BlockSpec(memory_space=pl.ANY)
    half = pltpu.VMEM((rows, width), f32)
    return pl.pallas_call(
        begin_kernel,
        out_shape=(
            jax.ShapeDtypeStruct((4 * count, cols // 4, width), f32),
            jax.ShapeDtypeStruct((4 * count, cols // 4, width), f32),
            jax.ShapeDtypeStruct((4,) + slots.shape, f32),
            jax.ShapeDtypeStruct(small.shape, f32),
            jax.ShapeDtypeStruct((4 * rows, 2 * width), f32),
            jax.ShapeDtypeStruct((8 * weight.shape[0], weight.shape[1]), f32),
        ),
        in_specs=[vmem] * 5 + [hbm],
        out_specs=[vmem] * 5 + [hbm],
        scratch_shapes=[
            pltpu.SemaphoreType.DMA,
            pltpu.VMEM(small.shape, f32), pltpu.VMEM(small.shape, f32),
            pltpu.VMEM((3,) + small.shape, f32), half, half, half, half, half,
            pltpu.SemaphoreType.DMA((48,)), pltpu.SemaphoreType.DMA((48,)),
        ],
        compiler_params=pltpu.CompilerParams(
            collective_id=2, has_side_effects=True, vmem_limit_bytes=36 << 20
        ),
        cost_estimate=LIGHT,
    )(tokens, later, slots, small, kv, weight)


UNITS = 6


def finish_kernel(
    first, attn, cross_q, cross_o, kv, tokens, small, caption, columns,
    first_out, attn_out, cross_q_out, cross_o_out, kv_out, tokens_out, small_out, caption_out,
    columns_out, columns_got, columns_sem,
    kept, theirs, by_x, by_y, from_x, from_y, along_z, across_z,
    small_sums, small_got, small_z, load_sems, credit, send_sems, recv_sems,
):
    me, z = lax.axis_index("patch"), lax.axis_index("frame")
    outer = (z == 0) | (z == 3)
    inner = (z == 1) | (z == 2)
    core, x, y = ({"patch": me ^ k} for k in (1, 2, 4))
    frames = [None] + [{"frame": z ^ k} for k in (1, 2, 3)]
    near, facing = frames[1], frames[3]
    chips = {2: x, 4: y, 6: {"patch": me ^ 6}}
    greet_all([core, x, y, chips[6]] + frames[1:])
    links = Links(send_sems, recv_sems)
    rows, width = by_x.shape[1] * 2, by_x.shape[2]
    upper, lower = pl.ds(0, rows // 2), pl.ds(rows // 2, rows // 2)
    count, part = tokens_out.shape[0], tokens_out.shape[1] // 4

    token_at = [None] + [links.plan() for _ in range(3)]

    def send_tokens(k):
        where = pl.ds(pl.multiple_of(z * part, part), part)
        if k == 0:
            tokens_out[:, where] = tokens[pl.ds(z * count, count)]
        else:
            source = tokens.at[pl.ds((z ^ k) * count, count)]
            links.send(source, tokens_out.at[:, where], token_at[k], frames[k])

    def frame_steps(value, result, near_got, facing_got):
        up, over, down = links.plan(), links.plan(), links.plan()

        def one():
            @pl.when(outer)
            def _():
                links.copy(value, near_got, up, near).start()

        def two():
            @pl.when(inner)
            def _():
                links.wait(near_got, up, near)
                near_got[...] = near_got[...] + value[...]
                links.copy(near_got, facing_got, over, facing).start()

        def three():
            @pl.when(inner)
            def _():
                links.wait(facing_got, over, facing)
                result[...] = near_got[...] + facing_got[...]
                links.copy(result, near_got, down, near).start()

        def four():
            @pl.when(outer)
            def _():
                links.wait(near_got, down, near)
                result[...] = near_got[...]
                links.copy(value, value, up, near).wait_send()

            @pl.when(inner)
            def _():
                links.copy(near_got, near_got, over, facing).wait_send()
                links.copy(result, result, down, near).wait_send()

        return one, two, three, four

    def piece(ref, u):
        return ref.at[:, pl.ds(u * width, width)]

    outs = [piece(first_out, u) for u in range(3)] + [attn_out, cross_q_out, cross_o_out]
    steps = [
        frame_steps(kept.at[u, 0], outs[u], along_z.at[u], across_z.at[u]) for u in range(UNITS)
    ] + [
        frame_steps(piece(kv, u), piece(kv_out, u), along_z.at[UNITS + u], across_z.at[UNITS + u])
        for u in range(2)
    ]
    small_steps = frame_steps(small_sums.at[2], small_out, small_z.at[0], small_z.at[1])

    core_at = [[links.plan() for _ in range(4)] for _ in range(UNITS)]
    link_at = [[links.plan() for _ in range(6)] for _ in range(UNITS)]

    def source(u, device, j):
        start = pl.multiple_of((device ^ (2 * j)) * rows, rows)
        ref = first if u < 3 else (attn, cross_q, cross_o)[u - 3]
        return ref.at[pl.ds(start, rows), pl.ds((u % 3) * width if u < 3 else 0, width)]

    def load(u, j):
        return pltpu.make_async_copy(source(u, me, j), kept.at[u, j], load_sems.at[u, j])

    def to_core(u):
        if u >= 2:
            pl.semaphore_wait(credit.at[u - 2], 1)
        for j in (3, 2, 1, 0):
            links.send(source(u, me ^ 1, j), theirs.at[u % 2, j], core_at[u][j], core)

    def add_cores(u, j):
        load(u, j).wait()
        links.wait(theirs.at[u % 2, j], core_at[u][j], core)
        kept[u, j] = kept[u, j] + theirs[u % 2, j]

    def stage_one(u):
        at = link_at[u]
        add_cores(u, 3)
        links.send(kept.at[u, 3, upper], by_x.at[u], at[0], x)
        links.send(kept.at[u, 3, lower], by_y.at[u], at[1], y)
        add_cores(u, 2)
        links.send(kept.at[u, 2, lower], from_y.at[u, lower], at[2], y)
        add_cores(u, 1)
        links.send(kept.at[u, 1, upper], from_x.at[u, upper], at[3], x)
        add_cores(u, 0)
        if u + 2 < UNITS:
            pl.semaphore_signal(
                credit.at[u], inc=1, device_id=core, device_id_type=pl.DeviceIdType.MESH
            )
            to_core(u + 2)

    def stage_two(u):
        at = link_at[u]
        links.wait(by_x.at[u], at[0], x)
        kept[u, 2, upper] = kept[u, 2, upper] + by_x[u]
        links.send(kept.at[u, 2, upper], from_y.at[u, upper], at[4], y)
        links.wait(by_y.at[u], at[1], y)
        kept[u, 1, lower] = kept[u, 1, lower] + by_y[u]
        links.send(kept.at[u, 1, lower], from_x.at[u, lower], at[5], x)

    def stage_three(u):
        at = link_at[u]
        links.wait(from_y.at[u, lower], at[2], y)
        links.wait(from_x.at[u, upper], at[3], x)
        links.wait(from_y.at[u, upper], at[4], y)
        links.wait(from_x.at[u, lower], at[5], x)
        kept[u, 0] = kept[u, 0] + from_x[u] + from_y[u]
        steps[u][0]()

    block = columns_got.shape[1] // 2
    columns_at = {k: links.plan() for k in (2, 4, 6)}
    columns_core = {k: links.plan() for k in (0, 2, 4, 6)}

    def chip_rows(k):
        return columns.at[pl.ds(pl.multiple_of((me ^ k) // 2 * (2 * block), 8), 2 * block)]

    own_rows = pltpu.make_async_copy(chip_rows(0), columns_got.at[0], columns_sem.at[0])

    def own_block(k):
        core_rows = pl.ds(pl.multiple_of(me % 2 * block, 8), block)
        return pltpu.make_async_copy(
            columns_got.at[k // 2, core_rows], columns_out.at[me ^ k], columns_sem.at[1 + k // 2]
        )

    def send_columns(k):
        links.send(chip_rows(k), columns_got.at[k // 2], columns_at[k], chips[k])

    def columns_over():
        other_rows = pl.ds(pl.multiple_of((1 - me % 2) * block, 8), block)
        own_rows.wait()
        for k in (0, 2, 4, 6):
            if k:
                links.wait(columns_got.at[k // 2], columns_at[k], chips[k])
            links.send(
                columns_got.at[k // 2, other_rows], columns_out.at[me ^ k], columns_core[k], core
            )
            own_block(k).start()

    def columns_end():
        for k in (0, 2, 4, 6):
            links.wait(columns_out.at[me ^ 1 ^ k], columns_core[k], core)
            own_block(k).wait()

    caption_at = [links.plan() for _ in range(10)]

    def caption_frames():
        caption_out[me, z] = caption[...]
        for k in (1, 2, 3):
            links.send(caption, caption_out.at[me, z], caption_at[k - 1], frames[k])

    def caption_x():
        for k in (1, 2, 3):
            links.wait(caption_out.at[me, z ^ k], caption_at[k - 1], frames[k])
        links.send(caption_out.at[me], caption_out.at[me], caption_at[3], x)

    def caption_y():
        links.wait(caption_out.at[me ^ 2], caption_at[3], x)
        for i, k in enumerate((0, 2)):
            links.send(caption_out.at[me ^ k], caption_out.at[me ^ k], caption_at[4 + i], y)

    def caption_core():
        for i, k in enumerate((0, 2)):
            links.wait(caption_out.at[me ^ 4 ^ k], caption_at[4 + i], y)
        for i, k in enumerate((0, 2, 4, 6)):
            links.send(caption_out.at[me ^ k], caption_out.at[me ^ k], caption_at[6 + i], core)

    def caption_end():
        for i, k in enumerate((0, 2, 4, 6)):
            links.wait(caption_out.at[me ^ 1 ^ k], caption_at[6 + i], core)

    small_at = [links.plan() for _ in range(3)]
    links.send(small, small_got.at[0], small_at[0], core)
    caption_frames()
    own_rows.start()
    for u in range(UNITS):
        for j in (3, 2, 1, 0):
            load(u, j).start()
    steps[6][0]()
    steps[7][0]()
    for u in range(2):
        to_core(u)
    links.wait(small_got.at[0], small_at[0], core)
    small_sums[0] = small[...] + small_got[0]
    links.send(small_sums.at[0], small_got.at[1], small_at[1], x)
    stage_one(0)
    links.wait(small_got.at[1], small_at[1], x)
    small_sums[1] = small_sums[0] + small_got[1]
    links.send(small_sums.at[1], small_got.at[2], small_at[2], y)
    stage_one(1)
    stage_two(0)
    links.wait(small_got.at[2], small_at[2], y)
    small_sums[2] = small_sums[1] + small_got[2]
    small_steps[0]()
    stage_one(2)
    steps[6][1]()
    steps[7][1]()
    send_tokens(0)
    send_tokens(1)
    stage_two(1)
    stage_three(0)
    stage_one(3)
    steps[6][2]()
    steps[7][2]()
    small_steps[1]()
    send_tokens(2)
    stage_two(2)
    stage_three(1)
    stage_one(4)
    steps[0][1]()
    small_steps[2]()
    send_tokens(3)
    stage_two(3)
    stage_three(2)
    stage_one(5)
    steps[1][1]()
    steps[0][2]()
    stage_two(4)
    stage_three(3)
    stage_two(5)
    caption_x()
    for k in (2, 4, 6):
        send_columns(k)
    steps[2][1]()
    steps[1][2]()
    stage_three(4)
    caption_y()
    steps[3][1]()
    steps[2][2]()
    stage_three(5)
    caption_core()
    steps[4][1]()
    steps[3][2]()
    steps[5][1]()
    steps[4][2]()
    steps[5][2]()
    for step in steps + [small_steps]:
        step[3]()
    columns_over()
    caption_end()
    columns_end()
    for k in (1, 2, 3):
        where = pl.ds(pl.multiple_of((z ^ k) * part, part), part)
        links.wait(tokens_out.at[:, where], token_at[k], frames[k])
    links.drain()


def finish(first, attn, cross_q, cross_o, kv, tokens, small, caption, columns):
    rows, width = first.shape[0] // 8, first.shape[1] // 3
    count, part = tokens.shape[0] // 4, tokens.shape[1]
    f32, vmem = jnp.float32, pl.BlockSpec(memory_space=pltpu.VMEM)
    hbm = pl.BlockSpec(memory_space=pl.ANY)

    def shape(*sizes):
        return jax.ShapeDtypeStruct(sizes, f32)

    return pl.pallas_call(
        finish_kernel,
        out_shape=(
            shape(rows, 3 * width), shape(rows, width), shape(rows, width), shape(rows, width),
            shape(rows, 2 * width), shape(count, 4 * part, tokens.shape[2]), shape(*small.shape),
            shape(8, 4, *caption.shape), shape(8, columns.shape[0] // 8, columns.shape[1]),
        ),
        in_specs=[hbm] * 4 + [vmem] * 4 + [hbm],
        out_specs=[vmem] * 8 + [hbm],
        scratch_shapes=[
            pltpu.VMEM((4, columns.shape[0] // 4, columns.shape[1]), f32),
            pltpu.SemaphoreType.DMA((5,)),
            pltpu.VMEM((UNITS, 4, rows, width), f32), pltpu.VMEM((2, 4, rows, width), f32),
            pltpu.VMEM((UNITS, rows // 2, width), f32), pltpu.VMEM((UNITS, rows // 2, width), f32),
            pltpu.VMEM((UNITS, rows, width), f32), pltpu.VMEM((UNITS, rows, width), f32),
            pltpu.VMEM((UNITS + 2, rows, width), f32), pltpu.VMEM((UNITS + 2, rows, width), f32),
            pltpu.VMEM((3,) + small.shape, f32), pltpu.VMEM((3,) + small.shape, f32),
            pltpu.VMEM((2,) + small.shape, f32),
            pltpu.SemaphoreType.DMA((UNITS, 4)), pltpu.SemaphoreType.REGULAR((4,)),
            pltpu.SemaphoreType.DMA((112,)), pltpu.SemaphoreType.DMA((112,)),
        ],
        compiler_params=pltpu.CompilerParams(
            collective_id=3, has_side_effects=True, vmem_limit_bytes=58 << 20
        ),
        cost_estimate=LIGHT,
    )(first, attn, cross_q, cross_o, kv, tokens, small, caption, columns)


def middle_kernel(
    parts, kv, residual, gate, bias,
    total, kv_out, block_out,
    block, kept, theirs, by_x, by_y, from_x, from_y,
    kv_half, kv_core, kv_got, kv_1, kv_2, kv_got_1, kv_got_2,
    load_sems, send_sems, recv_sems,
):
    me, z = lax.axis_index("patch"), lax.axis_index("frame")
    core, x, y = ({"patch": me ^ k} for k in (1, 2, 4))
    frames = [None] + [{"frame": z ^ k} for k in (1, 2, 3)]
    greet_all([core, x, y] + frames[1:])
    links = Links(send_sems, recv_sems)
    rows, width = kv_1.shape
    half = pl.multiple_of((me % 2) * width, 128)
    other = pl.multiple_of((1 - me % 2) * width, 128)
    mine, others = pl.ds(half, width), pl.ds(other, width)

    def share(ref, k):
        return ref.at[pl.ds(pl.multiple_of((z ^ k) * rows, rows), rows)]

    at_kv = links.plan()
    links.send(kv.at[:, others], kv_core, at_kv, core)
    core_at = [links.plan() for _ in range(4)]
    loads = [
        pltpu.make_async_copy(parts.at[me ^ (2 * j)], kept.at[j], load_sems.at[j])
        for j in range(4)
    ]
    for j in (3, 2, 1, 0):
        links.send(parts.at[me ^ 1 ^ (2 * j)], theirs.at[j], core_at[j], core)
        loads[j].start()
    links.wait(kv_core, at_kv, core)
    kv_half[...] = kv[:, mine] + kv_core[...]
    kv_at = [None] + [links.plan() for _ in range(3)]
    for k in (1, 2, 3):
        links.send(share(kv_half, k), kv_got.at[k - 1], kv_at[k], frames[k])

    count = total.shape[0] // 2
    upper, lower = pl.ds(0, count), pl.ds(count, count)
    at = [links.plan() for _ in range(6)]

    def add_cores(j):
        loads[j].wait()
        links.wait(theirs.at[j], core_at[j], core)
        kept[j] = kept[j] + theirs[j]

    add_cores(3)
    links.send(kept.at[3, upper], by_x, at[0], x)
    links.send(kept.at[3, lower], by_y, at[1], y)
    add_cores(2)
    links.send(kept.at[2, lower], from_y.at[lower], at[2], y)
    add_cores(1)
    links.send(kept.at[1, upper], from_x.at[upper], at[3], x)
    add_cores(0)
    links.wait(by_x, at[0], x)
    kept[2, upper] = kept[2, upper] + by_x[...]
    links.send(kept.at[2, upper], from_y.at[upper], at[4], y)
    links.wait(by_y, at[1], y)
    kept[1, lower] = kept[1, lower] + by_y[...]
    links.send(kept.at[1, lower], from_x.at[lower], at[5], x)

    for k in (1, 2, 3):
        links.wait(kv_got.at[k - 1], kv_at[k], frames[k])
    kv_1[...] = share(kv_half, 0)[...] + kv_got[0] + (kv_got[1] + kv_got[2])
    top, bottom = pl.ds(0, 64), pl.ds(64, rows - 64)
    at_u, at_l = links.plan(), links.plan()
    links.send(kv_1.at[top], kv_got_1.at[top], at_u, x)
    links.send(kv_1.at[bottom], kv_got_1.at[bottom], at_l, y)
    links.wait(from_y.at[lower], at[2], y)
    links.wait(from_x.at[upper], at[3], x)
    links.wait(from_y.at[upper], at[4], y)
    links.wait(from_x.at[lower], at[5], x)
    total[...] = kept[0] + from_x[...] + from_y[...]
    slots, part = residual.shape[0] // 4, residual.shape[1]
    block[...] = residual[...] + gate[...] * (total[...] + bias[...]).reshape(residual.shape)
    block_at = [None] + [links.plan() for _ in range(3)]
    place = pl.ds(pl.multiple_of(z * part, part), part)
    for k in (1, 2, 3):
        source = block.at[pl.ds((z ^ k) * slots, slots)]
        links.send(source, block_out.at[:, place], block_at[k], frames[k])
    block_out[:, place] = block[pl.ds(z * slots, slots)]
    links.wait(kv_got_1.at[top], at_u, x)
    links.wait(kv_got_1.at[bottom], at_l, y)
    kv_2[...] = kv_1[...] + kv_got_1[...]
    at_u, at_l = links.plan(), links.plan()
    links.send(kv_2.at[top], kv_got_2.at[top], at_u, y)
    links.send(kv_2.at[bottom], kv_got_2.at[bottom], at_l, x)
    links.wait(kv_got_2.at[top], at_u, y)
    links.wait(kv_got_2.at[bottom], at_l, x)
    kv_out[:, mine] = kv_2[...] + kv_got_2[...]
    at_core = links.plan()
    links.send(kv_out.at[:, mine], kv_out.at[:, mine], at_core, core)
    links.wait(kv_out.at[:, others], at_core, core)
    for k in (1, 2, 3):
        there = pl.ds(pl.multiple_of((z ^ k) * part, part), part)
        links.wait(block_out.at[:, there], block_at[k], frames[k])
    links.drain()


def middle(parts, kv, residual, gate, bias):
    slots, cols, _ = residual.shape
    length, width = parts.shape[0] // 8, parts.shape[1]
    rows = kv.shape[0] // 4
    f32, vmem = jnp.float32, pl.BlockSpec(memory_space=pltpu.VMEM)
    block, half = (length, width), pltpu.VMEM((rows, width), f32)
    return pl.pallas_call(
        middle_kernel,
        out_shape=(
            jax.ShapeDtypeStruct(block, f32), jax.ShapeDtypeStruct((rows, 2 * width), f32),
            jax.ShapeDtypeStruct((slots // 4, 4 * cols, width), f32),
        ),
        in_specs=[pl.BlockSpec(memory_space=pl.ANY)] + [vmem] * 4,
        out_specs=[vmem] * 3,
        scratch_shapes=[
            pltpu.VMEM((slots, cols, width), f32),
            pltpu.VMEM((4,) + block, f32), pltpu.VMEM((4,) + block, f32),
            pltpu.VMEM((length // 2, width), f32), pltpu.VMEM((length // 2, width), f32),
            pltpu.VMEM(block, f32), pltpu.VMEM(block, f32),
            pltpu.VMEM((4 * rows, width), f32), pltpu.VMEM((4 * rows, width), f32),
            pltpu.VMEM((3, rows, width), f32), half, half, half, half,
            pltpu.SemaphoreType.DMA((4,)), pltpu.SemaphoreType.DMA((24,)),
            pltpu.SemaphoreType.DMA((24,)),
        ],
        compiler_params=pltpu.CompilerParams(
            collective_id=4, has_side_effects=True, vmem_limit_bytes=48 << 20
        ),
        cost_estimate=LIGHT,
    )(parts.reshape((8,) + block), kv, residual, gate[None], bias[None])


def spread_kernel(block, whole, send_sems, recv_sems):
    me = lax.axis_index("patch")
    peers = [None] + [{"patch": me ^ k} for k in range(1, 8)]
    greet_all(peers[1:])
    links = Links(send_sems, recv_sems)
    at = [links.plan() for _ in range(8)]
    for k in range(1, 8):
        links.send(block, whole.at[me], at[k], peers[k])
    whole[me] = block[...]
    for k in range(1, 8):
        links.wait(whole.at[me ^ k], at[k], peers[k])
    links.drain()


def spread(block):
    vmem = pl.BlockSpec(memory_space=pltpu.VMEM)
    return pl.pallas_call(
        spread_kernel,
        out_shape=jax.ShapeDtypeStruct((8,) + block.shape, jnp.float32),
        in_specs=[vmem],
        out_specs=vmem,
        scratch_shapes=[pltpu.SemaphoreType.DMA((8,)), pltpu.SemaphoreType.DMA((8,))],
        compiler_params=pltpu.CompilerParams(collective_id=5, has_side_effects=True),
    )(block)


def halves(x):
    high = x.astype(jnp.bfloat16)
    return high, (x - high.astype(jnp.float32)).astype(jnp.bfloat16)


NN, NT, TN = (((1,), (0,)), ((), ())), (((1,), (1,)), ((), ())), (((0,), (0,)), ((), ()))


def three(left, right, dims):
    def dot(a, b):
        return lax.dot_general(a, b, dims, preferred_element_type=jnp.float32)

    return dot(left[0], right[0]) + (dot(left[0], right[1]) + dot(left[1], right[0]))


WINDOW = 256


def head_window(head, head_dim, width):
    start = jnp.minimum(head * head_dim // 128 * 128, width - WINDOW)
    lane = lax.broadcasted_iota(jnp.int32, (1, WINDOW), 1) - (head * head_dim - start)
    mask = ((lane >= 0) & (lane < head_dim)).astype(jnp.float32)
    return pl.ds(pl.multiple_of(start, 128), WINDOW), mask


def softmax_last(scores):
    exponent = jnp.exp(scores - jnp.max(scores, axis=-1, keepdims=True))
    return exponent / jnp.sum(exponent, axis=-1, keepdims=True)


GROUP = 8


def grouped(ref, group, lanes):
    slots = ref.shape[0]
    value = ref[:, group * GROUP : (group + 1) * GROUP, lanes]
    return value.reshape(slots * GROUP, value.shape[-1])


def store_halves(high, low, index, value):
    high[index], low[index] = halves(value)


def frame_attention_kernel(qkv, b_query, b_value, distance, allowed, probs, out, *split):
    (q_high, q_low, k_high, k_low, v_high, v_low), total = split[:6], split[6]
    slots, width = qkv.shape[0], out.shape[-1]
    head_dim = width // H
    scaling = head_dim**-0.5
    for g in range(2):
        store_halves(q_high, q_low, g, grouped(qkv, g, slice(0, width)) + b_query[...])
        store_halves(k_high, k_low, g, grouped(qkv, g, slice(width, 2 * width)))
        store_halves(
            v_high, v_low, g, grouped(qkv, g, slice(2 * width, 3 * width)) + b_value[...]
        )
    total[...] = jnp.zeros(total.shape, jnp.float32)

    def step(head, _):
        at, mask = head_window(head, head_dim, width)
        mask = mask.astype(jnp.bfloat16)
        slope = jnp.exp2(-8.0 / H * (jnp.full((1, 1), head, jnp.int32).astype(jnp.float32) + 1.0))
        for g in range(2):
            query = (q_high[g, :, at] * mask, q_low[g, :, at] * mask)
            scores = three(query, (k_high[g, :, at], k_low[g, :, at]), NT)
            scores = jnp.where(allowed[...] > 0, scores * scaling - slope * distance[...], -1e30)
            prob = softmax_last(scores)
            probs[head, g] = prob
            value = (v_high[g, :, at] * mask, v_low[g, :, at] * mask)
            total[g, :, at] = total[g, :, at] + three(halves(prob), value, NN)
        return 0

    lax.fori_loop(0, H, step, 0, unroll=4)
    for g in range(2):
        out[:, g * GROUP : (g + 1) * GROUP, :] = total[g].reshape(slots, GROUP, width)


def frame_tables(frame_pos):
    slots = frame_pos.shape[0]
    position = jnp.repeat(frame_pos, GROUP)
    column = jnp.tile(jnp.arange(GROUP), slots)
    distance = jnp.abs(position[:, None] - position[None, :])
    same = column[:, None] == column[None, :]
    return distance, (same & (position[None, :] < FRAMES - 0.5)).astype(jnp.float32)


VMEM_SPEC = pl.BlockSpec(memory_space=pltpu.VMEM)


def frame_attention(qkv, b_query, b_value, distance, allowed):
    slots, cols, width = qkv.shape[0], qkv.shape[1], qkv.shape[2] // 3
    rows = slots * GROUP
    part = pltpu.VMEM((2, rows, width), jnp.bfloat16)
    return pl.pallas_call(
        frame_attention_kernel,
        out_shape=(
            jax.ShapeDtypeStruct((H, 2, rows, rows), jnp.float32),
            jax.ShapeDtypeStruct((slots, cols, width), jnp.float32),
        ),
        in_specs=[VMEM_SPEC] * 5,
        out_specs=[VMEM_SPEC] * 2,
        scratch_shapes=[part] * 6 + [pltpu.VMEM((2, rows, width), jnp.float32)],
        compiler_params=pltpu.CompilerParams(vmem_limit_bytes=40 << 20),
        cost_estimate=LIGHT,
    )(qkv, b_query.reshape(1, width), b_value.reshape(1, width), distance, allowed)


def frame_attention_back_kernel(qkv, b_query, b_value, probs, attended, grad, out, *split):
    width = attended.shape[-1]
    slots, head_dim = qkv.shape[0], width // H
    scaling = head_dim**-0.5
    names = [(split[2 * i], split[2 * i + 1]) for i in range(4)]
    (q_high, q_low), (k_high, k_low), (v_high, v_low), (g_high, g_low) = names
    total, product = split[8], split[9]
    for g in range(2):
        store_halves(q_high, q_low, g, grouped(qkv, g, slice(0, width)) + b_query[...])
        store_halves(k_high, k_low, g, grouped(qkv, g, slice(width, 2 * width)))
        store_halves(
            v_high, v_low, g, grouped(qkv, g, slice(2 * width, 3 * width)) + b_value[...]
        )
        upstream = grouped(grad, g, slice(0, width))
        store_halves(g_high, g_low, g, upstream)
        product[g] = upstream * grouped(attended, g, slice(0, width))
    total[...] = jnp.zeros(total.shape, jnp.float32)

    def step(head, _):
        at, mask = head_window(head, head_dim, width)
        small = mask.astype(jnp.bfloat16)

        def masked(high, low, g):
            return high[g, :, at] * small, low[g, :, at] * small

        for g in range(2):
            upstream = masked(g_high, g_low, g)
            prob = probs[head, g]
            grad_prob = three(upstream, (v_high[g, :, at], v_low[g, :, at]), NT)
            term = jnp.sum(product[g, :, at] * mask, axis=-1, keepdims=True)
            score = halves(prob * (grad_prob - term) * scaling)
            total[0, g, :, at] = total[0, g, :, at] + three(score, masked(k_high, k_low, g), NN)
            total[1, g, :, at] = total[1, g, :, at] + three(score, masked(q_high, q_low, g), TN)
            total[2, g, :, at] = total[2, g, :, at] + three(halves(prob), upstream, TN)
        return 0

    lax.fori_loop(0, H, step, 0, unroll=4)
    for g in range(2):
        for i in range(3):
            out[:, g * GROUP : (g + 1) * GROUP, i * width : (i + 1) * width] = total[
                i, g
            ].reshape(slots, GROUP, width)


def frame_attention_back(qkv, b_query, b_value, probs, attended, grad):
    slots, cols, width = attended.shape
    rows = slots * GROUP
    part = pltpu.VMEM((2, rows, width), jnp.bfloat16)
    return pl.pallas_call(
        frame_attention_back_kernel,
        out_shape=jax.ShapeDtypeStruct((slots, cols, 3 * width), jnp.float32),
        in_specs=[VMEM_SPEC] * 6,
        out_specs=VMEM_SPEC,
        scratch_shapes=[part] * 8
        + [pltpu.VMEM((3, 2, rows, width), jnp.float32), pltpu.VMEM((2, rows, width), jnp.float32)],
        compiler_params=pltpu.CompilerParams(vmem_limit_bytes=48 << 20),
        cost_estimate=LIGHT,
    )(qkv, b_query.reshape(1, width), b_value.reshape(1, width), probs, attended, grad)


def cross_attention_kernel(queries, b_query, kv, b_value, allowed, probs, out, *split):
    q_high, q_low, k_high, k_low, v_high, v_low = split
    width = out.shape[-1]
    head_dim = width // H
    scaling = head_dim**-0.5
    store_halves(q_high, q_low, Ellipsis, queries[...] + b_query[...])
    store_halves(k_high, k_low, Ellipsis, kv[:, 0:width])
    store_halves(v_high, v_low, Ellipsis, kv[:, width : 2 * width] + b_value[...])
    out[...] = jnp.zeros(out.shape, jnp.float32)

    def step(head, _):
        at, mask = head_window(head, head_dim, width)
        mask = mask.astype(jnp.bfloat16)
        query = (q_high[:, at] * mask, q_low[:, at] * mask)
        scores = three(query, (k_high[:, at], k_low[:, at]), NT)
        prob = softmax_last(jnp.where(allowed[...] > 0, scores * scaling, -1e30))
        probs[head] = prob
        value = (v_high[:, at] * mask, v_low[:, at] * mask)
        out[:, at] = out[:, at] + three(halves(prob), value, NN)
        return 0

    lax.fori_loop(0, H, step, 0, unroll=4)


def cross_attention(queries, b_query, kv, b_value, allowed):
    rows, width = queries.shape
    keys = kv.shape[0]
    q_part = pltpu.VMEM((rows, width), jnp.bfloat16)
    k_part = pltpu.VMEM((keys, width), jnp.bfloat16)
    return pl.pallas_call(
        cross_attention_kernel,
        out_shape=(
            jax.ShapeDtypeStruct((H, rows, keys), jnp.float32),
            jax.ShapeDtypeStruct((rows, width), jnp.float32),
        ),
        in_specs=[VMEM_SPEC] * 5,
        out_specs=[VMEM_SPEC] * 2,
        scratch_shapes=[q_part] * 2 + [k_part] * 4,
        compiler_params=pltpu.CompilerParams(vmem_limit_bytes=48 << 20),
        cost_estimate=LIGHT,
    )(queries, b_query.reshape(1, width), kv, b_value.reshape(1, width), allowed)


def cross_attention_back_kernel(
    queries, b_query, kv, b_value, probs, attended, grad, grad_q, grad_kv, *split
):
    names = [(split[2 * i], split[2 * i + 1]) for i in range(4)]
    (q_high, q_low), (g_high, g_low), (k_high, k_low), (v_high, v_low) = names
    product = split[8]
    width = grad_q.shape[-1]
    head_dim = width // H
    scaling = head_dim**-0.5
    store_halves(q_high, q_low, Ellipsis, queries[...] + b_query[...])
    store_halves(k_high, k_low, Ellipsis, kv[:, 0:width])
    store_halves(v_high, v_low, Ellipsis, kv[:, width : 2 * width] + b_value[...])
    store_halves(g_high, g_low, Ellipsis, grad[...])
    product[...] = grad[...] * attended[...]
    grad_q[...] = jnp.zeros(grad_q.shape, jnp.float32)
    grad_kv[...] = jnp.zeros(grad_kv.shape, jnp.float32)

    def step(head, _):
        at, mask = head_window(head, head_dim, width)
        start = jnp.minimum(head * head_dim // 128 * 128, width - WINDOW)
        at_value = pl.ds(pl.multiple_of(start + width, 128), WINDOW)
        small = mask.astype(jnp.bfloat16)

        def masked(high, low):
            return high[:, at] * small, low[:, at] * small

        upstream = masked(g_high, g_low)
        prob = probs[head]
        grad_prob = three(upstream, (v_high[:, at], v_low[:, at]), NT)
        term = jnp.sum(product[:, at] * mask, axis=-1, keepdims=True)
        score = halves(prob * (grad_prob - term) * scaling)
        grad_q[:, at] = grad_q[:, at] + three(score, masked(k_high, k_low), NN)
        grad_kv[:, at] = grad_kv[:, at] + three(score, masked(q_high, q_low), TN)
        grad_kv[:, at_value] = grad_kv[:, at_value] + three(halves(prob), upstream, TN)
        return 0

    lax.fori_loop(0, H, step, 0, unroll=4)


def cross_attention_back(queries, b_query, kv, b_value, probs, attended, grad):
    rows, width = queries.shape
    keys = kv.shape[0]
    q_part = pltpu.VMEM((rows, width), jnp.bfloat16)
    k_part = pltpu.VMEM((keys, width), jnp.bfloat16)
    return pl.pallas_call(
        cross_attention_back_kernel,
        out_shape=(
            jax.ShapeDtypeStruct((rows, width), jnp.float32),
            jax.ShapeDtypeStruct(kv.shape, jnp.float32),
        ),
        in_specs=[VMEM_SPEC] * 7,
        out_specs=[VMEM_SPEC] * 2,
        scratch_shapes=[q_part] * 4 + [k_part] * 4 + [pltpu.VMEM((rows, width), jnp.float32)],
        compiler_params=pltpu.CompilerParams(vmem_limit_bytes=52 << 20),
        cost_estimate=LIGHT,
    )(queries, b_query.reshape(1, width), kv, b_value.reshape(1, width), probs, attended, grad)


MLP_ROWS = 256


def mlp_kernel(
    hidden, cotangent, w_first, b_first, w_second,
    grad_hidden, out, grad_first, grad_second, grad_bias,
    first_high, first_low, second_high, second_low,
):
    @pl.when(pl.program_id(0) == 0)
    def _():
        first_high[...], first_low[...] = halves(w_first[...])
        second_high[...], second_low[...] = halves(w_second[...])
        grad_first[...] = jnp.zeros(grad_first.shape, jnp.float32)
        grad_second[...] = jnp.zeros(grad_second.shape, jnp.float32)
        grad_bias[...] = jnp.zeros(grad_bias.shape, jnp.float32)

    first = (first_high[...], first_low[...])
    second = (second_high[...], second_low[...])
    tokens, upstream = halves(hidden[...]), halves(cotangent[...])
    u = three(tokens, first, NN) + b_first[...]
    slope = math.sqrt(2.0 / math.pi)
    t = jnp.tanh(slope * (u + 0.044715 * (u * u * u)))
    active = halves(0.5 * u * (1.0 + t))
    derivative = 0.5 * (1.0 + t) + 0.5 * u * (1.0 - t * t) * slope * (1.0 + 0.134145 * (u * u))
    grad_pre = three(upstream, second, NT) * derivative
    grad_bias[...] = grad_bias[...] + jnp.sum(grad_pre, axis=0, keepdims=True)
    grad_pre = halves(grad_pre)
    grad_hidden[...] = three(grad_pre, first, NT)
    out[...] = three(active, second, NN)
    grad_first[...] = grad_first[...] + three(tokens, grad_pre, TN)
    grad_second[...] = grad_second[...] + three(active, upstream, TN)


def mlp(hidden, cotangent, w_first, b_first, w_second):
    rows, width = hidden.shape
    units = w_first.shape[1]
    f32 = jnp.float32
    tile = pl.BlockSpec((MLP_ROWS, width), lambda i: (i, 0))

    def fixed(*shape):
        return pl.BlockSpec(shape, lambda i: (0, 0))

    return pl.pallas_call(
        mlp_kernel,
        grid=(rows // MLP_ROWS,),
        out_shape=(
            jax.ShapeDtypeStruct((rows, width), f32), jax.ShapeDtypeStruct((rows, width), f32),
            jax.ShapeDtypeStruct((width, units), f32), jax.ShapeDtypeStruct((units, width), f32),
            jax.ShapeDtypeStruct((1, units), f32),
        ),
        in_specs=[tile, tile, fixed(width, units), fixed(1, units), fixed(units, width)],
        out_specs=[tile, tile, fixed(width, units), fixed(units, width), fixed(1, units)],
        scratch_shapes=[
            pltpu.VMEM((width, units), jnp.bfloat16), pltpu.VMEM((width, units), jnp.bfloat16),
            pltpu.VMEM((units, width), jnp.bfloat16), pltpu.VMEM((units, width), jnp.bfloat16),
        ],
        compiler_params=pltpu.CompilerParams(vmem_limit_bytes=50 << 20),
        cost_estimate=LIGHT,
    )(hidden, cotangent, w_first, b_first.reshape(1, units), w_second)


def assemble_kernel(axis, dim, *refs):
    blocks, whole = refs[:-1], refs[-1]
    own = lax.axis_index(axis)
    for k, block in enumerate(blocks):
        length = block.shape[dim]
        start = pl.multiple_of((own ^ k) * length, length)
        where = (slice(None),) * dim + (pl.ds(start, length),)
        whole[where] = block[...]


def assemble(blocks, axis, dim):
    shape = list(blocks[0].shape)
    shape[dim] *= len(blocks)
    size = 4 * len(blocks) * blocks[0].size
    return pl.pallas_call(
        partial(assemble_kernel, axis, dim),
        out_shape=jax.ShapeDtypeStruct(tuple(shape), jnp.float32),
        in_specs=[pl.BlockSpec(memory_space=pltpu.VMEM)] * len(blocks),
        out_specs=pl.BlockSpec(memory_space=pltpu.VMEM),
        compiler_params=pltpu.CompilerParams(vmem_limit_bytes=24 << 20),
        cost_estimate=LIGHT,
    )(*blocks)


def gather_rows(shard):
    return lax.all_gather(shard, "patch", axis=0, tiled=True)


def scatter_rows(whole):
    return lax.psum_scatter(whole, "patch", scatter_dimension=0, tiled=True)


def gather_tokens(rows):
    return token_gather(rows) if small_patch() else gather_rows(rows)


def block_of(array, axis_name, k, dim):
    length = array.shape[dim] // lax.axis_size(axis_name)
    start = (lax.axis_index(axis_name) ^ k) * length
    return lax.dynamic_slice_in_dim(array, start, length, axis=dim)


def over_chips(blocks):
    return [
        blocks[0],
        swap(blocks[1], "patch", 2),
        swap(blocks[2], "patch", 4),
        swap(blocks[3], "patch", 6),
    ]


def to_own_columns(weight):
    if not small_patch():
        return lax.all_to_all(weight, "patch", 1, 0, tiled=True)
    length = weight.shape[0]
    blocks = [block_of(weight, "patch", k, 1) for k in range(8)]
    theirs = swap(jnp.concatenate(blocks[1::2], axis=0), "patch", 1)
    both = [
        jnp.concatenate([kept, theirs[j * length : (j + 1) * length]], axis=0)
        for j, kept in enumerate(blocks[::2])
    ]
    halves = []
    for block in over_chips(both):
        halves += [block[:length], block[length:]]
    return assemble(halves, "patch", 0)


def to_columns(x):
    return lax.all_to_all(x, "frame", split_axis=1, concat_axis=0, tiled=True)


def to_slots(x):
    return lax.all_to_all(x, "frame", split_axis=0, concat_axis=1, tiled=True)


def scatter_tokens(parts):
    return token_scatter(parts) if small_patch() else scatter_rows(parts)


def open_up(block_input, cotangent, frame_slot, small, kv_part, weight):
    frame_number = frame_slot.astype(jnp.float32)
    if not small_patch():
        kv = all_sum(kv_part, "patch")
        return (
            to_columns(block_input),
            to_columns(cotangent),
            all_sum(placed(frame_number, "frame"), "frame"),
            all_sum(small, "patch"),
            lax.all_gather(kv, "frame", axis=0, tiled=True),
            gather_rows(weight),
        )
    count = frame_slot.shape[0]
    rows = -(-small.shape[0] // 1024) * 8
    tokens, later, slots, summed, kv, whole = begin(
        block_input, cotangent, padded(frame_number, 8), padded(small, rows), kv_part, weight
    )
    summed = summed.reshape(-1)[: small.shape[0]]
    slots = slots[:, 0, :count].reshape(-1)
    return tokens, later, slots, summed, kv, whole


def mlp_part(hidden, cotangent, w_first, b_first, w_second):
    if small_patch():
        *parts, grad_bias = mlp(hidden, cotangent, w_first, b_first, w_second)
        return (*parts, grad_bias[0])
    pre = matmul(hidden, w_first) + b_first
    active, pull = jax.vjp(partial(jax.nn.gelu, approximate=True), pre)
    grad_pre = pull(matmul_nt(cotangent, w_second))[0]
    return (
        matmul_nt(grad_pre, w_first),
        matmul(active, w_second),
        matmul_tn(hidden, grad_pre),
        matmul_tn(active, cotangent),
        jnp.sum(grad_pre, axis=0),
    )


def mid_way(parts, kv, residual, gate, bias):
    if not small_patch():
        kv = lax.psum_scatter(all_sum(kv, "patch"), "frame", scatter_dimension=0, tiled=True)
        total = scatter_rows(parts)
        block = residual + gate * (total + bias).reshape(residual.shape)
        return total, kv, to_slots(block)
    return middle(parts, kv, residual, gate, bias)


def close_up(weights, kv, tokens, small, caption, columns):
    clips, length = lax.axis_size("frame"), caption.shape[1]
    if not small_patch():
        weights = [lax.psum(scatter_rows(w), "frame") for w in weights]
        whole = lax.all_gather(caption, "patch", axis=0, tiled=True)
        whole = lax.all_gather(whole, "frame", axis=0)
        whole = jnp.transpose(whole, (0, 2, 1))
        small = all_sum(all_sum(small, "patch"), "frame")
        columns = lax.all_to_all(columns, "patch", 0, 1, tiled=True)
        return weights, lax.psum(kv, "frame"), to_slots(tokens), small, whole, columns
    rows = -(-small.shape[0] // 1024) * 8
    *weights, kv, tokens, summed, whole, blocks = finish(
        *weights, kv, tokens, padded(small, rows), caption, columns
    )
    columns = jnp.transpose(blocks, (1, 0, 2)).reshape(blocks.shape[1], -1)
    whole = jnp.transpose(whole, (1, 3, 0, 2)).reshape(clips, length, -1)
    return weights, kv, tokens, summed.reshape(-1)[: small.shape[0]], whole, columns


def on_device(
    block_input,
    out_cotangent,
    caption,
    cond,
    ada_weight,
    ada_bias,
    qkv_weight,
    q_bias,
    v_bias,
    attn_out_weight,
    attn_out_bias,
    cross_q_weight,
    cross_q_bias,
    cross_kv_weight,
    cross_v_bias,
    cross_out_weight,
    cross_out_bias,
    fc1_weight,
    fc1_bias,
    fc2_weight,
    fc2_bias,
    frame_slot,
    clip_id,
    patch_mask,
    caption_mask,
):
    width = block_input.shape[-1]
    cond_act, silu_pull = jax.vjp(jax.nn.silu, cond)
    cond_own = own_part(cond_act, "patch", 1)
    modulation_part = matmul(cond_own, ada_weight)
    biases = (
        ada_bias, q_bias, v_bias, attn_out_bias, cross_q_bias, cross_v_bias, cross_out_bias,
        fc2_bias,
    )
    small = jnp.concatenate(
        [modulation_part.reshape(-1)] + [placed(b, "patch") for b in biases]
    )
    caption_rows = caption.reshape(CLIPS * CAP, width)
    caption_share = own_part(own_part(caption_rows, "frame", 0), "patch", 1)
    tokens_in, cotangent, frame_pos, small, caption_kv, w_qkv = open_up(
        block_input,
        out_cotangent,
        frame_slot,
        small,
        matmul(caption_share, cross_kv_weight),
        qkv_weight,
    )
    w_two = gather_rows(jnp.concatenate([attn_out_weight, cross_q_weight], axis=1))
    w_attn, w_cross_q = jnp.split(w_two, 2, axis=1)
    w_cross_o = gather_rows(cross_out_weight)
    slots, cols, _ = tokens_in.shape
    rows = slots * cols
    clip_own = own_part(clip_id, "frame", 0)
    column_mask = own_part(patch_mask, "frame", 0).astype(jnp.float32)[:, None]
    place = modulation_part.size
    modulation = small[:place].reshape(modulation_part.shape)
    whole = []
    for b in biases:
        length = b.shape[0] * lax.axis_size("patch")
        whole.append(small[place : place + length])
        place += length
    b_ada, b_query, b_value, b_attn, b_cross_q, b_cross_v, b_cross_o, b_second = whole
    modulation = modulation + b_ada
    clip_onehot = (clip_own[:, None] == jnp.arange(CLIPS, dtype=jnp.int32)[None, :]).astype(
        jnp.float32
    )
    per_column = jnp.dot(clip_onehot, modulation, precision=lax.Precision.HIGHEST)
    shift_one, scale_one, gate_one, shift_two, scale_two, gate_two = jnp.split(
        per_column, 6, axis=1
    )

    grad_mlp = (column_mask * gate_two * cotangent).reshape(rows, width)
    normed_one, inverse_one = normalize(tokens_in)
    hidden_one = (normed_one * (1.0 + scale_one) + shift_one).reshape(rows, width)
    qkv_rows = matmul(hidden_one, w_qkv)
    grad_mlp_all = gather_rows(after(grad_mlp, qkv_rows))
    qkv = qkv_rows.reshape(slots, cols, 3 * width)
    probs, attended = frame_attention(qkv, b_query, b_value, *frame_tables(frame_pos))
    attended_rows = attended.reshape(rows, width)
    attn_branch = (matmul(attended_rows, w_attn) + b_attn).reshape(slots, cols, width)
    after_attn = tokens_in + column_mask * gate_one * attn_branch
    after_attn_rows = after_attn.reshape(rows, width)
    cross_queries = matmul(after_attn_rows, w_cross_q)
    w_first = to_own_columns(after(fc1_weight, cross_queries))
    cross_queries = after(cross_queries, grad_mlp_all)
    key_clip = jnp.arange(CLIPS * CAP, dtype=jnp.int32) // CAP
    caption_ok = (clip_own[:, None] == key_clip[None, :]) & (
        caption_mask.reshape(CLIPS * CAP)[None, :] > 0
    )
    caption_ok = jnp.tile(caption_ok.astype(jnp.float32), (slots, 1))
    cross_probs, cross_rows = cross_attention(
        cross_queries, b_cross_q, caption_kv, b_cross_v, caption_ok
    )
    cross_branch = (matmul(cross_rows, w_cross_o) + b_cross_o).reshape(slots, cols, width)
    after_cross = after_attn + column_mask * cross_branch
    normed_two, inverse_two = normalize(after_cross)
    hidden_two = (normed_two * (1.0 + scale_two) + shift_two).reshape(rows, width)

    hidden_all = gather_tokens(after(hidden_two, w_first))
    grad_parts, mlp_parts, grad_w_first, grad_w_second, grad_b_first = mlp_part(
        hidden_all, grad_mlp_all, w_first, fc1_bias, fc2_weight
    )
    grad_hidden_two = scatter_tokens(grad_parts)
    grad_hidden_two = grad_hidden_two.reshape(slots, cols, width)
    grad_b_second = jnp.sum(grad_mlp, axis=0)

    grad_shift_two = jnp.sum(grad_hidden_two, axis=0)
    grad_scale_two = jnp.sum(grad_hidden_two * normed_two, axis=0)
    grad_after_cross = cotangent + normalize_back(
        grad_hidden_two * (1.0 + scale_two), normed_two, inverse_two
    )
    grad_cross_branch = (column_mask * grad_after_cross).reshape(rows, width)
    grad_w_cross_o = matmul_tn(cross_rows, grad_cross_branch)
    grad_b_cross_o = jnp.sum(grad_cross_branch, axis=0)
    grad_w_first = lax.psum(grad_w_first, "frame")
    grad_w_second = lax.psum(after(grad_w_second, grad_w_first), "frame")
    grad_cross_rows = matmul_nt(grad_cross_branch, w_cross_o)
    grad_cross_queries, grad_kv = cross_attention_back(
        cross_queries, b_cross_q, caption_kv, b_cross_v, cross_probs, cross_rows, grad_cross_rows
    )
    grad_cross_queries = after(grad_cross_queries, grad_w_first)
    grad_w_cross_q = matmul_tn(after_attn_rows, grad_cross_queries)
    grad_b_cross_q = jnp.sum(grad_cross_queries, axis=0)
    grad_cross_queries = after(grad_cross_queries, grad_w_cross_q)
    grad_after_attn = grad_after_cross + matmul_nt(grad_cross_queries, w_cross_q).reshape(
        slots, cols, width
    )
    grad_attn_rows = (column_mask * gate_one * grad_after_attn).reshape(rows, width)
    grad_gate_one = jnp.sum(column_mask * attn_branch * grad_after_attn, axis=0)
    grad_w_attn = matmul_tn(attended_rows, grad_attn_rows)
    grad_b_attn = jnp.sum(grad_attn_rows, axis=0)
    grad_attn_rows = after(grad_attn_rows, grad_w_attn)
    grad_attended = matmul_nt(grad_attn_rows, w_attn).reshape(slots, cols, width)
    grad_qkv = frame_attention_back(
        qkv, b_query, b_value, probs, attended, grad_attended
    ).reshape(rows, 3 * width)
    grad_w_qkv = matmul_tn(hidden_one, grad_qkv)
    mlp_sum, grad_kv_share, block_out = mid_way(
        after(mlp_parts, grad_w_qkv), grad_kv, after_cross, column_mask * gate_two, b_second
    )
    grad_w_cross_kv = matmul_tn(caption_share, grad_kv_share)
    grad_b_cross_v = jnp.sum(grad_kv_share[:, width:], axis=0)
    grad_caption_share = matmul_nt(cross_kv_weight, grad_kv_share)
    mlp_branch = (mlp_sum + b_second).reshape(slots, cols, width)
    grad_gate_two = jnp.sum(column_mask * mlp_branch * cotangent, axis=0)
    grad_b_query = jnp.sum(grad_qkv[:, :width], axis=0)
    grad_b_value = jnp.sum(grad_qkv[:, 2 * width :], axis=0)
    grad_hidden_one = matmul_nt(grad_qkv, w_qkv).reshape(slots, cols, width)
    grad_shift_one = jnp.sum(grad_hidden_one, axis=0)
    grad_scale_one = jnp.sum(grad_hidden_one * normed_one, axis=0)
    input_grad = grad_after_attn + normalize_back(
        grad_hidden_one * (1.0 + scale_one), normed_one, inverse_one
    )
    grad_per_column = jnp.concatenate(
        [
            grad_shift_one,
            grad_scale_one,
            grad_gate_one,
            grad_shift_two,
            grad_scale_two,
            grad_gate_two,
        ],
        axis=1,
    )
    grad_modulation_part = jnp.dot(
        clip_onehot.T, grad_per_column, precision=lax.Precision.HIGHEST
    )
    first = (lax.axis_index("patch") == 0).astype(jnp.float32)
    bias_grads = (
        grad_b_query,
        grad_b_value,
        grad_b_attn,
        grad_b_cross_q,
        grad_b_cross_v * first,
        grad_b_cross_o,
        grad_b_second,
    )
    small_grads = jnp.concatenate(
        [grad_modulation_part.reshape(-1)] + list(bias_grads) + [placed(grad_b_first, "patch")]
    )
    weights, grad_w_cross_kv, input_grad, small_grads, grad_caption, grad_w_first = close_up(
        (grad_w_qkv, grad_w_attn, grad_w_cross_q, grad_w_cross_o),
        grad_w_cross_kv, input_grad, small_grads, grad_caption_share, grad_w_first,
    )
    place = grad_modulation_part.size
    grad_modulation = small_grads[:place].reshape(grad_modulation_part.shape)
    own_biases = []
    for b in bias_grads:
        own_biases.append(own_part(small_grads[place : place + b.shape[0]], "patch", 0))
        place += b.shape[0]
    g_query, g_value, g_attn, g_cross_q, g_cross_v, g_cross_o, g_second = own_biases
    grad_b_first = own_part(small_grads[place:], "patch", 0)
    grad_w_ada = matmul_tn(cond_own, grad_modulation)
    grad_b_ada = own_part(jnp.sum(grad_modulation, axis=0), "patch", 0)
    grad_cond_own = matmul_nt(grad_modulation, ada_weight)
    if small_patch():
        grad_cond_act = jnp.transpose(spread(grad_cond_own), (1, 0, 2)).reshape(cond.shape)
    else:
        grad_cond_act = all_sum(placed(grad_cond_own, "patch"), "patch")
    grad_cond = silu_pull(grad_cond_act)[0]

    grad_w_qkv, grad_w_attn, grad_w_cross_q, grad_w_cross_o = weights
    return (
        block_out,
        input_grad,
        grad_caption,
        grad_cond,
        grad_w_ada,
        grad_b_ada,
        grad_w_qkv,
        g_query,
        g_value,
        grad_w_attn,
        g_attn,
        grad_w_cross_q,
        g_cross_q,
        grad_w_cross_kv,
        g_cross_v,
        grad_w_cross_o,
        g_cross_o,
        grad_w_first,
        grad_b_first,
        grad_w_second,
        g_second,
    )


def solution(mesh):
    tokens = P("frame", "patch", None)
    weight = P("patch", None)
    vector = P("patch")
    parameters = (
        weight, vector, weight, vector, vector, weight, vector, weight, vector,
        weight, vector, weight, vector, weight, vector, weight, vector,
    )
    in_specs = (tokens, tokens, P(), P()) + parameters + (P("frame"), vector, vector, P())
    out_specs = (tokens, tokens, P(), P()) + parameters
    return jax.shard_map(
        on_device, mesh=mesh, in_specs=in_specs, out_specs=out_specs, check_vma=False
    )
```

```python
import math
from functools import partial

import jax
import jax.numpy as jnp
from jax import lax
from jax.experimental import pallas as pl
from jax.experimental.pallas import tpu as pltpu
from jax.sharding import PartitionSpec as P

H = 16
CAP = 120
FRAMES = 17
CLIPS = 4


EPSILON = 1e-06
BEST = lax.Precision.HIGH
LIGHT = pl.CostEstimate(flops=0, bytes_accessed=1 << 16, transcendentals=0)


def matmul(left, right):
    return jnp.dot(left, right, precision=BEST)


def matmul_nt(left, right):
    return lax.dot_general(left, right, (((1,), (1,)), ((), ())), precision=BEST)


def matmul_tn(left, right):
    return lax.dot_general(left, right, (((0,), (0,)), ((), ())), precision=BEST)


def normalize(rows):
    average = jnp.mean(rows, axis=-1, keepdims=True)
    centred = rows - average
    spread = jnp.mean(centred * centred, axis=-1, keepdims=True)
    inverse = lax.rsqrt(spread + EPSILON)
    return (centred * inverse, inverse)


def normalize_back(grad_normed, normed, inverse):
    first_mean = jnp.mean(grad_normed, axis=-1, keepdims=True)
    second_mean = jnp.mean(grad_normed * normed, axis=-1, keepdims=True)
    return inverse * (grad_normed - first_mean - normed * second_mean)


def swap(value, axis, bit):
    size = lax.axis_size(axis)
    return lax.ppermute(value, axis, [(i, i ^ bit) for i in range(size)])


def all_sum(value, axis):
    bit = 1
    while bit < lax.axis_size(axis):
        value = value + swap(value, axis, bit)
        bit *= 2
    return value


def placed(vector, axis):
    length = vector.shape[-1]
    whole = jnp.zeros(vector.shape[:-1] + (length * lax.axis_size(axis),), vector.dtype)
    return lax.dynamic_update_slice_in_dim(
        whole, vector, lax.axis_index(axis) * length, axis=vector.ndim - 1
    )


def own_part(array, axis, dim):
    length = array.shape[dim] // lax.axis_size(axis)
    return lax.dynamic_slice_in_dim(array, lax.axis_index(axis) * length, length, axis=dim)


def after(value, done):
    return lax.optimization_barrier((value, done))[0]


def small_patch():
    return lax.axis_size("patch") == 8 and lax.axis_size("frame") == 4


def padded(vector, rows):
    return jnp.pad(vector, (0, rows * 128 - vector.shape[0])).reshape(rows, 128)


def greet(partners):
    barrier = pltpu.get_barrier_semaphore()
    for partner in partners:
        pl.semaphore_signal(barrier, inc=1, device_id={"patch": partner}, device_id_type=pl.DeviceIdType.MESH)
    pl.semaphore_wait(barrier, len(partners))


def remote(source, target, send_sems, recv_sems, index, device):
    return pltpu.make_async_remote_copy(
        src_ref=source, dst_ref=target, send_sem=send_sems.at[index], recv_sem=recv_sems.at[index],
        device_id={"patch": device}, device_id_type=pl.DeviceIdType.MESH)


def token_gather_kernel(rows, whole, local_sem, send_sems, recv_sems):
    own = lax.axis_index("patch")
    core, along_x, along_y, across = own ^ 1, own ^ 2, own ^ 4, own ^ 6
    greet((core, along_x, along_y))
    length = rows.shape[0] // 4
    sent = []

    def piece(owner, q):
        return whole.at[owner, pl.ds(q * length, length)]

    def send(source, owner, q, index, device):
        copy = remote(source, piece(owner, q), send_sems, recv_sems, index, device)
        copy.start()
        sent.append(copy)

    def arrived(owner, q, index, device):
        remote(piece(owner, q), piece(owner, q), send_sems, recv_sems, index, device).wait_recv()

    mine = pltpu.make_async_copy(rows, whole.at[own], local_sem)
    mine.start()
    for q_x, q_y in ((0, 2), (1, 3), (2, 0), (3, 1)):
        send(rows.at[pl.ds(q_x * length, length)], own, q_x, q_x, along_x)
        send(rows.at[pl.ds(q_y * length, length)], own, q_y, 4 + q_y, along_y)
    for q in range(4):
        send(rows.at[pl.ds(q * length, length)], own, q, 12 + q, core)
    for q_x, q_y in ((0, 2), (1, 3), (2, 0), (3, 1)):
        arrived(along_x, q_x, q_x, along_x)
        if q_x < 2:
            send(piece(along_x, q_x), along_x, q_x, 8 + q_x, along_y)
        send(piece(along_x, q_x), along_x, q_x, 16 + q_x, core)
        arrived(along_y, q_y, 4 + q_y, along_y)
        if q_y >= 2:
            send(piece(along_y, q_y), along_y, q_y, 8 + q_y, along_x)
        send(piece(along_y, q_y), along_y, q_y, 20 + q_y, core)
    for q in (0, 2, 1, 3):
        arrived(across, q, 8 + q, along_y if q < 2 else along_x)
        send(piece(across, q), across, q, 24 + q, core)
    for q in range(4):
        arrived(core, q, 12 + q, core)
        arrived(core ^ 2, q, 16 + q, core)
        arrived(core ^ 4, q, 20 + q, core)
        arrived(core ^ 6, q, 24 + q, core)
    for copy in sent:
        copy.wait_send()
    mine.wait()


def token_gather(rows):
    length, width = rows.shape
    return pl.pallas_call(
        token_gather_kernel,
        out_shape=jax.ShapeDtypeStruct((8, length, width), jnp.float32),
        in_specs=[pl.BlockSpec(memory_space=pltpu.VMEM)],
        out_specs=pl.BlockSpec(memory_space=pl.ANY),
        scratch_shapes=[pltpu.SemaphoreType.DMA, pltpu.SemaphoreType.DMA((28,)), pltpu.SemaphoreType.DMA((28,))],
        compiler_params=pltpu.CompilerParams(collective_id=0, has_side_effects=True, vmem_limit_bytes=16 << 20),
        cost_estimate=LIGHT,
    )(rows).reshape(8 * length, width)


def token_scatter_kernel(parts, total, kept, theirs, by_x, by_y, from_x, from_y, local_sems, send_sems, recv_sems):
    own = lax.axis_index("patch")
    core, along_x, along_y = own ^ 1, own ^ 2, own ^ 4
    greet((core, along_x, along_y))
    half = total.shape[0] // 2
    upper, lower = pl.ds(0, half), pl.ds(half, half)
    order = (3, 2, 1, 0)
    sent, loads = [], {}

    def send(source, target, index, device):
        copy = remote(source, target, send_sems, recv_sems, index, device)
        copy.start()
        sent.append(copy)

    def arrived(target, index, device):
        remote(target, target, send_sems, recv_sems, index, device).wait_recv()

    for j in order:
        send(parts.at[core ^ (2 * j)], theirs.at[j], j, core)
        loads[j] = pltpu.make_async_copy(parts.at[own ^ (2 * j)], kept.at[j], local_sems.at[j])
        loads[j].start()

    def add_cores(j):
        loads[j].wait()
        arrived(theirs.at[j], j, core)
        kept[j] = kept[j] + theirs[j]

    add_cores(3)
    send(kept.at[3, upper], by_x, 4, along_x)
    send(kept.at[3, lower], by_y, 5, along_y)
    add_cores(2)
    send(kept.at[2, lower], from_y.at[lower], 6, along_y)
    add_cores(1)
    send(kept.at[1, upper], from_x.at[upper], 7, along_x)
    add_cores(0)
    arrived(by_x, 4, along_x)
    kept[2, upper] = kept[2, upper] + by_x[...]
    send(kept.at[2, upper], from_y.at[upper], 8, along_y)
    arrived(by_y, 5, along_y)
    kept[1, lower] = kept[1, lower] + by_y[...]
    send(kept.at[1, lower], from_x.at[lower], 9, along_x)
    arrived(from_y.at[lower], 6, along_y)
    arrived(from_x.at[upper], 7, along_x)
    arrived(from_y.at[upper], 8, along_y)
    arrived(from_x.at[lower], 9, along_x)
    total[...] = kept[0] + from_x[...] + from_y[...]
    for copy in sent:
        copy.wait_send()


def token_scatter(parts):
    length, width = parts.shape[0] // 8, parts.shape[1]
    block = (length, width)
    return pl.pallas_call(
        token_scatter_kernel,
        out_shape=jax.ShapeDtypeStruct(block, jnp.float32),
        in_specs=[pl.BlockSpec(memory_space=pl.ANY)],
        out_specs=pl.BlockSpec(memory_space=pltpu.VMEM),
        scratch_shapes=[
            pltpu.VMEM((4,) + block, jnp.float32), pltpu.VMEM((4,) + block, jnp.float32),
            pltpu.VMEM((length // 2, width), jnp.float32), pltpu.VMEM((length // 2, width), jnp.float32),
            pltpu.VMEM(block, jnp.float32), pltpu.VMEM(block, jnp.float32),
            pltpu.SemaphoreType.DMA((4,)), pltpu.SemaphoreType.DMA((10,)), pltpu.SemaphoreType.DMA((10,)),
        ],
        compiler_params=pltpu.CompilerParams(collective_id=1, has_side_effects=True, vmem_limit_bytes=32 << 20),
        cost_estimate=LIGHT,
    )(parts.reshape((8,) + block))


class Links:
    def __init__(self, send_sems, recv_sems):
        self.send_sems, self.recv_sems = send_sems, recv_sems
        self.count = 0
        self.sent = []

    def plan(self):
        self.count += 1
        return self.count - 1

    def copy(self, source, target, index, device):
        return pltpu.make_async_remote_copy(
            src_ref=source, dst_ref=target, send_sem=self.send_sems.at[index],
            recv_sem=self.recv_sems.at[index], device_id=device,
            device_id_type=pl.DeviceIdType.MESH,
        )

    def send(self, source, target, index, device):
        self.copy(source, target, index, device).start()
        self.sent.append((source, index, device))

    def wait(self, target, index, device):
        self.copy(target, target, index, device).wait_recv()

    def drain(self):
        for source, index, device in self.sent:
            self.copy(source, source, index, device).wait_send()


def greet_all(devices):
    barrier = pltpu.get_barrier_semaphore()
    for device in devices:
        pl.semaphore_signal(barrier, inc=1, device_id=device, device_id_type=pl.DeviceIdType.MESH)
    pl.semaphore_wait(barrier, len(devices))


def begin_kernel(
    tokens, later, slots, small, kv, weight,
    tokens_out, later_out, slots_out, small_out, kv_out, weight_out,
    weight_sem, small_1, small_2, small_got, kv_1, kv_2, kv_got_core, kv_got_1, kv_got_2,
    send_sems, recv_sems,
):
    me, z = lax.axis_index("patch"), lax.axis_index("frame")
    core, x, y = ({"patch": me ^ k} for k in (1, 2, 4))
    frames = [None] + [{"frame": z ^ k} for k in (1, 2, 3)]
    greet_all([core, x, y] + frames[1:])
    links = Links(send_sems, recv_sems)
    count, part = tokens.shape[0], tokens.shape[1] // 4
    rows, width = kv_1.shape

    def columns(k):
        return pl.ds(pl.multiple_of((z ^ k) * part, part), part)

    def of_slots(k):
        return pl.ds((z ^ k) * count, count)

    half = pl.multiple_of((me % 2) * width, 128)
    other = pl.multiple_of((1 - me % 2) * width, 128)
    mine, theirs = pl.ds(half, width), pl.ds(other, width)

    length = weight.shape[0]
    weight_at = [[links.plan() for _ in range(7)] for _ in range(3)]
    weight_core = links.plan()

    def piece(k, u, first=0, size=length):
        start = pl.multiple_of((me ^ k) * length + first, 8)
        return weight_out.at[pl.ds(start, size), pl.ds(u * width, width)]

    whole = weight_out.at[pl.ds(pl.multiple_of(me * length, 8), length)]
    sibling = weight_out.at[pl.ds(pl.multiple_of((me ^ 1) * length, 8), length)]
    own_copy = pltpu.make_async_copy(weight, whole, weight_sem)

    def weight_links(u):
        source = weight.at[:, pl.ds(u * width, width)]
        links.send(source, piece(0, u), weight_at[u][0], x)
        links.send(source, piece(0, u), weight_at[u][1], y)

    def weight_across(u):
        middle_row = length // 2
        links.wait(piece(2, u), weight_at[u][0], x)
        upper = piece(2, u, 0, middle_row)
        links.send(upper, upper, weight_at[u][2], y)
        links.send(piece(2, u), piece(2, u), weight_at[u][4], core)
        links.wait(piece(4, u), weight_at[u][1], y)
        lower = piece(4, u, middle_row, middle_row)
        links.send(lower, lower, weight_at[u][3], x)
        links.send(piece(4, u), piece(4, u), weight_at[u][5], core)

    def weight_last(u):
        middle_row = length // 2
        links.wait(piece(6, u, 0, middle_row), weight_at[u][2], y)
        links.wait(piece(6, u, middle_row, middle_row), weight_at[u][3], x)
        links.send(piece(6, u), piece(6, u), weight_at[u][6], core)

    at = links.plan()
    links.send(small, small_got.at[0], at, core)
    at_kv = links.plan()
    links.send(kv.at[:, theirs], kv_got_core, at_kv, core)
    own_copy.start()
    token_at = [None] + [links.plan() for _ in range(3)]
    slot_at = [None] + [links.plan() for _ in range(3)]
    later_at = [None] + [links.plan() for _ in range(3)]
    for k in (1, 2, 3):
        links.send(slots, slots_out.at[z], slot_at[k], frames[k])
        links.send(tokens.at[:, columns(k)], tokens_out.at[of_slots(0)], token_at[k], frames[k])
    for k in (1, 2, 3):
        links.send(later.at[:, columns(k)], later_out.at[of_slots(0)], later_at[k], frames[k])

    links.wait(small_got.at[0], at, core)
    small_1[...] = small[...] + small_got[0]
    at = links.plan()
    links.send(small_1, small_got.at[1], at, x)
    links.wait(kv_got_core, at_kv, core)
    kv_1[...] = kv[:, mine] + kv_got_core[...]
    upper, lower = pl.ds(0, 64), pl.ds(64, rows - 64)
    at_u, at_l = links.plan(), links.plan()
    links.send(kv_1.at[upper], kv_got_1.at[upper], at_u, x)
    links.send(kv_1.at[lower], kv_got_1.at[lower], at_l, y)
    weight_links(0)
    links.send(weight, whole, weight_core, core)
    slots_out[z] = slots[...]
    tokens_out[of_slots(0)] = tokens[:, columns(0)]
    later_out[of_slots(0)] = later[:, columns(0)]
    links.wait(small_got.at[1], at, x)
    small_2[...] = small_1[...] + small_got[1]
    at = links.plan()
    links.send(small_2, small_got.at[2], at, y)
    links.wait(kv_got_1.at[upper], at_u, x)
    links.wait(kv_got_1.at[lower], at_l, y)
    kv_2[...] = kv_1[...] + kv_got_1[...]
    at_u, at_l = links.plan(), links.plan()
    links.send(kv_2.at[upper], kv_got_2.at[upper], at_u, y)
    links.send(kv_2.at[lower], kv_got_2.at[lower], at_l, x)
    weight_links(1)
    links.wait(small_got.at[2], at, y)
    small_out[...] = small_2[...] + small_got[2]
    weight_across(0)
    weight_links(2)
    links.wait(kv_got_2.at[upper], at_u, y)
    links.wait(kv_got_2.at[lower], at_l, x)

    def share(k, columns):
        return kv_out.at[pl.ds(pl.multiple_of((z ^ k) * rows, rows), rows), columns]

    kv_out[pl.ds(pl.multiple_of(z * rows, rows), rows), mine] = kv_2[...] + kv_got_2[...]
    kv_at = [None] + [links.plan() for _ in range(3)]
    core_at = [links.plan() for _ in range(4)]
    for k in (1, 2, 3):
        links.send(share(0, mine), share(0, mine), kv_at[k], frames[k])
    links.send(share(0, mine), share(0, mine), core_at[0], core)
    weight_across(1)
    weight_last(0)
    weight_across(2)
    weight_last(1)
    for k in (1, 2, 3):
        links.wait(slots_out.at[z ^ k], slot_at[k], frames[k])
        links.wait(tokens_out.at[of_slots(k)], token_at[k], frames[k])
        links.wait(later_out.at[of_slots(k)], later_at[k], frames[k])
    for k in (1, 2, 3):
        links.wait(share(k, mine), kv_at[k], frames[k])
        links.send(share(k, mine), share(k, mine), core_at[k], core)
    weight_last(2)
    for k in range(4):
        links.wait(share(k, theirs), core_at[k], core)
    links.wait(sibling, weight_core, core)
    for u in range(3):
        for i, k in enumerate((2, 4, 6)):
            links.wait(piece(k ^ 1, u), weight_at[u][4 + i], core)
    own_copy.wait()
    links.drain()


def begin(tokens, later, slots, small, kv, weight):
    count, cols, width = tokens.shape
    rows = kv.shape[0]
    f32, vmem = jnp.float32, pl.BlockSpec(memory_space=pltpu.VMEM)
    hbm = pl.BlockSpec(memory_space=pl.ANY)
    half = pltpu.VMEM((rows, width), f32)
    return pl.pallas_call(
        begin_kernel,
        out_shape=(
            jax.ShapeDtypeStruct((4 * count, cols // 4, width), f32),
            jax.ShapeDtypeStruct((4 * count, cols // 4, width), f32),
            jax.ShapeDtypeStruct((4,) + slots.shape, f32),
            jax.ShapeDtypeStruct(small.shape, f32),
            jax.ShapeDtypeStruct((4 * rows, 2 * width), f32),
            jax.ShapeDtypeStruct((8 * weight.shape[0], weight.shape[1]), f32),
        ),
        in_specs=[vmem] * 5 + [hbm],
        out_specs=[vmem] * 5 + [hbm],
        scratch_shapes=[
            pltpu.SemaphoreType.DMA,
            pltpu.VMEM(small.shape, f32), pltpu.VMEM(small.shape, f32),
            pltpu.VMEM((3,) + small.shape, f32), half, half, half, half, half,
            pltpu.SemaphoreType.DMA((48,)), pltpu.SemaphoreType.DMA((48,)),
        ],
        compiler_params=pltpu.CompilerParams(
            collective_id=2, has_side_effects=True, vmem_limit_bytes=36 << 20
        ),
        cost_estimate=LIGHT,
    )(tokens, later, slots, small, kv, weight)


UNITS = 3


def finish_kernel(
    first, attn, cross_q, cross_o, kv, tokens, small, caption, columns,
    first_out, attn_out, cross_q_out, cross_o_out, kv_out, tokens_out, small_out, caption_out,
    columns_out, columns_got, columns_sem,
    kept, theirs, by_x, by_y, from_x, from_y, along_z, across_z,
    small_sums, small_got, small_z, load_sems, credit, send_sems, recv_sems,
):
    me, z = lax.axis_index("patch"), lax.axis_index("frame")
    outer = (z == 0) | (z == 3)
    inner = (z == 1) | (z == 2)
    core, x, y = ({"patch": me ^ k} for k in (1, 2, 4))
    frames = [None] + [{"frame": z ^ k} for k in (1, 2, 3)]
    near, facing = frames[1], frames[3]
    chips = {2: x, 4: y, 6: {"patch": me ^ 6}}
    greet_all([core, x, y, chips[6]] + frames[1:])
    links = Links(send_sems, recv_sems)
    rows, width = by_x.shape[1] * 2, by_x.shape[2]
    upper, lower = pl.ds(0, rows // 2), pl.ds(rows // 2, rows // 2)
    count, part = tokens_out.shape[0], tokens_out.shape[1] // 4

    token_at = [None] + [links.plan() for _ in range(3)]

    def send_tokens(k):
        where = pl.ds(pl.multiple_of(z * part, part), part)
        if k == 0:
            tokens_out[:, where] = tokens[pl.ds(z * count, count)]
        else:
            source = tokens.at[pl.ds((z ^ k) * count, count)]
            links.send(source, tokens_out.at[:, where], token_at[k], frames[k])

    def frame_steps(value, result, near_got, facing_got):
        up, over, down = links.plan(), links.plan(), links.plan()

        def one():
            @pl.when(outer)
            def _():
                links.copy(value, near_got, up, near).start()

        def two():
            @pl.when(inner)
            def _():
                links.wait(near_got, up, near)
                near_got[...] = near_got[...] + value[...]
                links.copy(near_got, facing_got, over, facing).start()

        def three():
            @pl.when(inner)
            def _():
                links.wait(facing_got, over, facing)
                result[...] = near_got[...] + facing_got[...]
                links.copy(result, near_got, down, near).start()

        def four():
            @pl.when(outer)
            def _():
                links.wait(near_got, down, near)
                result[...] = near_got[...]
                links.copy(value, value, up, near).wait_send()

            @pl.when(inner)
            def _():
                links.copy(near_got, near_got, over, facing).wait_send()
                links.copy(result, result, down, near).wait_send()

        return one, two, three, four

    def piece(ref, u):
        return ref.at[:, pl.ds(u * width, width)]

    pairs = [(kept.at[u, 0], piece(first_out, u)) for u in range(UNITS)]
    pairs += [(attn, attn_out), (cross_q, cross_q_out), (cross_o, cross_o_out)]
    pairs += [(piece(kv, u), piece(kv_out, u)) for u in range(2)]
    steps = [
        frame_steps(value, result, along_z.at[i], across_z.at[i])
        for i, (value, result) in enumerate(pairs)
    ]
    small_steps = frame_steps(small_sums.at[2], small_out, small_z.at[0], small_z.at[1])

    core_at = [[links.plan() for _ in range(4)] for _ in range(UNITS)]
    link_at = [[links.plan() for _ in range(6)] for _ in range(UNITS)]

    def source(u, device, j):
        start = pl.multiple_of((device ^ (2 * j)) * rows, rows)
        return first.at[pl.ds(start, rows), pl.ds(u * width, width)]

    def load(u, j):
        return pltpu.make_async_copy(source(u, me, j), kept.at[u, j], load_sems.at[u, j])

    def to_core(u):
        if u >= 2:
            pl.semaphore_wait(credit.at[u - 2], 1)
        for j in (3, 2, 1, 0):
            links.send(source(u, me ^ 1, j), theirs.at[u % 2, j], core_at[u][j], core)

    def add_cores(u, j):
        load(u, j).wait()
        links.wait(theirs.at[u % 2, j], core_at[u][j], core)
        kept[u, j] = kept[u, j] + theirs[u % 2, j]

    def stage_one(u):
        at = link_at[u]
        add_cores(u, 3)
        links.send(kept.at[u, 3, upper], by_x.at[u], at[0], x)
        links.send(kept.at[u, 3, lower], by_y.at[u], at[1], y)
        add_cores(u, 2)
        links.send(kept.at[u, 2, lower], from_y.at[u, lower], at[2], y)
        add_cores(u, 1)
        links.send(kept.at[u, 1, upper], from_x.at[u, upper], at[3], x)
        add_cores(u, 0)
        if u + 2 < UNITS:
            pl.semaphore_signal(
                credit.at[u], inc=1, device_id=core, device_id_type=pl.DeviceIdType.MESH
            )
            to_core(u + 2)

    def stage_two(u):
        at = link_at[u]
        links.wait(by_x.at[u], at[0], x)
        kept[u, 2, upper] = kept[u, 2, upper] + by_x[u]
        links.send(kept.at[u, 2, upper], from_y.at[u, upper], at[4], y)
        links.wait(by_y.at[u], at[1], y)
        kept[u, 1, lower] = kept[u, 1, lower] + by_y[u]
        links.send(kept.at[u, 1, lower], from_x.at[u, lower], at[5], x)

    def stage_three(u):
        at = link_at[u]
        links.wait(from_y.at[u, lower], at[2], y)
        links.wait(from_x.at[u, upper], at[3], x)
        links.wait(from_y.at[u, upper], at[4], y)
        links.wait(from_x.at[u, lower], at[5], x)
        kept[u, 0] = kept[u, 0] + from_x[u] + from_y[u]
        steps[u][0]()

    block = columns_got.shape[1] // 2
    columns_at = {k: links.plan() for k in (2, 4, 6)}
    columns_core = {k: links.plan() for k in (0, 2, 4, 6)}

    def chip_rows(k):
        return columns.at[pl.ds(pl.multiple_of((me ^ k) // 2 * (2 * block), 8), 2 * block)]

    own_rows = pltpu.make_async_copy(chip_rows(0), columns_got.at[0], columns_sem.at[0])

    def own_block(k):
        core_rows = pl.ds(pl.multiple_of(me % 2 * block, 8), block)
        return pltpu.make_async_copy(
            columns_got.at[k // 2, core_rows], columns_out.at[me ^ k], columns_sem.at[1 + k // 2]
        )

    def send_columns(k):
        links.send(chip_rows(k), columns_got.at[k // 2], columns_at[k], chips[k])

    def columns_over():
        other_rows = pl.ds(pl.multiple_of((1 - me % 2) * block, 8), block)
        own_rows.wait()
        for k in (0, 2, 4, 6):
            if k:
                links.wait(columns_got.at[k // 2], columns_at[k], chips[k])
            links.send(
                columns_got.at[k // 2, other_rows], columns_out.at[me ^ k], columns_core[k], core
            )
            own_block(k).start()

    def columns_end():
        for k in (0, 2, 4, 6):
            links.wait(columns_out.at[me ^ 1 ^ k], columns_core[k], core)
            own_block(k).wait()

    caption_at = [links.plan() for _ in range(10)]

    def caption_frames():
        caption_out[me, z] = caption[...]
        for k in (1, 2, 3):
            links.send(caption, caption_out.at[me, z], caption_at[k - 1], frames[k])

    def caption_x():
        for k in (1, 2, 3):
            links.wait(caption_out.at[me, z ^ k], caption_at[k - 1], frames[k])
        links.send(caption_out.at[me], caption_out.at[me], caption_at[3], x)

    def caption_y():
        links.wait(caption_out.at[me ^ 2], caption_at[3], x)
        for i, k in enumerate((0, 2)):
            links.send(caption_out.at[me ^ k], caption_out.at[me ^ k], caption_at[4 + i], y)

    def caption_core():
        for i, k in enumerate((0, 2)):
            links.wait(caption_out.at[me ^ 4 ^ k], caption_at[4 + i], y)
        for i, k in enumerate((0, 2, 4, 6)):
            links.send(caption_out.at[me ^ k], caption_out.at[me ^ k], caption_at[6 + i], core)

    def caption_end():
        for i, k in enumerate((0, 2, 4, 6)):
            links.wait(caption_out.at[me ^ 1 ^ k], caption_at[6 + i], core)

    small_at = [links.plan() for _ in range(3)]
    links.send(small, small_got.at[0], small_at[0], core)
    caption_frames()
    own_rows.start()
    for u in range(UNITS):
        for j in (3, 2, 1, 0):
            load(u, j).start()
    for i in (6, 7, 3, 4, 5):
        steps[i][0]()
    for u in range(2):
        to_core(u)
    links.wait(small_got.at[0], small_at[0], core)
    small_sums[0] = small[...] + small_got[0]
    links.send(small_sums.at[0], small_got.at[1], small_at[1], x)
    stage_one(0)
    links.wait(small_got.at[1], small_at[1], x)
    small_sums[1] = small_sums[0] + small_got[1]
    links.send(small_sums.at[1], small_got.at[2], small_at[2], y)
    stage_one(1)
    stage_two(0)
    links.wait(small_got.at[2], small_at[2], y)
    small_sums[2] = small_sums[1] + small_got[2]
    small_steps[0]()
    steps[6][1]()
    steps[7][1]()
    stage_one(2)
    stage_three(0)
    steps[3][1]()
    stage_two(1)
    steps[6][2]()
    steps[7][2]()
    steps[4][1]()
    stage_two(2)
    stage_three(1)
    caption_x()
    for k in (2, 4, 6):
        send_columns(k)
    steps[3][2]()
    steps[5][1]()
    small_steps[1]()
    stage_three(2)
    for k in range(4):
        send_tokens(k)
    steps[4][2]()
    small_steps[2]()
    steps[0][1]()
    caption_y()
    steps[5][2]()
    steps[1][1]()
    steps[0][2]()
    caption_core()
    steps[2][1]()
    steps[1][2]()
    steps[2][2]()
    for step in steps + [small_steps]:
        step[3]()
    columns_over()
    caption_end()
    columns_end()
    for k in (1, 2, 3):
        where = pl.ds(pl.multiple_of((z ^ k) * part, part), part)
        links.wait(tokens_out.at[:, where], token_at[k], frames[k])
    links.drain()


def finish(first, attn, cross_q, cross_o, kv, tokens, small, caption, columns):
    rows, width = attn.shape
    count, part = tokens.shape[0] // 4, tokens.shape[1]
    f32, vmem = jnp.float32, pl.BlockSpec(memory_space=pltpu.VMEM)
    hbm = pl.BlockSpec(memory_space=pl.ANY)

    def shape(*sizes):
        return jax.ShapeDtypeStruct(sizes, f32)

    return pl.pallas_call(
        finish_kernel,
        out_shape=(
            shape(rows, 3 * width), shape(rows, width), shape(rows, width), shape(rows, width),
            shape(rows, 2 * width), shape(count, 4 * part, tokens.shape[2]), shape(*small.shape),
            shape(8, 4, *caption.shape), shape(8, columns.shape[0] // 8, columns.shape[1]),
        ),
        in_specs=[hbm] + [vmem] * 7 + [hbm],
        out_specs=[vmem] * 8 + [hbm],
        scratch_shapes=[
            pltpu.VMEM((4, columns.shape[0] // 4, columns.shape[1]), f32),
            pltpu.SemaphoreType.DMA((5,)),
            pltpu.VMEM((UNITS, 4, rows, width), f32), pltpu.VMEM((2, 4, rows, width), f32),
            pltpu.VMEM((UNITS, rows // 2, width), f32), pltpu.VMEM((UNITS, rows // 2, width), f32),
            pltpu.VMEM((UNITS, rows, width), f32), pltpu.VMEM((UNITS, rows, width), f32),
            pltpu.VMEM((8, rows, width), f32), pltpu.VMEM((8, rows, width), f32),
            pltpu.VMEM((3,) + small.shape, f32), pltpu.VMEM((3,) + small.shape, f32),
            pltpu.VMEM((2,) + small.shape, f32),
            pltpu.SemaphoreType.DMA((UNITS, 4)), pltpu.SemaphoreType.REGULAR((1,)),
            pltpu.SemaphoreType.DMA((112,)), pltpu.SemaphoreType.DMA((112,)),
        ],
        compiler_params=pltpu.CompilerParams(
            collective_id=3, has_side_effects=True, vmem_limit_bytes=58 << 20
        ),
        cost_estimate=LIGHT,
    )(first, attn, cross_q, cross_o, kv, tokens, small, caption, columns)


def middle_kernel(
    parts, kv, residual, gate, bias, attn, cross_q, cross_o,
    total, kv_out, block_out, attn_out, cross_q_out, cross_o_out,
    w_kept, w_theirs, w_by_x, w_by_y, w_from_x, w_from_y, w_loads, credit, kv_sem,
    block, kept, theirs, by_x, by_y, from_x, from_y,
    kv_half, kv_core, kv_got, kv_1, kv_2, kv_got_1, kv_got_2,
    load_sems, send_sems, recv_sems,
):
    me, z = lax.axis_index("patch"), lax.axis_index("frame")
    core, x, y = ({"patch": me ^ k} for k in (1, 2, 4))
    frames = [None] + [{"frame": z ^ k} for k in (1, 2, 3)]
    greet_all([core, x, y] + frames[1:])
    links = Links(send_sems, recv_sems)
    rows, width = kv_1.shape
    half = pl.multiple_of((me % 2) * width, 128)
    other = pl.multiple_of((1 - me % 2) * width, 128)
    mine, others = pl.ds(half, width), pl.ds(other, width)

    def share(ref, k):
        return ref.at[pl.ds(pl.multiple_of((z ^ k) * rows, rows), rows)]

    grads, sums = (attn, cross_q, cross_o), (attn_out, cross_q_out, cross_o_out)
    length = attn_out.shape[0]
    top_rows, low_rows = pl.ds(0, length // 2), pl.ds(length // 2, length // 2)
    w_core_at = [[links.plan() for _ in range(4)] for _ in grads]
    w_at = [[links.plan() for _ in range(6)] for _ in grads]

    def w_source(u, device, j):
        start = pl.multiple_of((device ^ (2 * j)) * length, length)
        return grads[u].at[pl.ds(start, length)]

    def w_load(u, j):
        return pltpu.make_async_copy(w_source(u, me, j), w_kept.at[u, j], w_loads.at[u, j])

    def w_to_core(u):
        if u >= 2:
            pl.semaphore_wait(credit.at[u - 2], 1)
        for j in (3, 2, 1, 0):
            links.send(w_source(u, me ^ 1, j), w_theirs.at[u % 2, j], w_core_at[u][j], core)

    def w_add(u, j):
        w_load(u, j).wait()
        links.wait(w_theirs.at[u % 2, j], w_core_at[u][j], core)
        w_kept[u, j] = w_kept[u, j] + w_theirs[u % 2, j]

    def w_one(u):
        w_add(u, 3)
        links.send(w_kept.at[u, 3, top_rows], w_by_x.at[u], w_at[u][0], x)
        links.send(w_kept.at[u, 3, low_rows], w_by_y.at[u], w_at[u][1], y)
        w_add(u, 2)
        links.send(w_kept.at[u, 2, low_rows], w_from_y.at[u, low_rows], w_at[u][2], y)
        w_add(u, 1)
        links.send(w_kept.at[u, 1, top_rows], w_from_x.at[u, top_rows], w_at[u][3], x)
        w_add(u, 0)
        if u == 0:
            pl.semaphore_signal(
                credit.at[u], inc=1, device_id=core, device_id_type=pl.DeviceIdType.MESH
            )
            w_to_core(2)

    def w_two(u):
        links.wait(w_by_x.at[u], w_at[u][0], x)
        w_kept[u, 2, top_rows] = w_kept[u, 2, top_rows] + w_by_x[u]
        links.send(w_kept.at[u, 2, top_rows], w_from_y.at[u, top_rows], w_at[u][4], y)
        links.wait(w_by_y.at[u], w_at[u][1], y)
        w_kept[u, 1, low_rows] = w_kept[u, 1, low_rows] + w_by_y[u]
        links.send(w_kept.at[u, 1, low_rows], w_from_x.at[u, low_rows], w_at[u][5], x)

    def w_three(u):
        links.wait(w_from_y.at[u, low_rows], w_at[u][2], y)
        links.wait(w_from_x.at[u, top_rows], w_at[u][3], x)
        links.wait(w_from_y.at[u, top_rows], w_at[u][4], y)
        links.wait(w_from_x.at[u, low_rows], w_at[u][5], x)
        sums[u][...] = w_kept[u, 0] + w_from_x[u] + w_from_y[u]

    at_kv = links.plan()
    links.send(kv.at[:, others], kv_core, at_kv, core)
    kv_load = pltpu.make_async_copy(kv.at[:, mine], kv_half, kv_sem)
    kv_load.start()
    core_at = [links.plan() for _ in range(4)]
    loads = [
        pltpu.make_async_copy(parts.at[me ^ (2 * j)], kept.at[j], load_sems.at[j])
        for j in range(4)
    ]
    for j in (3, 2, 1, 0):
        links.send(parts.at[me ^ 1 ^ (2 * j)], theirs.at[j], core_at[j], core)
        loads[j].start()
    for u in range(3):
        for j in (3, 2, 1, 0):
            w_load(u, j).start()
    for u in range(2):
        w_to_core(u)
    kv_load.wait()
    links.wait(kv_core, at_kv, core)
    kv_half[...] = kv_half[...] + kv_core[...]
    kv_at = [None] + [links.plan() for _ in range(3)]
    for k in (1, 2, 3):
        links.send(share(kv_half, k), kv_got.at[k - 1], kv_at[k], frames[k])

    count = total.shape[0] // 2
    upper, lower = pl.ds(0, count), pl.ds(count, count)
    at = [links.plan() for _ in range(6)]

    def add_cores(j):
        loads[j].wait()
        links.wait(theirs.at[j], core_at[j], core)
        kept[j] = kept[j] + theirs[j]

    add_cores(3)
    links.send(kept.at[3, upper], by_x, at[0], x)
    links.send(kept.at[3, lower], by_y, at[1], y)
    add_cores(2)
    links.send(kept.at[2, lower], from_y.at[lower], at[2], y)
    add_cores(1)
    links.send(kept.at[1, upper], from_x.at[upper], at[3], x)
    add_cores(0)
    links.wait(by_x, at[0], x)
    kept[2, upper] = kept[2, upper] + by_x[...]
    links.send(kept.at[2, upper], from_y.at[upper], at[4], y)
    links.wait(by_y, at[1], y)
    kept[1, lower] = kept[1, lower] + by_y[...]
    links.send(kept.at[1, lower], from_x.at[lower], at[5], x)

    w_one(0)
    links.wait(from_y.at[lower], at[2], y)
    links.wait(from_x.at[upper], at[3], x)
    links.wait(from_y.at[upper], at[4], y)
    links.wait(from_x.at[lower], at[5], x)
    total[...] = kept[0] + from_x[...] + from_y[...]
    slots, part = residual.shape[0] // 4, residual.shape[1]
    block[...] = residual[...] + gate[...] * (total[...] + bias[...]).reshape(residual.shape)
    block_at = [None] + [links.plan() for _ in range(3)]
    place = pl.ds(pl.multiple_of(z * part, part), part)
    for k in (1, 2, 3):
        source = block.at[pl.ds((z ^ k) * slots, slots)]
        links.send(source, block_out.at[:, place], block_at[k], frames[k])
    block_out[:, place] = block[pl.ds(z * slots, slots)]
    w_one(1)
    w_two(0)
    for k in (1, 2, 3):
        links.wait(kv_got.at[k - 1], kv_at[k], frames[k])
    kv_1[...] = share(kv_half, 0)[...] + kv_got[0] + (kv_got[1] + kv_got[2])
    top, bottom = pl.ds(0, 64), pl.ds(64, rows - 64)
    at_u, at_l = links.plan(), links.plan()
    links.send(kv_1.at[top], kv_got_1.at[top], at_u, x)
    links.send(kv_1.at[bottom], kv_got_1.at[bottom], at_l, y)
    w_one(2)
    w_two(1)
    w_three(0)
    links.wait(kv_got_1.at[top], at_u, x)
    links.wait(kv_got_1.at[bottom], at_l, y)
    kv_2[...] = kv_1[...] + kv_got_1[...]
    at_u, at_l = links.plan(), links.plan()
    links.send(kv_2.at[top], kv_got_2.at[top], at_u, y)
    links.send(kv_2.at[bottom], kv_got_2.at[bottom], at_l, x)
    links.wait(kv_got_2.at[top], at_u, y)
    links.wait(kv_got_2.at[bottom], at_l, x)
    kv_out[:, mine] = kv_2[...] + kv_got_2[...]
    at_core = links.plan()
    links.send(kv_out.at[:, mine], kv_out.at[:, mine], at_core, core)
    w_two(2)
    w_three(1)
    w_three(2)
    links.wait(kv_out.at[:, others], at_core, core)
    for k in (1, 2, 3):
        there = pl.ds(pl.multiple_of((z ^ k) * part, part), part)
        links.wait(block_out.at[:, there], block_at[k], frames[k])
    links.drain()


def middle(parts, kv, residual, gate, bias, attn, cross_q, cross_o):
    slots, cols, _ = residual.shape
    count = attn.shape[0] // 8
    length, width = parts.shape[0] // 8, parts.shape[1]
    rows = kv.shape[0] // 4
    f32, vmem = jnp.float32, pl.BlockSpec(memory_space=pltpu.VMEM)
    hbm = pl.BlockSpec(memory_space=pl.ANY)
    block, half = (length, width), pltpu.VMEM((rows, width), f32)
    return pl.pallas_call(
        middle_kernel,
        out_shape=(
            jax.ShapeDtypeStruct(block, f32), jax.ShapeDtypeStruct((rows, 2 * width), f32),
            jax.ShapeDtypeStruct((slots // 4, 4 * cols, width), f32),
            *[jax.ShapeDtypeStruct((count, width), f32)] * 3,
        ),
        in_specs=[hbm] * 2 + [vmem] * 3 + [hbm] * 3,
        out_specs=[vmem] * 6,
        scratch_shapes=[
            pltpu.VMEM((3, 4, count, width), f32), pltpu.VMEM((2, 4, count, width), f32),
            pltpu.VMEM((3, count // 2, width), f32), pltpu.VMEM((3, count // 2, width), f32),
            pltpu.VMEM((3, count, width), f32), pltpu.VMEM((3, count, width), f32),
            pltpu.SemaphoreType.DMA((3, 4)), pltpu.SemaphoreType.REGULAR((1,)),
            pltpu.SemaphoreType.DMA,
            pltpu.VMEM((slots, cols, width), f32),
            pltpu.VMEM((4,) + block, f32), pltpu.VMEM((4,) + block, f32),
            pltpu.VMEM((length // 2, width), f32), pltpu.VMEM((length // 2, width), f32),
            pltpu.VMEM(block, f32), pltpu.VMEM(block, f32),
            pltpu.VMEM((4 * rows, width), f32), pltpu.VMEM((4 * rows, width), f32),
            pltpu.VMEM((3, rows, width), f32), half, half, half, half,
            pltpu.SemaphoreType.DMA((4,)), pltpu.SemaphoreType.DMA((56,)),
            pltpu.SemaphoreType.DMA((56,)),
        ],
        compiler_params=pltpu.CompilerParams(
            collective_id=4, has_side_effects=True, vmem_limit_bytes=58 << 20
        ),
        cost_estimate=LIGHT,
    )(parts.reshape((8,) + block), kv, residual, gate[None], bias[None], attn, cross_q, cross_o)


def spread_kernel(block, whole, send_sems, recv_sems):
    me = lax.axis_index("patch")
    peers = [None] + [{"patch": me ^ k} for k in range(1, 8)]
    greet_all(peers[1:])
    links = Links(send_sems, recv_sems)
    at = [links.plan() for _ in range(8)]
    for k in range(1, 8):
        links.send(block, whole.at[me], at[k], peers[k])
    whole[me] = block[...]
    for k in range(1, 8):
        links.wait(whole.at[me ^ k], at[k], peers[k])
    links.drain()


def spread(block):
    vmem = pl.BlockSpec(memory_space=pltpu.VMEM)
    return pl.pallas_call(
        spread_kernel,
        out_shape=jax.ShapeDtypeStruct((8,) + block.shape, jnp.float32),
        in_specs=[vmem],
        out_specs=vmem,
        scratch_shapes=[pltpu.SemaphoreType.DMA((8,)), pltpu.SemaphoreType.DMA((8,))],
        compiler_params=pltpu.CompilerParams(collective_id=5, has_side_effects=True),
    )(block)


def halves(x):
    high = x.astype(jnp.bfloat16)
    return high, (x - high.astype(jnp.float32)).astype(jnp.bfloat16)


NN, NT, TN = (((1,), (0,)), ((), ())), (((1,), (1,)), ((), ())), (((0,), (0,)), ((), ()))


def three(left, right, dims):
    def dot(a, b):
        return lax.dot_general(a, b, dims, preferred_element_type=jnp.float32)

    return dot(left[0], right[0]) + (dot(left[0], right[1]) + dot(left[1], right[0]))


WINDOW = 256


def head_window(head, head_dim, width):
    start = jnp.minimum(head * head_dim // 128 * 128, width - WINDOW)
    lane = lax.broadcasted_iota(jnp.int32, (1, WINDOW), 1) - (head * head_dim - start)
    mask = ((lane >= 0) & (lane < head_dim)).astype(jnp.float32)
    return pl.ds(pl.multiple_of(start, 128), WINDOW), mask


def softmax_last(scores):
    exponent = jnp.exp(scores - jnp.max(scores, axis=-1, keepdims=True))
    return exponent / jnp.sum(exponent, axis=-1, keepdims=True)


GROUP = 8


def grouped(ref, group, lanes):
    slots = ref.shape[0]
    value = ref[:, group * GROUP : (group + 1) * GROUP, lanes]
    return value.reshape(slots * GROUP, value.shape[-1])


def store_halves(high, low, index, value):
    high[index], low[index] = halves(value)


def frame_attention_kernel(qkv, b_query, b_value, distance, allowed, probs, out, *split):
    (q_high, q_low, k_high, k_low, v_high, v_low), total = split[:6], split[6]
    slots, width = qkv.shape[0], out.shape[-1]
    head_dim = width // H
    scaling = head_dim**-0.5
    for g in range(2):
        store_halves(q_high, q_low, g, grouped(qkv, g, slice(0, width)) + b_query[...])
        store_halves(k_high, k_low, g, grouped(qkv, g, slice(width, 2 * width)))
        store_halves(
            v_high, v_low, g, grouped(qkv, g, slice(2 * width, 3 * width)) + b_value[...]
        )
    total[...] = jnp.zeros(total.shape, jnp.float32)

    def step(head, _):
        at, mask = head_window(head, head_dim, width)
        mask = mask.astype(jnp.bfloat16)
        slope = jnp.exp2(-8.0 / H * (jnp.full((1, 1), head, jnp.int32).astype(jnp.float32) + 1.0))
        for g in range(2):
            query = (q_high[g, :, at] * mask, q_low[g, :, at] * mask)
            scores = three(query, (k_high[g, :, at], k_low[g, :, at]), NT)
            scores = jnp.where(allowed[...] > 0, scores * scaling - slope * distance[...], -1e30)
            prob = softmax_last(scores)
            probs[head, g] = prob
            value = (v_high[g, :, at] * mask, v_low[g, :, at] * mask)
            total[g, :, at] = total[g, :, at] + three(halves(prob), value, NN)
        return 0

    lax.fori_loop(0, H, step, 0, unroll=4)
    for g in range(2):
        out[:, g * GROUP : (g + 1) * GROUP, :] = total[g].reshape(slots, GROUP, width)


def frame_tables(frame_pos):
    slots = frame_pos.shape[0]
    position = jnp.repeat(frame_pos, GROUP)
    column = jnp.tile(jnp.arange(GROUP), slots)
    distance = jnp.abs(position[:, None] - position[None, :])
    same = column[:, None] == column[None, :]
    return distance, (same & (position[None, :] < FRAMES - 0.5)).astype(jnp.float32)


VMEM_SPEC = pl.BlockSpec(memory_space=pltpu.VMEM)


def frame_attention(qkv, b_query, b_value, distance, allowed):
    slots, cols, width = qkv.shape[0], qkv.shape[1], qkv.shape[2] // 3
    rows = slots * GROUP
    part = pltpu.VMEM((2, rows, width), jnp.bfloat16)
    return pl.pallas_call(
        frame_attention_kernel,
        out_shape=(
            jax.ShapeDtypeStruct((H, 2, rows, rows), jnp.float32),
            jax.ShapeDtypeStruct((slots, cols, width), jnp.float32),
        ),
        in_specs=[VMEM_SPEC] * 5,
        out_specs=[VMEM_SPEC] * 2,
        scratch_shapes=[part] * 6 + [pltpu.VMEM((2, rows, width), jnp.float32)],
        compiler_params=pltpu.CompilerParams(vmem_limit_bytes=40 << 20),
        cost_estimate=LIGHT,
    )(qkv, b_query.reshape(1, width), b_value.reshape(1, width), distance, allowed)


def frame_attention_back_kernel(qkv, b_query, b_value, probs, attended, grad, out, *split):
    width = attended.shape[-1]
    slots, head_dim = qkv.shape[0], width // H
    scaling = head_dim**-0.5
    names = [(split[2 * i], split[2 * i + 1]) for i in range(4)]
    (q_high, q_low), (k_high, k_low), (v_high, v_low), (g_high, g_low) = names
    total, product = split[8], split[9]
    for g in range(2):
        store_halves(q_high, q_low, g, grouped(qkv, g, slice(0, width)) + b_query[...])
        store_halves(k_high, k_low, g, grouped(qkv, g, slice(width, 2 * width)))
        store_halves(
            v_high, v_low, g, grouped(qkv, g, slice(2 * width, 3 * width)) + b_value[...]
        )
        upstream = grouped(grad, g, slice(0, width))
        store_halves(g_high, g_low, g, upstream)
        product[g] = upstream * grouped(attended, g, slice(0, width))
    total[...] = jnp.zeros(total.shape, jnp.float32)

    def step(head, _):
        at, mask = head_window(head, head_dim, width)
        small = mask.astype(jnp.bfloat16)

        def masked(high, low, g):
            return high[g, :, at] * small, low[g, :, at] * small

        for g in range(2):
            upstream = masked(g_high, g_low, g)
            prob = probs[head, g]
            grad_prob = three(upstream, (v_high[g, :, at], v_low[g, :, at]), NT)
            term = jnp.sum(product[g, :, at] * mask, axis=-1, keepdims=True)
            score = halves(prob * (grad_prob - term) * scaling)
            total[0, g, :, at] = total[0, g, :, at] + three(score, masked(k_high, k_low, g), NN)
            total[1, g, :, at] = total[1, g, :, at] + three(score, masked(q_high, q_low, g), TN)
            total[2, g, :, at] = total[2, g, :, at] + three(halves(prob), upstream, TN)
        return 0

    lax.fori_loop(0, H, step, 0, unroll=4)
    for g in range(2):
        for i in range(3):
            out[:, g * GROUP : (g + 1) * GROUP, i * width : (i + 1) * width] = total[
                i, g
            ].reshape(slots, GROUP, width)


def frame_attention_back(qkv, b_query, b_value, probs, attended, grad):
    slots, cols, width = attended.shape
    rows = slots * GROUP
    part = pltpu.VMEM((2, rows, width), jnp.bfloat16)
    return pl.pallas_call(
        frame_attention_back_kernel,
        out_shape=jax.ShapeDtypeStruct((slots, cols, 3 * width), jnp.float32),
        in_specs=[VMEM_SPEC] * 6,
        out_specs=VMEM_SPEC,
        scratch_shapes=[part] * 8
        + [pltpu.VMEM((3, 2, rows, width), jnp.float32), pltpu.VMEM((2, rows, width), jnp.float32)],
        compiler_params=pltpu.CompilerParams(vmem_limit_bytes=48 << 20),
        cost_estimate=LIGHT,
    )(qkv, b_query.reshape(1, width), b_value.reshape(1, width), probs, attended, grad)


def cross_attention_kernel(queries, b_query, kv, b_value, allowed, probs, out, *split):
    q_high, q_low, k_high, k_low, v_high, v_low = split
    width = out.shape[-1]
    head_dim = width // H
    scaling = head_dim**-0.5
    store_halves(q_high, q_low, Ellipsis, queries[...] + b_query[...])
    store_halves(k_high, k_low, Ellipsis, kv[:, 0:width])
    store_halves(v_high, v_low, Ellipsis, kv[:, width : 2 * width] + b_value[...])
    out[...] = jnp.zeros(out.shape, jnp.float32)

    def step(head, _):
        at, mask = head_window(head, head_dim, width)
        mask = mask.astype(jnp.bfloat16)
        query = (q_high[:, at] * mask, q_low[:, at] * mask)
        scores = three(query, (k_high[:, at], k_low[:, at]), NT)
        prob = softmax_last(jnp.where(allowed[...] > 0, scores * scaling, -1e30))
        probs[head] = prob
        value = (v_high[:, at] * mask, v_low[:, at] * mask)
        out[:, at] = out[:, at] + three(halves(prob), value, NN)
        return 0

    lax.fori_loop(0, H, step, 0, unroll=4)


def cross_attention(queries, b_query, kv, b_value, allowed):
    rows, width = queries.shape
    keys = kv.shape[0]
    q_part = pltpu.VMEM((rows, width), jnp.bfloat16)
    k_part = pltpu.VMEM((keys, width), jnp.bfloat16)
    return pl.pallas_call(
        cross_attention_kernel,
        out_shape=(
            jax.ShapeDtypeStruct((H, rows, keys), jnp.float32),
            jax.ShapeDtypeStruct((rows, width), jnp.float32),
        ),
        in_specs=[VMEM_SPEC] * 5,
        out_specs=[VMEM_SPEC] * 2,
        scratch_shapes=[q_part] * 2 + [k_part] * 4,
        compiler_params=pltpu.CompilerParams(vmem_limit_bytes=48 << 20),
        cost_estimate=LIGHT,
    )(queries, b_query.reshape(1, width), kv, b_value.reshape(1, width), allowed)


def cross_attention_back_kernel(
    queries, b_query, kv, b_value, probs, attended, grad, grad_q, grad_kv, *split
):
    names = [(split[2 * i], split[2 * i + 1]) for i in range(4)]
    (q_high, q_low), (g_high, g_low), (k_high, k_low), (v_high, v_low) = names
    product = split[8]
    width = grad_q.shape[-1]
    head_dim = width // H
    scaling = head_dim**-0.5
    store_halves(q_high, q_low, Ellipsis, queries[...] + b_query[...])
    store_halves(k_high, k_low, Ellipsis, kv[:, 0:width])
    store_halves(v_high, v_low, Ellipsis, kv[:, width : 2 * width] + b_value[...])
    store_halves(g_high, g_low, Ellipsis, grad[...])
    product[...] = grad[...] * attended[...]
    grad_q[...] = jnp.zeros(grad_q.shape, jnp.float32)
    grad_kv[...] = jnp.zeros(grad_kv.shape, jnp.float32)

    def step(head, _):
        at, mask = head_window(head, head_dim, width)
        start = jnp.minimum(head * head_dim // 128 * 128, width - WINDOW)
        at_value = pl.ds(pl.multiple_of(start + width, 128), WINDOW)
        small = mask.astype(jnp.bfloat16)

        def masked(high, low):
            return high[:, at] * small, low[:, at] * small

        upstream = masked(g_high, g_low)
        prob = probs[head]
        grad_prob = three(upstream, (v_high[:, at], v_low[:, at]), NT)
        term = jnp.sum(product[:, at] * mask, axis=-1, keepdims=True)
        score = halves(prob * (grad_prob - term) * scaling)
        grad_q[:, at] = grad_q[:, at] + three(score, masked(k_high, k_low), NN)
        grad_kv[:, at] = grad_kv[:, at] + three(score, masked(q_high, q_low), TN)
        grad_kv[:, at_value] = grad_kv[:, at_value] + three(halves(prob), upstream, TN)
        return 0

    lax.fori_loop(0, H, step, 0, unroll=4)


def cross_attention_back(queries, b_query, kv, b_value, probs, attended, grad):
    rows, width = queries.shape
    keys = kv.shape[0]
    q_part = pltpu.VMEM((rows, width), jnp.bfloat16)
    k_part = pltpu.VMEM((keys, width), jnp.bfloat16)
    return pl.pallas_call(
        cross_attention_back_kernel,
        out_shape=(
            jax.ShapeDtypeStruct((rows, width), jnp.float32),
            jax.ShapeDtypeStruct(kv.shape, jnp.float32),
        ),
        in_specs=[VMEM_SPEC] * 7,
        out_specs=[VMEM_SPEC] * 2,
        scratch_shapes=[q_part] * 4 + [k_part] * 4 + [pltpu.VMEM((rows, width), jnp.float32)],
        compiler_params=pltpu.CompilerParams(vmem_limit_bytes=52 << 20),
        cost_estimate=LIGHT,
    )(queries, b_query.reshape(1, width), kv, b_value.reshape(1, width), probs, attended, grad)


MLP_ROWS = 256


def mlp_kernel(
    hidden, cotangent, w_first, b_first, w_second,
    grad_hidden, out, grad_first, grad_second, grad_bias,
    first_high, first_low, second_high, second_low,
):
    @pl.when(pl.program_id(0) == 0)
    def _():
        first_high[...], first_low[...] = halves(w_first[...])
        second_high[...], second_low[...] = halves(w_second[...])
        grad_first[...] = jnp.zeros(grad_first.shape, jnp.float32)
        grad_second[...] = jnp.zeros(grad_second.shape, jnp.float32)
        grad_bias[...] = jnp.zeros(grad_bias.shape, jnp.float32)

    first = (first_high[...], first_low[...])
    second = (second_high[...], second_low[...])
    tokens, upstream = halves(hidden[...]), halves(cotangent[...])
    u = three(tokens, first, NN) + b_first[...]
    slope = math.sqrt(2.0 / math.pi)
    t = jnp.tanh(slope * (u + 0.044715 * (u * u * u)))
    active = halves(0.5 * u * (1.0 + t))
    derivative = 0.5 * (1.0 + t) + 0.5 * u * (1.0 - t * t) * slope * (1.0 + 0.134145 * (u * u))
    grad_pre = three(upstream, second, NT) * derivative
    grad_bias[...] = grad_bias[...] + jnp.sum(grad_pre, axis=0, keepdims=True)
    grad_pre = halves(grad_pre)
    grad_hidden[...] = three(grad_pre, first, NT)
    out[...] = three(active, second, NN)
    grad_first[...] = grad_first[...] + three(tokens, grad_pre, TN)
    grad_second[...] = grad_second[...] + three(active, upstream, TN)


def mlp(hidden, cotangent, w_first, b_first, w_second):
    rows, width = hidden.shape
    units = w_first.shape[1]
    f32 = jnp.float32
    tile = pl.BlockSpec((MLP_ROWS, width), lambda i: (i, 0))

    def fixed(*shape):
        return pl.BlockSpec(shape, lambda i: (0, 0))

    return pl.pallas_call(
        mlp_kernel,
        grid=(rows // MLP_ROWS,),
        out_shape=(
            jax.ShapeDtypeStruct((rows, width), f32), jax.ShapeDtypeStruct((rows, width), f32),
            jax.ShapeDtypeStruct((width, units), f32), jax.ShapeDtypeStruct((units, width), f32),
            jax.ShapeDtypeStruct((1, units), f32),
        ),
        in_specs=[tile, tile, fixed(width, units), fixed(1, units), fixed(units, width)],
        out_specs=[tile, tile, fixed(width, units), fixed(units, width), fixed(1, units)],
        scratch_shapes=[
            pltpu.VMEM((width, units), jnp.bfloat16), pltpu.VMEM((width, units), jnp.bfloat16),
            pltpu.VMEM((units, width), jnp.bfloat16), pltpu.VMEM((units, width), jnp.bfloat16),
        ],
        compiler_params=pltpu.CompilerParams(vmem_limit_bytes=50 << 20),
        cost_estimate=LIGHT,
    )(hidden, cotangent, w_first, b_first.reshape(1, units), w_second)


def assemble_kernel(axis, dim, *refs):
    blocks, whole = refs[:-1], refs[-1]
    own = lax.axis_index(axis)
    for k, block in enumerate(blocks):
        length = block.shape[dim]
        start = pl.multiple_of((own ^ k) * length, length)
        where = (slice(None),) * dim + (pl.ds(start, length),)
        whole[where] = block[...]


def assemble(blocks, axis, dim):
    shape = list(blocks[0].shape)
    shape[dim] *= len(blocks)
    size = 4 * len(blocks) * blocks[0].size
    return pl.pallas_call(
        partial(assemble_kernel, axis, dim),
        out_shape=jax.ShapeDtypeStruct(tuple(shape), jnp.float32),
        in_specs=[pl.BlockSpec(memory_space=pltpu.VMEM)] * len(blocks),
        out_specs=pl.BlockSpec(memory_space=pltpu.VMEM),
        compiler_params=pltpu.CompilerParams(vmem_limit_bytes=24 << 20),
        cost_estimate=LIGHT,
    )(*blocks)


def gather_rows(shard):
    return lax.all_gather(shard, "patch", axis=0, tiled=True)


def scatter_rows(whole):
    return lax.psum_scatter(whole, "patch", scatter_dimension=0, tiled=True)


def gather_tokens(rows):
    return token_gather(rows) if small_patch() else gather_rows(rows)


def block_of(array, axis_name, k, dim):
    length = array.shape[dim] // lax.axis_size(axis_name)
    start = (lax.axis_index(axis_name) ^ k) * length
    return lax.dynamic_slice_in_dim(array, start, length, axis=dim)


def over_chips(blocks):
    return [
        blocks[0],
        swap(blocks[1], "patch", 2),
        swap(blocks[2], "patch", 4),
        swap(blocks[3], "patch", 6),
    ]


def to_own_columns(weight):
    if not small_patch():
        return lax.all_to_all(weight, "patch", 1, 0, tiled=True)
    length = weight.shape[0]
    blocks = [block_of(weight, "patch", k, 1) for k in range(8)]
    theirs = swap(jnp.concatenate(blocks[1::2], axis=0), "patch", 1)
    both = [
        jnp.concatenate([kept, theirs[j * length : (j + 1) * length]], axis=0)
        for j, kept in enumerate(blocks[::2])
    ]
    halves = []
    for block in over_chips(both):
        halves += [block[:length], block[length:]]
    return assemble(halves, "patch", 0)


def to_columns(x):
    return lax.all_to_all(x, "frame", split_axis=1, concat_axis=0, tiled=True)


def to_slots(x):
    return lax.all_to_all(x, "frame", split_axis=0, concat_axis=1, tiled=True)


def scatter_tokens(parts):
    return token_scatter(parts) if small_patch() else scatter_rows(parts)


def open_up(block_input, cotangent, frame_slot, small, kv_part, weight):
    frame_number = frame_slot.astype(jnp.float32)
    if not small_patch():
        kv = all_sum(kv_part, "patch")
        return (
            to_columns(block_input),
            to_columns(cotangent),
            all_sum(placed(frame_number, "frame"), "frame"),
            all_sum(small, "patch"),
            lax.all_gather(kv, "frame", axis=0, tiled=True),
            gather_rows(weight),
        )
    count = frame_slot.shape[0]
    rows = -(-small.shape[0] // 1024) * 8
    tokens, later, slots, summed, kv, whole = begin(
        block_input, cotangent, padded(frame_number, 8), padded(small, rows), kv_part, weight
    )
    summed = summed.reshape(-1)[: small.shape[0]]
    slots = slots[:, 0, :count].reshape(-1)
    return tokens, later, slots, summed, kv, whole


def mlp_part(hidden, cotangent, w_first, b_first, w_second):
    if small_patch():
        *parts, grad_bias = mlp(hidden, cotangent, w_first, b_first, w_second)
        return (*parts, grad_bias[0])
    pre = matmul(hidden, w_first) + b_first
    active, pull = jax.vjp(partial(jax.nn.gelu, approximate=True), pre)
    grad_pre = pull(matmul_nt(cotangent, w_second))[0]
    return (
        matmul_nt(grad_pre, w_first),
        matmul(active, w_second),
        matmul_tn(hidden, grad_pre),
        matmul_tn(active, cotangent),
        jnp.sum(grad_pre, axis=0),
    )


def mid_way(parts, kv, residual, gate, bias, weights):
    if not small_patch():
        kv = lax.psum_scatter(all_sum(kv, "patch"), "frame", scatter_dimension=0, tiled=True)
        total = scatter_rows(parts)
        block = residual + gate * (total + bias).reshape(residual.shape)
        return total, kv, to_slots(block), [scatter_rows(w) for w in weights]
    total, kv, block, *weights = middle(parts, kv, residual, gate, bias, *weights)
    return total, kv, block, weights


def close_up(weights, kv, tokens, small, caption, columns):
    clips, length = lax.axis_size("frame"), caption.shape[1]
    if not small_patch():
        weights = [scatter_rows(weights[0]), *weights[1:]]
        weights = [lax.psum(w, "frame") for w in weights]
        whole = lax.all_gather(caption, "patch", axis=0, tiled=True)
        whole = lax.all_gather(whole, "frame", axis=0)
        whole = jnp.transpose(whole, (0, 2, 1))
        small = all_sum(all_sum(small, "patch"), "frame")
        columns = lax.all_to_all(columns, "patch", 0, 1, tiled=True)
        return weights, lax.psum(kv, "frame"), to_slots(tokens), small, whole, columns
    rows = -(-small.shape[0] // 1024) * 8
    *weights, kv, tokens, summed, whole, blocks = finish(
        *weights, kv, tokens, padded(small, rows), caption, columns
    )
    columns = jnp.transpose(blocks, (1, 0, 2)).reshape(blocks.shape[1], -1)
    whole = jnp.transpose(whole, (1, 3, 0, 2)).reshape(clips, length, -1)
    return weights, kv, tokens, summed.reshape(-1)[: small.shape[0]], whole, columns


def on_device(
    block_input,
    out_cotangent,
    caption,
    cond,
    ada_weight,
    ada_bias,
    qkv_weight,
    q_bias,
    v_bias,
    attn_out_weight,
    attn_out_bias,
    cross_q_weight,
    cross_q_bias,
    cross_kv_weight,
    cross_v_bias,
    cross_out_weight,
    cross_out_bias,
    fc1_weight,
    fc1_bias,
    fc2_weight,
    fc2_bias,
    frame_slot,
    clip_id,
    patch_mask,
    caption_mask,
):
    width = block_input.shape[-1]
    cond_act, silu_pull = jax.vjp(jax.nn.silu, cond)
    cond_own = own_part(cond_act, "patch", 1)
    modulation_part = matmul(cond_own, ada_weight)
    biases = (
        ada_bias, q_bias, v_bias, attn_out_bias, cross_q_bias, cross_v_bias, cross_out_bias,
        fc2_bias,
    )
    small = jnp.concatenate(
        [modulation_part.reshape(-1)] + [placed(b, "patch") for b in biases]
    )
    caption_rows = caption.reshape(CLIPS * CAP, width)
    caption_share = own_part(own_part(caption_rows, "frame", 0), "patch", 1)
    tokens_in, cotangent, frame_pos, small, caption_kv, w_qkv = open_up(
        block_input,
        out_cotangent,
        frame_slot,
        small,
        matmul(caption_share, cross_kv_weight),
        qkv_weight,
    )
    w_two = gather_rows(jnp.concatenate([attn_out_weight, cross_q_weight], axis=1))
    w_attn, w_cross_q = jnp.split(w_two, 2, axis=1)
    w_cross_o = gather_rows(cross_out_weight)
    slots, cols, _ = tokens_in.shape
    rows = slots * cols
    clip_own = own_part(clip_id, "frame", 0)
    column_mask = own_part(patch_mask, "frame", 0).astype(jnp.float32)[:, None]
    place = modulation_part.size
    modulation = small[:place].reshape(modulation_part.shape)
    whole = []
    for b in biases:
        length = b.shape[0] * lax.axis_size("patch")
        whole.append(small[place : place + length])
        place += length
    b_ada, b_query, b_value, b_attn, b_cross_q, b_cross_v, b_cross_o, b_second = whole
    modulation = modulation + b_ada
    clip_onehot = (clip_own[:, None] == jnp.arange(CLIPS, dtype=jnp.int32)[None, :]).astype(
        jnp.float32
    )
    per_column = jnp.dot(clip_onehot, modulation, precision=lax.Precision.HIGHEST)
    shift_one, scale_one, gate_one, shift_two, scale_two, gate_two = jnp.split(
        per_column, 6, axis=1
    )

    grad_mlp = (column_mask * gate_two * cotangent).reshape(rows, width)
    normed_one, inverse_one = normalize(tokens_in)
    hidden_one = (normed_one * (1.0 + scale_one) + shift_one).reshape(rows, width)
    qkv_rows = matmul(hidden_one, w_qkv)
    grad_mlp_all = gather_rows(after(grad_mlp, qkv_rows))
    qkv = qkv_rows.reshape(slots, cols, 3 * width)
    probs, attended = frame_attention(qkv, b_query, b_value, *frame_tables(frame_pos))
    attended_rows = attended.reshape(rows, width)
    attn_branch = (matmul(attended_rows, w_attn) + b_attn).reshape(slots, cols, width)
    after_attn = tokens_in + column_mask * gate_one * attn_branch
    after_attn_rows = after_attn.reshape(rows, width)
    cross_queries = matmul(after_attn_rows, w_cross_q)
    w_first = to_own_columns(after(fc1_weight, cross_queries))
    cross_queries = after(cross_queries, grad_mlp_all)
    key_clip = jnp.arange(CLIPS * CAP, dtype=jnp.int32) // CAP
    caption_ok = (clip_own[:, None] == key_clip[None, :]) & (
        caption_mask.reshape(CLIPS * CAP)[None, :] > 0
    )
    caption_ok = jnp.tile(caption_ok.astype(jnp.float32), (slots, 1))
    cross_probs, cross_rows = cross_attention(
        cross_queries, b_cross_q, caption_kv, b_cross_v, caption_ok
    )
    cross_branch = (matmul(cross_rows, w_cross_o) + b_cross_o).reshape(slots, cols, width)
    after_cross = after_attn + column_mask * cross_branch
    normed_two, inverse_two = normalize(after_cross)
    hidden_two = (normed_two * (1.0 + scale_two) + shift_two).reshape(rows, width)

    hidden_all = gather_tokens(after(hidden_two, w_first))
    grad_parts, mlp_parts, grad_w_first, grad_w_second, grad_b_first = mlp_part(
        hidden_all, grad_mlp_all, w_first, fc1_bias, fc2_weight
    )
    grad_hidden_two = scatter_tokens(grad_parts)
    grad_hidden_two = grad_hidden_two.reshape(slots, cols, width)
    grad_b_second = jnp.sum(grad_mlp, axis=0)

    grad_shift_two = jnp.sum(grad_hidden_two, axis=0)
    grad_scale_two = jnp.sum(grad_hidden_two * normed_two, axis=0)
    grad_after_cross = cotangent + normalize_back(
        grad_hidden_two * (1.0 + scale_two), normed_two, inverse_two
    )
    grad_cross_branch = (column_mask * grad_after_cross).reshape(rows, width)
    grad_w_cross_o = matmul_tn(cross_rows, grad_cross_branch)
    grad_b_cross_o = jnp.sum(grad_cross_branch, axis=0)
    grad_w_first = lax.psum(grad_w_first, "frame")
    grad_w_second = lax.psum(after(grad_w_second, grad_w_first), "frame")
    grad_cross_rows = matmul_nt(grad_cross_branch, w_cross_o)
    grad_cross_queries, grad_kv = cross_attention_back(
        cross_queries, b_cross_q, caption_kv, b_cross_v, cross_probs, cross_rows, grad_cross_rows
    )
    grad_cross_queries = after(grad_cross_queries, grad_w_first)
    grad_w_cross_q = matmul_tn(after_attn_rows, grad_cross_queries)
    grad_b_cross_q = jnp.sum(grad_cross_queries, axis=0)
    grad_cross_queries = after(grad_cross_queries, grad_w_cross_q)
    grad_after_attn = grad_after_cross + matmul_nt(grad_cross_queries, w_cross_q).reshape(
        slots, cols, width
    )
    grad_attn_rows = (column_mask * gate_one * grad_after_attn).reshape(rows, width)
    grad_gate_one = jnp.sum(column_mask * attn_branch * grad_after_attn, axis=0)
    grad_w_attn = matmul_tn(attended_rows, grad_attn_rows)
    grad_b_attn = jnp.sum(grad_attn_rows, axis=0)
    grad_attn_rows = after(grad_attn_rows, grad_w_attn)
    grad_attended = matmul_nt(grad_attn_rows, w_attn).reshape(slots, cols, width)
    grad_qkv = frame_attention_back(
        qkv, b_query, b_value, probs, attended, grad_attended
    ).reshape(rows, 3 * width)
    grad_w_qkv = matmul_tn(hidden_one, grad_qkv)
    mlp_sum, grad_kv_share, block_out, shares = mid_way(
        after(mlp_parts, grad_w_qkv),
        grad_kv,
        after_cross,
        column_mask * gate_two,
        b_second,
        (grad_w_attn, grad_w_cross_q, grad_w_cross_o),
    )
    grad_w_cross_kv = matmul_tn(caption_share, grad_kv_share)
    grad_b_cross_v = jnp.sum(grad_kv_share[:, width:], axis=0)
    grad_caption_share = matmul_nt(cross_kv_weight, grad_kv_share)
    mlp_branch = (mlp_sum + b_second).reshape(slots, cols, width)
    grad_gate_two = jnp.sum(column_mask * mlp_branch * cotangent, axis=0)
    grad_b_query = jnp.sum(grad_qkv[:, :width], axis=0)
    grad_b_value = jnp.sum(grad_qkv[:, 2 * width :], axis=0)
    grad_hidden_one = matmul_nt(grad_qkv, w_qkv).reshape(slots, cols, width)
    grad_shift_one = jnp.sum(grad_hidden_one, axis=0)
    grad_scale_one = jnp.sum(grad_hidden_one * normed_one, axis=0)
    input_grad = grad_after_attn + normalize_back(
        grad_hidden_one * (1.0 + scale_one), normed_one, inverse_one
    )
    grad_per_column = jnp.concatenate(
        [
            grad_shift_one,
            grad_scale_one,
            grad_gate_one,
            grad_shift_two,
            grad_scale_two,
            grad_gate_two,
        ],
        axis=1,
    )
    grad_modulation_part = jnp.dot(
        clip_onehot.T, grad_per_column, precision=lax.Precision.HIGHEST
    )
    first = (lax.axis_index("patch") == 0).astype(jnp.float32)
    bias_grads = (
        grad_b_query,
        grad_b_value,
        grad_b_attn,
        grad_b_cross_q,
        grad_b_cross_v * first,
        grad_b_cross_o,
        grad_b_second,
    )
    small_grads = jnp.concatenate(
        [grad_modulation_part.reshape(-1)] + list(bias_grads) + [placed(grad_b_first, "patch")]
    )
    weights, grad_w_cross_kv, input_grad, small_grads, grad_caption, grad_w_first = close_up(
        (grad_w_qkv, *shares),
        grad_w_cross_kv, input_grad, small_grads, grad_caption_share, grad_w_first,
    )
    place = grad_modulation_part.size
    grad_modulation = small_grads[:place].reshape(grad_modulation_part.shape)
    own_biases = []
    for b in bias_grads:
        own_biases.append(own_part(small_grads[place : place + b.shape[0]], "patch", 0))
        place += b.shape[0]
    g_query, g_value, g_attn, g_cross_q, g_cross_v, g_cross_o, g_second = own_biases
    grad_b_first = own_part(small_grads[place:], "patch", 0)
    grad_w_ada = matmul_tn(cond_own, grad_modulation)
    grad_b_ada = own_part(jnp.sum(grad_modulation, axis=0), "patch", 0)
    grad_cond_own = matmul_nt(grad_modulation, ada_weight)
    if small_patch():
        grad_cond_act = jnp.transpose(spread(grad_cond_own), (1, 0, 2)).reshape(cond.shape)
    else:
        grad_cond_act = all_sum(placed(grad_cond_own, "patch"), "patch")
    grad_cond = silu_pull(grad_cond_act)[0]

    grad_w_qkv, grad_w_attn, grad_w_cross_q, grad_w_cross_o = weights
    return (
        block_out,
        input_grad,
        grad_caption,
        grad_cond,
        grad_w_ada,
        grad_b_ada,
        grad_w_qkv,
        g_query,
        g_value,
        grad_w_attn,
        g_attn,
        grad_w_cross_q,
        g_cross_q,
        grad_w_cross_kv,
        g_cross_v,
        grad_w_cross_o,
        g_cross_o,
        grad_w_first,
        grad_b_first,
        grad_w_second,
        g_second,
    )


def solution(mesh):
    tokens = P("frame", "patch", None)
    weight = P("patch", None)
    vector = P("patch")
    parameters = (
        weight, vector, weight, vector, vector, weight, vector, weight, vector,
        weight, vector, weight, vector, weight, vector, weight, vector,
    )
    in_specs = (tokens, tokens, P(), P()) + parameters + (P("frame"), vector, vector, P())
    out_specs = (tokens, tokens, P(), P()) + parameters
    return jax.shard_map(
        on_device, mesh=mesh, in_specs=in_specs, out_specs=out_specs, check_vma=False
    )
```

```python
import math
from functools import partial

import jax
import jax.numpy as jnp
from jax import lax
from jax.experimental import pallas as pl
from jax.experimental.pallas import tpu as pltpu
from jax.sharding import PartitionSpec as P

H = 16
CAP = 120
FRAMES = 17
CLIPS = 4


EPSILON = 1e-06
BEST = lax.Precision.HIGH
LIGHT = pl.CostEstimate(flops=0, bytes_accessed=1 << 16, transcendentals=0)


def matmul(left, right):
    return jnp.dot(left, right, precision=BEST)


def matmul_nt(left, right):
    return lax.dot_general(left, right, (((1,), (1,)), ((), ())), precision=BEST)


def matmul_tn(left, right):
    return lax.dot_general(left, right, (((0,), (0,)), ((), ())), precision=BEST)


def normalize(rows):
    average = jnp.mean(rows, axis=-1, keepdims=True)
    centred = rows - average
    spread = jnp.mean(centred * centred, axis=-1, keepdims=True)
    inverse = lax.rsqrt(spread + EPSILON)
    return (centred * inverse, inverse)


def normalize_back(grad_normed, normed, inverse):
    first_mean = jnp.mean(grad_normed, axis=-1, keepdims=True)
    second_mean = jnp.mean(grad_normed * normed, axis=-1, keepdims=True)
    return inverse * (grad_normed - first_mean - normed * second_mean)


def swap(value, axis, bit):
    size = lax.axis_size(axis)
    return lax.ppermute(value, axis, [(i, i ^ bit) for i in range(size)])


def all_sum(value, axis):
    bit = 1
    while bit < lax.axis_size(axis):
        value = value + swap(value, axis, bit)
        bit *= 2
    return value


def placed(vector, axis):
    length = vector.shape[-1]
    whole = jnp.zeros(vector.shape[:-1] + (length * lax.axis_size(axis),), vector.dtype)
    return lax.dynamic_update_slice_in_dim(
        whole, vector, lax.axis_index(axis) * length, axis=vector.ndim - 1
    )


def own_part(array, axis, dim):
    length = array.shape[dim] // lax.axis_size(axis)
    return lax.dynamic_slice_in_dim(array, lax.axis_index(axis) * length, length, axis=dim)


def after(value, done):
    return lax.optimization_barrier((value, done))[0]


def small_patch():
    return lax.axis_size("patch") == 8 and lax.axis_size("frame") == 4


def padded(vector, rows):
    return jnp.pad(vector, (0, rows * 128 - vector.shape[0])).reshape(rows, 128)


def greet(partners):
    barrier = pltpu.get_barrier_semaphore()
    for partner in partners:
        pl.semaphore_signal(barrier, inc=1, device_id={"patch": partner}, device_id_type=pl.DeviceIdType.MESH)
    pl.semaphore_wait(barrier, len(partners))


def remote(source, target, send_sems, recv_sems, index, device):
    return pltpu.make_async_remote_copy(
        src_ref=source, dst_ref=target, send_sem=send_sems.at[index], recv_sem=recv_sems.at[index],
        device_id={"patch": device}, device_id_type=pl.DeviceIdType.MESH)


def token_gather_kernel(rows, whole, local_sem, send_sems, recv_sems):
    own = lax.axis_index("patch")
    core, along_x, along_y, across = own ^ 1, own ^ 2, own ^ 4, own ^ 6
    greet((core, along_x, along_y))
    length = rows.shape[0] // 4
    sent = []

    def piece(owner, q):
        return whole.at[owner, pl.ds(q * length, length)]

    def send(source, owner, q, index, device):
        copy = remote(source, piece(owner, q), send_sems, recv_sems, index, device)
        copy.start()
        sent.append(copy)

    def arrived(owner, q, index, device):
        remote(piece(owner, q), piece(owner, q), send_sems, recv_sems, index, device).wait_recv()

    mine = pltpu.make_async_copy(rows, whole.at[own], local_sem)
    mine.start()
    for q_x, q_y in ((0, 2), (1, 3), (2, 0), (3, 1)):
        send(rows.at[pl.ds(q_x * length, length)], own, q_x, q_x, along_x)
        send(rows.at[pl.ds(q_y * length, length)], own, q_y, 4 + q_y, along_y)
    for q in range(4):
        send(rows.at[pl.ds(q * length, length)], own, q, 12 + q, core)
    for q_x, q_y in ((0, 2), (1, 3), (2, 0), (3, 1)):
        arrived(along_x, q_x, q_x, along_x)
        if q_x < 2:
            send(piece(along_x, q_x), along_x, q_x, 8 + q_x, along_y)
        send(piece(along_x, q_x), along_x, q_x, 16 + q_x, core)
        arrived(along_y, q_y, 4 + q_y, along_y)
        if q_y >= 2:
            send(piece(along_y, q_y), along_y, q_y, 8 + q_y, along_x)
        send(piece(along_y, q_y), along_y, q_y, 20 + q_y, core)
    for q in (0, 2, 1, 3):
        arrived(across, q, 8 + q, along_y if q < 2 else along_x)
        send(piece(across, q), across, q, 24 + q, core)
    for q in range(4):
        arrived(core, q, 12 + q, core)
        arrived(core ^ 2, q, 16 + q, core)
        arrived(core ^ 4, q, 20 + q, core)
        arrived(core ^ 6, q, 24 + q, core)
    for copy in sent:
        copy.wait_send()
    mine.wait()


def token_gather(rows):
    length, width = rows.shape
    return pl.pallas_call(
        token_gather_kernel,
        out_shape=jax.ShapeDtypeStruct((8, length, width), jnp.float32),
        in_specs=[pl.BlockSpec(memory_space=pltpu.VMEM)],
        out_specs=pl.BlockSpec(memory_space=pl.ANY),
        scratch_shapes=[pltpu.SemaphoreType.DMA, pltpu.SemaphoreType.DMA((28,)), pltpu.SemaphoreType.DMA((28,))],
        compiler_params=pltpu.CompilerParams(collective_id=0, has_side_effects=True, vmem_limit_bytes=16 << 20),
        cost_estimate=LIGHT,
    )(rows).reshape(8 * length, width)


def token_scatter_kernel(parts, total, kept, theirs, by_x, by_y, from_x, from_y, local_sems, send_sems, recv_sems):
    own = lax.axis_index("patch")
    core, along_x, along_y = own ^ 1, own ^ 2, own ^ 4
    greet((core, along_x, along_y))
    half = total.shape[0] // 2
    upper, lower = pl.ds(0, half), pl.ds(half, half)
    order = (3, 2, 1, 0)
    sent, loads = [], {}

    def send(source, target, index, device):
        copy = remote(source, target, send_sems, recv_sems, index, device)
        copy.start()
        sent.append(copy)

    def arrived(target, index, device):
        remote(target, target, send_sems, recv_sems, index, device).wait_recv()

    for j in order:
        send(parts.at[core ^ (2 * j)], theirs.at[j], j, core)
        loads[j] = pltpu.make_async_copy(parts.at[own ^ (2 * j)], kept.at[j], local_sems.at[j])
        loads[j].start()

    def add_cores(j):
        loads[j].wait()
        arrived(theirs.at[j], j, core)
        kept[j] = kept[j] + theirs[j]

    add_cores(3)
    send(kept.at[3, upper], by_x, 4, along_x)
    send(kept.at[3, lower], by_y, 5, along_y)
    add_cores(2)
    send(kept.at[2, lower], from_y.at[lower], 6, along_y)
    add_cores(1)
    send(kept.at[1, upper], from_x.at[upper], 7, along_x)
    add_cores(0)
    arrived(by_x, 4, along_x)
    kept[2, upper] = kept[2, upper] + by_x[...]
    send(kept.at[2, upper], from_y.at[upper], 8, along_y)
    arrived(by_y, 5, along_y)
    kept[1, lower] = kept[1, lower] + by_y[...]
    send(kept.at[1, lower], from_x.at[lower], 9, along_x)
    arrived(from_y.at[lower], 6, along_y)
    arrived(from_x.at[upper], 7, along_x)
    arrived(from_y.at[upper], 8, along_y)
    arrived(from_x.at[lower], 9, along_x)
    total[...] = kept[0] + from_x[...] + from_y[...]
    for copy in sent:
        copy.wait_send()


def token_scatter(parts):
    length, width = parts.shape[0] // 8, parts.shape[1]
    block = (length, width)
    return pl.pallas_call(
        token_scatter_kernel,
        out_shape=jax.ShapeDtypeStruct(block, jnp.float32),
        in_specs=[pl.BlockSpec(memory_space=pl.ANY)],
        out_specs=pl.BlockSpec(memory_space=pltpu.VMEM),
        scratch_shapes=[
            pltpu.VMEM((4,) + block, jnp.float32), pltpu.VMEM((4,) + block, jnp.float32),
            pltpu.VMEM((length // 2, width), jnp.float32), pltpu.VMEM((length // 2, width), jnp.float32),
            pltpu.VMEM(block, jnp.float32), pltpu.VMEM(block, jnp.float32),
            pltpu.SemaphoreType.DMA((4,)), pltpu.SemaphoreType.DMA((10,)), pltpu.SemaphoreType.DMA((10,)),
        ],
        compiler_params=pltpu.CompilerParams(collective_id=1, has_side_effects=True, vmem_limit_bytes=32 << 20),
        cost_estimate=LIGHT,
    )(parts.reshape((8,) + block))


class Links:
    def __init__(self, send_sems, recv_sems):
        self.send_sems, self.recv_sems = send_sems, recv_sems
        self.count = 0
        self.sent = []

    def plan(self):
        self.count += 1
        return self.count - 1

    def copy(self, source, target, index, device):
        return pltpu.make_async_remote_copy(
            src_ref=source, dst_ref=target, send_sem=self.send_sems.at[index],
            recv_sem=self.recv_sems.at[index], device_id=device,
            device_id_type=pl.DeviceIdType.MESH,
        )

    def send(self, source, target, index, device):
        self.copy(source, target, index, device).start()
        self.sent.append((source, index, device))

    def wait(self, target, index, device):
        self.copy(target, target, index, device).wait_recv()

    def drain(self):
        for source, index, device in self.sent:
            self.copy(source, source, index, device).wait_send()


def greet_all(devices):
    barrier = pltpu.get_barrier_semaphore()
    for device in devices:
        pl.semaphore_signal(barrier, inc=1, device_id=device, device_id_type=pl.DeviceIdType.MESH)
    pl.semaphore_wait(barrier, len(devices))


def begin_kernel(
    tokens, later, slots, small, kv, weight,
    tokens_out, later_out, slots_out, small_out, kv_out, weight_out,
    weight_sem, small_1, small_2, small_got, kv_1, kv_2, kv_got_core, kv_got_1, kv_got_2,
    send_sems, recv_sems,
):
    me, z = lax.axis_index("patch"), lax.axis_index("frame")
    core, x, y = ({"patch": me ^ k} for k in (1, 2, 4))
    frames = [None] + [{"frame": z ^ k} for k in (1, 2, 3)]
    greet_all([core, x, y] + frames[1:])
    links = Links(send_sems, recv_sems)
    count, part = tokens.shape[0], tokens.shape[1] // 4
    rows, width = kv_1.shape

    def columns(k):
        return pl.ds(pl.multiple_of((z ^ k) * part, part), part)

    def of_slots(k):
        return pl.ds((z ^ k) * count, count)

    half = pl.multiple_of((me % 2) * width, 128)
    other = pl.multiple_of((1 - me % 2) * width, 128)
    mine, theirs = pl.ds(half, width), pl.ds(other, width)

    length = weight.shape[0]
    weight_at = [[links.plan() for _ in range(7)] for _ in range(3)]
    weight_core = links.plan()

    def piece(k, u, first=0, size=length):
        start = pl.multiple_of((me ^ k) * length + first, 8)
        return weight_out.at[pl.ds(start, size), pl.ds(u * width, width)]

    whole = weight_out.at[pl.ds(pl.multiple_of(me * length, 8), length)]
    sibling = weight_out.at[pl.ds(pl.multiple_of((me ^ 1) * length, 8), length)]
    own_copy = pltpu.make_async_copy(weight, whole, weight_sem)

    def weight_links(u):
        source = weight.at[:, pl.ds(u * width, width)]
        links.send(source, piece(0, u), weight_at[u][0], x)
        links.send(source, piece(0, u), weight_at[u][1], y)

    def weight_across(u):
        middle_row = length // 2
        links.wait(piece(2, u), weight_at[u][0], x)
        upper = piece(2, u, 0, middle_row)
        links.send(upper, upper, weight_at[u][2], y)
        links.send(piece(2, u), piece(2, u), weight_at[u][4], core)
        links.wait(piece(4, u), weight_at[u][1], y)
        lower = piece(4, u, middle_row, middle_row)
        links.send(lower, lower, weight_at[u][3], x)
        links.send(piece(4, u), piece(4, u), weight_at[u][5], core)

    def weight_last(u):
        middle_row = length // 2
        links.wait(piece(6, u, 0, middle_row), weight_at[u][2], y)
        links.wait(piece(6, u, middle_row, middle_row), weight_at[u][3], x)
        links.send(piece(6, u), piece(6, u), weight_at[u][6], core)

    at = links.plan()
    links.send(small, small_got.at[0], at, core)
    at_kv = links.plan()
    links.send(kv.at[:, theirs], kv_got_core, at_kv, core)
    own_copy.start()
    token_at = [None] + [links.plan() for _ in range(3)]
    slot_at = [None] + [links.plan() for _ in range(3)]
    later_at = [None] + [links.plan() for _ in range(3)]
    for k in (1, 2, 3):
        links.send(slots, slots_out.at[z], slot_at[k], frames[k])
        links.send(tokens.at[:, columns(k)], tokens_out.at[of_slots(0)], token_at[k], frames[k])
    for k in (1, 2, 3):
        links.send(later.at[:, columns(k)], later_out.at[of_slots(0)], later_at[k], frames[k])

    links.wait(small_got.at[0], at, core)
    small_1[...] = small[...] + small_got[0]
    at = links.plan()
    links.send(small_1, small_got.at[1], at, x)
    links.wait(kv_got_core, at_kv, core)
    kv_1[...] = kv[:, mine] + kv_got_core[...]
    upper, lower = pl.ds(0, 64), pl.ds(64, rows - 64)
    at_u, at_l = links.plan(), links.plan()
    links.send(kv_1.at[upper], kv_got_1.at[upper], at_u, x)
    links.send(kv_1.at[lower], kv_got_1.at[lower], at_l, y)
    weight_links(0)
    links.send(weight, whole, weight_core, core)
    slots_out[z] = slots[...]
    tokens_out[of_slots(0)] = tokens[:, columns(0)]
    later_out[of_slots(0)] = later[:, columns(0)]
    links.wait(small_got.at[1], at, x)
    small_2[...] = small_1[...] + small_got[1]
    at = links.plan()
    links.send(small_2, small_got.at[2], at, y)
    links.wait(kv_got_1.at[upper], at_u, x)
    links.wait(kv_got_1.at[lower], at_l, y)
    kv_2[...] = kv_1[...] + kv_got_1[...]
    at_u, at_l = links.plan(), links.plan()
    links.send(kv_2.at[upper], kv_got_2.at[upper], at_u, y)
    links.send(kv_2.at[lower], kv_got_2.at[lower], at_l, x)
    weight_links(1)
    links.wait(small_got.at[2], at, y)
    small_out[...] = small_2[...] + small_got[2]
    weight_across(0)
    weight_links(2)
    links.wait(kv_got_2.at[upper], at_u, y)
    links.wait(kv_got_2.at[lower], at_l, x)

    def share(k, columns):
        return kv_out.at[pl.ds(pl.multiple_of((z ^ k) * rows, rows), rows), columns]

    kv_out[pl.ds(pl.multiple_of(z * rows, rows), rows), mine] = kv_2[...] + kv_got_2[...]
    kv_at = [None] + [links.plan() for _ in range(3)]
    core_at = [links.plan() for _ in range(4)]
    for k in (1, 2, 3):
        links.send(share(0, mine), share(0, mine), kv_at[k], frames[k])
    links.send(share(0, mine), share(0, mine), core_at[0], core)
    weight_across(1)
    weight_last(0)
    weight_across(2)
    weight_last(1)
    for k in (1, 2, 3):
        links.wait(slots_out.at[z ^ k], slot_at[k], frames[k])
        links.wait(tokens_out.at[of_slots(k)], token_at[k], frames[k])
        links.wait(later_out.at[of_slots(k)], later_at[k], frames[k])
    for k in (1, 2, 3):
        links.wait(share(k, mine), kv_at[k], frames[k])
        links.send(share(k, mine), share(k, mine), core_at[k], core)
    weight_last(2)
    for k in range(4):
        links.wait(share(k, theirs), core_at[k], core)
    links.wait(sibling, weight_core, core)
    for u in range(3):
        for i, k in enumerate((2, 4, 6)):
            links.wait(piece(k ^ 1, u), weight_at[u][4 + i], core)
    own_copy.wait()
    links.drain()


def begin(tokens, later, slots, small, kv, weight):
    count, cols, width = tokens.shape
    rows = kv.shape[0]
    f32, vmem = jnp.float32, pl.BlockSpec(memory_space=pltpu.VMEM)
    hbm = pl.BlockSpec(memory_space=pl.ANY)
    half = pltpu.VMEM((rows, width), f32)
    return pl.pallas_call(
        begin_kernel,
        out_shape=(
            jax.ShapeDtypeStruct((4 * count, cols // 4, width), f32),
            jax.ShapeDtypeStruct((4 * count, cols // 4, width), f32),
            jax.ShapeDtypeStruct((4,) + slots.shape, f32),
            jax.ShapeDtypeStruct(small.shape, f32),
            jax.ShapeDtypeStruct((4 * rows, 2 * width), f32),
            jax.ShapeDtypeStruct((8 * weight.shape[0], weight.shape[1]), f32),
        ),
        in_specs=[vmem] * 5 + [hbm],
        out_specs=[vmem] * 5 + [hbm],
        scratch_shapes=[
            pltpu.SemaphoreType.DMA,
            pltpu.VMEM(small.shape, f32), pltpu.VMEM(small.shape, f32),
            pltpu.VMEM((3,) + small.shape, f32), half, half, half, half, half,
            pltpu.SemaphoreType.DMA((48,)), pltpu.SemaphoreType.DMA((48,)),
        ],
        compiler_params=pltpu.CompilerParams(
            collective_id=2, has_side_effects=True, vmem_limit_bytes=36 << 20
        ),
        cost_estimate=LIGHT,
    )(tokens, later, slots, small, kv, weight)


UNITS = 3


def finish_kernel(
    first, attn, cross_q, cross_o, kv, tokens, small, caption, columns,
    first_out, attn_out, cross_q_out, cross_o_out, kv_out, tokens_out, small_out, caption_out,
    columns_out, columns_got, columns_sem,
    kept, theirs, by_x, by_y, from_x, from_y, along_z, across_z,
    small_sums, small_got, small_z, load_sems, credit, send_sems, recv_sems,
):
    me, z = lax.axis_index("patch"), lax.axis_index("frame")
    outer = (z == 0) | (z == 3)
    inner = (z == 1) | (z == 2)
    core, x, y = ({"patch": me ^ k} for k in (1, 2, 4))
    frames = [None] + [{"frame": z ^ k} for k in (1, 2, 3)]
    near, facing = frames[1], frames[3]
    chips = {2: x, 4: y, 6: {"patch": me ^ 6}}
    greet_all([core, x, y, chips[6]] + frames[1:])
    links = Links(send_sems, recv_sems)
    rows, width = by_x.shape[1] * 2, by_x.shape[2]
    upper, lower = pl.ds(0, rows // 2), pl.ds(rows // 2, rows // 2)
    count, part = tokens_out.shape[0], tokens_out.shape[1] // 4

    token_at = [None] + [links.plan() for _ in range(3)]

    def send_tokens(k):
        where = pl.ds(pl.multiple_of(z * part, part), part)
        if k == 0:
            tokens_out[:, where] = tokens[pl.ds(z * count, count)]
        else:
            source = tokens.at[pl.ds((z ^ k) * count, count)]
            links.send(source, tokens_out.at[:, where], token_at[k], frames[k])

    def frame_steps(value, result, near_got, facing_got):
        up, over, down = links.plan(), links.plan(), links.plan()

        def one():
            @pl.when(outer)
            def _():
                links.copy(value, near_got, up, near).start()

        def two():
            @pl.when(inner)
            def _():
                links.wait(near_got, up, near)
                near_got[...] = near_got[...] + value[...]
                links.copy(near_got, facing_got, over, facing).start()

        def three():
            @pl.when(inner)
            def _():
                links.wait(facing_got, over, facing)
                result[...] = near_got[...] + facing_got[...]
                links.copy(result, near_got, down, near).start()

        def four():
            @pl.when(outer)
            def _():
                links.wait(near_got, down, near)
                result[...] = near_got[...]
                links.copy(value, value, up, near).wait_send()

            @pl.when(inner)
            def _():
                links.copy(near_got, near_got, over, facing).wait_send()
                links.copy(result, result, down, near).wait_send()

        return one, two, three, four

    def piece(ref, u):
        return ref.at[:, pl.ds(u * width, width)]

    pairs = [(kept.at[u, 0], piece(first_out, u)) for u in range(UNITS)]
    pairs += [(attn, attn_out), (cross_q, cross_q_out), (cross_o, cross_o_out)]
    pairs += [(piece(kv, u), piece(kv_out, u)) for u in range(2)]
    steps = [
        frame_steps(value, result, along_z.at[i], across_z.at[i])
        for i, (value, result) in enumerate(pairs)
    ]
    small_steps = frame_steps(small_sums.at[2], small_out, small_z.at[0], small_z.at[1])

    core_at = [[links.plan() for _ in range(4)] for _ in range(UNITS)]
    link_at = [[links.plan() for _ in range(6)] for _ in range(UNITS)]

    def source(u, device, j):
        start = pl.multiple_of((device ^ (2 * j)) * rows, rows)
        return first.at[pl.ds(start, rows), pl.ds(u * width, width)]

    def load(u, j):
        return pltpu.make_async_copy(source(u, me, j), kept.at[u, j], load_sems.at[u, j])

    def to_core(u):
        if u >= 2:
            pl.semaphore_wait(credit.at[u - 2], 1)
        for j in (3, 2, 1, 0):
            links.send(source(u, me ^ 1, j), theirs.at[u % 2, j], core_at[u][j], core)

    def add_cores(u, j):
        load(u, j).wait()
        links.wait(theirs.at[u % 2, j], core_at[u][j], core)
        kept[u, j] = kept[u, j] + theirs[u % 2, j]

    def stage_one(u):
        at = link_at[u]
        add_cores(u, 3)
        links.send(kept.at[u, 3, upper], by_x.at[u], at[0], x)
        links.send(kept.at[u, 3, lower], by_y.at[u], at[1], y)
        add_cores(u, 2)
        links.send(kept.at[u, 2, lower], from_y.at[u, lower], at[2], y)
        add_cores(u, 1)
        links.send(kept.at[u, 1, upper], from_x.at[u, upper], at[3], x)
        add_cores(u, 0)
        if u + 2 < UNITS:
            pl.semaphore_signal(
                credit.at[u], inc=1, device_id=core, device_id_type=pl.DeviceIdType.MESH
            )
            to_core(u + 2)

    def stage_two(u):
        at = link_at[u]
        links.wait(by_x.at[u], at[0], x)
        kept[u, 2, upper] = kept[u, 2, upper] + by_x[u]
        links.send(kept.at[u, 2, upper], from_y.at[u, upper], at[4], y)
        links.wait(by_y.at[u], at[1], y)
        kept[u, 1, lower] = kept[u, 1, lower] + by_y[u]
        links.send(kept.at[u, 1, lower], from_x.at[u, lower], at[5], x)

    def stage_three(u):
        at = link_at[u]
        links.wait(from_y.at[u, lower], at[2], y)
        links.wait(from_x.at[u, upper], at[3], x)
        links.wait(from_y.at[u, upper], at[4], y)
        links.wait(from_x.at[u, lower], at[5], x)
        kept[u, 0] = kept[u, 0] + from_x[u] + from_y[u]
        steps[u][0]()

    block = columns_got.shape[1] // 2
    columns_at = {k: links.plan() for k in (2, 4, 6)}
    columns_core = {k: links.plan() for k in (0, 2, 4, 6)}

    def chip_rows(k):
        return columns.at[pl.ds(pl.multiple_of((me ^ k) // 2 * (2 * block), 8), 2 * block)]

    own_rows = pltpu.make_async_copy(chip_rows(0), columns_got.at[0], columns_sem.at[0])

    def own_block(k):
        core_rows = pl.ds(pl.multiple_of(me % 2 * block, 8), block)
        return pltpu.make_async_copy(
            columns_got.at[k // 2, core_rows], columns_out.at[me ^ k], columns_sem.at[1 + k // 2]
        )

    def send_columns(k):
        links.send(chip_rows(k), columns_got.at[k // 2], columns_at[k], chips[k])

    def columns_over():
        other_rows = pl.ds(pl.multiple_of((1 - me % 2) * block, 8), block)
        own_rows.wait()
        for k in (0, 2, 4, 6):
            if k:
                links.wait(columns_got.at[k // 2], columns_at[k], chips[k])
            links.send(
                columns_got.at[k // 2, other_rows], columns_out.at[me ^ k], columns_core[k], core
            )
            own_block(k).start()

    def columns_end():
        for k in (0, 2, 4, 6):
            links.wait(columns_out.at[me ^ 1 ^ k], columns_core[k], core)
            own_block(k).wait()

    caption_at = [links.plan() for _ in range(10)]

    def caption_frames():
        caption_out[me, z] = caption[...]
        for k in (1, 2, 3):
            links.send(caption, caption_out.at[me, z], caption_at[k - 1], frames[k])

    def caption_x():
        for k in (1, 2, 3):
            links.wait(caption_out.at[me, z ^ k], caption_at[k - 1], frames[k])
        links.send(caption_out.at[me], caption_out.at[me], caption_at[3], x)

    def caption_y():
        links.wait(caption_out.at[me ^ 2], caption_at[3], x)
        for i, k in enumerate((0, 2)):
            links.send(caption_out.at[me ^ k], caption_out.at[me ^ k], caption_at[4 + i], y)

    def caption_core():
        for i, k in enumerate((0, 2)):
            links.wait(caption_out.at[me ^ 4 ^ k], caption_at[4 + i], y)
        for i, k in enumerate((0, 2, 4, 6)):
            links.send(caption_out.at[me ^ k], caption_out.at[me ^ k], caption_at[6 + i], core)

    def caption_end():
        for i, k in enumerate((0, 2, 4, 6)):
            links.wait(caption_out.at[me ^ 1 ^ k], caption_at[6 + i], core)

    small_at = [links.plan() for _ in range(3)]
    links.send(small, small_got.at[0], small_at[0], core)
    caption_frames()
    own_rows.start()
    for u in range(UNITS):
        for j in (3, 2, 1, 0):
            load(u, j).start()
    for i in (6, 7, 3, 4, 5):
        steps[i][0]()
    for u in range(2):
        to_core(u)
    links.wait(small_got.at[0], small_at[0], core)
    small_sums[0] = small[...] + small_got[0]
    links.send(small_sums.at[0], small_got.at[1], small_at[1], x)
    stage_one(0)
    links.wait(small_got.at[1], small_at[1], x)
    small_sums[1] = small_sums[0] + small_got[1]
    links.send(small_sums.at[1], small_got.at[2], small_at[2], y)
    stage_one(1)
    stage_two(0)
    links.wait(small_got.at[2], small_at[2], y)
    small_sums[2] = small_sums[1] + small_got[2]
    small_steps[0]()
    steps[6][1]()
    steps[7][1]()
    stage_one(2)
    stage_three(0)
    steps[3][1]()
    stage_two(1)
    steps[6][2]()
    steps[7][2]()
    steps[4][1]()
    stage_two(2)
    stage_three(1)
    caption_x()
    for k in (2, 4, 6):
        send_columns(k)
    steps[3][2]()
    steps[5][1]()
    small_steps[1]()
    stage_three(2)
    for k in range(4):
        send_tokens(k)
    steps[4][2]()
    small_steps[2]()
    steps[0][1]()
    caption_y()
    steps[5][2]()
    steps[1][1]()
    steps[0][2]()
    caption_core()
    steps[2][1]()
    steps[1][2]()
    steps[2][2]()
    for step in steps + [small_steps]:
        step[3]()
    columns_over()
    caption_end()
    columns_end()
    for k in (1, 2, 3):
        where = pl.ds(pl.multiple_of((z ^ k) * part, part), part)
        links.wait(tokens_out.at[:, where], token_at[k], frames[k])
    links.drain()


def finish(first, attn, cross_q, cross_o, kv, tokens, small, caption, columns):
    rows, width = attn.shape
    count, part = tokens.shape[0] // 4, tokens.shape[1]
    f32, vmem = jnp.float32, pl.BlockSpec(memory_space=pltpu.VMEM)
    hbm = pl.BlockSpec(memory_space=pl.ANY)

    def shape(*sizes):
        return jax.ShapeDtypeStruct(sizes, f32)

    return pl.pallas_call(
        finish_kernel,
        out_shape=(
            shape(rows, 3 * width), shape(rows, width), shape(rows, width), shape(rows, width),
            shape(rows, 2 * width), shape(count, 4 * part, tokens.shape[2]), shape(*small.shape),
            shape(8, 4, *caption.shape), shape(8, columns.shape[0] // 8, columns.shape[1]),
        ),
        in_specs=[hbm] + [vmem] * 7 + [hbm],
        out_specs=[vmem] * 8 + [hbm],
        scratch_shapes=[
            pltpu.VMEM((4, columns.shape[0] // 4, columns.shape[1]), f32),
            pltpu.SemaphoreType.DMA((5,)),
            pltpu.VMEM((UNITS, 4, rows, width), f32), pltpu.VMEM((2, 4, rows, width), f32),
            pltpu.VMEM((UNITS, rows // 2, width), f32), pltpu.VMEM((UNITS, rows // 2, width), f32),
            pltpu.VMEM((UNITS, rows, width), f32), pltpu.VMEM((UNITS, rows, width), f32),
            pltpu.VMEM((8, rows, width), f32), pltpu.VMEM((8, rows, width), f32),
            pltpu.VMEM((3,) + small.shape, f32), pltpu.VMEM((3,) + small.shape, f32),
            pltpu.VMEM((2,) + small.shape, f32),
            pltpu.SemaphoreType.DMA((UNITS, 4)), pltpu.SemaphoreType.REGULAR((1,)),
            pltpu.SemaphoreType.DMA((112,)), pltpu.SemaphoreType.DMA((112,)),
        ],
        compiler_params=pltpu.CompilerParams(
            collective_id=3, has_side_effects=True, vmem_limit_bytes=58 << 20
        ),
        cost_estimate=LIGHT,
    )(first, attn, cross_q, cross_o, kv, tokens, small, caption, columns)


def middle_kernel(
    parts, kv, residual, gate, bias, attn, cross_q, cross_o,
    total, kv_out, block_out, attn_out, cross_q_out, cross_o_out,
    w_kept, w_theirs, w_by_x, w_by_y, w_from_x, w_from_y, w_loads, credit, kv_sem,
    block, kept, theirs, by_x, by_y, from_x, from_y,
    kv_half, kv_core, kv_got, kv_1, kv_2, kv_got_1, kv_got_2,
    load_sems, send_sems, recv_sems,
):
    me, z = lax.axis_index("patch"), lax.axis_index("frame")
    core, x, y = ({"patch": me ^ k} for k in (1, 2, 4))
    frames = [None] + [{"frame": z ^ k} for k in (1, 2, 3)]
    greet_all([core, x, y] + frames[1:])
    links = Links(send_sems, recv_sems)
    rows, width = kv_1.shape
    half = pl.multiple_of((me % 2) * width, 128)
    other = pl.multiple_of((1 - me % 2) * width, 128)
    mine, others = pl.ds(half, width), pl.ds(other, width)

    def share(ref, k):
        return ref.at[pl.ds(pl.multiple_of((z ^ k) * rows, rows), rows)]

    grads, sums = (attn, cross_q, cross_o), (attn_out, cross_q_out, cross_o_out)
    length = attn_out.shape[0]
    top_rows, low_rows = pl.ds(0, length // 2), pl.ds(length // 2, length // 2)
    w_core_at = [[links.plan() for _ in range(4)] for _ in grads]
    w_at = [[links.plan() for _ in range(6)] for _ in grads]

    def w_source(u, device, j):
        start = pl.multiple_of((device ^ (2 * j)) * length, length)
        return grads[u].at[pl.ds(start, length)]

    def w_load(u, j):
        return pltpu.make_async_copy(w_source(u, me, j), w_kept.at[u, j], w_loads.at[u, j])

    def w_to_core(u):
        if u >= 2:
            pl.semaphore_wait(credit.at[u - 2], 1)
        for j in (3, 2, 1, 0):
            links.send(w_source(u, me ^ 1, j), w_theirs.at[u % 2, j], w_core_at[u][j], core)

    def w_add(u, j):
        w_load(u, j).wait()
        links.wait(w_theirs.at[u % 2, j], w_core_at[u][j], core)
        w_kept[u, j] = w_kept[u, j] + w_theirs[u % 2, j]

    def w_one(u):
        w_add(u, 3)
        links.send(w_kept.at[u, 3, top_rows], w_by_x.at[u], w_at[u][0], x)
        links.send(w_kept.at[u, 3, low_rows], w_by_y.at[u], w_at[u][1], y)
        w_add(u, 2)
        links.send(w_kept.at[u, 2, low_rows], w_from_y.at[u, low_rows], w_at[u][2], y)
        w_add(u, 1)
        links.send(w_kept.at[u, 1, top_rows], w_from_x.at[u, top_rows], w_at[u][3], x)
        w_add(u, 0)
        if u == 0:
            pl.semaphore_signal(
                credit.at[u], inc=1, device_id=core, device_id_type=pl.DeviceIdType.MESH
            )
            w_to_core(2)

    def w_two(u):
        links.wait(w_by_x.at[u], w_at[u][0], x)
        w_kept[u, 2, top_rows] = w_kept[u, 2, top_rows] + w_by_x[u]
        links.send(w_kept.at[u, 2, top_rows], w_from_y.at[u, top_rows], w_at[u][4], y)
        links.wait(w_by_y.at[u], w_at[u][1], y)
        w_kept[u, 1, low_rows] = w_kept[u, 1, low_rows] + w_by_y[u]
        links.send(w_kept.at[u, 1, low_rows], w_from_x.at[u, low_rows], w_at[u][5], x)

    def w_three(u):
        links.wait(w_from_y.at[u, low_rows], w_at[u][2], y)
        links.wait(w_from_x.at[u, top_rows], w_at[u][3], x)
        links.wait(w_from_y.at[u, top_rows], w_at[u][4], y)
        links.wait(w_from_x.at[u, low_rows], w_at[u][5], x)
        sums[u][...] = w_kept[u, 0] + w_from_x[u] + w_from_y[u]

    at_kv = links.plan()
    links.send(kv.at[:, others], kv_core, at_kv, core)
    kv_load = pltpu.make_async_copy(kv.at[:, mine], kv_half, kv_sem)
    kv_load.start()
    core_at = [links.plan() for _ in range(4)]
    loads = [
        pltpu.make_async_copy(parts.at[me ^ (2 * j)], kept.at[j], load_sems.at[j])
        for j in range(4)
    ]
    for j in (3, 2, 1, 0):
        links.send(parts.at[me ^ 1 ^ (2 * j)], theirs.at[j], core_at[j], core)
        loads[j].start()
    for u in range(3):
        for j in (3, 2, 1, 0):
            w_load(u, j).start()
    for u in range(2):
        w_to_core(u)
    kv_load.wait()
    links.wait(kv_core, at_kv, core)
    kv_half[...] = kv_half[...] + kv_core[...]
    kv_at = [None] + [links.plan() for _ in range(3)]
    for k in (1, 2, 3):
        links.send(share(kv_half, k), kv_got.at[k - 1], kv_at[k], frames[k])

    count = total.shape[0] // 2
    upper, lower = pl.ds(0, count), pl.ds(count, count)
    at = [links.plan() for _ in range(6)]

    def add_cores(j):
        loads[j].wait()
        links.wait(theirs.at[j], core_at[j], core)
        kept[j] = kept[j] + theirs[j]

    add_cores(3)
    links.send(kept.at[3, upper], by_x, at[0], x)
    links.send(kept.at[3, lower], by_y, at[1], y)
    add_cores(2)
    links.send(kept.at[2, lower], from_y.at[lower], at[2], y)
    add_cores(1)
    links.send(kept.at[1, upper], from_x.at[upper], at[3], x)
    add_cores(0)
    links.wait(by_x, at[0], x)
    kept[2, upper] = kept[2, upper] + by_x[...]
    links.send(kept.at[2, upper], from_y.at[upper], at[4], y)
    links.wait(by_y, at[1], y)
    kept[1, lower] = kept[1, lower] + by_y[...]
    links.send(kept.at[1, lower], from_x.at[lower], at[5], x)

    w_one(0)
    links.wait(from_y.at[lower], at[2], y)
    links.wait(from_x.at[upper], at[3], x)
    links.wait(from_y.at[upper], at[4], y)
    links.wait(from_x.at[lower], at[5], x)
    total[...] = kept[0] + from_x[...] + from_y[...]
    slots, part = residual.shape[0] // 4, residual.shape[1]
    block[...] = residual[...] + gate[...] * (total[...] + bias[...]).reshape(residual.shape)
    block_at = [None] + [links.plan() for _ in range(3)]
    place = pl.ds(pl.multiple_of(z * part, part), part)
    for k in (1, 2, 3):
        source = block.at[pl.ds((z ^ k) * slots, slots)]
        links.send(source, block_out.at[:, place], block_at[k], frames[k])
    block_out[:, place] = block[pl.ds(z * slots, slots)]
    w_one(1)
    w_two(0)
    for k in (1, 2, 3):
        links.wait(kv_got.at[k - 1], kv_at[k], frames[k])
    kv_1[...] = share(kv_half, 0)[...] + kv_got[0] + (kv_got[1] + kv_got[2])
    top, bottom = pl.ds(0, 64), pl.ds(64, rows - 64)
    at_u, at_l = links.plan(), links.plan()
    links.send(kv_1.at[top], kv_got_1.at[top], at_u, x)
    links.send(kv_1.at[bottom], kv_got_1.at[bottom], at_l, y)
    w_one(2)
    w_two(1)
    w_three(0)
    links.wait(kv_got_1.at[top], at_u, x)
    links.wait(kv_got_1.at[bottom], at_l, y)
    kv_2[...] = kv_1[...] + kv_got_1[...]
    at_u, at_l = links.plan(), links.plan()
    links.send(kv_2.at[top], kv_got_2.at[top], at_u, y)
    links.send(kv_2.at[bottom], kv_got_2.at[bottom], at_l, x)
    links.wait(kv_got_2.at[top], at_u, y)
    links.wait(kv_got_2.at[bottom], at_l, x)
    kv_out[:, mine] = kv_2[...] + kv_got_2[...]
    at_core = links.plan()
    links.send(kv_out.at[:, mine], kv_out.at[:, mine], at_core, core)
    w_two(2)
    w_three(1)
    w_three(2)
    links.wait(kv_out.at[:, others], at_core, core)
    for k in (1, 2, 3):
        there = pl.ds(pl.multiple_of((z ^ k) * part, part), part)
        links.wait(block_out.at[:, there], block_at[k], frames[k])
    links.drain()


def middle(parts, kv, residual, gate, bias, attn, cross_q, cross_o):
    slots, cols, _ = residual.shape
    count = attn.shape[0] // 8
    length, width = parts.shape[0] // 8, parts.shape[1]
    rows = kv.shape[0] // 4
    f32, vmem = jnp.float32, pl.BlockSpec(memory_space=pltpu.VMEM)
    hbm = pl.BlockSpec(memory_space=pl.ANY)
    block, half = (length, width), pltpu.VMEM((rows, width), f32)
    return pl.pallas_call(
        middle_kernel,
        out_shape=(
            jax.ShapeDtypeStruct(block, f32), jax.ShapeDtypeStruct((rows, 2 * width), f32),
            jax.ShapeDtypeStruct((slots // 4, 4 * cols, width), f32),
            *[jax.ShapeDtypeStruct((count, width), f32)] * 3,
        ),
        in_specs=[hbm] * 2 + [vmem] * 3 + [hbm] * 3,
        out_specs=[vmem] * 6,
        scratch_shapes=[
            pltpu.VMEM((3, 4, count, width), f32), pltpu.VMEM((2, 4, count, width), f32),
            pltpu.VMEM((3, count // 2, width), f32), pltpu.VMEM((3, count // 2, width), f32),
            pltpu.VMEM((3, count, width), f32), pltpu.VMEM((3, count, width), f32),
            pltpu.SemaphoreType.DMA((3, 4)), pltpu.SemaphoreType.REGULAR((1,)),
            pltpu.SemaphoreType.DMA,
            pltpu.VMEM((slots, cols, width), f32),
            pltpu.VMEM((4,) + block, f32), pltpu.VMEM((4,) + block, f32),
            pltpu.VMEM((length // 2, width), f32), pltpu.VMEM((length // 2, width), f32),
            pltpu.VMEM(block, f32), pltpu.VMEM(block, f32),
            pltpu.VMEM((4 * rows, width), f32), pltpu.VMEM((4 * rows, width), f32),
            pltpu.VMEM((3, rows, width), f32), half, half, half, half,
            pltpu.SemaphoreType.DMA((4,)), pltpu.SemaphoreType.DMA((56,)),
            pltpu.SemaphoreType.DMA((56,)),
        ],
        compiler_params=pltpu.CompilerParams(
            collective_id=4, has_side_effects=True, vmem_limit_bytes=58 << 20
        ),
        cost_estimate=LIGHT,
    )(parts.reshape((8,) + block), kv, residual, gate[None], bias[None], attn, cross_q, cross_o)


def spread_kernel(block, whole, send_sems, recv_sems):
    me = lax.axis_index("patch")
    peers = [None] + [{"patch": me ^ k} for k in range(1, 8)]
    greet_all(peers[1:])
    links = Links(send_sems, recv_sems)
    at = [links.plan() for _ in range(8)]
    for k in range(1, 8):
        links.send(block, whole.at[me], at[k], peers[k])
    whole[me] = block[...]
    for k in range(1, 8):
        links.wait(whole.at[me ^ k], at[k], peers[k])
    links.drain()


def spread(block):
    vmem = pl.BlockSpec(memory_space=pltpu.VMEM)
    return pl.pallas_call(
        spread_kernel,
        out_shape=jax.ShapeDtypeStruct((8,) + block.shape, jnp.float32),
        in_specs=[vmem],
        out_specs=vmem,
        scratch_shapes=[pltpu.SemaphoreType.DMA((8,)), pltpu.SemaphoreType.DMA((8,))],
        compiler_params=pltpu.CompilerParams(collective_id=5, has_side_effects=True),
    )(block)


def halves(x):
    high = x.astype(jnp.bfloat16)
    return high, (x - high.astype(jnp.float32)).astype(jnp.bfloat16)


NN, NT, TN = (((1,), (0,)), ((), ())), (((1,), (1,)), ((), ())), (((0,), (0,)), ((), ()))


def three(left, right, dims):
    def dot(a, b):
        return lax.dot_general(a, b, dims, preferred_element_type=jnp.float32)

    return dot(left[0], right[0]) + (dot(left[0], right[1]) + dot(left[1], right[0]))


WINDOW = 256


def head_window(head, head_dim, width):
    start = jnp.minimum(head * head_dim // 128 * 128, width - WINDOW)
    lane = lax.broadcasted_iota(jnp.int32, (1, WINDOW), 1) - (head * head_dim - start)
    mask = ((lane >= 0) & (lane < head_dim)).astype(jnp.float32)
    return pl.ds(pl.multiple_of(start, 128), WINDOW), mask


def softmax_last(scores):
    exponent = jnp.exp(scores - jnp.max(scores, axis=-1, keepdims=True))
    return exponent / jnp.sum(exponent, axis=-1, keepdims=True)


GROUP = 8


def grouped(ref, group, lanes):
    slots = ref.shape[0]
    value = ref[:, group * GROUP : (group + 1) * GROUP, lanes]
    return value.reshape(slots * GROUP, value.shape[-1])


def store_halves(high, low, index, value):
    high[index], low[index] = halves(value)


def frame_attention_kernel(qkv, b_query, b_value, distance, allowed, probs, out, *split):
    (q_high, q_low, k_high, k_low, v_high, v_low), total = split[:6], split[6]
    slots, width = qkv.shape[0], out.shape[-1]
    head_dim = width // H
    scaling = head_dim**-0.5
    for g in range(2):
        store_halves(q_high, q_low, g, grouped(qkv, g, slice(0, width)) + b_query[...])
        store_halves(k_high, k_low, g, grouped(qkv, g, slice(width, 2 * width)))
        store_halves(
            v_high, v_low, g, grouped(qkv, g, slice(2 * width, 3 * width)) + b_value[...]
        )
    total[...] = jnp.zeros(total.shape, jnp.float32)

    def step(head, _):
        at, mask = head_window(head, head_dim, width)
        mask = mask.astype(jnp.bfloat16)
        slope = jnp.exp2(-8.0 / H * (jnp.full((1, 1), head, jnp.int32).astype(jnp.float32) + 1.0))
        for g in range(2):
            query = (q_high[g, :, at] * mask, q_low[g, :, at] * mask)
            scores = three(query, (k_high[g, :, at], k_low[g, :, at]), NT)
            scores = jnp.where(allowed[...] > 0, scores * scaling - slope * distance[...], -1e30)
            prob = softmax_last(scores)
            probs[head, g] = prob
            value = (v_high[g, :, at] * mask, v_low[g, :, at] * mask)
            total[g, :, at] = total[g, :, at] + three(halves(prob), value, NN)
        return 0

    lax.fori_loop(0, H, step, 0, unroll=4)
    for g in range(2):
        out[:, g * GROUP : (g + 1) * GROUP, :] = total[g].reshape(slots, GROUP, width)


def frame_tables(frame_pos):
    slots = frame_pos.shape[0]
    position = jnp.repeat(frame_pos, GROUP)
    column = jnp.tile(jnp.arange(GROUP), slots)
    distance = jnp.abs(position[:, None] - position[None, :])
    same = column[:, None] == column[None, :]
    return distance, (same & (position[None, :] < FRAMES - 0.5)).astype(jnp.float32)


VMEM_SPEC = pl.BlockSpec(memory_space=pltpu.VMEM)


def frame_attention(qkv, b_query, b_value, distance, allowed):
    slots, cols, width = qkv.shape[0], qkv.shape[1], qkv.shape[2] // 3
    rows = slots * GROUP
    part = pltpu.VMEM((2, rows, width), jnp.bfloat16)
    return pl.pallas_call(
        frame_attention_kernel,
        out_shape=(
            jax.ShapeDtypeStruct((H, 2, rows, rows), jnp.float32),
            jax.ShapeDtypeStruct((slots, cols, width), jnp.float32),
        ),
        in_specs=[VMEM_SPEC] * 5,
        out_specs=[VMEM_SPEC] * 2,
        scratch_shapes=[part] * 6 + [pltpu.VMEM((2, rows, width), jnp.float32)],
        compiler_params=pltpu.CompilerParams(vmem_limit_bytes=40 << 20),
        cost_estimate=LIGHT,
    )(qkv, b_query.reshape(1, width), b_value.reshape(1, width), distance, allowed)


def frame_attention_back_kernel(qkv, b_query, b_value, probs, attended, grad, out, *split):
    width = attended.shape[-1]
    slots, head_dim = qkv.shape[0], width // H
    scaling = head_dim**-0.5
    names = [(split[2 * i], split[2 * i + 1]) for i in range(4)]
    (q_high, q_low), (k_high, k_low), (v_high, v_low), (g_high, g_low) = names
    total, product = split[8], split[9]
    for g in range(2):
        store_halves(q_high, q_low, g, grouped(qkv, g, slice(0, width)) + b_query[...])
        store_halves(k_high, k_low, g, grouped(qkv, g, slice(width, 2 * width)))
        store_halves(
            v_high, v_low, g, grouped(qkv, g, slice(2 * width, 3 * width)) + b_value[...]
        )
        upstream = grouped(grad, g, slice(0, width))
        store_halves(g_high, g_low, g, upstream)
        product[g] = upstream * grouped(attended, g, slice(0, width))
    total[...] = jnp.zeros(total.shape, jnp.float32)

    def step(head, _):
        at, mask = head_window(head, head_dim, width)
        small = mask.astype(jnp.bfloat16)

        def masked(high, low, g):
            return high[g, :, at] * small, low[g, :, at] * small

        for g in range(2):
            upstream = masked(g_high, g_low, g)
            prob = probs[head, g]
            grad_prob = three(upstream, (v_high[g, :, at], v_low[g, :, at]), NT)
            term = jnp.sum(product[g, :, at] * mask, axis=-1, keepdims=True)
            score = halves(prob * (grad_prob - term) * scaling)
            total[0, g, :, at] = total[0, g, :, at] + three(score, masked(k_high, k_low, g), NN)
            total[1, g, :, at] = total[1, g, :, at] + three(score, masked(q_high, q_low, g), TN)
            total[2, g, :, at] = total[2, g, :, at] + three(halves(prob), upstream, TN)
        return 0

    lax.fori_loop(0, H, step, 0, unroll=4)
    for g in range(2):
        for i in range(3):
            out[:, g * GROUP : (g + 1) * GROUP, i * width : (i + 1) * width] = total[
                i, g
            ].reshape(slots, GROUP, width)


def frame_attention_back(qkv, b_query, b_value, probs, attended, grad):
    slots, cols, width = attended.shape
    rows = slots * GROUP
    part = pltpu.VMEM((2, rows, width), jnp.bfloat16)
    return pl.pallas_call(
        frame_attention_back_kernel,
        out_shape=jax.ShapeDtypeStruct((slots, cols, 3 * width), jnp.float32),
        in_specs=[VMEM_SPEC] * 6,
        out_specs=VMEM_SPEC,
        scratch_shapes=[part] * 8
        + [pltpu.VMEM((3, 2, rows, width), jnp.float32), pltpu.VMEM((2, rows, width), jnp.float32)],
        compiler_params=pltpu.CompilerParams(vmem_limit_bytes=48 << 20),
        cost_estimate=LIGHT,
    )(qkv, b_query.reshape(1, width), b_value.reshape(1, width), probs, attended, grad)


def cross_attention_kernel(queries, b_query, kv, b_value, allowed, probs, out, *split):
    q_high, q_low, k_high, k_low, v_high, v_low = split
    width = out.shape[-1]
    head_dim = width // H
    scaling = head_dim**-0.5
    store_halves(q_high, q_low, Ellipsis, queries[...] + b_query[...])
    store_halves(k_high, k_low, Ellipsis, kv[:, 0:width])
    store_halves(v_high, v_low, Ellipsis, kv[:, width : 2 * width] + b_value[...])
    out[...] = jnp.zeros(out.shape, jnp.float32)

    def step(head, _):
        at, mask = head_window(head, head_dim, width)
        mask = mask.astype(jnp.bfloat16)
        query = (q_high[:, at] * mask, q_low[:, at] * mask)
        scores = three(query, (k_high[:, at], k_low[:, at]), NT)
        prob = softmax_last(jnp.where(allowed[...] > 0, scores * scaling, -1e30))
        probs[head] = prob
        value = (v_high[:, at] * mask, v_low[:, at] * mask)
        out[:, at] = out[:, at] + three(halves(prob), value, NN)
        return 0

    lax.fori_loop(0, H, step, 0, unroll=4)


def cross_attention(queries, b_query, kv, b_value, allowed):
    rows, width = queries.shape
    keys = kv.shape[0]
    q_part = pltpu.VMEM((rows, width), jnp.bfloat16)
    k_part = pltpu.VMEM((keys, width), jnp.bfloat16)
    return pl.pallas_call(
        cross_attention_kernel,
        out_shape=(
            jax.ShapeDtypeStruct((H, rows, keys), jnp.float32),
            jax.ShapeDtypeStruct((rows, width), jnp.float32),
        ),
        in_specs=[VMEM_SPEC] * 5,
        out_specs=[VMEM_SPEC] * 2,
        scratch_shapes=[q_part] * 2 + [k_part] * 4,
        compiler_params=pltpu.CompilerParams(vmem_limit_bytes=48 << 20),
        cost_estimate=LIGHT,
    )(queries, b_query.reshape(1, width), kv, b_value.reshape(1, width), allowed)


def cross_attention_back_kernel(
    queries, b_query, kv, b_value, probs, attended, grad, grad_q, grad_kv, *split
):
    names = [(split[2 * i], split[2 * i + 1]) for i in range(4)]
    (q_high, q_low), (g_high, g_low), (k_high, k_low), (v_high, v_low) = names
    product = split[8]
    width = grad_q.shape[-1]
    head_dim = width // H
    scaling = head_dim**-0.5
    store_halves(q_high, q_low, Ellipsis, queries[...] + b_query[...])
    store_halves(k_high, k_low, Ellipsis, kv[:, 0:width])
    store_halves(v_high, v_low, Ellipsis, kv[:, width : 2 * width] + b_value[...])
    store_halves(g_high, g_low, Ellipsis, grad[...])
    product[...] = grad[...] * attended[...]
    grad_q[...] = jnp.zeros(grad_q.shape, jnp.float32)
    grad_kv[...] = jnp.zeros(grad_kv.shape, jnp.float32)

    def step(head, _):
        at, mask = head_window(head, head_dim, width)
        start = jnp.minimum(head * head_dim // 128 * 128, width - WINDOW)
        at_value = pl.ds(pl.multiple_of(start + width, 128), WINDOW)
        small = mask.astype(jnp.bfloat16)

        def masked(high, low):
            return high[:, at] * small, low[:, at] * small

        upstream = masked(g_high, g_low)
        prob = probs[head]
        grad_prob = three(upstream, (v_high[:, at], v_low[:, at]), NT)
        term = jnp.sum(product[:, at] * mask, axis=-1, keepdims=True)
        score = halves(prob * (grad_prob - term) * scaling)
        grad_q[:, at] = grad_q[:, at] + three(score, masked(k_high, k_low), NN)
        grad_kv[:, at] = grad_kv[:, at] + three(score, masked(q_high, q_low), TN)
        grad_kv[:, at_value] = grad_kv[:, at_value] + three(halves(prob), upstream, TN)
        return 0

    lax.fori_loop(0, H, step, 0, unroll=4)


def cross_attention_back(queries, b_query, kv, b_value, probs, attended, grad):
    rows, width = queries.shape
    keys = kv.shape[0]
    q_part = pltpu.VMEM((rows, width), jnp.bfloat16)
    k_part = pltpu.VMEM((keys, width), jnp.bfloat16)
    return pl.pallas_call(
        cross_attention_back_kernel,
        out_shape=(
            jax.ShapeDtypeStruct((rows, width), jnp.float32),
            jax.ShapeDtypeStruct(kv.shape, jnp.float32),
        ),
        in_specs=[VMEM_SPEC] * 7,
        out_specs=[VMEM_SPEC] * 2,
        scratch_shapes=[q_part] * 4 + [k_part] * 4 + [pltpu.VMEM((rows, width), jnp.float32)],
        compiler_params=pltpu.CompilerParams(vmem_limit_bytes=52 << 20),
        cost_estimate=LIGHT,
    )(queries, b_query.reshape(1, width), kv, b_value.reshape(1, width), probs, attended, grad)


MLP_ROWS = 256


def mlp_kernel(
    hidden, cotangent, w_first, b_first, w_second,
    grad_hidden, out, grad_first, grad_second, grad_bias,
    first_high, first_low, second_high, second_low,
):
    @pl.when(pl.program_id(0) == 0)
    def _():
        first_high[...], first_low[...] = halves(w_first[...])
        second_high[...], second_low[...] = halves(w_second[...])
        grad_first[...] = jnp.zeros(grad_first.shape, jnp.float32)
        grad_second[...] = jnp.zeros(grad_second.shape, jnp.float32)
        grad_bias[...] = jnp.zeros(grad_bias.shape, jnp.float32)

    first = (first_high[...], first_low[...])
    second = (second_high[...], second_low[...])
    tokens, upstream = halves(hidden[...]), halves(cotangent[...])
    u = three(tokens, first, NN) + b_first[...]
    slope = math.sqrt(2.0 / math.pi)
    t = jnp.tanh(slope * (u + 0.044715 * (u * u * u)))
    active = halves(0.5 * u * (1.0 + t))
    derivative = 0.5 * (1.0 + t) + 0.5 * u * (1.0 - t * t) * slope * (1.0 + 0.134145 * (u * u))
    grad_pre = three(upstream, second, NT) * derivative
    grad_bias[...] = grad_bias[...] + jnp.sum(grad_pre, axis=0, keepdims=True)
    grad_pre = halves(grad_pre)
    grad_hidden[...] = three(grad_pre, first, NT)
    out[...] = three(active, second, NN)
    grad_first[...] = grad_first[...] + three(tokens, grad_pre, TN)
    grad_second[...] = grad_second[...] + three(active, upstream, TN)


def mlp(hidden, cotangent, w_first, b_first, w_second):
    rows, width = hidden.shape
    units = w_first.shape[1]
    f32 = jnp.float32
    tile = pl.BlockSpec((MLP_ROWS, width), lambda i: (i, 0))

    def fixed(*shape):
        return pl.BlockSpec(shape, lambda i: (0, 0))

    return pl.pallas_call(
        mlp_kernel,
        grid=(rows // MLP_ROWS,),
        out_shape=(
            jax.ShapeDtypeStruct((rows, width), f32), jax.ShapeDtypeStruct((rows, width), f32),
            jax.ShapeDtypeStruct((width, units), f32), jax.ShapeDtypeStruct((units, width), f32),
            jax.ShapeDtypeStruct((1, units), f32),
        ),
        in_specs=[tile, tile, fixed(width, units), fixed(1, units), fixed(units, width)],
        out_specs=[tile, tile, fixed(width, units), fixed(units, width), fixed(1, units)],
        scratch_shapes=[
            pltpu.VMEM((width, units), jnp.bfloat16), pltpu.VMEM((width, units), jnp.bfloat16),
            pltpu.VMEM((units, width), jnp.bfloat16), pltpu.VMEM((units, width), jnp.bfloat16),
        ],
        compiler_params=pltpu.CompilerParams(vmem_limit_bytes=50 << 20),
        cost_estimate=LIGHT,
    )(hidden, cotangent, w_first, b_first.reshape(1, units), w_second)


def assemble_kernel(axis, dim, *refs):
    blocks, whole = refs[:-1], refs[-1]
    own = lax.axis_index(axis)
    for k, block in enumerate(blocks):
        length = block.shape[dim]
        start = pl.multiple_of((own ^ k) * length, length)
        where = (slice(None),) * dim + (pl.ds(start, length),)
        whole[where] = block[...]


def assemble(blocks, axis, dim):
    shape = list(blocks[0].shape)
    shape[dim] *= len(blocks)
    size = 4 * len(blocks) * blocks[0].size
    return pl.pallas_call(
        partial(assemble_kernel, axis, dim),
        out_shape=jax.ShapeDtypeStruct(tuple(shape), jnp.float32),
        in_specs=[pl.BlockSpec(memory_space=pltpu.VMEM)] * len(blocks),
        out_specs=pl.BlockSpec(memory_space=pltpu.VMEM),
        compiler_params=pltpu.CompilerParams(vmem_limit_bytes=24 << 20),
        cost_estimate=LIGHT,
    )(*blocks)


def gather_rows(shard):
    return lax.all_gather(shard, "patch", axis=0, tiled=True)


def scatter_rows(whole):
    return lax.psum_scatter(whole, "patch", scatter_dimension=0, tiled=True)


def gather_tokens(rows):
    return token_gather(rows) if small_patch() else gather_rows(rows)


def block_of(array, axis_name, k, dim):
    length = array.shape[dim] // lax.axis_size(axis_name)
    start = (lax.axis_index(axis_name) ^ k) * length
    return lax.dynamic_slice_in_dim(array, start, length, axis=dim)


def over_chips(blocks):
    return [
        blocks[0],
        swap(blocks[1], "patch", 2),
        swap(blocks[2], "patch", 4),
        swap(blocks[3], "patch", 6),
    ]


def to_own_columns(weight):
    if not small_patch():
        return lax.all_to_all(weight, "patch", 1, 0, tiled=True)
    length = weight.shape[0]
    blocks = [block_of(weight, "patch", k, 1) for k in range(8)]
    theirs = swap(jnp.concatenate(blocks[1::2], axis=0), "patch", 1)
    both = [
        jnp.concatenate([kept, theirs[j * length : (j + 1) * length]], axis=0)
        for j, kept in enumerate(blocks[::2])
    ]
    halves = []
    for block in over_chips(both):
        halves += [block[:length], block[length:]]
    return assemble(halves, "patch", 0)


def to_columns(x):
    return lax.all_to_all(x, "frame", split_axis=1, concat_axis=0, tiled=True)


def to_slots(x):
    return lax.all_to_all(x, "frame", split_axis=0, concat_axis=1, tiled=True)


def scatter_tokens(parts):
    return token_scatter(parts) if small_patch() else scatter_rows(parts)


def open_up(block_input, cotangent, frame_slot, small, kv_part, weight):
    frame_number = frame_slot.astype(jnp.float32)
    if not small_patch():
        kv = all_sum(kv_part, "patch")
        return (
            to_columns(block_input),
            to_columns(cotangent),
            all_sum(placed(frame_number, "frame"), "frame"),
            all_sum(small, "patch"),
            lax.all_gather(kv, "frame", axis=0, tiled=True),
            gather_rows(weight),
        )
    count = frame_slot.shape[0]
    rows = -(-small.shape[0] // 1024) * 8
    tokens, later, slots, summed, kv, whole = begin(
        block_input, cotangent, padded(frame_number, 8), padded(small, rows), kv_part, weight
    )
    summed = summed.reshape(-1)[: small.shape[0]]
    slots = slots[:, 0, :count].reshape(-1)
    return tokens, later, slots, summed, kv, whole


def mlp_part(hidden, cotangent, w_first, b_first, w_second):
    if small_patch():
        *parts, grad_bias = mlp(hidden, cotangent, w_first, b_first, w_second)
        return (*parts, grad_bias[0])
    pre = matmul(hidden, w_first) + b_first
    active, pull = jax.vjp(partial(jax.nn.gelu, approximate=True), pre)
    grad_pre = pull(matmul_nt(cotangent, w_second))[0]
    return (
        matmul_nt(grad_pre, w_first),
        matmul(active, w_second),
        matmul_tn(hidden, grad_pre),
        matmul_tn(active, cotangent),
        jnp.sum(grad_pre, axis=0),
    )


def mid_way(parts, kv, residual, gate, bias, weights):
    if not small_patch():
        kv = lax.psum_scatter(all_sum(kv, "patch"), "frame", scatter_dimension=0, tiled=True)
        total = scatter_rows(parts)
        block = residual + gate * (total + bias).reshape(residual.shape)
        return total, kv, to_slots(block), [scatter_rows(w) for w in weights]
    total, kv, block, *weights = middle(parts, kv, residual, gate, bias, *weights)
    return total, kv, block, weights


def close_up(weights, kv, tokens, small, caption, columns):
    clips, length = lax.axis_size("frame"), caption.shape[1]
    if not small_patch():
        weights = [scatter_rows(weights[0]), *weights[1:]]
        weights = [lax.psum(w, "frame") for w in weights]
        whole = lax.all_gather(caption, "patch", axis=0, tiled=True)
        whole = lax.all_gather(whole, "frame", axis=0)
        whole = jnp.transpose(whole, (0, 2, 1))
        small = all_sum(all_sum(small, "patch"), "frame")
        columns = lax.all_to_all(columns, "patch", 0, 1, tiled=True)
        return weights, lax.psum(kv, "frame"), to_slots(tokens), small, whole, columns
    rows = -(-small.shape[0] // 1024) * 8
    *weights, kv, tokens, summed, whole, blocks = finish(
        *weights, kv, tokens, padded(small, rows), caption, columns
    )
    columns = jnp.transpose(blocks, (1, 0, 2)).reshape(blocks.shape[1], -1)
    whole = jnp.transpose(whole, (1, 3, 0, 2)).reshape(clips, length, -1)
    return weights, kv, tokens, summed.reshape(-1)[: small.shape[0]], whole, columns


def on_device(
    block_input,
    out_cotangent,
    caption,
    cond,
    ada_weight,
    ada_bias,
    qkv_weight,
    q_bias,
    v_bias,
    attn_out_weight,
    attn_out_bias,
    cross_q_weight,
    cross_q_bias,
    cross_kv_weight,
    cross_v_bias,
    cross_out_weight,
    cross_out_bias,
    fc1_weight,
    fc1_bias,
    fc2_weight,
    fc2_bias,
    frame_slot,
    clip_id,
    patch_mask,
    caption_mask,
):
    width = block_input.shape[-1]
    cond_act, silu_pull = jax.vjp(jax.nn.silu, cond)
    cond_own = own_part(cond_act, "patch", 1)
    modulation_part = matmul(cond_own, ada_weight)
    biases = (
        ada_bias, q_bias, v_bias, attn_out_bias, cross_q_bias, cross_v_bias, cross_out_bias,
        fc2_bias,
    )
    small = jnp.concatenate(
        [modulation_part.reshape(-1), placed(jnp.concatenate(biases), "patch")]
    )
    caption_rows = caption.reshape(CLIPS * CAP, width)
    caption_share = own_part(own_part(caption_rows, "frame", 0), "patch", 1)
    tokens_in, cotangent, frame_pos, small, caption_kv, w_qkv = open_up(
        block_input,
        out_cotangent,
        frame_slot,
        small,
        matmul(caption_share, cross_kv_weight),
        qkv_weight,
    )
    w_two = gather_rows(jnp.concatenate([attn_out_weight, cross_q_weight], axis=1))
    w_attn, w_cross_q = jnp.split(w_two, 2, axis=1)
    w_cross_o = gather_rows(cross_out_weight)
    slots, cols, _ = tokens_in.shape
    rows = slots * cols
    clip_own = own_part(clip_id, "frame", 0)
    column_mask = own_part(patch_mask, "frame", 0).astype(jnp.float32)[:, None]
    place = modulation_part.size
    modulation = small[:place].reshape(modulation_part.shape)
    table = small[place:].reshape(lax.axis_size("patch"), -1)
    whole, place = [], 0
    for b in biases:
        whole.append(table[:, place : place + b.shape[0]].reshape(-1))
        place += b.shape[0]
    b_ada, b_query, b_value, b_attn, b_cross_q, b_cross_v, b_cross_o, b_second = whole
    modulation = modulation + b_ada
    clip_onehot = (clip_own[:, None] == jnp.arange(CLIPS, dtype=jnp.int32)[None, :]).astype(
        jnp.float32
    )
    per_column = jnp.dot(clip_onehot, modulation, precision=lax.Precision.HIGHEST)
    shift_one, scale_one, gate_one, shift_two, scale_two, gate_two = jnp.split(
        per_column, 6, axis=1
    )

    grad_mlp = (column_mask * gate_two * cotangent).reshape(rows, width)
    normed_one, inverse_one = normalize(tokens_in)
    hidden_one = (normed_one * (1.0 + scale_one) + shift_one).reshape(rows, width)
    qkv_rows = matmul(hidden_one, w_qkv)
    grad_mlp_all = gather_rows(after(grad_mlp, qkv_rows))
    qkv = qkv_rows.reshape(slots, cols, 3 * width)
    probs, attended = frame_attention(qkv, b_query, b_value, *frame_tables(frame_pos))
    attended_rows = attended.reshape(rows, width)
    attn_branch = (matmul(attended_rows, w_attn) + b_attn).reshape(slots, cols, width)
    after_attn = tokens_in + column_mask * gate_one * attn_branch
    after_attn_rows = after_attn.reshape(rows, width)
    cross_queries = matmul(after_attn_rows, w_cross_q)
    w_first = to_own_columns(after(fc1_weight, cross_queries))
    cross_queries = after(cross_queries, grad_mlp_all)
    key_clip = jnp.arange(CLIPS * CAP, dtype=jnp.int32) // CAP
    caption_ok = (clip_own[:, None] == key_clip[None, :]) & (
        caption_mask.reshape(CLIPS * CAP)[None, :] > 0
    )
    caption_ok = jnp.tile(caption_ok.astype(jnp.float32), (slots, 1))
    cross_probs, cross_rows = cross_attention(
        cross_queries, b_cross_q, caption_kv, b_cross_v, caption_ok
    )
    cross_branch = (matmul(cross_rows, w_cross_o) + b_cross_o).reshape(slots, cols, width)
    after_cross = after_attn + column_mask * cross_branch
    normed_two, inverse_two = normalize(after_cross)
    hidden_two = (normed_two * (1.0 + scale_two) + shift_two).reshape(rows, width)

    hidden_all = gather_tokens(after(hidden_two, w_first))
    grad_parts, mlp_parts, grad_w_first, grad_w_second, grad_b_first = mlp_part(
        hidden_all, grad_mlp_all, w_first, fc1_bias, fc2_weight
    )
    grad_hidden_two = scatter_tokens(grad_parts)
    grad_hidden_two = grad_hidden_two.reshape(slots, cols, width)
    grad_b_second = jnp.sum(grad_mlp, axis=0)

    grad_shift_two = jnp.sum(grad_hidden_two, axis=0)
    grad_scale_two = jnp.sum(grad_hidden_two * normed_two, axis=0)
    grad_after_cross = cotangent + normalize_back(
        grad_hidden_two * (1.0 + scale_two), normed_two, inverse_two
    )
    grad_cross_branch = (column_mask * grad_after_cross).reshape(rows, width)
    grad_w_cross_o = matmul_tn(cross_rows, grad_cross_branch)
    grad_b_cross_o = jnp.sum(grad_cross_branch, axis=0)
    grad_w_first = lax.psum(grad_w_first, "frame")
    grad_w_second = lax.psum(after(grad_w_second, grad_w_first), "frame")
    grad_cross_rows = matmul_nt(grad_cross_branch, w_cross_o)
    grad_cross_queries, grad_kv = cross_attention_back(
        cross_queries, b_cross_q, caption_kv, b_cross_v, cross_probs, cross_rows, grad_cross_rows
    )
    grad_cross_queries = after(grad_cross_queries, grad_w_first)
    grad_w_cross_q = matmul_tn(after_attn_rows, grad_cross_queries)
    grad_b_cross_q = jnp.sum(grad_cross_queries, axis=0)
    grad_cross_queries = after(grad_cross_queries, grad_w_cross_q)
    grad_after_attn = grad_after_cross + matmul_nt(grad_cross_queries, w_cross_q).reshape(
        slots, cols, width
    )
    grad_attn_rows = (column_mask * gate_one * grad_after_attn).reshape(rows, width)
    grad_gate_one = jnp.sum(column_mask * attn_branch * grad_after_attn, axis=0)
    grad_w_attn = matmul_tn(attended_rows, grad_attn_rows)
    grad_b_attn = jnp.sum(grad_attn_rows, axis=0)
    grad_attn_rows = after(grad_attn_rows, grad_w_attn)
    grad_attended = matmul_nt(grad_attn_rows, w_attn).reshape(slots, cols, width)
    grad_qkv = frame_attention_back(
        qkv, b_query, b_value, probs, attended, grad_attended
    ).reshape(rows, 3 * width)
    grad_w_qkv = matmul_tn(hidden_one, grad_qkv)
    mlp_sum, grad_kv_share, block_out, shares = mid_way(
        after(mlp_parts, grad_w_qkv),
        grad_kv,
        after_cross,
        column_mask * gate_two,
        b_second,
        (grad_w_attn, grad_w_cross_q, grad_w_cross_o),
    )
    grad_w_cross_kv = matmul_tn(caption_share, grad_kv_share)
    grad_b_cross_v = jnp.sum(grad_kv_share[:, width:], axis=0)
    grad_caption_share = matmul_nt(cross_kv_weight, grad_kv_share)
    mlp_branch = (mlp_sum + b_second).reshape(slots, cols, width)
    grad_gate_two = jnp.sum(column_mask * mlp_branch * cotangent, axis=0)
    grad_b_query = jnp.sum(grad_qkv[:, :width], axis=0)
    grad_b_value = jnp.sum(grad_qkv[:, 2 * width :], axis=0)
    grad_hidden_one = matmul_nt(grad_qkv, w_qkv).reshape(slots, cols, width)
    grad_shift_one = jnp.sum(grad_hidden_one, axis=0)
    grad_scale_one = jnp.sum(grad_hidden_one * normed_one, axis=0)
    input_grad = grad_after_attn + normalize_back(
        grad_hidden_one * (1.0 + scale_one), normed_one, inverse_one
    )
    grad_per_column = jnp.concatenate(
        [
            grad_shift_one,
            grad_scale_one,
            grad_gate_one,
            grad_shift_two,
            grad_scale_two,
            grad_gate_two,
        ],
        axis=1,
    )
    grad_modulation_part = jnp.dot(
        clip_onehot.T, grad_per_column, precision=lax.Precision.HIGHEST
    )
    first = (lax.axis_index("patch") == 0).astype(jnp.float32)
    bias_grads = (
        grad_b_query,
        grad_b_value,
        grad_b_attn,
        grad_b_cross_q,
        grad_b_cross_v * first,
        grad_b_cross_o,
        grad_b_second,
    )
    bias_rows = jnp.concatenate(
        [b.reshape(lax.axis_size("patch"), -1) for b in bias_grads]
        + [placed(grad_b_first, "patch").reshape(lax.axis_size("patch"), -1)],
        axis=1,
    )
    small_grads = jnp.concatenate([grad_modulation_part.reshape(-1), bias_rows.reshape(-1)])
    weights, grad_w_cross_kv, input_grad, small_grads, grad_caption, grad_w_first = close_up(
        (grad_w_qkv, *shares),
        grad_w_cross_kv, input_grad, small_grads, grad_caption_share, grad_w_first,
    )
    place = grad_modulation_part.size
    grad_modulation = small_grads[:place].reshape(grad_modulation_part.shape)
    own_row = own_part(small_grads[place:], "patch", 0)
    length = bias_grads[0].shape[0] // lax.axis_size("patch")
    g_query, g_value, g_attn, g_cross_q, g_cross_v, g_cross_o, g_second = (
        own_row[i * length : (i + 1) * length] for i in range(7)
    )
    grad_b_first = own_row[7 * length :]
    grad_w_ada = matmul_tn(cond_own, grad_modulation)
    grad_b_ada = own_part(jnp.sum(grad_modulation, axis=0), "patch", 0)
    grad_cond_own = matmul_nt(grad_modulation, ada_weight)
    if small_patch():
        grad_cond_act = jnp.transpose(spread(grad_cond_own), (1, 0, 2)).reshape(cond.shape)
    else:
        grad_cond_act = all_sum(placed(grad_cond_own, "patch"), "patch")
    grad_cond = silu_pull(grad_cond_act)[0]

    grad_w_qkv, grad_w_attn, grad_w_cross_q, grad_w_cross_o = weights
    return (
        block_out,
        input_grad,
        grad_caption,
        grad_cond,
        grad_w_ada,
        grad_b_ada,
        grad_w_qkv,
        g_query,
        g_value,
        grad_w_attn,
        g_attn,
        grad_w_cross_q,
        g_cross_q,
        grad_w_cross_kv,
        g_cross_v,
        grad_w_cross_o,
        g_cross_o,
        grad_w_first,
        grad_b_first,
        grad_w_second,
        g_second,
    )


def solution(mesh):
    tokens = P("frame", "patch", None)
    weight = P("patch", None)
    vector = P("patch")
    parameters = (
        weight, vector, weight, vector, vector, weight, vector, weight, vector,
        weight, vector, weight, vector, weight, vector, weight, vector,
    )
    in_specs = (tokens, tokens, P(), P()) + parameters + (P("frame"), vector, vector, P())
    out_specs = (tokens, tokens, P(), P()) + parameters
    return jax.shard_map(
        on_device, mesh=mesh, in_specs=in_specs, out_specs=out_specs, check_vma=False
    )
```

```python
import math
from functools import partial

import jax
import jax.numpy as jnp
from jax import lax
from jax.experimental import pallas as pl
from jax.experimental.pallas import tpu as pltpu
from jax.sharding import PartitionSpec as P

H = 16
CAP = 120
FRAMES = 17
CLIPS = 4


EPSILON = 1e-06
BEST = lax.Precision.HIGH
LIGHT = pl.CostEstimate(flops=0, bytes_accessed=1 << 16, transcendentals=0)


def matmul(left, right):
    return jnp.dot(left, right, precision=BEST)


def matmul_nt(left, right):
    return lax.dot_general(left, right, (((1,), (1,)), ((), ())), precision=BEST)


def matmul_tn(left, right):
    return lax.dot_general(left, right, (((0,), (0,)), ((), ())), precision=BEST)


def normalize(rows):
    average = jnp.mean(rows, axis=-1, keepdims=True)
    centred = rows - average
    spread = jnp.mean(centred * centred, axis=-1, keepdims=True)
    inverse = lax.rsqrt(spread + EPSILON)
    return (centred * inverse, inverse)


def normalize_back(grad_normed, normed, inverse):
    first_mean = jnp.mean(grad_normed, axis=-1, keepdims=True)
    second_mean = jnp.mean(grad_normed * normed, axis=-1, keepdims=True)
    return inverse * (grad_normed - first_mean - normed * second_mean)


def swap(value, axis, bit):
    size = lax.axis_size(axis)
    return lax.ppermute(value, axis, [(i, i ^ bit) for i in range(size)])


def all_sum(value, axis):
    bit = 1
    while bit < lax.axis_size(axis):
        value = value + swap(value, axis, bit)
        bit *= 2
    return value


def placed(vector, axis):
    length = vector.shape[-1]
    whole = jnp.zeros(vector.shape[:-1] + (length * lax.axis_size(axis),), vector.dtype)
    return lax.dynamic_update_slice_in_dim(
        whole, vector, lax.axis_index(axis) * length, axis=vector.ndim - 1
    )


def own_part(array, axis, dim):
    length = array.shape[dim] // lax.axis_size(axis)
    return lax.dynamic_slice_in_dim(array, lax.axis_index(axis) * length, length, axis=dim)


def after(value, done):
    return lax.optimization_barrier((value, done))[0]


def small_patch():
    return lax.axis_size("patch") == 8 and lax.axis_size("frame") == 4


def padded(vector, rows):
    return jnp.pad(vector, (0, rows * 128 - vector.shape[0])).reshape(rows, 128)


def greet(partners):
    barrier = pltpu.get_barrier_semaphore()
    for partner in partners:
        pl.semaphore_signal(barrier, inc=1, device_id={"patch": partner}, device_id_type=pl.DeviceIdType.MESH)
    pl.semaphore_wait(barrier, len(partners))


def remote(source, target, send_sems, recv_sems, index, device):
    return pltpu.make_async_remote_copy(
        src_ref=source, dst_ref=target, send_sem=send_sems.at[index], recv_sem=recv_sems.at[index],
        device_id={"patch": device}, device_id_type=pl.DeviceIdType.MESH)


def token_gather_kernel(rows, whole, local_sem, send_sems, recv_sems):
    own = lax.axis_index("patch")
    core, along_x, along_y, across = own ^ 1, own ^ 2, own ^ 4, own ^ 6
    greet((core, along_x, along_y))
    length = rows.shape[0] // 4
    sent = []

    def piece(owner, q):
        return whole.at[owner, pl.ds(q * length, length)]

    def send(source, owner, q, index, device):
        copy = remote(source, piece(owner, q), send_sems, recv_sems, index, device)
        copy.start()
        sent.append(copy)

    def arrived(owner, q, index, device):
        remote(piece(owner, q), piece(owner, q), send_sems, recv_sems, index, device).wait_recv()

    mine = pltpu.make_async_copy(rows, whole.at[own], local_sem)
    mine.start()
    for q_x, q_y in ((0, 2), (1, 3), (2, 0), (3, 1)):
        send(rows.at[pl.ds(q_x * length, length)], own, q_x, q_x, along_x)
        send(rows.at[pl.ds(q_y * length, length)], own, q_y, 4 + q_y, along_y)
    for q in range(4):
        send(rows.at[pl.ds(q * length, length)], own, q, 12 + q, core)
    for q_x, q_y in ((0, 2), (1, 3), (2, 0), (3, 1)):
        arrived(along_x, q_x, q_x, along_x)
        if q_x < 2:
            send(piece(along_x, q_x), along_x, q_x, 8 + q_x, along_y)
        send(piece(along_x, q_x), along_x, q_x, 16 + q_x, core)
        arrived(along_y, q_y, 4 + q_y, along_y)
        if q_y >= 2:
            send(piece(along_y, q_y), along_y, q_y, 8 + q_y, along_x)
        send(piece(along_y, q_y), along_y, q_y, 20 + q_y, core)
    for q in (0, 2, 1, 3):
        arrived(across, q, 8 + q, along_y if q < 2 else along_x)
        send(piece(across, q), across, q, 24 + q, core)
    for q in range(4):
        arrived(core, q, 12 + q, core)
        arrived(core ^ 2, q, 16 + q, core)
        arrived(core ^ 4, q, 20 + q, core)
        arrived(core ^ 6, q, 24 + q, core)
    for copy in sent:
        copy.wait_send()
    mine.wait()


def token_gather(rows):
    length, width = rows.shape
    return pl.pallas_call(
        token_gather_kernel,
        out_shape=jax.ShapeDtypeStruct((8, length, width), jnp.float32),
        in_specs=[pl.BlockSpec(memory_space=pltpu.VMEM)],
        out_specs=pl.BlockSpec(memory_space=pl.ANY),
        scratch_shapes=[pltpu.SemaphoreType.DMA, pltpu.SemaphoreType.DMA((28,)), pltpu.SemaphoreType.DMA((28,))],
        compiler_params=pltpu.CompilerParams(collective_id=0, has_side_effects=True, vmem_limit_bytes=16 << 20),
        cost_estimate=LIGHT,
    )(rows).reshape(8 * length, width)


def token_scatter_kernel(parts, total, kept, theirs, by_x, by_y, from_x, from_y, local_sems, send_sems, recv_sems):
    own = lax.axis_index("patch")
    core, along_x, along_y = own ^ 1, own ^ 2, own ^ 4
    greet((core, along_x, along_y))
    half = total.shape[0] // 2
    upper, lower = pl.ds(0, half), pl.ds(half, half)
    order = (3, 2, 1, 0)
    sent, loads = [], {}

    def send(source, target, index, device):
        copy = remote(source, target, send_sems, recv_sems, index, device)
        copy.start()
        sent.append(copy)

    def arrived(target, index, device):
        remote(target, target, send_sems, recv_sems, index, device).wait_recv()

    for j in order:
        send(parts.at[core ^ (2 * j)], theirs.at[j], j, core)
        loads[j] = pltpu.make_async_copy(parts.at[own ^ (2 * j)], kept.at[j], local_sems.at[j])
        loads[j].start()

    def add_cores(j):
        loads[j].wait()
        arrived(theirs.at[j], j, core)
        kept[j] = kept[j] + theirs[j]

    add_cores(3)
    send(kept.at[3, upper], by_x, 4, along_x)
    send(kept.at[3, lower], by_y, 5, along_y)
    add_cores(2)
    send(kept.at[2, lower], from_y.at[lower], 6, along_y)
    add_cores(1)
    send(kept.at[1, upper], from_x.at[upper], 7, along_x)
    add_cores(0)
    arrived(by_x, 4, along_x)
    kept[2, upper] = kept[2, upper] + by_x[...]
    send(kept.at[2, upper], from_y.at[upper], 8, along_y)
    arrived(by_y, 5, along_y)
    kept[1, lower] = kept[1, lower] + by_y[...]
    send(kept.at[1, lower], from_x.at[lower], 9, along_x)
    arrived(from_y.at[lower], 6, along_y)
    arrived(from_x.at[upper], 7, along_x)
    arrived(from_y.at[upper], 8, along_y)
    arrived(from_x.at[lower], 9, along_x)
    total[...] = kept[0] + from_x[...] + from_y[...]
    for copy in sent:
        copy.wait_send()


def token_scatter(parts):
    length, width = parts.shape[0] // 8, parts.shape[1]
    block = (length, width)
    return pl.pallas_call(
        token_scatter_kernel,
        out_shape=jax.ShapeDtypeStruct(block, jnp.float32),
        in_specs=[pl.BlockSpec(memory_space=pl.ANY)],
        out_specs=pl.BlockSpec(memory_space=pltpu.VMEM),
        scratch_shapes=[
            pltpu.VMEM((4,) + block, jnp.float32), pltpu.VMEM((4,) + block, jnp.float32),
            pltpu.VMEM((length // 2, width), jnp.float32), pltpu.VMEM((length // 2, width), jnp.float32),
            pltpu.VMEM(block, jnp.float32), pltpu.VMEM(block, jnp.float32),
            pltpu.SemaphoreType.DMA((4,)), pltpu.SemaphoreType.DMA((10,)), pltpu.SemaphoreType.DMA((10,)),
        ],
        compiler_params=pltpu.CompilerParams(collective_id=1, has_side_effects=True, vmem_limit_bytes=32 << 20),
        cost_estimate=LIGHT,
    )(parts.reshape((8,) + block))


class Links:
    def __init__(self, send_sems, recv_sems):
        self.send_sems, self.recv_sems = send_sems, recv_sems
        self.count = 0
        self.sent = []

    def plan(self):
        self.count += 1
        return self.count - 1

    def copy(self, source, target, index, device):
        return pltpu.make_async_remote_copy(
            src_ref=source, dst_ref=target, send_sem=self.send_sems.at[index],
            recv_sem=self.recv_sems.at[index], device_id=device,
            device_id_type=pl.DeviceIdType.MESH,
        )

    def send(self, source, target, index, device):
        self.copy(source, target, index, device).start()
        self.sent.append((source, index, device))

    def wait(self, target, index, device):
        self.copy(target, target, index, device).wait_recv()

    def drain(self):
        for source, index, device in self.sent:
            self.copy(source, source, index, device).wait_send()


def greet_all(devices):
    barrier = pltpu.get_barrier_semaphore()
    for device in devices:
        pl.semaphore_signal(barrier, inc=1, device_id=device, device_id_type=pl.DeviceIdType.MESH)
    pl.semaphore_wait(barrier, len(devices))


def begin_kernel(
    tokens, later, slots, small, kv, weight,
    tokens_out, later_out, slots_out, small_out, kv_out, weight_out,
    weight_sem, small_1, small_2, small_got, kv_1, kv_2, kv_got_core, kv_got_1, kv_got_2,
    send_sems, recv_sems,
):
    me, z = lax.axis_index("patch"), lax.axis_index("frame")
    core, x, y = ({"patch": me ^ k} for k in (1, 2, 4))
    frames = [None] + [{"frame": z ^ k} for k in (1, 2, 3)]
    greet_all([core, x, y] + frames[1:])
    links = Links(send_sems, recv_sems)
    count, part = tokens.shape[0], tokens.shape[1] // 4
    rows, width = kv_1.shape

    def columns(k):
        return pl.ds(pl.multiple_of((z ^ k) * part, part), part)

    def of_slots(k):
        return pl.ds((z ^ k) * count, count)

    half = pl.multiple_of((me % 2) * width, 128)
    other = pl.multiple_of((1 - me % 2) * width, 128)
    mine, theirs = pl.ds(half, width), pl.ds(other, width)

    length = weight.shape[0]
    weight_at = [[links.plan() for _ in range(7)] for _ in range(3)]
    weight_core = links.plan()

    def piece(k, u, first=0, size=length):
        start = pl.multiple_of((me ^ k) * length + first, 8)
        return weight_out.at[pl.ds(start, size), pl.ds(u * width, width)]

    whole = weight_out.at[pl.ds(pl.multiple_of(me * length, 8), length)]
    sibling = weight_out.at[pl.ds(pl.multiple_of((me ^ 1) * length, 8), length)]
    own_copy = pltpu.make_async_copy(weight, whole, weight_sem)

    def weight_links(u):
        source = weight.at[:, pl.ds(u * width, width)]
        links.send(source, piece(0, u), weight_at[u][0], x)
        links.send(source, piece(0, u), weight_at[u][1], y)

    def weight_across(u):
        middle_row = length // 2
        links.wait(piece(2, u), weight_at[u][0], x)
        upper = piece(2, u, 0, middle_row)
        links.send(upper, upper, weight_at[u][2], y)
        links.send(piece(2, u), piece(2, u), weight_at[u][4], core)
        links.wait(piece(4, u), weight_at[u][1], y)
        lower = piece(4, u, middle_row, middle_row)
        links.send(lower, lower, weight_at[u][3], x)
        links.send(piece(4, u), piece(4, u), weight_at[u][5], core)

    def weight_last(u):
        middle_row = length // 2
        links.wait(piece(6, u, 0, middle_row), weight_at[u][2], y)
        links.wait(piece(6, u, middle_row, middle_row), weight_at[u][3], x)
        links.send(piece(6, u), piece(6, u), weight_at[u][6], core)

    at = links.plan()
    links.send(small, small_got.at[0], at, core)
    at_kv = links.plan()
    links.send(kv.at[:, theirs], kv_got_core, at_kv, core)
    own_copy.start()
    token_at = [None] + [links.plan() for _ in range(3)]
    slot_at = [None] + [links.plan() for _ in range(3)]
    later_at = [None] + [links.plan() for _ in range(3)]
    for k in (1, 2, 3):
        links.send(slots, slots_out.at[z], slot_at[k], frames[k])
        links.send(tokens.at[:, columns(k)], tokens_out.at[of_slots(0)], token_at[k], frames[k])
    for k in (1, 2, 3):
        links.send(later.at[:, columns(k)], later_out.at[of_slots(0)], later_at[k], frames[k])

    links.wait(small_got.at[0], at, core)
    small_1[...] = small[...] + small_got[0]
    at = links.plan()
    links.send(small_1, small_got.at[1], at, x)
    links.wait(kv_got_core, at_kv, core)
    kv_1[...] = kv[:, mine] + kv_got_core[...]
    upper, lower = pl.ds(0, 64), pl.ds(64, rows - 64)
    at_u, at_l = links.plan(), links.plan()
    links.send(kv_1.at[upper], kv_got_1.at[upper], at_u, x)
    links.send(kv_1.at[lower], kv_got_1.at[lower], at_l, y)
    weight_links(0)
    links.send(weight, whole, weight_core, core)
    slots_out[z] = slots[...]
    tokens_out[of_slots(0)] = tokens[:, columns(0)]
    later_out[of_slots(0)] = later[:, columns(0)]
    links.wait(small_got.at[1], at, x)
    small_2[...] = small_1[...] + small_got[1]
    at = links.plan()
    links.send(small_2, small_got.at[2], at, y)
    links.wait(kv_got_1.at[upper], at_u, x)
    links.wait(kv_got_1.at[lower], at_l, y)
    kv_2[...] = kv_1[...] + kv_got_1[...]
    at_u, at_l = links.plan(), links.plan()
    links.send(kv_2.at[upper], kv_got_2.at[upper], at_u, y)
    links.send(kv_2.at[lower], kv_got_2.at[lower], at_l, x)
    weight_links(1)
    links.wait(small_got.at[2], at, y)
    small_out[...] = small_2[...] + small_got[2]
    weight_across(0)
    weight_links(2)
    links.wait(kv_got_2.at[upper], at_u, y)
    links.wait(kv_got_2.at[lower], at_l, x)

    def share(k, columns):
        return kv_out.at[pl.ds(pl.multiple_of((z ^ k) * rows, rows), rows), columns]

    kv_out[pl.ds(pl.multiple_of(z * rows, rows), rows), mine] = kv_2[...] + kv_got_2[...]
    kv_at = [None] + [links.plan() for _ in range(3)]
    core_at = [links.plan() for _ in range(4)]
    for k in (1, 2, 3):
        links.send(share(0, mine), share(0, mine), kv_at[k], frames[k])
    links.send(share(0, mine), share(0, mine), core_at[0], core)
    weight_across(1)
    weight_last(0)
    weight_across(2)
    weight_last(1)
    for k in (1, 2, 3):
        links.wait(slots_out.at[z ^ k], slot_at[k], frames[k])
        links.wait(tokens_out.at[of_slots(k)], token_at[k], frames[k])
        links.wait(later_out.at[of_slots(k)], later_at[k], frames[k])
    for k in (1, 2, 3):
        links.wait(share(k, mine), kv_at[k], frames[k])
        links.send(share(k, mine), share(k, mine), core_at[k], core)
    weight_last(2)
    for k in range(4):
        links.wait(share(k, theirs), core_at[k], core)
    links.wait(sibling, weight_core, core)
    for u in range(3):
        for i, k in enumerate((2, 4, 6)):
            links.wait(piece(k ^ 1, u), weight_at[u][4 + i], core)
    own_copy.wait()
    links.drain()


def begin(tokens, later, slots, small, kv, weight):
    count, cols, width = tokens.shape
    rows = kv.shape[0]
    f32, vmem = jnp.float32, pl.BlockSpec(memory_space=pltpu.VMEM)
    hbm = pl.BlockSpec(memory_space=pl.ANY)
    half = pltpu.VMEM((rows, width), f32)
    return pl.pallas_call(
        begin_kernel,
        out_shape=(
            jax.ShapeDtypeStruct((4 * count, cols // 4, width), f32),
            jax.ShapeDtypeStruct((4 * count, cols // 4, width), f32),
            jax.ShapeDtypeStruct((4,) + slots.shape, f32),
            jax.ShapeDtypeStruct(small.shape, f32),
            jax.ShapeDtypeStruct((4 * rows, 2 * width), f32),
            jax.ShapeDtypeStruct((8 * weight.shape[0], weight.shape[1]), f32),
        ),
        in_specs=[vmem] * 5 + [hbm],
        out_specs=[vmem] * 5 + [hbm],
        scratch_shapes=[
            pltpu.SemaphoreType.DMA,
            pltpu.VMEM(small.shape, f32), pltpu.VMEM(small.shape, f32),
            pltpu.VMEM((3,) + small.shape, f32), half, half, half, half, half,
            pltpu.SemaphoreType.DMA((48,)), pltpu.SemaphoreType.DMA((48,)),
        ],
        compiler_params=pltpu.CompilerParams(
            collective_id=2, has_side_effects=True, vmem_limit_bytes=36 << 20
        ),
        cost_estimate=LIGHT,
    )(tokens, later, slots, small, kv, weight)


UNITS = 3


def finish_kernel(
    first, attn, cross_q, cross_o, kv, tokens, small, caption, columns,
    first_out, attn_out, cross_q_out, cross_o_out, kv_out, tokens_out, small_out, caption_out,
    columns_out, columns_got, columns_sem,
    kept, theirs, by_x, by_y, from_x, from_y, along_z, across_z,
    small_sums, small_got, small_z, load_sems, credit, send_sems, recv_sems,
):
    me, z = lax.axis_index("patch"), lax.axis_index("frame")
    outer = (z == 0) | (z == 3)
    inner = (z == 1) | (z == 2)
    core, x, y = ({"patch": me ^ k} for k in (1, 2, 4))
    frames = [None] + [{"frame": z ^ k} for k in (1, 2, 3)]
    near, facing = frames[1], frames[3]
    chips = {2: x, 4: y, 6: {"patch": me ^ 6}}
    greet_all([core, x, y, chips[6]] + frames[1:])
    links = Links(send_sems, recv_sems)
    rows, width = by_x.shape[1] * 2, by_x.shape[2]
    upper, lower = pl.ds(0, rows // 2), pl.ds(rows // 2, rows // 2)
    count, part = tokens_out.shape[0], tokens_out.shape[1] // 4

    token_at = [None] + [links.plan() for _ in range(3)]

    def send_tokens(k):
        where = pl.ds(pl.multiple_of(z * part, part), part)
        if k == 0:
            tokens_out[:, where] = tokens[pl.ds(z * count, count)]
        else:
            source = tokens.at[pl.ds((z ^ k) * count, count)]
            links.send(source, tokens_out.at[:, where], token_at[k], frames[k])

    def frame_steps(value, result, near_got, facing_got):
        up, over, down = links.plan(), links.plan(), links.plan()

        def one():
            @pl.when(outer)
            def _():
                links.copy(value, near_got, up, near).start()

        def two():
            @pl.when(inner)
            def _():
                links.wait(near_got, up, near)
                near_got[...] = near_got[...] + value[...]
                links.copy(near_got, facing_got, over, facing).start()

        def three():
            @pl.when(inner)
            def _():
                links.wait(facing_got, over, facing)
                result[...] = near_got[...] + facing_got[...]
                links.copy(result, near_got, down, near).start()

        def four():
            @pl.when(outer)
            def _():
                links.wait(near_got, down, near)
                result[...] = near_got[...]
                links.copy(value, value, up, near).wait_send()

            @pl.when(inner)
            def _():
                links.copy(near_got, near_got, over, facing).wait_send()
                links.copy(result, result, down, near).wait_send()

        return one, two, three, four

    def piece(ref, u):
        return ref.at[:, pl.ds(u * width, width)]

    pairs = [(kept.at[u, 0], piece(first_out, u)) for u in range(UNITS)]
    pairs += [(attn, attn_out), (cross_q, cross_q_out), (cross_o, cross_o_out)]
    pairs += [(piece(kv, u), piece(kv_out, u)) for u in range(2)]
    steps = [
        frame_steps(value, result, along_z.at[i], across_z.at[i])
        for i, (value, result) in enumerate(pairs)
    ]
    small_steps = frame_steps(small_sums.at[2], small_out, small_z.at[0], small_z.at[1])

    core_at = [[links.plan() for _ in range(4)] for _ in range(UNITS)]
    link_at = [[links.plan() for _ in range(6)] for _ in range(UNITS)]

    def source(u, device, j):
        start = pl.multiple_of((device ^ (2 * j)) * rows, rows)
        return first.at[pl.ds(start, rows), pl.ds(u * width, width)]

    def load(u, j):
        return pltpu.make_async_copy(source(u, me, j), kept.at[u, j], load_sems.at[u, j])

    def to_core(u):
        if u >= 2:
            pl.semaphore_wait(credit.at[u - 2], 1)
        for j in (3, 2, 1, 0):
            links.send(source(u, me ^ 1, j), theirs.at[u % 2, j], core_at[u][j], core)

    def add_cores(u, j):
        load(u, j).wait()
        links.wait(theirs.at[u % 2, j], core_at[u][j], core)
        kept[u, j] = kept[u, j] + theirs[u % 2, j]

    def stage_one(u):
        at = link_at[u]
        add_cores(u, 3)
        links.send(kept.at[u, 3, upper], by_x.at[u], at[0], x)
        links.send(kept.at[u, 3, lower], by_y.at[u], at[1], y)
        add_cores(u, 2)
        links.send(kept.at[u, 2, lower], from_y.at[u, lower], at[2], y)
        add_cores(u, 1)
        links.send(kept.at[u, 1, upper], from_x.at[u, upper], at[3], x)
        add_cores(u, 0)
        if u + 2 < UNITS:
            pl.semaphore_signal(
                credit.at[u], inc=1, device_id=core, device_id_type=pl.DeviceIdType.MESH
            )
            to_core(u + 2)

    def stage_two(u):
        at = link_at[u]
        links.wait(by_x.at[u], at[0], x)
        kept[u, 2, upper] = kept[u, 2, upper] + by_x[u]
        links.send(kept.at[u, 2, upper], from_y.at[u, upper], at[4], y)
        links.wait(by_y.at[u], at[1], y)
        kept[u, 1, lower] = kept[u, 1, lower] + by_y[u]
        links.send(kept.at[u, 1, lower], from_x.at[u, lower], at[5], x)

    def stage_three(u):
        at = link_at[u]
        links.wait(from_y.at[u, lower], at[2], y)
        links.wait(from_x.at[u, upper], at[3], x)
        links.wait(from_y.at[u, upper], at[4], y)
        links.wait(from_x.at[u, lower], at[5], x)
        kept[u, 0] = kept[u, 0] + from_x[u] + from_y[u]
        steps[u][0]()

    block = columns_got.shape[1] // 2
    columns_at = {k: links.plan() for k in (2, 4, 6)}
    columns_core = {k: links.plan() for k in (0, 2, 4, 6)}

    def chip_rows(k):
        return columns.at[pl.ds(pl.multiple_of((me ^ k) // 2 * (2 * block), 8), 2 * block)]

    own_rows = pltpu.make_async_copy(chip_rows(0), columns_got.at[0], columns_sem.at[0])

    def own_block(k):
        core_rows = pl.ds(pl.multiple_of(me % 2 * block, 8), block)
        return pltpu.make_async_copy(
            columns_got.at[k // 2, core_rows], columns_out.at[me ^ k], columns_sem.at[1 + k // 2]
        )

    def send_columns(k):
        links.send(chip_rows(k), columns_got.at[k // 2], columns_at[k], chips[k])

    def columns_over():
        other_rows = pl.ds(pl.multiple_of((1 - me % 2) * block, 8), block)
        own_rows.wait()
        for k in (0, 2, 4, 6):
            if k:
                links.wait(columns_got.at[k // 2], columns_at[k], chips[k])
            links.send(
                columns_got.at[k // 2, other_rows], columns_out.at[me ^ k], columns_core[k], core
            )
            own_block(k).start()

    def columns_end():
        for k in (0, 2, 4, 6):
            links.wait(columns_out.at[me ^ 1 ^ k], columns_core[k], core)
            own_block(k).wait()

    caption_at = [links.plan() for _ in range(10)]

    def caption_frames():
        caption_out[me, z] = caption[...]
        for k in (1, 2, 3):
            links.send(caption, caption_out.at[me, z], caption_at[k - 1], frames[k])

    def caption_x():
        for k in (1, 2, 3):
            links.wait(caption_out.at[me, z ^ k], caption_at[k - 1], frames[k])
        links.send(caption_out.at[me], caption_out.at[me], caption_at[3], x)

    def caption_y():
        links.wait(caption_out.at[me ^ 2], caption_at[3], x)
        for i, k in enumerate((0, 2)):
            links.send(caption_out.at[me ^ k], caption_out.at[me ^ k], caption_at[4 + i], y)

    def caption_core():
        for i, k in enumerate((0, 2)):
            links.wait(caption_out.at[me ^ 4 ^ k], caption_at[4 + i], y)
        for i, k in enumerate((0, 2, 4, 6)):
            links.send(caption_out.at[me ^ k], caption_out.at[me ^ k], caption_at[6 + i], core)

    def caption_end():
        for i, k in enumerate((0, 2, 4, 6)):
            links.wait(caption_out.at[me ^ 1 ^ k], caption_at[6 + i], core)

    small_at = [links.plan() for _ in range(3)]
    links.send(small, small_got.at[0], small_at[0], core)
    caption_frames()
    own_rows.start()
    for u in range(UNITS):
        for j in (3, 2, 1, 0):
            load(u, j).start()
    for i in (6, 7, 3, 4, 5):
        steps[i][0]()
    for u in range(2):
        to_core(u)
    links.wait(small_got.at[0], small_at[0], core)
    small_sums[0] = small[...] + small_got[0]
    links.send(small_sums.at[0], small_got.at[1], small_at[1], x)
    stage_one(0)
    links.wait(small_got.at[1], small_at[1], x)
    small_sums[1] = small_sums[0] + small_got[1]
    links.send(small_sums.at[1], small_got.at[2], small_at[2], y)
    stage_one(1)
    stage_two(0)
    links.wait(small_got.at[2], small_at[2], y)
    small_sums[2] = small_sums[1] + small_got[2]
    small_steps[0]()
    steps[6][1]()
    steps[7][1]()
    stage_one(2)
    stage_three(0)
    steps[3][1]()
    stage_two(1)
    steps[6][2]()
    steps[7][2]()
    steps[4][1]()
    stage_two(2)
    stage_three(1)
    caption_x()
    for k in (2, 4, 6):
        send_columns(k)
    steps[3][2]()
    steps[5][1]()
    small_steps[1]()
    stage_three(2)
    for k in range(4):
        send_tokens(k)
    steps[4][2]()
    small_steps[2]()
    steps[0][1]()
    caption_y()
    steps[5][2]()
    steps[1][1]()
    steps[0][2]()
    caption_core()
    steps[2][1]()
    steps[1][2]()
    steps[2][2]()
    for step in steps + [small_steps]:
        step[3]()
    columns_over()
    caption_end()
    columns_end()
    for k in (1, 2, 3):
        where = pl.ds(pl.multiple_of((z ^ k) * part, part), part)
        links.wait(tokens_out.at[:, where], token_at[k], frames[k])
    links.drain()


def finish(first, attn, cross_q, cross_o, kv, tokens, small, caption, columns):
    rows, width = attn.shape
    count, part = tokens.shape[0] // 4, tokens.shape[1]
    f32, vmem = jnp.float32, pl.BlockSpec(memory_space=pltpu.VMEM)
    hbm = pl.BlockSpec(memory_space=pl.ANY)

    def shape(*sizes):
        return jax.ShapeDtypeStruct(sizes, f32)

    return pl.pallas_call(
        finish_kernel,
        out_shape=(
            shape(rows, 3 * width), shape(rows, width), shape(rows, width), shape(rows, width),
            shape(rows, 2 * width), shape(count, 4 * part, tokens.shape[2]), shape(*small.shape),
            shape(8, 4, *caption.shape), shape(8, columns.shape[0] // 8, columns.shape[1]),
        ),
        in_specs=[hbm] + [vmem] * 7 + [hbm],
        out_specs=[vmem] * 8 + [hbm],
        scratch_shapes=[
            pltpu.VMEM((4, columns.shape[0] // 4, columns.shape[1]), f32),
            pltpu.SemaphoreType.DMA((5,)),
            pltpu.VMEM((UNITS, 4, rows, width), f32), pltpu.VMEM((2, 4, rows, width), f32),
            pltpu.VMEM((UNITS, rows // 2, width), f32), pltpu.VMEM((UNITS, rows // 2, width), f32),
            pltpu.VMEM((UNITS, rows, width), f32), pltpu.VMEM((UNITS, rows, width), f32),
            pltpu.VMEM((8, rows, width), f32), pltpu.VMEM((8, rows, width), f32),
            pltpu.VMEM((3,) + small.shape, f32), pltpu.VMEM((3,) + small.shape, f32),
            pltpu.VMEM((2,) + small.shape, f32),
            pltpu.SemaphoreType.DMA((UNITS, 4)), pltpu.SemaphoreType.REGULAR((1,)),
            pltpu.SemaphoreType.DMA((112,)), pltpu.SemaphoreType.DMA((112,)),
        ],
        compiler_params=pltpu.CompilerParams(
            collective_id=3, has_side_effects=True, vmem_limit_bytes=58 << 20
        ),
        cost_estimate=LIGHT,
    )(first, attn, cross_q, cross_o, kv, tokens, small, caption, columns)


def middle_kernel(
    parts, kv, residual, gate, bias, attn, cross_q, cross_o,
    total, kv_out, block_out, attn_out, cross_q_out, cross_o_out,
    w_kept, w_theirs, w_by_x, w_by_y, w_from_x, w_from_y, w_loads, credit, kv_sem,
    block, kept, theirs, by_x, by_y, from_x, from_y,
    kv_half, kv_core, kv_got, kv_1, kv_2, kv_got_1, kv_got_2,
    load_sems, send_sems, recv_sems,
):
    me, z = lax.axis_index("patch"), lax.axis_index("frame")
    core, x, y = ({"patch": me ^ k} for k in (1, 2, 4))
    frames = [None] + [{"frame": z ^ k} for k in (1, 2, 3)]
    greet_all([core, x, y] + frames[1:])
    links = Links(send_sems, recv_sems)
    rows, width = kv_1.shape
    half = pl.multiple_of((me % 2) * width, 128)
    other = pl.multiple_of((1 - me % 2) * width, 128)
    mine, others = pl.ds(half, width), pl.ds(other, width)

    def share(ref, k):
        return ref.at[pl.ds(pl.multiple_of((z ^ k) * rows, rows), rows)]

    grads, sums = (attn, cross_q, cross_o), (attn_out, cross_q_out, cross_o_out)
    length = attn_out.shape[0]
    top_rows, low_rows = pl.ds(0, length // 2), pl.ds(length // 2, length // 2)
    w_core_at = [[links.plan() for _ in range(4)] for _ in grads]
    w_at = [[links.plan() for _ in range(6)] for _ in grads]

    def w_source(u, device, j):
        start = pl.multiple_of((device ^ (2 * j)) * length, length)
        return grads[u].at[pl.ds(start, length)]

    def w_load(u, j):
        return pltpu.make_async_copy(w_source(u, me, j), w_kept.at[u, j], w_loads.at[u, j])

    def w_to_core(u):
        if u >= 2:
            pl.semaphore_wait(credit.at[u - 2], 1)
        for j in (3, 2, 1, 0):
            links.send(w_source(u, me ^ 1, j), w_theirs.at[u % 2, j], w_core_at[u][j], core)

    def w_add(u, j):
        w_load(u, j).wait()
        links.wait(w_theirs.at[u % 2, j], w_core_at[u][j], core)
        w_kept[u, j] = w_kept[u, j] + w_theirs[u % 2, j]

    def w_one(u):
        w_add(u, 3)
        links.send(w_kept.at[u, 3, top_rows], w_by_x.at[u], w_at[u][0], x)
        links.send(w_kept.at[u, 3, low_rows], w_by_y.at[u], w_at[u][1], y)
        w_add(u, 2)
        links.send(w_kept.at[u, 2, low_rows], w_from_y.at[u, low_rows], w_at[u][2], y)
        w_add(u, 1)
        links.send(w_kept.at[u, 1, top_rows], w_from_x.at[u, top_rows], w_at[u][3], x)
        w_add(u, 0)
        if u == 0:
            pl.semaphore_signal(
                credit.at[u], inc=1, device_id=core, device_id_type=pl.DeviceIdType.MESH
            )
            w_to_core(2)

    def w_two(u):
        links.wait(w_by_x.at[u], w_at[u][0], x)
        w_kept[u, 2, top_rows] = w_kept[u, 2, top_rows] + w_by_x[u]
        links.send(w_kept.at[u, 2, top_rows], w_from_y.at[u, top_rows], w_at[u][4], y)
        links.wait(w_by_y.at[u], w_at[u][1], y)
        w_kept[u, 1, low_rows] = w_kept[u, 1, low_rows] + w_by_y[u]
        links.send(w_kept.at[u, 1, low_rows], w_from_x.at[u, low_rows], w_at[u][5], x)

    def w_three(u):
        links.wait(w_from_y.at[u, low_rows], w_at[u][2], y)
        links.wait(w_from_x.at[u, top_rows], w_at[u][3], x)
        links.wait(w_from_y.at[u, top_rows], w_at[u][4], y)
        links.wait(w_from_x.at[u, low_rows], w_at[u][5], x)
        sums[u][...] = w_kept[u, 0] + w_from_x[u] + w_from_y[u]

    at_kv = links.plan()
    links.send(kv.at[:, others], kv_core, at_kv, core)
    kv_load = pltpu.make_async_copy(kv.at[:, mine], kv_half, kv_sem)
    kv_load.start()
    core_at = [links.plan() for _ in range(4)]
    loads = [
        pltpu.make_async_copy(parts.at[me ^ (2 * j)], kept.at[j], load_sems.at[j])
        for j in range(4)
    ]
    for j in (3, 2, 1, 0):
        links.send(parts.at[me ^ 1 ^ (2 * j)], theirs.at[j], core_at[j], core)
        loads[j].start()
    for u in range(3):
        for j in (3, 2, 1, 0):
            w_load(u, j).start()
    for u in range(2):
        w_to_core(u)
    kv_load.wait()
    links.wait(kv_core, at_kv, core)
    kv_half[...] = kv_half[...] + kv_core[...]
    kv_at = [None] + [links.plan() for _ in range(3)]
    for k in (1, 2, 3):
        links.send(share(kv_half, k), kv_got.at[k - 1], kv_at[k], frames[k])

    count = total.shape[0] // 2
    upper, lower = pl.ds(0, count), pl.ds(count, count)
    at = [links.plan() for _ in range(6)]

    def add_cores(j):
        loads[j].wait()
        links.wait(theirs.at[j], core_at[j], core)
        kept[j] = kept[j] + theirs[j]

    add_cores(3)
    links.send(kept.at[3, upper], by_x, at[0], x)
    links.send(kept.at[3, lower], by_y, at[1], y)
    add_cores(2)
    links.send(kept.at[2, lower], from_y.at[lower], at[2], y)
    add_cores(1)
    links.send(kept.at[1, upper], from_x.at[upper], at[3], x)
    add_cores(0)
    links.wait(by_x, at[0], x)
    kept[2, upper] = kept[2, upper] + by_x[...]
    links.send(kept.at[2, upper], from_y.at[upper], at[4], y)
    links.wait(by_y, at[1], y)
    kept[1, lower] = kept[1, lower] + by_y[...]
    links.send(kept.at[1, lower], from_x.at[lower], at[5], x)

    w_one(0)
    links.wait(from_y.at[lower], at[2], y)
    links.wait(from_x.at[upper], at[3], x)
    links.wait(from_y.at[upper], at[4], y)
    links.wait(from_x.at[lower], at[5], x)
    total[...] = kept[0] + from_x[...] + from_y[...]
    slots, part = residual.shape[0] // 4, residual.shape[1]
    block[...] = residual[...] + gate[...] * (total[...] + bias[...]).reshape(residual.shape)
    block_at = [None] + [links.plan() for _ in range(3)]
    place = pl.ds(pl.multiple_of(z * part, part), part)
    for k in (1, 2, 3):
        source = block.at[pl.ds((z ^ k) * slots, slots)]
        links.send(source, block_out.at[:, place], block_at[k], frames[k])
    block_out[:, place] = block[pl.ds(z * slots, slots)]
    w_one(1)
    w_two(0)
    for k in (1, 2, 3):
        links.wait(kv_got.at[k - 1], kv_at[k], frames[k])
    kv_1[...] = share(kv_half, 0)[...] + kv_got[0] + (kv_got[1] + kv_got[2])
    top, bottom = pl.ds(0, 64), pl.ds(64, rows - 64)
    at_u, at_l = links.plan(), links.plan()
    links.send(kv_1.at[top], kv_got_1.at[top], at_u, x)
    links.send(kv_1.at[bottom], kv_got_1.at[bottom], at_l, y)
    w_one(2)
    w_two(1)
    w_three(0)
    links.wait(kv_got_1.at[top], at_u, x)
    links.wait(kv_got_1.at[bottom], at_l, y)
    kv_2[...] = kv_1[...] + kv_got_1[...]
    at_u, at_l = links.plan(), links.plan()
    links.send(kv_2.at[top], kv_got_2.at[top], at_u, y)
    links.send(kv_2.at[bottom], kv_got_2.at[bottom], at_l, x)
    links.wait(kv_got_2.at[top], at_u, y)
    links.wait(kv_got_2.at[bottom], at_l, x)
    kv_out[:, mine] = kv_2[...] + kv_got_2[...]
    at_core = links.plan()
    links.send(kv_out.at[:, mine], kv_out.at[:, mine], at_core, core)
    w_two(2)
    w_three(1)
    w_three(2)
    links.wait(kv_out.at[:, others], at_core, core)
    for k in (1, 2, 3):
        there = pl.ds(pl.multiple_of((z ^ k) * part, part), part)
        links.wait(block_out.at[:, there], block_at[k], frames[k])
    links.drain()


def middle(parts, kv, residual, gate, bias, attn, cross_q, cross_o):
    slots, cols, _ = residual.shape
    count = attn.shape[0] // 8
    length, width = parts.shape[0] // 8, parts.shape[1]
    rows = kv.shape[0] // 4
    f32, vmem = jnp.float32, pl.BlockSpec(memory_space=pltpu.VMEM)
    hbm = pl.BlockSpec(memory_space=pl.ANY)
    block, half = (length, width), pltpu.VMEM((rows, width), f32)
    return pl.pallas_call(
        middle_kernel,
        out_shape=(
            jax.ShapeDtypeStruct(block, f32), jax.ShapeDtypeStruct((rows, 2 * width), f32),
            jax.ShapeDtypeStruct((slots // 4, 4 * cols, width), f32),
            *[jax.ShapeDtypeStruct((count, width), f32)] * 3,
        ),
        in_specs=[hbm] * 2 + [vmem] * 3 + [hbm] * 3,
        out_specs=[vmem] * 6,
        scratch_shapes=[
            pltpu.VMEM((3, 4, count, width), f32), pltpu.VMEM((2, 4, count, width), f32),
            pltpu.VMEM((3, count // 2, width), f32), pltpu.VMEM((3, count // 2, width), f32),
            pltpu.VMEM((3, count, width), f32), pltpu.VMEM((3, count, width), f32),
            pltpu.SemaphoreType.DMA((3, 4)), pltpu.SemaphoreType.REGULAR((1,)),
            pltpu.SemaphoreType.DMA,
            pltpu.VMEM((slots, cols, width), f32),
            pltpu.VMEM((4,) + block, f32), pltpu.VMEM((4,) + block, f32),
            pltpu.VMEM((length // 2, width), f32), pltpu.VMEM((length // 2, width), f32),
            pltpu.VMEM(block, f32), pltpu.VMEM(block, f32),
            pltpu.VMEM((4 * rows, width), f32), pltpu.VMEM((4 * rows, width), f32),
            pltpu.VMEM((3, rows, width), f32), half, half, half, half,
            pltpu.SemaphoreType.DMA((4,)), pltpu.SemaphoreType.DMA((56,)),
            pltpu.SemaphoreType.DMA((56,)),
        ],
        compiler_params=pltpu.CompilerParams(
            collective_id=4, has_side_effects=True, vmem_limit_bytes=58 << 20
        ),
        cost_estimate=LIGHT,
    )(parts.reshape((8,) + block), kv, residual, gate[None], bias[None], attn, cross_q, cross_o)


def spread_kernel(block, whole, send_sems, recv_sems):
    me = lax.axis_index("patch")
    peers = [None] + [{"patch": me ^ k} for k in range(1, 8)]
    greet_all(peers[1:])
    links = Links(send_sems, recv_sems)
    at = [links.plan() for _ in range(8)]
    for k in range(1, 8):
        links.send(block, whole.at[me], at[k], peers[k])
    whole[me] = block[...]
    for k in range(1, 8):
        links.wait(whole.at[me ^ k], at[k], peers[k])
    links.drain()


def spread(block):
    vmem = pl.BlockSpec(memory_space=pltpu.VMEM)
    return pl.pallas_call(
        spread_kernel,
        out_shape=jax.ShapeDtypeStruct((8,) + block.shape, jnp.float32),
        in_specs=[vmem],
        out_specs=vmem,
        scratch_shapes=[pltpu.SemaphoreType.DMA((8,)), pltpu.SemaphoreType.DMA((8,))],
        compiler_params=pltpu.CompilerParams(collective_id=5, has_side_effects=True),
    )(block)


def halves(x):
    high = x.astype(jnp.bfloat16)
    return high, (x - high.astype(jnp.float32)).astype(jnp.bfloat16)


NN, NT, TN = (((1,), (0,)), ((), ())), (((1,), (1,)), ((), ())), (((0,), (0,)), ((), ()))


def three(left, right, dims):
    def dot(a, b):
        return lax.dot_general(a, b, dims, preferred_element_type=jnp.float32)

    return dot(left[0], right[0]) + (dot(left[0], right[1]) + dot(left[1], right[0]))


WINDOW = 256


def head_window(head, head_dim, width):
    start = jnp.minimum(head * head_dim // 128 * 128, width - WINDOW)
    lane = lax.broadcasted_iota(jnp.int32, (1, WINDOW), 1) - (head * head_dim - start)
    mask = ((lane >= 0) & (lane < head_dim)).astype(jnp.float32)
    return pl.ds(pl.multiple_of(start, 128), WINDOW), mask


def softmax_last(scores):
    exponent = jnp.exp(scores - jnp.max(scores, axis=-1, keepdims=True))
    return exponent / jnp.sum(exponent, axis=-1, keepdims=True)


GROUP = 8


def grouped(ref, group, lanes):
    slots = ref.shape[0]
    value = ref[:, group * GROUP : (group + 1) * GROUP, lanes]
    return value.reshape(slots * GROUP, value.shape[-1])


def store_halves(high, low, index, value):
    high[index], low[index] = halves(value)


def frame_attention_kernel(qkv, b_query, b_value, distance, allowed, probs, out, *split):
    (q_high, q_low, k_high, k_low, v_high, v_low), total = split[:6], split[6]
    slots, width = qkv.shape[0], out.shape[-1]
    head_dim = width // H
    scaling = head_dim**-0.5
    for g in range(2):
        store_halves(q_high, q_low, g, grouped(qkv, g, slice(0, width)) + b_query[...])
        store_halves(k_high, k_low, g, grouped(qkv, g, slice(width, 2 * width)))
        store_halves(
            v_high, v_low, g, grouped(qkv, g, slice(2 * width, 3 * width)) + b_value[...]
        )
    total[...] = jnp.zeros(total.shape, jnp.float32)

    def step(head, _):
        at, mask = head_window(head, head_dim, width)
        mask = mask.astype(jnp.bfloat16)
        slope = jnp.exp2(-8.0 / H * (jnp.full((1, 1), head, jnp.int32).astype(jnp.float32) + 1.0))
        for g in range(2):
            query = (q_high[g, :, at] * mask, q_low[g, :, at] * mask)
            scores = three(query, (k_high[g, :, at], k_low[g, :, at]), NT)
            scores = jnp.where(allowed[...] > 0, scores * scaling - slope * distance[...], -1e30)
            prob = softmax_last(scores)
            probs[head, g] = prob
            value = (v_high[g, :, at] * mask, v_low[g, :, at] * mask)
            total[g, :, at] = total[g, :, at] + three(halves(prob), value, NN)
        return 0

    lax.fori_loop(0, H, step, 0, unroll=4)
    for g in range(2):
        out[:, g * GROUP : (g + 1) * GROUP, :] = total[g].reshape(slots, GROUP, width)


def frame_tables(frame_pos):
    slots = frame_pos.shape[0]
    position = jnp.repeat(frame_pos, GROUP)
    column = jnp.tile(jnp.arange(GROUP), slots)
    distance = jnp.abs(position[:, None] - position[None, :])
    same = column[:, None] == column[None, :]
    return distance, (same & (position[None, :] < FRAMES - 0.5)).astype(jnp.float32)


VMEM_SPEC = pl.BlockSpec(memory_space=pltpu.VMEM)


def frame_attention(qkv, b_query, b_value, distance, allowed):
    slots, cols, width = qkv.shape[0], qkv.shape[1], qkv.shape[2] // 3
    rows = slots * GROUP
    part = pltpu.VMEM((2, rows, width), jnp.bfloat16)
    return pl.pallas_call(
        frame_attention_kernel,
        out_shape=(
            jax.ShapeDtypeStruct((H, 2, rows, rows), jnp.float32),
            jax.ShapeDtypeStruct((slots, cols, width), jnp.float32),
        ),
        in_specs=[VMEM_SPEC] * 5,
        out_specs=[VMEM_SPEC] * 2,
        scratch_shapes=[part] * 6 + [pltpu.VMEM((2, rows, width), jnp.float32)],
        compiler_params=pltpu.CompilerParams(vmem_limit_bytes=40 << 20),
        cost_estimate=LIGHT,
    )(qkv, b_query.reshape(1, width), b_value.reshape(1, width), distance, allowed)


def frame_attention_back_kernel(qkv, b_query, b_value, probs, attended, grad, out, *split):
    width = attended.shape[-1]
    slots, head_dim = qkv.shape[0], width // H
    scaling = head_dim**-0.5
    names = [(split[2 * i], split[2 * i + 1]) for i in range(4)]
    (q_high, q_low), (k_high, k_low), (v_high, v_low), (g_high, g_low) = names
    total, product = split[8], split[9]
    for g in range(2):
        store_halves(q_high, q_low, g, grouped(qkv, g, slice(0, width)) + b_query[...])
        store_halves(k_high, k_low, g, grouped(qkv, g, slice(width, 2 * width)))
        store_halves(
            v_high, v_low, g, grouped(qkv, g, slice(2 * width, 3 * width)) + b_value[...]
        )
        upstream = grouped(grad, g, slice(0, width))
        store_halves(g_high, g_low, g, upstream)
        product[g] = upstream * grouped(attended, g, slice(0, width))
    total[...] = jnp.zeros(total.shape, jnp.float32)

    def step(head, _):
        at, mask = head_window(head, head_dim, width)
        small = mask.astype(jnp.bfloat16)

        def masked(high, low, g):
            return high[g, :, at] * small, low[g, :, at] * small

        for g in range(2):
            upstream = masked(g_high, g_low, g)
            prob = probs[head, g]
            grad_prob = three(upstream, (v_high[g, :, at], v_low[g, :, at]), NT)
            term = jnp.sum(product[g, :, at] * mask, axis=-1, keepdims=True)
            score = halves(prob * (grad_prob - term) * scaling)
            total[0, g, :, at] = total[0, g, :, at] + three(score, masked(k_high, k_low, g), NN)
            total[1, g, :, at] = total[1, g, :, at] + three(score, masked(q_high, q_low, g), TN)
            total[2, g, :, at] = total[2, g, :, at] + three(halves(prob), upstream, TN)
        return 0

    lax.fori_loop(0, H, step, 0, unroll=4)
    for g in range(2):
        for i in range(3):
            out[:, g * GROUP : (g + 1) * GROUP, i * width : (i + 1) * width] = total[
                i, g
            ].reshape(slots, GROUP, width)


def frame_attention_back(qkv, b_query, b_value, probs, attended, grad):
    slots, cols, width = attended.shape
    rows = slots * GROUP
    part = pltpu.VMEM((2, rows, width), jnp.bfloat16)
    return pl.pallas_call(
        frame_attention_back_kernel,
        out_shape=jax.ShapeDtypeStruct((slots, cols, 3 * width), jnp.float32),
        in_specs=[VMEM_SPEC] * 6,
        out_specs=VMEM_SPEC,
        scratch_shapes=[part] * 8
        + [pltpu.VMEM((3, 2, rows, width), jnp.float32), pltpu.VMEM((2, rows, width), jnp.float32)],
        compiler_params=pltpu.CompilerParams(vmem_limit_bytes=48 << 20),
        cost_estimate=LIGHT,
    )(qkv, b_query.reshape(1, width), b_value.reshape(1, width), probs, attended, grad)


def cross_attention_kernel(queries, b_query, kv, b_value, allowed, probs, out, *split):
    q_high, q_low, k_high, k_low, v_high, v_low = split
    width = out.shape[-1]
    head_dim = width // H
    scaling = head_dim**-0.5
    store_halves(q_high, q_low, Ellipsis, queries[...] + b_query[...])
    store_halves(k_high, k_low, Ellipsis, kv[:, 0:width])
    store_halves(v_high, v_low, Ellipsis, kv[:, width : 2 * width] + b_value[...])
    out[...] = jnp.zeros(out.shape, jnp.float32)

    def step(head, _):
        at, mask = head_window(head, head_dim, width)
        mask = mask.astype(jnp.bfloat16)
        query = (q_high[:, at] * mask, q_low[:, at] * mask)
        scores = three(query, (k_high[:, at], k_low[:, at]), NT)
        prob = softmax_last(jnp.where(allowed[...] > 0, scores * scaling, -1e30))
        probs[head] = prob
        value = (v_high[:, at] * mask, v_low[:, at] * mask)
        out[:, at] = out[:, at] + three(halves(prob), value, NN)
        return 0

    lax.fori_loop(0, H, step, 0, unroll=4)


def cross_attention(queries, b_query, kv, b_value, allowed):
    rows, width = queries.shape
    keys = kv.shape[0]
    q_part = pltpu.VMEM((rows, width), jnp.bfloat16)
    k_part = pltpu.VMEM((keys, width), jnp.bfloat16)
    return pl.pallas_call(
        cross_attention_kernel,
        out_shape=(
            jax.ShapeDtypeStruct((H, rows, keys), jnp.float32),
            jax.ShapeDtypeStruct((rows, width), jnp.float32),
        ),
        in_specs=[VMEM_SPEC] * 5,
        out_specs=[VMEM_SPEC] * 2,
        scratch_shapes=[q_part] * 2 + [k_part] * 4,
        compiler_params=pltpu.CompilerParams(vmem_limit_bytes=48 << 20),
        cost_estimate=LIGHT,
    )(queries, b_query.reshape(1, width), kv, b_value.reshape(1, width), allowed)


def cross_attention_back_kernel(
    queries, b_query, kv, b_value, probs, attended, grad, grad_q, grad_kv, *split
):
    names = [(split[2 * i], split[2 * i + 1]) for i in range(4)]
    (q_high, q_low), (g_high, g_low), (k_high, k_low), (v_high, v_low) = names
    product = split[8]
    width = grad_q.shape[-1]
    head_dim = width // H
    scaling = head_dim**-0.5
    store_halves(q_high, q_low, Ellipsis, queries[...] + b_query[...])
    store_halves(k_high, k_low, Ellipsis, kv[:, 0:width])
    store_halves(v_high, v_low, Ellipsis, kv[:, width : 2 * width] + b_value[...])
    store_halves(g_high, g_low, Ellipsis, grad[...])
    product[...] = grad[...] * attended[...]
    grad_q[...] = jnp.zeros(grad_q.shape, jnp.float32)
    grad_kv[...] = jnp.zeros(grad_kv.shape, jnp.float32)

    def step(head, _):
        at, mask = head_window(head, head_dim, width)
        start = jnp.minimum(head * head_dim // 128 * 128, width - WINDOW)
        at_value = pl.ds(pl.multiple_of(start + width, 128), WINDOW)
        small = mask.astype(jnp.bfloat16)

        def masked(high, low):
            return high[:, at] * small, low[:, at] * small

        upstream = masked(g_high, g_low)
        prob = probs[head]
        grad_prob = three(upstream, (v_high[:, at], v_low[:, at]), NT)
        term = jnp.sum(product[:, at] * mask, axis=-1, keepdims=True)
        score = halves(prob * (grad_prob - term) * scaling)
        grad_q[:, at] = grad_q[:, at] + three(score, masked(k_high, k_low), NN)
        grad_kv[:, at] = grad_kv[:, at] + three(score, masked(q_high, q_low), TN)
        grad_kv[:, at_value] = grad_kv[:, at_value] + three(halves(prob), upstream, TN)
        return 0

    lax.fori_loop(0, H, step, 0, unroll=4)


def cross_attention_back(queries, b_query, kv, b_value, probs, attended, grad):
    rows, width = queries.shape
    keys = kv.shape[0]
    q_part = pltpu.VMEM((rows, width), jnp.bfloat16)
    k_part = pltpu.VMEM((keys, width), jnp.bfloat16)
    return pl.pallas_call(
        cross_attention_back_kernel,
        out_shape=(
            jax.ShapeDtypeStruct((rows, width), jnp.float32),
            jax.ShapeDtypeStruct(kv.shape, jnp.float32),
        ),
        in_specs=[VMEM_SPEC] * 7,
        out_specs=[VMEM_SPEC] * 2,
        scratch_shapes=[q_part] * 4 + [k_part] * 4 + [pltpu.VMEM((rows, width), jnp.float32)],
        compiler_params=pltpu.CompilerParams(vmem_limit_bytes=52 << 20),
        cost_estimate=LIGHT,
    )(queries, b_query.reshape(1, width), kv, b_value.reshape(1, width), probs, attended, grad)


MLP_ROWS = 256


def mlp_kernel(
    hidden, cotangent, w_first, b_first, w_second,
    grad_hidden, out, grad_first, grad_second, grad_bias,
    first_high, first_low, second_high, second_low,
):
    @pl.when(pl.program_id(0) == 0)
    def _():
        first_high[...], first_low[...] = halves(w_first[...])
        second_high[...], second_low[...] = halves(w_second[...])
        grad_first[...] = jnp.zeros(grad_first.shape, jnp.float32)
        grad_second[...] = jnp.zeros(grad_second.shape, jnp.float32)
        grad_bias[...] = jnp.zeros(grad_bias.shape, jnp.float32)

    first = (first_high[...], first_low[...])
    second = (second_high[...], second_low[...])
    tokens, upstream = halves(hidden[...]), halves(cotangent[...])
    u = three(tokens, first, NN) + b_first[...]
    slope = math.sqrt(2.0 / math.pi)
    t = jnp.tanh(slope * (u + 0.044715 * (u * u * u)))
    active = halves(0.5 * u * (1.0 + t))
    derivative = 0.5 * (1.0 + t) + 0.5 * u * (1.0 - t * t) * slope * (1.0 + 0.134145 * (u * u))
    grad_pre = three(upstream, second, NT) * derivative
    grad_bias[...] = grad_bias[...] + jnp.sum(grad_pre, axis=0, keepdims=True)
    grad_pre = halves(grad_pre)
    grad_hidden[...] = three(grad_pre, first, NT)
    out[...] = three(active, second, NN)
    grad_first[...] = grad_first[...] + three(tokens, grad_pre, TN)
    grad_second[...] = grad_second[...] + three(active, upstream, TN)


def mlp(hidden, cotangent, w_first, b_first, w_second):
    rows, width = hidden.shape
    units = w_first.shape[1]
    f32 = jnp.float32
    tile = pl.BlockSpec((MLP_ROWS, width), lambda i: (i, 0))

    def fixed(*shape):
        return pl.BlockSpec(shape, lambda i: (0, 0))

    return pl.pallas_call(
        mlp_kernel,
        grid=(rows // MLP_ROWS,),
        out_shape=(
            jax.ShapeDtypeStruct((rows, width), f32), jax.ShapeDtypeStruct((rows, width), f32),
            jax.ShapeDtypeStruct((width, units), f32), jax.ShapeDtypeStruct((units, width), f32),
            jax.ShapeDtypeStruct((1, units), f32),
        ),
        in_specs=[tile, tile, fixed(width, units), fixed(1, units), fixed(units, width)],
        out_specs=[tile, tile, fixed(width, units), fixed(units, width), fixed(1, units)],
        scratch_shapes=[
            pltpu.VMEM((width, units), jnp.bfloat16), pltpu.VMEM((width, units), jnp.bfloat16),
            pltpu.VMEM((units, width), jnp.bfloat16), pltpu.VMEM((units, width), jnp.bfloat16),
        ],
        compiler_params=pltpu.CompilerParams(vmem_limit_bytes=50 << 20),
        cost_estimate=LIGHT,
    )(hidden, cotangent, w_first, b_first.reshape(1, units), w_second)


def assemble_kernel(axis, dim, *refs):
    blocks, whole = refs[:-1], refs[-1]
    own = lax.axis_index(axis)
    for k, block in enumerate(blocks):
        length = block.shape[dim]
        start = pl.multiple_of((own ^ k) * length, length)
        where = (slice(None),) * dim + (pl.ds(start, length),)
        whole[where] = block[...]


def assemble(blocks, axis, dim):
    shape = list(blocks[0].shape)
    shape[dim] *= len(blocks)
    size = 4 * len(blocks) * blocks[0].size
    return pl.pallas_call(
        partial(assemble_kernel, axis, dim),
        out_shape=jax.ShapeDtypeStruct(tuple(shape), jnp.float32),
        in_specs=[pl.BlockSpec(memory_space=pltpu.VMEM)] * len(blocks),
        out_specs=pl.BlockSpec(memory_space=pltpu.VMEM),
        compiler_params=pltpu.CompilerParams(vmem_limit_bytes=24 << 20),
        cost_estimate=LIGHT,
    )(*blocks)


def gather_rows(shard):
    return lax.all_gather(shard, "patch", axis=0, tiled=True)


def scatter_rows(whole):
    return lax.psum_scatter(whole, "patch", scatter_dimension=0, tiled=True)


def gather_tokens(rows):
    return token_gather(rows) if small_patch() else gather_rows(rows)


def block_of(array, axis_name, k, dim):
    length = array.shape[dim] // lax.axis_size(axis_name)
    start = (lax.axis_index(axis_name) ^ k) * length
    return lax.dynamic_slice_in_dim(array, start, length, axis=dim)


def over_chips(blocks):
    return [
        blocks[0],
        swap(blocks[1], "patch", 2),
        swap(blocks[2], "patch", 4),
        swap(blocks[3], "patch", 6),
    ]


def to_own_columns(weight):
    if not small_patch():
        return lax.all_to_all(weight, "patch", 1, 0, tiled=True)
    length = weight.shape[0]
    blocks = [block_of(weight, "patch", k, 1) for k in range(8)]
    theirs = swap(jnp.concatenate(blocks[1::2], axis=0), "patch", 1)
    both = [
        jnp.concatenate([kept, theirs[j * length : (j + 1) * length]], axis=0)
        for j, kept in enumerate(blocks[::2])
    ]
    halves = []
    for block in over_chips(both):
        halves += [block[:length], block[length:]]
    return assemble(halves, "patch", 0)


def to_columns(x):
    return lax.all_to_all(x, "frame", split_axis=1, concat_axis=0, tiled=True)


def to_slots(x):
    return lax.all_to_all(x, "frame", split_axis=0, concat_axis=1, tiled=True)


def scatter_tokens(parts):
    return token_scatter(parts) if small_patch() else scatter_rows(parts)


def open_up(block_input, cotangent, frame_slot, small, kv_part, weight):
    frame_number = frame_slot.astype(jnp.float32)
    if not small_patch():
        kv = all_sum(kv_part, "patch")
        return (
            to_columns(block_input),
            to_columns(cotangent),
            all_sum(placed(frame_number, "frame"), "frame"),
            all_sum(small, "patch"),
            lax.all_gather(kv, "frame", axis=0, tiled=True),
            gather_rows(weight),
        )
    count = frame_slot.shape[0]
    rows = -(-small.shape[0] // 1024) * 8
    tokens, later, slots, summed, kv, whole = begin(
        block_input, cotangent, padded(frame_number, 8), padded(small, rows), kv_part, weight
    )
    summed = summed.reshape(-1)[: small.shape[0]]
    slots = slots[:, 0, :count].reshape(-1)
    return tokens, later, slots, summed, kv, whole


def mlp_part(hidden, cotangent, w_first, b_first, w_second):
    if small_patch():
        *parts, grad_bias = mlp(hidden, cotangent, w_first, b_first, w_second)
        return (*parts, grad_bias[0])
    pre = matmul(hidden, w_first) + b_first
    active, pull = jax.vjp(partial(jax.nn.gelu, approximate=True), pre)
    grad_pre = pull(matmul_nt(cotangent, w_second))[0]
    return (
        matmul_nt(grad_pre, w_first),
        matmul(active, w_second),
        matmul_tn(hidden, grad_pre),
        matmul_tn(active, cotangent),
        jnp.sum(grad_pre, axis=0),
    )


def mid_way(parts, kv, residual, gate, bias, weights):
    if not small_patch():
        kv = lax.psum_scatter(all_sum(kv, "patch"), "frame", scatter_dimension=0, tiled=True)
        total = scatter_rows(parts)
        block = residual + gate * (total + bias).reshape(residual.shape)
        return total, kv, to_slots(block), [scatter_rows(w) for w in weights]
    total, kv, block, *weights = middle(parts, kv, residual, gate, bias, *weights)
    return total, kv, block, weights


def close_up(weights, kv, tokens, small, caption, columns):
    clips, length = lax.axis_size("frame"), caption.shape[1]
    if not small_patch():
        weights = [scatter_rows(weights[0]), *weights[1:]]
        weights = [lax.psum(w, "frame") for w in weights]
        whole = lax.all_gather(caption, "patch", axis=0, tiled=True)
        whole = lax.all_gather(whole, "frame", axis=0)
        whole = jnp.transpose(whole, (0, 2, 1))
        small = all_sum(all_sum(small, "patch"), "frame")
        columns = lax.all_to_all(columns, "patch", 0, 1, tiled=True)
        return weights, lax.psum(kv, "frame"), to_slots(tokens), small, whole, columns
    rows = -(-small.shape[0] // 1024) * 8
    *weights, kv, tokens, summed, whole, blocks = finish(
        *weights, kv, tokens, padded(small, rows), caption, columns
    )
    columns = jnp.transpose(blocks, (1, 0, 2)).reshape(blocks.shape[1], -1)
    whole = jnp.transpose(whole, (1, 3, 0, 2)).reshape(clips, length, -1)
    return weights, kv, tokens, summed.reshape(-1)[: small.shape[0]], whole, columns


def on_device(
    block_input,
    out_cotangent,
    caption,
    cond,
    ada_weight,
    ada_bias,
    qkv_weight,
    q_bias,
    v_bias,
    attn_out_weight,
    attn_out_bias,
    cross_q_weight,
    cross_q_bias,
    cross_kv_weight,
    cross_v_bias,
    cross_out_weight,
    cross_out_bias,
    fc1_weight,
    fc1_bias,
    fc2_weight,
    fc2_bias,
    frame_slot,
    clip_id,
    patch_mask,
    caption_mask,
):
    width = block_input.shape[-1]
    cond_act, silu_pull = jax.vjp(jax.nn.silu, cond)
    cond_own = own_part(cond_act, "patch", 1)
    modulation_part = matmul(cond_own, ada_weight)
    biases = (
        ada_bias, q_bias, v_bias, attn_out_bias, cross_q_bias, cross_v_bias, cross_out_bias,
        fc2_bias,
    )
    small = jnp.concatenate(
        [modulation_part.reshape(-1), placed(jnp.concatenate(biases), "patch")]
    )
    caption_rows = caption.reshape(CLIPS * CAP, width)
    caption_share = own_part(own_part(caption_rows, "frame", 0), "patch", 1)
    tokens_in, cotangent, frame_pos, small, caption_kv, w_qkv = open_up(
        block_input,
        out_cotangent,
        frame_slot,
        small,
        matmul(caption_share, cross_kv_weight),
        qkv_weight,
    )
    w_three = gather_rows(
        jnp.concatenate([attn_out_weight, cross_q_weight, cross_out_weight], axis=1)
    )
    w_attn, w_cross_q, w_cross_o = jnp.split(w_three, 3, axis=1)
    slots, cols, _ = tokens_in.shape
    rows = slots * cols
    clip_own = own_part(clip_id, "frame", 0)
    column_mask = own_part(patch_mask, "frame", 0).astype(jnp.float32)[:, None]
    place = modulation_part.size
    modulation = small[:place].reshape(modulation_part.shape)
    table = small[place:].reshape(lax.axis_size("patch"), -1)
    whole, place = [], 0
    for b in biases:
        whole.append(table[:, place : place + b.shape[0]].reshape(-1))
        place += b.shape[0]
    b_ada, b_query, b_value, b_attn, b_cross_q, b_cross_v, b_cross_o, b_second = whole
    modulation = modulation + b_ada
    clip_onehot = (clip_own[:, None] == jnp.arange(CLIPS, dtype=jnp.int32)[None, :]).astype(
        jnp.float32
    )
    per_column = jnp.dot(clip_onehot, modulation, precision=lax.Precision.HIGHEST)
    shift_one, scale_one, gate_one, shift_two, scale_two, gate_two = jnp.split(
        per_column, 6, axis=1
    )

    grad_mlp = (column_mask * gate_two * cotangent).reshape(rows, width)
    normed_one, inverse_one = normalize(tokens_in)
    hidden_one = (normed_one * (1.0 + scale_one) + shift_one).reshape(rows, width)
    qkv_rows = matmul(hidden_one, w_qkv)
    grad_mlp_all = gather_rows(after(grad_mlp, qkv_rows))
    qkv = qkv_rows.reshape(slots, cols, 3 * width)
    probs, attended = frame_attention(qkv, b_query, b_value, *frame_tables(frame_pos))
    attended_rows = attended.reshape(rows, width)
    attn_branch = (matmul(attended_rows, w_attn) + b_attn).reshape(slots, cols, width)
    after_attn = tokens_in + column_mask * gate_one * attn_branch
    after_attn_rows = after_attn.reshape(rows, width)
    cross_queries = matmul(after_attn_rows, w_cross_q)
    w_first = to_own_columns(after(fc1_weight, cross_queries))
    cross_queries = after(cross_queries, grad_mlp_all)
    key_clip = jnp.arange(CLIPS * CAP, dtype=jnp.int32) // CAP
    caption_ok = (clip_own[:, None] == key_clip[None, :]) & (
        caption_mask.reshape(CLIPS * CAP)[None, :] > 0
    )
    caption_ok = jnp.tile(caption_ok.astype(jnp.float32), (slots, 1))
    cross_probs, cross_rows = cross_attention(
        cross_queries, b_cross_q, caption_kv, b_cross_v, caption_ok
    )
    cross_branch = (matmul(cross_rows, w_cross_o) + b_cross_o).reshape(slots, cols, width)
    after_cross = after_attn + column_mask * cross_branch
    normed_two, inverse_two = normalize(after_cross)
    hidden_two = (normed_two * (1.0 + scale_two) + shift_two).reshape(rows, width)

    hidden_all = gather_tokens(after(hidden_two, w_first))
    grad_parts, mlp_parts, grad_w_first, grad_w_second, grad_b_first = mlp_part(
        hidden_all, grad_mlp_all, w_first, fc1_bias, fc2_weight
    )
    grad_hidden_two = scatter_tokens(grad_parts)
    grad_hidden_two = grad_hidden_two.reshape(slots, cols, width)
    grad_b_second = jnp.sum(grad_mlp, axis=0)

    grad_shift_two = jnp.sum(grad_hidden_two, axis=0)
    grad_scale_two = jnp.sum(grad_hidden_two * normed_two, axis=0)
    grad_after_cross = cotangent + normalize_back(
        grad_hidden_two * (1.0 + scale_two), normed_two, inverse_two
    )
    grad_cross_branch = (column_mask * grad_after_cross).reshape(rows, width)
    grad_w_cross_o = matmul_tn(cross_rows, grad_cross_branch)
    grad_b_cross_o = jnp.sum(grad_cross_branch, axis=0)
    grad_w_first = lax.psum(grad_w_first, "frame")
    grad_w_second = lax.psum(after(grad_w_second, grad_w_first), "frame")
    grad_cross_rows = matmul_nt(grad_cross_branch, w_cross_o)
    grad_cross_queries, grad_kv = cross_attention_back(
        cross_queries, b_cross_q, caption_kv, b_cross_v, cross_probs, cross_rows, grad_cross_rows
    )
    grad_cross_queries = after(grad_cross_queries, grad_w_first)
    grad_w_cross_q = matmul_tn(after_attn_rows, grad_cross_queries)
    grad_b_cross_q = jnp.sum(grad_cross_queries, axis=0)
    grad_cross_queries = after(grad_cross_queries, grad_w_cross_q)
    grad_after_attn = grad_after_cross + matmul_nt(grad_cross_queries, w_cross_q).reshape(
        slots, cols, width
    )
    grad_attn_rows = (column_mask * gate_one * grad_after_attn).reshape(rows, width)
    grad_gate_one = jnp.sum(column_mask * attn_branch * grad_after_attn, axis=0)
    grad_w_attn = matmul_tn(attended_rows, grad_attn_rows)
    grad_b_attn = jnp.sum(grad_attn_rows, axis=0)
    grad_attn_rows = after(grad_attn_rows, grad_w_attn)
    grad_attended = matmul_nt(grad_attn_rows, w_attn).reshape(slots, cols, width)
    grad_qkv = frame_attention_back(
        qkv, b_query, b_value, probs, attended, grad_attended
    ).reshape(rows, 3 * width)
    grad_w_qkv = matmul_tn(hidden_one, grad_qkv)
    mlp_sum, grad_kv_share, block_out, shares = mid_way(
        after(mlp_parts, grad_w_qkv),
        grad_kv,
        after_cross,
        column_mask * gate_two,
        b_second,
        (grad_w_attn, grad_w_cross_q, grad_w_cross_o),
    )
    grad_w_cross_kv = matmul_tn(caption_share, grad_kv_share)
    grad_b_cross_v = jnp.sum(grad_kv_share[:, width:], axis=0)
    grad_caption_share = matmul_nt(cross_kv_weight, grad_kv_share)
    mlp_branch = (mlp_sum + b_second).reshape(slots, cols, width)
    grad_gate_two = jnp.sum(column_mask * mlp_branch * cotangent, axis=0)
    grad_b_query = jnp.sum(grad_qkv[:, :width], axis=0)
    grad_b_value = jnp.sum(grad_qkv[:, 2 * width :], axis=0)
    grad_hidden_one = matmul_nt(grad_qkv, w_qkv).reshape(slots, cols, width)
    grad_shift_one = jnp.sum(grad_hidden_one, axis=0)
    grad_scale_one = jnp.sum(grad_hidden_one * normed_one, axis=0)
    input_grad = grad_after_attn + normalize_back(
        grad_hidden_one * (1.0 + scale_one), normed_one, inverse_one
    )
    grad_per_column = jnp.concatenate(
        [
            grad_shift_one,
            grad_scale_one,
            grad_gate_one,
            grad_shift_two,
            grad_scale_two,
            grad_gate_two,
        ],
        axis=1,
    )
    grad_modulation_part = jnp.dot(
        clip_onehot.T, grad_per_column, precision=lax.Precision.HIGHEST
    )
    first = (lax.axis_index("patch") == 0).astype(jnp.float32)
    bias_grads = (
        grad_b_query,
        grad_b_value,
        grad_b_attn,
        grad_b_cross_q,
        grad_b_cross_v * first,
        grad_b_cross_o,
        grad_b_second,
    )
    bias_rows = jnp.concatenate(
        [b.reshape(lax.axis_size("patch"), -1) for b in bias_grads]
        + [placed(grad_b_first, "patch").reshape(lax.axis_size("patch"), -1)],
        axis=1,
    )
    small_grads = jnp.concatenate([grad_modulation_part.reshape(-1), bias_rows.reshape(-1)])
    weights, grad_w_cross_kv, input_grad, small_grads, grad_caption, grad_w_first = close_up(
        (grad_w_qkv, *shares),
        grad_w_cross_kv, input_grad, small_grads, grad_caption_share, grad_w_first,
    )
    place = grad_modulation_part.size
    grad_modulation = small_grads[:place].reshape(grad_modulation_part.shape)
    own_row = own_part(small_grads[place:], "patch", 0)
    length = bias_grads[0].shape[0] // lax.axis_size("patch")
    g_query, g_value, g_attn, g_cross_q, g_cross_v, g_cross_o, g_second = (
        own_row[i * length : (i + 1) * length] for i in range(7)
    )
    grad_b_first = own_row[7 * length :]
    grad_w_ada = matmul_tn(cond_own, grad_modulation)
    grad_b_ada = own_part(jnp.sum(grad_modulation, axis=0), "patch", 0)
    grad_cond_own = matmul_nt(grad_modulation, ada_weight)
    if small_patch():
        grad_cond_act = jnp.transpose(spread(grad_cond_own), (1, 0, 2)).reshape(cond.shape)
    else:
        grad_cond_act = all_sum(placed(grad_cond_own, "patch"), "patch")
    grad_cond = silu_pull(grad_cond_act)[0]

    grad_w_qkv, grad_w_attn, grad_w_cross_q, grad_w_cross_o = weights
    return (
        block_out,
        input_grad,
        grad_caption,
        grad_cond,
        grad_w_ada,
        grad_b_ada,
        grad_w_qkv,
        g_query,
        g_value,
        grad_w_attn,
        g_attn,
        grad_w_cross_q,
        g_cross_q,
        grad_w_cross_kv,
        g_cross_v,
        grad_w_cross_o,
        g_cross_o,
        grad_w_first,
        grad_b_first,
        grad_w_second,
        g_second,
    )


def solution(mesh):
    tokens = P("frame", "patch", None)
    weight = P("patch", None)
    vector = P("patch")
    parameters = (
        weight, vector, weight, vector, vector, weight, vector, weight, vector,
        weight, vector, weight, vector, weight, vector, weight, vector,
    )
    in_specs = (tokens, tokens, P(), P()) + parameters + (P("frame"), vector, vector, P())
    out_specs = (tokens, tokens, P(), P()) + parameters
    return jax.shard_map(
        on_device, mesh=mesh, in_specs=in_specs, out_specs=out_specs, check_vma=False
    )
```
